32 devices in a mesh: wide: 8 (over z, y), narrow: 4 (over x, core).
Axes of the slice: x: 2, y: 2, z: 4, core: 2. Of those that a mesh axis runs over, the one named last changes fastest.
Arguments:
- hidden: bfloat16 [8, 1024, 1024], P('wide', 'narrow'), may hold values from -6 to 6
- lengths: int32 [8], P('wide'), may hold values from 256 to 1024, as said below
- routes: int32 [8, 1024, 8], P('wide', 'narrow'), may hold values from 0 to 31, all different within a row; in each aligned block of 256 rows (0 to 255, 256 to 511, ..., all dimensions but the last counted through in order) at most 128 rows name the same one
- cotangent: bfloat16 [8, 1024, 1024], P('wide', 'narrow'), may hold values from -6 to 6
- attn_gain: float32 [1024], replicated, may hold values from 0.1 to 1.9
- w_query: bfloat16 [1024, 1024], P(None, 'narrow'), may hold values from -0.1875 to 0.1875
- w_key: bfloat16 [1024, 512], P(None, 'narrow'), may hold values from -0.1875 to 0.1875
- w_value: bfloat16 [1024, 512], P(None, 'narrow'), may hold values from -0.1875 to 0.1875
- w_out: bfloat16 [1024, 1024], P('narrow'), may hold values from -3 to 3
- moe_gain: float32 [1024], replicated, may hold values from 0.1 to 1.9
- w_router: bfloat16 [1024, 32], replicated, may hold values from -0.09375 to 0.09375
- w_gate_up: bfloat16 [32, 1024, 1024], P('wide'), may hold values from -0.1875 to 0.1875
- w_down: bfloat16 [32, 512, 1024], P('wide'), may hold values from -1 to 1
Outputs:
- out: bfloat16 [8, 1024, 1024], P('wide', 'narrow')
- grad_hidden: bfloat16 [8, 1024, 1024], P('wide', 'narrow')
- grad_attn_gain: float32 [1024], replicated
- grad_query: float32 [1024, 1024], P(None, 'narrow')
- grad_key: float32 [1024, 512], P(None, 'narrow')
- grad_value: float32 [1024, 512], P(None, 'narrow')
- grad_out: float32 [1024, 1024], P('narrow')
- grad_moe_gain: float32 [1024], replicated
- grad_router: float32 [1024, 32], replicated
- grad_gate_up: float32 [32, 1024, 1024], P('wide')
- grad_down: float32 [32, 512, 1024], P('wide')
The draws below stay inside these ranges and needn't reach their ends.
Inputs may be any that keep to these rules, and one draw needn't show every extreme that they name: Row lengths; every row reaches 256 or more, one row has all 1024 positions and one exactly 256. A token's 8 routes name different experts. Within the 256 positions of one device (aligned blocks of a row) no expert is named by more than 128 tokens, a bound that some block reaches. Positions past a row's length carry routes too.
All inputs are finite; a program needn't handle non-finite values.
Results may differ from the reference program's by a relative error of at most 0.028.
Values may be sent and summed in bfloat16 or wider, within the bound.
A program may use at most 192 MiB of HBM per device.

```python
import math
import jax
import jax.numpy as jnp
import numpy as np
from jax import lax

D = 1024
HEADS = 16
KV_HEADS = 8
HEAD_DIM = 64
EXPERTS = 32
FFE = 512
TOPK = 8
SEQ = 1024
MIN_LEN = 256
ROWS = 8
T_DEV = 256
CAP = 128


def draw_lengths(key, part):
    key = jax.random.fold_in(key, 7)
    first, second, third = jax.random.split(key, 3)
    drawn = jax.random.randint(first, (ROWS,), MIN_LEN, SEQ + 1)
    longest = jax.random.randint(second, (), 0, ROWS)
    shortest = (longest + jax.random.randint(third, (), 1, ROWS)) % ROWS
    drawn = drawn.at[longest].set(SEQ)
    drawn = drawn.at[shortest].set(MIN_LEN)
    return drawn.astype(jnp.int32)


def block_levels(key, extent, shards, smallest, high):
    factor_of, own = 1.0, jax.random.fold_in(key, 6)
    for position, shards_of in shards:
        draws = jnp.exp(jax.random.uniform(jax.random.fold_in(own, position), (shards_of,), jnp.float32, smallest / len(shards), high / len(shards)))
        factor_of = factor_of * jnp.repeat(draws, extent[position] // shards_of).reshape([-1 if axis == position else 1 for axis in range(len(extent))])
    return factor_of


def assign_block(rng, own, number, rows, count, top, most, lean):
    order = jax.random.permutation(rng, count)
    heavy_load, common = portions_of(count, rows * top, most, lean, True), portions_of(count, rows * top, most, lean, False)
    places = jnp.arange(count)

    def named(sizes, offset_by):
        used = int((sizes > 0).sum())
        fixed = max(1, used // 4)
        moved = fixed + (places - fixed + offset_by * (used - fixed)) % max(1, count - fixed)
        return jnp.zeros((count,), jnp.int32).at[order[jnp.where(places < fixed, places, moved)]].set(jnp.asarray(sizes, jnp.int32))

    sizes = jnp.where(number % 4 == 0, named(heavy_load, number // 4), named(common, number - number // 4 - 1))
    mixed = jax.random.permutation(jax.random.fold_in(own, 3), count)
    donor, sink = mixed[0:count // 2 * 2:2], mixed[1:count // 2 * 2:2]
    room = jnp.minimum(sizes[donor] - 1, most - sizes[sink]) // 2
    room = jnp.where((donor == order[0]) | (sink == order[0]) | (sizes[sink] == 0), 0, jnp.maximum(room, 0))
    moved = jax.random.randint(jax.random.fold_in(own, 4), (count // 2,), 0, 1 << 20) % (room + 1)
    sizes = sizes.at[donor].add(-moved).at[sink].add(moved)
    items = jnp.searchsorted(jnp.cumsum(sizes), jnp.arange(rows * top), side="right").astype(jnp.int32)
    grid = items.reshape(top, rows).T
    grid = grid[jax.random.permutation(jax.random.fold_in(own, 1), rows)]
    offset_by = jax.random.randint(jax.random.fold_in(own, 2), (rows, 1), 0, top)
    return jnp.take_along_axis(grid, (jnp.arange(top)[None, :] + offset_by) % top, axis=1)


def portions_of(number_of, total, reach, lean, full):
    portions = [(1 << 20) // math.isqrt(rank ** lean) + 1 for rank in range(1, number_of + 1)]
    largest = reach if full else min(reach, max(-(-total // number_of), total * portions[0] // sum(portions)))
    least = 1 if total - largest >= number_of - 1 else 0
    given, spare = [largest] + [least] * (number_of - 1), total - largest - least * (number_of - 1)
    while spare > 0:
        movable = [i for i in range(1, number_of) if given[i] < largest] or [i for i in range(1, number_of) if given[i] < reach]
        pool, remaining = sum([portions[i] for i in movable]), spare
        for i in movable:
            addition = min(reach - given[i], max(1, remaining * portions[i] // pool), spare)
            given[i] = given[i] + addition
            spare = spare - addition
    return np.array(given)


def centred(stream_key, dims, width, bound, shards=(), kind=jnp.bfloat16):
    values = jax.random.normal(stream_key, dims, jnp.float32) * width
    if len(shards) > 0:
        values = block_levels(stream_key, dims, shards, -0.22, 0.18) * values
    return jnp.clip(values, min=-bound, max=bound).astype(kind)


def setup_inputs(seed: int = 0) -> dict:
    seeds = jax.random.split(jax.random.key(seed), 14)
    hidden = centred(seeds[0], (ROWS, SEQ, D), 1.0, 6.0, ((0, 8), (1, 4)))
    lengths = draw_lengths(jax.random.fold_in(seeds[13], 71), 0)
    routes_keys = jax.random.split(jax.random.fold_in(seeds[2], 1), ROWS * SEQ // T_DEV)
    routes_turns = jax.random.permutation(jax.random.fold_in(seeds[2], 3), ROWS * SEQ // T_DEV)
    routes = jax.vmap(lambda own, number: assign_block(jax.random.fold_in(seeds[2], 2), own, number, T_DEV, EXPERTS, TOPK, CAP, 1))(routes_keys, routes_turns).reshape((ROWS, SEQ, TOPK))
    cotangent = centred(seeds[3], (ROWS, SEQ, D), 1.0, 6.0, ((0, 8), (1, 4)))
    attn_gain = jnp.clip(1.0 + 0.18 * jax.random.normal(seeds[4], (D,), jnp.float32), 0.1, 1.9)
    w_query = centred(seeds[5], (D, HEADS * HEAD_DIM), D ** -0.5, 0.1875, ((1, 4),))
    w_key = centred(seeds[6], (D, KV_HEADS * HEAD_DIM), D ** -0.5, 0.1875, ((1, 4),))
    w_value = centred(seeds[7], (D, KV_HEADS * HEAD_DIM), D ** -0.5, 0.1875, ((1, 4),))
    w_out = centred(seeds[8], (HEADS * HEAD_DIM, D), (max(1, 4 * D // SEQ)) ** -0.5, 3.0, ((0, 4),))
    moe_gain = jnp.clip(1.0 + 0.18 * jax.random.normal(seeds[9], (D,), jnp.float32), 0.1, 1.9)
    w_router = centred(seeds[10], (D, EXPERTS), (4 * D) ** -0.5, 0.09375)
    w_gate_up = centred(seeds[11], (EXPERTS, D, 2 * FFE), D ** -0.5, 0.1875, ((0, 8),))
    w_down = centred(seeds[12], (EXPERTS, FFE, D), (FFE // 16) ** -0.5, 1.0, ((0, 8),))
    return {"hidden": hidden, "lengths": lengths, "routes": routes, "cotangent": cotangent, "attn_gain": attn_gain, "w_query": w_query, "w_key": w_key, "w_value": w_value, "w_out": w_out, "moe_gain": moe_gain, "w_router": w_router, "w_gate_up": w_gate_up, "w_down": w_down}


EPSILON = 1e-06
THETA = 10000.0
HIGHEST = lax.Precision.HIGHEST

@jax.custom_vjp
def low(v):
    return lax.optimization_barrier(v.astype(jnp.bfloat16)).astype(jnp.float32)

@jax.custom_vjp
def low_back(v):
    return v

def low_keep(v):
    return (low(v), None)

def low_pass(kept, grad):
    return (grad,)

def back_keep(v):
    return (v, None)

def back_low(kept, grad):
    return (low(grad),)
low.defvjp(low_keep, low_pass)
low_back.defvjp(back_keep, back_low)

def normalize(values, gain):
    scaling = lax.rsqrt(lax.optimization_barrier(jnp.mean(values * values, axis=-1, keepdims=True)) + EPSILON)
    return values * scaling * gain

def rotate(values, positions):
    half_dim = values.shape[-1] // 2
    inverse = THETA ** (-jnp.arange(half_dim, dtype=jnp.float32) * 2.0 / values.shape[-1])
    angles = positions.astype(jnp.float32)[:, None] * inverse[None, :]
    cosine = jnp.cos(angles)[:, None, :]
    sine_part = jnp.sin(angles)[:, None, :]
    first = values[..., :half_dim]
    second = values[..., half_dim:]
    return jnp.concatenate([first * cosine - second * sine_part, second * cosine + first * sine_part], axis=-1)

def attention(queries, keys_rot, values_low, length_here):
    group_size = HEADS // KV_HEADS
    keys_all = jnp.repeat(keys_rot, group_size, axis=1)
    values_all = jnp.repeat(values_low, group_size, axis=1)
    block_rows = min(512, SEQ)
    key_places = jnp.arange(SEQ, dtype=jnp.int32)

    def one_block(start):
        query_block = lax.dynamic_slice_in_dim(queries, start, block_rows, 0)
        scores = low_back(jnp.einsum('qhd,khd->hqk', query_block, keys_all, precision=HIGHEST) * HEAD_DIM ** (-0.5))
        query_places = start + jnp.arange(block_rows, dtype=jnp.int32)
        allowed = (key_places[None, :] <= query_places[:, None]) & (key_places[None, :] < length_here)
        scores = jnp.where(allowed[None], scores, -1e+30)
        weights = low(jax.nn.softmax(scores, axis=-1))
        return jnp.einsum('hqk,khd->qhd', weights, values_all, precision=HIGHEST)
    starts = (jnp.arange(SEQ // block_rows) * block_rows).astype(jnp.int32)
    context = lax.map(jax.checkpoint(one_block), starts)
    return context.reshape(SEQ, HEADS * HEAD_DIM)

def layer_row(params, row_values, length_here, route_row):
    attn_gain, w_query, w_key, w_value, w_out, moe_gain, w_router, w_gate_up, w_down = params
    positions = jnp.arange(SEQ, dtype=jnp.int32)
    valid = (positions < length_here).astype(jnp.float32)[:, None]
    normed = low(normalize(row_values, attn_gain))
    query_lin = low_back(jnp.dot(normed, w_query, precision=HIGHEST))
    key_lin = low_back(jnp.dot(normed, w_key, precision=HIGHEST))
    values = low_back(low(jnp.dot(normed, w_value, precision=HIGHEST)))
    query_rot = low(rotate(query_lin.reshape(SEQ, HEADS, HEAD_DIM), positions))
    key_rot = low(rotate(key_lin.reshape(SEQ, KV_HEADS, HEAD_DIM), positions))
    context = attention(query_rot, key_rot, values.reshape(SEQ, KV_HEADS, HEAD_DIM), length_here)
    context = low_back(low(context))
    mixed = row_values + low_back(jnp.dot(context, w_out, precision=HIGHEST))
    entry = low(normalize(mixed, moe_gain))
    logits = jnp.dot(entry, w_router, precision=HIGHEST)
    chosen = jnp.take_along_axis(logits, route_row, axis=1)
    gates = jax.nn.softmax(chosen, axis=-1) * valid
    expert_ids = jnp.arange(EXPERTS, dtype=jnp.int32)
    member = (route_row[:, :, None] == expert_ids[None, None, :]).astype(jnp.float32)
    weights = jnp.einsum('tk,tke->et', gates, member, precision=HIGHEST)

    def expert_step(running, inputs):
        gate_up, down_proj, weight_row = inputs
        expert_in = low_back(entry)
        pre = low_back(jnp.dot(expert_in, gate_up, precision=HIGHEST))
        act = low(jax.nn.silu(pre[:, :FFE]) * pre[:, FFE:])
        result = low_back(low(jnp.dot(act, down_proj, precision=HIGHEST)))
        return (running + weight_row[:, None] * result, None)
    expert_sum, unused = lax.scan(jax.checkpoint(expert_step), jnp.zeros_like(mixed), (w_gate_up, w_down, weights))
    return valid * (mixed + expert_sum)

def reference(hidden, lengths, routes, cotangent, attn_gain, w_query, w_key, w_value, w_out, moe_gain, w_router, w_gate_up, w_down):
    params = tuple((weight.astype(jnp.float32) for weight in (attn_gain, w_query, w_key, w_value, w_out, moe_gain, w_router, w_gate_up, w_down)))

    def row_step(totals, inputs):
        row_values, length_here, route_row, cot_row = inputs

        def forward(weights, row_input):
            return layer_row(weights, row_input, length_here, route_row)
        result, pullback = jax.vjp(forward, params, row_values.astype(jnp.float32))
        grad_params, grad_row = pullback(cot_row.astype(jnp.float32))
        totals = jax.tree.map(jnp.add, totals, grad_params)
        return (totals, (result.astype(jnp.bfloat16), grad_row.astype(jnp.bfloat16)))
    zeros = jax.tree.map(jnp.zeros_like, params)
    totals, (outputs, grad_rows) = lax.scan(row_step, zeros, (hidden, lengths, routes, cotangent))
    return (outputs, grad_rows, totals[0], totals[1], totals[2], totals[3], totals[4], totals[5], totals[6], totals[7], totals[8])
```

```python
import functools
import jax
import jax.numpy as jnp
from jax import lax
from jax.experimental import pallas as pl
from jax.experimental.pallas import tpu as pltpu
from jax.sharding import PartitionSpec as P

HEADS = 16
KV_HEADS = 8
HEAD_DIM = 64
BF = jnp.bfloat16
F32 = jnp.float32
EPSILON = 1e-06
THETA = 10000.0
HIGHEST = lax.Precision.HIGHEST


def rope_tables(count, head_dim):
    half_dim = head_dim // 2
    inverse = THETA ** (-jnp.arange(half_dim, dtype=jnp.float32) * 2.0 / head_dim)
    angles = jnp.arange(count, dtype=jnp.float32)[:, None] * inverse[None, :]
    return (jnp.cos(angles), jnp.sin(angles))


def turn(values, cosine, sine_part, direction):
    half_dim = values.shape[-1] // 2
    shape_here = (cosine.shape[0],) + (1,) * (values.ndim - 2) + (half_dim,)
    cosine = cosine.reshape(shape_here)
    sine_part = direction * sine_part.reshape(shape_here)
    first = values[..., :half_dim]
    second = values[..., half_dim:]
    return jnp.concatenate(
        [first * cosine - second * sine_part, second * cosine + first * sine_part], axis=-1
    )


def norm_forward(values, gain):
    scaling = lax.rsqrt(jnp.mean(values * values, axis=-1, keepdims=True) + EPSILON)
    return (values * scaling * gain, scaling)


def norm_backward(values, scaling, gain, incoming):
    unit_values = values * scaling
    gain_grad = jnp.sum(incoming * unit_values, axis=0)
    inner = incoming * gain
    input_grad = scaling * (
        inner - unit_values * jnp.mean(inner * unit_values, axis=-1, keepdims=True)
    )
    return (input_grad, gain_grad)


def visible(start, block_rows, key_places, length_here):
    query_places = start + jnp.arange(block_rows, dtype=jnp.int32)
    return (key_places[None, :] <= query_places[:, None]) & (key_places[None, :] < length_here)


def attend_forward(queries, keys_low, values_low, length_here, scaling):
    key_places = jnp.arange(keys_low.shape[1], dtype=jnp.int32)
    block_rows = queries.shape[3]

    def one_block(inputs):
        query_block, start = inputs
        scores = (
            jnp.einsum("kgqd,ksd->kgqs", query_block, keys_low, preferred_element_type=jnp.float32)
            * scaling
        )
        scores = jnp.where(visible(start, block_rows, key_places, length_here), scores, -1e30)
        highest = jnp.max(scores, axis=-1, keepdims=True)
        weights = jnp.exp(scores - highest)
        totals = jnp.sum(weights, axis=-1, keepdims=True)
        chances = (weights / totals).astype(jnp.bfloat16)
        context = jnp.einsum(
            "kgqs,ksd->kgqd", chances, values_low, preferred_element_type=jnp.float32
        )
        return (context.astype(jnp.bfloat16), (highest + jnp.log(totals))[..., 0])

    starts = jnp.arange(queries.shape[0], dtype=jnp.int32) * block_rows
    return lax.map(one_block, (queries, starts))


def attend_backward(queries, keys_low, values_low, context_grad, log_sums, length_here, scaling):
    key_places = jnp.arange(keys_low.shape[1], dtype=jnp.int32)
    block_rows = queries.shape[3]

    def one_block(carry, inputs):
        key_grad, value_grad = carry
        query_block, grad_block, sum_block, start = inputs
        scores = (
            jnp.einsum("kgqd,ksd->kgqs", query_block, keys_low, preferred_element_type=jnp.float32)
            * scaling
        )
        allowed = visible(start, block_rows, key_places, length_here)
        scores = jnp.where(allowed, scores, -1e30)
        chances = jnp.where(allowed, jnp.exp(scores - sum_block[..., None]), 0.0)
        chance_grad = jnp.einsum(
            "kgqd,ksd->kgqs", grad_block, values_low, preferred_element_type=jnp.float32
        )
        inner = jnp.sum(chances * chance_grad, axis=-1, keepdims=True)
        score_grad = (chances * (chance_grad - inner)).astype(jnp.bfloat16)
        query_grad = (
            jnp.einsum("kgqs,ksd->kgqd", score_grad, keys_low, preferred_element_type=jnp.float32)
            * scaling
        )
        key_grad = (
            key_grad
            + jnp.einsum(
                "kgqs,kgqd->ksd", score_grad, query_block, preferred_element_type=jnp.float32
            )
            * scaling
        )
        value_grad = value_grad + jnp.einsum(
            "kgqs,kgqd->ksd",
            chances.astype(jnp.bfloat16),
            grad_block,
            preferred_element_type=jnp.float32,
        )
        return ((key_grad, value_grad), query_grad)

    starts = jnp.arange(queries.shape[0], dtype=jnp.int32) * block_rows
    zeros = jnp.zeros(keys_low.shape, jnp.float32)
    (key_grad, value_grad), query_grad = lax.scan(
        one_block, (zeros, zeros), (queries, context_grad, log_sums, starts)
    )
    return (query_grad, key_grad, value_grad)


MESH = pl.DeviceIdType.MESH

def ring_place(index, count):
    half = index // 2
    odd = index % 2
    return (1 - odd) * half + odd * (count - 1 - half)

def ring_index(place, count):
    odd = place // (count // 2)
    half = (1 - odd) * place + odd * (count - 1 - place)
    return 2 * half + odd

def ring_greet(nxt, prv):
    barrier = pltpu.get_barrier_semaphore()
    for peer in (nxt, prv):
        pl.semaphore_signal(barrier, inc=1, device_id={"wide": peer}, device_id_type=MESH)
    pl.semaphore_wait(barrier, 2)

def ring_gather(block, count, cid):
    rows, cols = block.shape
    hops = count // 2
    part = rows // 2

    def kernel(x_ref, o_ref, own_sem, send_sem, recv_sem):
        me = lax.axis_index("wide")
        place = ring_place(me, count)
        at = lambda shift: ring_index((place + shift + 2 * count) % count, count)
        peers = (at(1), at(-1))
        ring_greet(*peers)
        own = pltpu.make_async_copy(x_ref, o_ref.at[me], own_sem)
        own.start()
        live = lambda way, hop, k: hop < hops - 1 or k == way

        def copy(way, hop, k, source):
            sign = 1 if way == 0 else -1
            index = at(-sign * hop)
            span = pl.ds(k * part, part)
            return pltpu.make_async_remote_copy(
                src_ref=x_ref.at[span] if hop == 0 else o_ref.at[index, span],
                dst_ref=o_ref.at[index, span],
                send_sem=send_sem.at[way, hop, k],
                recv_sem=recv_sem.at[way, hop, k],
                device_id={"wide": peers[way]},
                device_id_type=MESH,
            )

        def arrival(way, hop, k):
            sign = 1 if way == 0 else -1
            index = at(-sign * (hop + 1))
            span = pl.ds(k * part, part)
            return pltpu.make_async_remote_copy(
                src_ref=o_ref.at[index, span],
                dst_ref=o_ref.at[index, span],
                send_sem=send_sem.at[way, hop, k],
                recv_sem=recv_sem.at[way, hop, k],
                device_id={"wide": peers[way]},
                device_id_type=MESH,
            )

        order = [(h, k, w) for h in range(hops) for k in range(2) for w in range(2) if live(w, h, k)]
        for hop, k, way in order:
            if hop > 0:
                arrival(way, hop - 1, k).wait_recv()
            copy(way, hop, k, None).start()
        for hop, k, way in order:
            if not (hop + 1 < hops and live(way, hop + 1, k)):
                arrival(way, hop, k).wait_recv()
        for hop, k, way in order:
            copy(way, hop, k, None).wait_send()
        own.wait()

    return pl.pallas_call(
        kernel,
        out_shape=jax.ShapeDtypeStruct((count, rows, cols), block.dtype),
        in_specs=[pl.BlockSpec(memory_space=pl.ANY)],
        out_specs=pl.BlockSpec(memory_space=pl.ANY),
        scratch_shapes=[
            pltpu.SemaphoreType.DMA,
            pltpu.SemaphoreType.DMA((2, hops, 2)),
            pltpu.SemaphoreType.DMA((2, hops, 2)),
        ],
        compiler_params=pltpu.CompilerParams(collective_id=cid, has_side_effects=True),
    )(block)

def ring_scatter(parts, cid):
    count, rows, cols = parts.shape
    lane = rows // 2
    part = lane // 2

    def kernel(p_ref, o_ref, held, send_sem, recv_sem):
        me = lax.axis_index("wide")
        place = ring_place(me, count)
        at = lambda shift: ring_index((place + shift + 2 * count) % count, count)
        peers = (at(1), at(-1))
        ring_greet(*peers)

        def copy(way, step, k):
            sign = 1 if way == 0 else -1
            span = pl.ds(k * part, part)
            src = (
                p_ref.at[at(-sign), pl.ds(way * lane + k * part, part)]
                if step == 0
                else held.at[way, step - 1, span]
            )
            return pltpu.make_async_remote_copy(
                src_ref=src,
                dst_ref=held.at[way, step, span],
                send_sem=send_sem.at[way, step, k],
                recv_sem=recv_sem.at[way, step, k],
                device_id={"wide": peers[way]},
                device_id_type=MESH,
            )

        for step in range(count - 1):
            for k in range(2):
                for way in range(2):
                    sign = 1 if way == 0 else -1
                    if step > 0:
                        copy(way, step - 1, k).wait_recv()
                        span = pl.ds(k * part, part)
                        mine = p_ref[at(-sign * (1 + step)), pl.ds(way * lane + k * part, part)]
                        held[way, step - 1, span] = (
                            held[way, step - 1, span].astype(F32) + mine.astype(F32)
                        ).astype(held.dtype)
                    copy(way, step, k).start()
        for k in range(2):
            for way in range(2):
                copy(way, count - 2, k).wait_recv()
                rows_here = pl.ds(way * lane + k * part, part)
                o_ref[rows_here] = held[way, count - 2, pl.ds(k * part, part)].astype(F32) + p_ref[
                    me, rows_here
                ].astype(F32)
        for step in range(count - 1):
            for k in range(2):
                for way in range(2):
                    copy(way, step, k).wait_send()

    return pl.pallas_call(
        kernel,
        out_shape=jax.ShapeDtypeStruct((rows, cols), F32),
        in_specs=[pl.BlockSpec(memory_space=pltpu.VMEM)],
        out_specs=pl.BlockSpec(memory_space=pltpu.VMEM),
        scratch_shapes=[
            pltpu.VMEM((2, count - 1, lane, cols), parts.dtype),
            pltpu.SemaphoreType.DMA((2, count - 1, 2)),
            pltpu.SemaphoreType.DMA((2, count - 1, 2)),
        ],
        compiler_params=pltpu.CompilerParams(
            collective_id=cid, has_side_effects=True, vmem_limit_bytes=40 * 2**20
        ),
    )(parts)


TILE = 256

def nt(a, b):
    return lax.dot_general(a, b, (((1,), (1,)), ((), ())), preferred_element_type=F32)

def tn(a, b):
    return lax.dot_general(a, b, (((0,), (0,)), ((), ())), preferred_element_type=F32)

def nn(a, b):
    return jnp.dot(a, b, preferred_element_type=F32)

def expert_pair(offsets, entry_all, grad_all, slots, slots_turned, gates, w_gate_up, w_down, earlier, first, pair, capacity):
    count, tokens, width = entry_all.shape
    ffe = w_down.shape[1]
    local = w_down.shape[0]
    room = count * capacity + TILE
    most = count * capacity // TILE
    adding = earlier is not None

    def kernel(off_ref, e_ref, g_ref, s_ref, st_ref, gate_ref, wgu_ref, wd_ref, *rest):
        if adding:
            pc_ref, pb_ref = rest[:2]
            rest = rest[2:]
        c_ref, b_ref, pick_ref, dgu_ref, dd_ref, x_s, s_s, act_s, pg_s, cr_s, bk_s, gcol, pcol, sems = rest
        e = pl.program_id(0)
        if adding:
            fetch = [
                pltpu.make_async_copy(pc_ref, c_ref, sems.at[0]),
                pltpu.make_async_copy(pb_ref, b_ref, sems.at[1]),
            ]

        @pl.when(e == 0)
        def _():
            if adding:
                for f in fetch:
                    f.start()
            cr_s[...] = jnp.zeros_like(cr_s)
            bk_s[...] = jnp.zeros_like(bk_s)
            pcol[...] = jnp.zeros_like(pcol)

        def start_of(expert, b):
            return pl.multiple_of(off_ref[(first + expert) * (count + 1) + b], 16)

        places = lax.broadcasted_iota(jnp.int32, (capacity, tokens), 0)
        for b in range(count):
            pick_out = places == s_ref[first + e, b : b + 1, :]
            chosen = jnp.where(pick_out, 1.0, 0.0).astype(BF)
            span = pl.ds(start_of(e, b), capacity)
            x_s[span] = nn(chosen, e_ref[b]).astype(BF)
            s_s[span] = nn(chosen, g_ref[b]).astype(BF)
            gate_col = jnp.sum(
                jnp.where(pick_out, gate_ref[first + e, b : b + 1, :], 0.0), axis=1, keepdims=True
            )
            gcol[span] = jnp.broadcast_to(gate_col, (capacity, 128))
        total = start_of(e, count)
        tail = pl.ds(total, TILE)
        x_s[tail] = jnp.zeros((TILE, width), BF)
        s_s[tail] = jnp.zeros((TILE, width), BF)
        gcol[tail] = jnp.zeros((TILE, 128), F32)
        tiles = (total + TILE - 1) // TILE

        def step(i, carry):
            rows = pl.ds(pl.multiple_of(i * TILE, TILE), TILE)
            pre = nn(x_s[rows], wgu_ref[0])
            gate_part = pre[:, :ffe]
            up_part = pre[:, ffe:]
            sig = jax.nn.sigmoid(gate_part)
            swish = gate_part * sig
            act = (swish * up_part).astype(BF)
            act_s[rows] = act
            result = nn(act, wd_ref[0]).astype(BF).astype(F32)
            grad_rows = s_s[rows].astype(F32)
            gate = gcol[rows][:, :1]
            pcol[rows] = jnp.broadcast_to(
                jnp.sum(result * grad_rows, axis=1, keepdims=True), (TILE, 128)
            )
            cr_s[e, rows] = (gate * result).astype(BF)
            slot_grad = (gate * grad_rows).astype(BF)
            s_s[rows] = slot_grad
            act_grad = nt(slot_grad, wd_ref[0])
            gate_grad = act_grad * up_part * sig * (1.0 + gate_part * (1.0 - sig))
            pre_grad = jnp.concatenate([gate_grad, act_grad * swish], axis=1).astype(BF)
            pg_s[rows] = pre_grad
            bk_s[e, rows] = nt(pre_grad, wgu_ref[0]).astype(BF)
            return carry

        lax.fori_loop(0, tiles, step, 0)
        for b in range(count):
            pick_out = places == s_ref[first + e, b : b + 1, :]
            span = pl.ds(start_of(e, b), capacity)
            pick_ref[0, b : b + 1, :] = jnp.sum(
                jnp.where(pick_out, pcol[span][:, :1], 0.0), axis=0, keepdims=True
            )

        @pl.when(tiles == 0)
        def _():
            dgu_ref[...] = jnp.zeros_like(dgu_ref)
            dd_ref[...] = jnp.zeros_like(dd_ref)

        block = 256
        for k in range(1, most + 1):

            @pl.when(tiles == k)
            def _(k=k):
                def columns(j, carry):
                    cols = pl.ds(pl.multiple_of(j * block, block), block)
                    dgu_ref[0, :, cols] = tn(x_s[: k * TILE], pg_s[: k * TILE, cols]).astype(BF)
                    dd_ref[0, :, cols] = tn(act_s[: k * TILE], s_s[: k * TILE, cols]).astype(BF)
                    return carry

                lax.fori_loop(0, width // block, columns, 0)

        @pl.when(e == pair - 1)
        def _():
            if adding:
                for f in fetch:
                    f.wait()
            across = lax.broadcasted_iota(jnp.int32, (tokens, capacity), 1)
            for b in range(count):
                sum_c = sum_b = None
                for x in range(pair):
                    back = jnp.where(across == st_ref[b][:, first + x : first + x + 1], 1.0, 0.0).astype(BF)
                    span = pl.ds(start_of(x, b), capacity)
                    one_c, one_b = nn(back, cr_s[x, span]), nn(back, bk_s[x, span])
                    sum_c = one_c if sum_c is None else sum_c + one_c
                    sum_b = one_b if sum_b is None else sum_b + one_b
                if adding:
                    sum_c = sum_c + c_ref[b].astype(F32)
                    sum_b = sum_b + b_ref[b].astype(F32)
                c_ref[b] = sum_c.astype(BF)
                b_ref[b] = sum_b.astype(BF)

    once = pl.Buffered(1)
    whole = lambda shape: pl.BlockSpec(shape, lambda e, off: (0,) * len(shape), pipeline_mode=once)
    any_space = pl.BlockSpec(memory_space=pl.ANY)
    cube = (count, tokens, width)
    in_specs = [
        whole(cube), whole(cube), whole(slots.shape), whole(slots_turned.shape), whole(gates.shape),
        pl.BlockSpec((1, width, 2 * ffe), lambda e, off: (first + e, 0, 0)),
        pl.BlockSpec((1, ffe, width), lambda e, off: (first + e, 0, 0)),
    ]
    operands = [entry_all, grad_all, slots, slots_turned, gates, w_gate_up, w_down]
    if adding:
        in_specs += [any_space, any_space]
        operands += list(earlier)
    return pl.pallas_call(
        kernel,
        grid_spec=pltpu.PrefetchScalarGridSpec(
            num_scalar_prefetch=1,
            grid=(pair,),
            in_specs=in_specs,
            out_specs=[
                whole(cube), whole(cube),
                pl.BlockSpec((1, count, tokens), lambda e, off: (e, 0, 0)),
                pl.BlockSpec((1, width, 2 * ffe), lambda e, off: (e, 0, 0)),
                pl.BlockSpec((1, ffe, width), lambda e, off: (e, 0, 0)),
            ],
            scratch_shapes=[
                pltpu.VMEM((room, width), BF),
                pltpu.VMEM((room, width), BF),
                pltpu.VMEM((room, ffe), BF),
                pltpu.VMEM((room, 2 * ffe), BF),
                pltpu.VMEM((pair, room, width), BF),
                pltpu.VMEM((pair, room, width), BF),
                pltpu.VMEM((room, 128), F32),
                pltpu.VMEM((room, 128), F32),
                pltpu.SemaphoreType.DMA((2,)),
            ],
        ),
        out_shape=[
            jax.ShapeDtypeStruct(cube, BF),
            jax.ShapeDtypeStruct(cube, BF),
            jax.ShapeDtypeStruct((pair, count, tokens), F32),
            jax.ShapeDtypeStruct((pair, width, 2 * ffe), BF),
            jax.ShapeDtypeStruct((pair, ffe, width), BF),
        ],
        compiler_params=pltpu.CompilerParams(
            dimension_semantics=("arbitrary",), vmem_limit_bytes=60 * 2**20
        ),
        cost_estimate=pl.CostEstimate(
            flops=pair * count * capacity * 6 * width * ffe * 3, bytes_accessed=40 * 2**20, transcendentals=0
        ),
    )(offsets, *operands)


def pair_sum(parts):
    here = lax.axis_index("narrow")
    chip, core = here // 2, here % 2
    to_core = [(0, 1), (1, 0), (2, 3), (3, 2)]
    to_chip = [(0, 2), (2, 0), (1, 3), (3, 1)]
    pick = lambda array, index, axis: lax.dynamic_index_in_dim(array, index, axis, keepdims=False)
    add = lambda one, two: (one.astype(F32) + two.astype(F32)).astype(BF)
    cubes = [p.reshape(p.shape[0], 2, 2, p.shape[1] // 4, p.shape[2]) for p in parts]
    got = [lax.ppermute(pick(c, 1 - core, 2), "narrow", to_core) for c in cubes]
    half = [add(pick(c, core, 2), g) for c, g in zip(cubes, got)]
    got = [lax.ppermute(pick(h, 1 - chip, 1), "narrow", to_chip) for h in half]
    own = [add(pick(h, chip, 1), g) for h, g in zip(half, got)]
    other = [lax.ppermute(o, "narrow", to_chip) for o in own]
    done = []
    for o, t in zip(own, other):
        mine = jnp.stack([jnp.where(chip == 0, o, t), jnp.where(chip == 0, t, o)], axis=1)
        theirs = lax.ppermute(mine, "narrow", to_core)
        both = jnp.stack([jnp.where(core == 0, mine, theirs), jnp.where(core == 0, theirs, mine)], axis=2)
        done.append(both.reshape(o.shape[0], 4 * o.shape[1], o.shape[2]).astype(F32))
    return done


def narrow_sum(parts):
    if lax.axis_size("narrow") == 4:
        return pair_sum(parts)
    return [lax.psum(p, "narrow").astype(F32) for p in parts]


def local(
    hidden,
    lengths,
    routes,
    cotangent,
    attn_gain,
    w_query,
    w_key,
    w_value,
    w_out,
    moe_gain,
    w_router,
    w_gate_up,
    w_down,
):
    rows_here = hidden.shape[1]
    width = hidden.shape[2]
    wide = lax.axis_size("wide")
    seq_len = rows_here * lax.axis_size("narrow")
    head_dim = HEAD_DIM
    group_size = HEADS // KV_HEADS
    kv_here = w_key.shape[1] // head_dim
    query_cols = kv_here * group_size * head_dim
    key_cols = kv_here * head_dim
    scaling = head_dim ** (-0.5)
    block_rows = min(512, seq_len)
    block_count = seq_len // block_rows
    length_here = lengths[0]
    offset = lax.axis_index("narrow") * rows_here
    local_places = offset + jnp.arange(rows_here, dtype=jnp.int32)
    valid = (local_places < length_here).astype(jnp.float32)[:, None]
    grad_all = lax.all_gather(cotangent[0], "wide", axis=0)
    picks = routes.shape[2]
    expert_total = w_router.shape[1]
    expert_here = w_gate_up.shape[0]
    first_expert = lax.axis_index("wide") * expert_here
    capacity = 2 * rows_here * picks // expert_total
    labels = jnp.concatenate(
        [routes[0].T, jnp.broadcast_to(lengths[0], (1, rows_here)).astype(jnp.int32)], axis=0
    )
    labels_all = lax.all_gather(labels, "wide", axis=0)
    routes_all = labels_all[:, :picks]
    valid_all = local_places[None, None, :] < labels_all[:, picks:]
    experts = jnp.arange(expert_total, dtype=jnp.int32)
    member_all = jnp.any(routes_all[:, :, None, :] == experts[None, None, :, None], axis=1)
    member_here = lax.dynamic_slice_in_dim(member_all, first_expert, expert_here, 1) & valid_all
    upper = jnp.triu(jnp.ones((rows_here, rows_here), BF))
    reached = jnp.einsum(
        "bet,ts->bes", member_here.astype(BF), upper, preferred_element_type=F32
    ).astype(jnp.int32)
    slots = jnp.where(member_here, reached - 1, -1).transpose(1, 0, 2)
    slots_turned = slots.transpose(1, 2, 0)
    padded = (reached[:, :, -1].T + 15) // 16 * 16
    offsets = jnp.concatenate(
        [jnp.zeros((expert_here, 1), jnp.int32), jnp.cumsum(padded, axis=1)], axis=1
    ).reshape(-1)

    source = hidden[0].astype(jnp.float32)
    normed, scale_one = norm_forward(source, attn_gain)
    normed_low = normed.astype(jnp.bfloat16)
    whole = lax.all_gather(normed_low, "narrow", axis=0, tiled=True)
    w_qkv = jnp.concatenate([w_query, w_key, w_value], axis=1)
    projected = jnp.dot(whole, w_qkv, preferred_element_type=jnp.float32)
    cosine, sine_part = rope_tables(seq_len, head_dim)
    query_rot = turn(
        projected[:, :query_cols].reshape(seq_len, kv_here, group_size, head_dim),
        cosine,
        sine_part,
        1.0,
    )
    key_rot = turn(
        projected[:, query_cols : query_cols + key_cols].reshape(seq_len, kv_here, head_dim),
        cosine,
        sine_part,
        1.0,
    )
    queries = (
        query_rot.astype(jnp.bfloat16)
        .reshape(block_count, block_rows, kv_here, group_size, head_dim)
        .transpose(0, 2, 3, 1, 4)
    )
    keys_low = key_rot.astype(jnp.bfloat16).transpose(1, 0, 2)
    values_low = (
        projected[:, query_cols + key_cols :]
        .astype(jnp.bfloat16)
        .reshape(seq_len, kv_here, head_dim)
        .transpose(1, 0, 2)
    )
    context, log_sums = attend_forward(queries, keys_low, values_low, length_here, scaling)
    context_rows = context.transpose(0, 3, 1, 2, 4).reshape(seq_len, query_cols)
    attn_part = lax.psum_scatter(
        jnp.dot(context_rows, w_out, preferred_element_type=jnp.float32).astype(jnp.bfloat16),
        "narrow",
        scatter_dimension=0,
        tiled=True,
    ).astype(jnp.float32)
    mixed = source + attn_part
    normed_two, scale_two = norm_forward(mixed, moe_gain)
    entry = normed_two.astype(jnp.bfloat16)

    entry_all = ring_gather(entry, wide, 1)
    logits = jnp.einsum("btd,de->bet", entry_all, w_router, preferred_element_type=F32)
    masked = jnp.where(member_all, logits, -jnp.inf)
    raised = jnp.exp(masked - jnp.max(masked, axis=1, keepdims=True))
    shares_all = raised / jnp.sum(raised, axis=1, keepdims=True)
    gates = (
        lax.dynamic_slice_in_dim(shares_all, first_expert, expert_here, 1) * valid_all.astype(F32)
    ).transpose(1, 0, 2)
    pair = min(2, expert_here)
    earlier, pick_parts, weight_parts = None, [], []
    for first in range(0, expert_here, pair):
        expert_part, back_part, pick_part, up_part, down_part = expert_pair(
            offsets, entry_all, grad_all, slots, slots_turned, gates, w_gate_up, w_down,
            earlier, first, pair, capacity,
        )
        earlier = (expert_part, back_part)
        pick_parts.append(pick_part)
        weight_parts.append((up_part, down_part))
    entry_home = ring_scatter(back_part, 2)
    pick_home = lax.all_to_all(
        jnp.concatenate(pick_parts, axis=0), "wide", split_axis=1, concat_axis=0, tiled=True
    ).reshape(expert_total, rows_here)
    summed = [narrow_sum(p) for p in weight_parts]
    gate_up_grad = jnp.concatenate([s[0] for s in summed], axis=0)
    down_grad = jnp.concatenate([s[1] for s in summed], axis=0)

    expert_part, entry_home = lax.optimization_barrier((expert_part, entry_home))
    expert_sum = lax.psum_scatter(expert_part, "wide", scatter_dimension=0, tiled=False).astype(F32)
    output_rows = (valid * (mixed + expert_sum)).astype(jnp.bfloat16)
    grad_rows_here = cotangent[0].astype(jnp.float32) * valid

    shares = lax.dynamic_index_in_dim(shares_all, lax.axis_index("wide"), 0, keepdims=False)
    logit_grad = shares * (pick_home - jnp.sum(shares * pick_home, axis=0, keepdims=True))
    router_grad = lax.dot_general(
        entry.astype(jnp.float32), logit_grad, (((0,), (1,)), ((), ())), precision=HIGHEST
    )
    entry_grad = entry_home + lax.dot_general(
        logit_grad, w_router.astype(jnp.float32), (((0,), (1,)), ((), ())), precision=HIGHEST
    )
    mixed_from_norm, gain_two_grad = norm_backward(mixed, scale_two, moe_gain, entry_grad)
    mixed_grad = grad_rows_here + mixed_from_norm
    attn_grad_low = mixed_grad.astype(jnp.bfloat16)
    grad_whole = lax.all_gather(attn_grad_low, "narrow", axis=0, tiled=True)
    context_grad = lax.dot_general(
        grad_whole, w_out, (((1,), (1,)), ((), ())), preferred_element_type=jnp.float32
    ).astype(jnp.bfloat16)
    out_grad = lax.dot_general(
        context_rows, grad_whole, (((0,), (0,)), ((), ())), preferred_element_type=jnp.float32
    )
    context_blocks = context_grad.reshape(
        block_count, block_rows, kv_here, group_size, head_dim
    ).transpose(0, 2, 3, 1, 4)
    query_grad, key_grad, value_grad = attend_backward(
        queries, keys_low, values_low, context_blocks, log_sums, length_here, scaling
    )
    query_rows = turn(
        query_grad.transpose(0, 3, 1, 2, 4).reshape(seq_len, kv_here, group_size, head_dim),
        cosine,
        sine_part,
        -1.0,
    )
    key_rows = turn(key_grad.transpose(1, 0, 2), cosine, sine_part, -1.0)
    value_rows = value_grad.transpose(1, 0, 2)
    qkv_grad = jnp.concatenate(
        [
            query_rows.reshape(seq_len, query_cols),
            key_rows.reshape(seq_len, key_cols),
            value_rows.reshape(seq_len, key_cols),
        ],
        axis=1,
    ).astype(jnp.bfloat16)
    qkv_weight_grad = lax.dot_general(
        whole, qkv_grad, (((0,), (0,)), ((), ())), preferred_element_type=jnp.float32
    )
    normed_grad = lax.psum_scatter(
        lax.dot_general(
            qkv_grad, w_qkv, (((1,), (1,)), ((), ())), preferred_element_type=jnp.float32
        ).astype(jnp.bfloat16),
        "narrow",
        scatter_dimension=0,
        tiled=True,
    ).astype(jnp.float32)
    source_from_norm, gain_one_grad = norm_backward(source, scale_one, attn_gain, normed_grad)
    grad_input = (mixed_grad + source_from_norm).astype(jnp.bfloat16)
    gain_one_grad = jnp.sum(qkv_weight_grad * w_qkv.astype(F32), axis=1) / attn_gain
    small = jnp.concatenate([router_grad, gain_one_grad[:, None], gain_two_grad[:, None]], axis=1)
    small = lax.psum(small, ("wide", "narrow"))
    router_grad = small[:, :expert_total]
    gain_one_grad = small[:, expert_total]
    gain_two_grad = small[:, expert_total + 1]
    qkv_weight_grad, out_grad = (
        lax.psum(qkv_weight_grad.astype(jnp.bfloat16), "wide").astype(jnp.float32),
        lax.psum(out_grad.astype(jnp.bfloat16), "wide").astype(jnp.float32),
    )
    query_weight_grad = qkv_weight_grad[:, :query_cols]
    key_weight_grad = qkv_weight_grad[:, query_cols : query_cols + key_cols]
    value_weight_grad = qkv_weight_grad[:, query_cols + key_cols :]
    return (
        output_rows[None],
        grad_input[None],
        gain_one_grad,
        query_weight_grad,
        key_weight_grad,
        value_weight_grad,
        out_grad,
        gain_two_grad,
        router_grad,
        gate_up_grad,
        down_grad,
    )


def solution(mesh):
    in_specs = (
        P("wide", "narrow", None),
        P("wide"),
        P("wide", "narrow", None),
        P("wide", "narrow", None),
        P(),
        P(None, "narrow"),
        P(None, "narrow"),
        P(None, "narrow"),
        P("narrow", None),
        P(),
        P(),
        P("wide", None, None),
        P("wide", None, None),
    )
    out_specs = (
        P("wide", "narrow", None),
        P("wide", "narrow", None),
        P(),
        P(None, "narrow"),
        P(None, "narrow"),
        P(None, "narrow"),
        P("narrow", None),
        P(),
        P(),
        P("wide", None, None),
        P("wide", None, None),
    )
    return jax.shard_map(local, mesh=mesh, in_specs=in_specs, out_specs=out_specs, check_vma=False)
```

```python
import functools
import jax
import jax.numpy as jnp
from jax import lax
from jax.experimental import pallas as pl
from jax.experimental.pallas import tpu as pltpu
from jax.sharding import PartitionSpec as P

HEADS = 16
KV_HEADS = 8
HEAD_DIM = 64
BF = jnp.bfloat16
F32 = jnp.float32
EPSILON = 1e-06
THETA = 10000.0
HIGHEST = lax.Precision.HIGHEST


def rope_tables(count, head_dim):
    half_dim = head_dim // 2
    inverse = THETA ** (-jnp.arange(half_dim, dtype=jnp.float32) * 2.0 / head_dim)
    angles = jnp.arange(count, dtype=jnp.float32)[:, None] * inverse[None, :]
    return (jnp.cos(angles), jnp.sin(angles))


def turn(values, cosine, sine_part, direction):
    half_dim = values.shape[-1] // 2
    shape_here = (cosine.shape[0],) + (1,) * (values.ndim - 2) + (half_dim,)
    cosine = cosine.reshape(shape_here)
    sine_part = direction * sine_part.reshape(shape_here)
    first = values[..., :half_dim]
    second = values[..., half_dim:]
    return jnp.concatenate(
        [first * cosine - second * sine_part, second * cosine + first * sine_part], axis=-1
    )


def norm_forward(values, gain):
    scaling = lax.rsqrt(jnp.mean(values * values, axis=-1, keepdims=True) + EPSILON)
    return (values * scaling * gain, scaling)


def norm_backward(values, scaling, gain, incoming):
    unit_values = values * scaling
    gain_grad = jnp.sum(incoming * unit_values, axis=0)
    inner = incoming * gain
    input_grad = scaling * (
        inner - unit_values * jnp.mean(inner * unit_values, axis=-1, keepdims=True)
    )
    return (input_grad, gain_grad)


def visible(start, block_rows, key_places, length_here):
    query_places = start + jnp.arange(block_rows, dtype=jnp.int32)
    return (key_places[None, :] <= query_places[:, None]) & (key_places[None, :] < length_here)


def attend_forward(queries, keys_low, values_low, length_here, scaling):
    key_places = jnp.arange(keys_low.shape[1], dtype=jnp.int32)
    block_rows = queries.shape[3]

    def one_block(inputs):
        query_block, start = inputs
        scores = (
            jnp.einsum("kgqd,ksd->kgqs", query_block, keys_low, preferred_element_type=jnp.float32)
            * scaling
        )
        scores = jnp.where(visible(start, block_rows, key_places, length_here), scores, -1e30)
        highest = jnp.max(scores, axis=-1, keepdims=True)
        weights = jnp.exp(scores - highest)
        totals = jnp.sum(weights, axis=-1, keepdims=True)
        chances = (weights / totals).astype(jnp.bfloat16)
        context = jnp.einsum(
            "kgqs,ksd->kgqd", chances, values_low, preferred_element_type=jnp.float32
        )
        return (context.astype(jnp.bfloat16), (highest + jnp.log(totals))[..., 0])

    starts = jnp.arange(queries.shape[0], dtype=jnp.int32) * block_rows
    return lax.map(one_block, (queries, starts))


def attend_backward(queries, keys_low, values_low, context_grad, log_sums, length_here, scaling):
    key_places = jnp.arange(keys_low.shape[1], dtype=jnp.int32)
    block_rows = queries.shape[3]

    def one_block(carry, inputs):
        key_grad, value_grad = carry
        query_block, grad_block, sum_block, start = inputs
        scores = (
            jnp.einsum("kgqd,ksd->kgqs", query_block, keys_low, preferred_element_type=jnp.float32)
            * scaling
        )
        allowed = visible(start, block_rows, key_places, length_here)
        scores = jnp.where(allowed, scores, -1e30)
        chances = jnp.where(allowed, jnp.exp(scores - sum_block[..., None]), 0.0)
        chance_grad = jnp.einsum(
            "kgqd,ksd->kgqs", grad_block, values_low, preferred_element_type=jnp.float32
        )
        inner = jnp.sum(chances * chance_grad, axis=-1, keepdims=True)
        score_grad = (chances * (chance_grad - inner)).astype(jnp.bfloat16)
        query_grad = (
            jnp.einsum("kgqs,ksd->kgqd", score_grad, keys_low, preferred_element_type=jnp.float32)
            * scaling
        )
        key_grad = (
            key_grad
            + jnp.einsum(
                "kgqs,kgqd->ksd", score_grad, query_block, preferred_element_type=jnp.float32
            )
            * scaling
        )
        value_grad = value_grad + jnp.einsum(
            "kgqs,kgqd->ksd",
            chances.astype(jnp.bfloat16),
            grad_block,
            preferred_element_type=jnp.float32,
        )
        return ((key_grad, value_grad), query_grad)

    starts = jnp.arange(queries.shape[0], dtype=jnp.int32) * block_rows
    zeros = jnp.zeros(keys_low.shape, jnp.float32)
    (key_grad, value_grad), query_grad = lax.scan(
        one_block, (zeros, zeros), (queries, context_grad, log_sums, starts)
    )
    return (query_grad, key_grad, value_grad)


MESH = pl.DeviceIdType.MESH

def ring_place(index, count):
    half = index // 2
    odd = index % 2
    return (1 - odd) * half + odd * (count - 1 - half)

def ring_index(place, count):
    odd = place // (count // 2)
    half = (1 - odd) * place + odd * (count - 1 - place)
    return 2 * half + odd

def ring_greet(nxt, prv):
    barrier = pltpu.get_barrier_semaphore()
    for peer in (nxt, prv):
        pl.semaphore_signal(barrier, inc=1, device_id={"wide": peer}, device_id_type=MESH)
    pl.semaphore_wait(barrier, 2)

def ring_gather(block, count, cid):
    rows, cols = block.shape
    hops = count // 2
    part = rows // 2

    def kernel(x_ref, o_ref, own_sem, send_sem, recv_sem):
        me = lax.axis_index("wide")
        place = ring_place(me, count)
        at = lambda shift: ring_index((place + shift + 2 * count) % count, count)
        peers = (at(1), at(-1))
        ring_greet(*peers)
        own = pltpu.make_async_copy(x_ref, o_ref.at[me], own_sem)
        own.start()
        live = lambda way, hop, k: hop < hops - 1 or k == way

        def copy(way, hop, k, source):
            sign = 1 if way == 0 else -1
            index = at(-sign * hop)
            span = pl.ds(k * part, part)
            return pltpu.make_async_remote_copy(
                src_ref=x_ref.at[span] if hop == 0 else o_ref.at[index, span],
                dst_ref=o_ref.at[index, span],
                send_sem=send_sem.at[way, hop, k],
                recv_sem=recv_sem.at[way, hop, k],
                device_id={"wide": peers[way]},
                device_id_type=MESH,
            )

        def arrival(way, hop, k):
            sign = 1 if way == 0 else -1
            index = at(-sign * (hop + 1))
            span = pl.ds(k * part, part)
            return pltpu.make_async_remote_copy(
                src_ref=o_ref.at[index, span],
                dst_ref=o_ref.at[index, span],
                send_sem=send_sem.at[way, hop, k],
                recv_sem=recv_sem.at[way, hop, k],
                device_id={"wide": peers[way]},
                device_id_type=MESH,
            )

        order = [(h, k, w) for h in range(hops) for k in range(2) for w in range(2) if live(w, h, k)]
        for hop, k, way in order:
            if hop > 0:
                arrival(way, hop - 1, k).wait_recv()
            copy(way, hop, k, None).start()
        for hop, k, way in order:
            if not (hop + 1 < hops and live(way, hop + 1, k)):
                arrival(way, hop, k).wait_recv()
        for hop, k, way in order:
            copy(way, hop, k, None).wait_send()
        own.wait()

    return pl.pallas_call(
        kernel,
        out_shape=jax.ShapeDtypeStruct((count, rows, cols), block.dtype),
        in_specs=[pl.BlockSpec(memory_space=pl.ANY)],
        out_specs=pl.BlockSpec(memory_space=pl.ANY),
        scratch_shapes=[
            pltpu.SemaphoreType.DMA,
            pltpu.SemaphoreType.DMA((2, hops, 2)),
            pltpu.SemaphoreType.DMA((2, hops, 2)),
        ],
        compiler_params=pltpu.CompilerParams(collective_id=cid, has_side_effects=True),
    )(block)


def add_low(one, two):
    return (one.astype(F32) + two.astype(F32)).astype(BF)

class Ring:
    def __init__(self, count):
        self.count = count
        self.me = lax.axis_index("wide")
        self.place = ring_place(self.me, count)
        self.peers = (self.at(1), self.at(-1))

    def at(self, shift):
        return ring_index((self.place + shift + 2 * self.count) % self.count, self.count)

def greet(wide_peers, narrow_peers):
    barrier = pltpu.get_barrier_semaphore()
    for peer in wide_peers:
        pl.semaphore_signal(barrier, inc=1, device_id={"wide": peer}, device_id_type=MESH)
    for peer in narrow_peers:
        pl.semaphore_signal(barrier, inc=1, device_id={"narrow": peer}, device_id_type=MESH)
    pl.semaphore_wait(barrier, len(wide_peers) + len(narrow_peers))

def remote(source, target, send, recv, **device):
    return pltpu.make_async_remote_copy(
        src_ref=source, dst_ref=target, send_sem=send, recv_sem=recv,
        device_id=device, device_id_type=MESH,
    )

def cuts(rows):
    first = (rows // 2 + 15) // 16 * 16
    return ((0, first), (first, rows - first))

def scatter_steps(ring, p_ref, held, send_sem, recv_sem, finish):
    count = ring.count
    lane = p_ref.shape[1] // 2

    def copy(way, step, k):
        sign = 1 if way == 0 else -1
        start, size = cuts(lane)[k]
        src = (
            p_ref.at[ring.at(-sign), pl.ds(way * lane + start, size)]
            if step == 0
            else held.at[way, step - 1, pl.ds(start, size)]
        )
        return remote(
            src, held.at[way, step, pl.ds(start, size)],
            send_sem.at[way, step, k], recv_sem.at[way, step, k], wide=ring.peers[way],
        )

    for step in range(count - 1):
        for k in range(2):
            for way in range(2):
                sign = 1 if way == 0 else -1
                start, size = cuts(lane)[k]
                if step > 0:
                    copy(way, step - 1, k).wait_recv()
                    span = pl.ds(start, size)
                    mine = p_ref[ring.at(-sign * (1 + step)), pl.ds(way * lane + start, size)]
                    held[way, step - 1, span] = add_low(held[way, step - 1, span], mine)
                copy(way, step, k).start()
        yield
    for k in range(2):
        for way in range(2):
            start, size = cuts(lane)[k]
            copy(way, count - 2, k).wait_recv()
            row = way * lane + start
            finish(
                row, size,
                held[way, count - 2, pl.ds(start, size)].astype(F32)
                + p_ref[ring.me, pl.ds(row, size)].astype(F32),
            )
    for step in range(count - 1):
        for k in range(2):
            for way in range(2):
                copy(way, step, k).wait_send()
    yield

def gather_steps(ring, o_ref, send_sem, recv_sem):
    count = ring.count
    hops = count // 2
    rows = o_ref.shape[1]
    live = lambda way, hop, k: hop < hops - 1 or k == way

    def copy(way, hop, k, shift):
        sign = 1 if way == 0 else -1
        start, size = cuts(rows)[k]
        block = o_ref.at[ring.at(-sign * (hop + shift)), pl.ds(start, size)]
        return remote(
            block, block, send_sem.at[way, hop, k], recv_sem.at[way, hop, k], wide=ring.peers[way]
        )

    for hop in range(hops):
        for k in range(2):
            for way in range(2):
                if live(way, hop, k):
                    if hop > 0:
                        copy(way, hop - 1, k, 1).wait_recv()
                    copy(way, hop, k, 0).start()
        yield
    for hop in range(hops):
        for k in range(2):
            for way in range(2):
                if live(way, hop, k) and not (hop + 1 < hops and live(way, hop + 1, k)):
                    copy(way, hop, k, 1).wait_recv()
    for hop in range(hops):
        for k in range(2):
            for way in range(2):
                if live(way, hop, k):
                    copy(way, hop, k, 0).wait_send()
    yield

def scatter_scratch(count, rows, cols):
    return [
        pltpu.VMEM((2, count - 1, rows // 2, cols), BF),
        pltpu.SemaphoreType.DMA((2, count - 1, 2)),
        pltpu.SemaphoreType.DMA((2, count - 1, 2)),
    ]

def gather_scratch(count):
    return [pltpu.SemaphoreType.DMA((2, count // 2, 2)), pltpu.SemaphoreType.DMA((2, count // 2, 2))]

def run(*makers):
    live = list(makers)
    while live:
        for one in list(live):
            if next(one, "end") == "end":
                live.remove(one)

def block_add(out, one, two, rows):
    def step(i, carry):
        span = pl.ds(pl.multiple_of(i * 128, 128), 128)
        out[span] = add_low(one[span], two[span])
        return carry
    lax.fori_loop(0, rows // 128, step, 0)

def home_kernel(back, picks, expert_part, up_grads, down_grads, cid):
    count, rows, cols = back.shape
    paired = len(up_grads) > 0
    pairs = len(up_grads)
    each = up_grads[0].shape[0] if paired else 0
    experts = pairs * each
    quarter_up = up_grads[0].shape[1] // 4 if paired else 0
    quarter_down = down_grads[0].shape[1] // 4 if paired else 0
    quarter = quarter_up + quarter_down

    def kernel(*refs):
        refs = list(refs)
        take = lambda number: [refs.pop(0) for _ in range(number)]
        b_ref, p_ref, c_ref = take(3)
        up_refs, down_refs = take(pairs), take(pairs)
        ob_ref, op_ref, oc_ref = take(3)
        if paired:
            (own_ref,) = take(1)
        b_scr, c_scr = take(3), take(3)
        p_send, p_recv, p_own = take(3)
        if paired:
            got_a, mine, got_b, a_send, a_recv, l_sem, x_send, x_recv = take(8)
        ring = Ring(count)
        here = lax.axis_index("narrow")
        chip, core = here // 2, here % 2
        others = [(ring.me + shift) % count for shift in range(1, count)]
        core_peer = 2 * chip + 1 - core
        chip_peer = 2 * (1 - chip) + core
        greet(others, [core_peer, chip_peer] if paired else [])

        def piece_refs(expert, owner):
            up, down = up_refs[expert // each], down_refs[expert // each]
            return (
                (up.at[expert % each, pl.ds(owner * quarter_up, quarter_up)], 0, quarter_up),
                (down.at[expert % each, pl.ds(owner * quarter_down, quarter_down)], quarter_up, quarter_down),
            )

        def to_core(e):
            return [
                remote(src, got_a.at[e, x, pl.ds(start, size)], a_send.at[e, x, k], a_recv.at[e, x, k], narrow=core_peer)
                for x in range(2)
                for k, (src, start, size) in enumerate(piece_refs(e, 2 * x + 1 - core))
            ]

        def load(e):
            return [
                pltpu.make_async_copy(src, mine.at[e, x, pl.ds(start, size)], l_sem.at[e, x, k])
                for x in range(2)
                for k, (src, start, size) in enumerate(piece_refs(e, 2 * x + core))
            ]

        def to_chip(e):
            return remote(mine.at[e, 1 - chip], got_b.at[e], x_send.at[e], x_recv.at[e], narrow=chip_peer)

        def expert_first(e):
            for c in to_core(e):
                c.wait_recv()
            for c in load(e):
                c.wait()
            block_add(mine.at[e, 1 - chip], mine.at[e, 1 - chip], got_a.at[e, 1 - chip], quarter)
            to_chip(e).start()
            block_add(mine.at[e, chip], mine.at[e, chip], got_a.at[e, chip], quarter)

        def expert_last(e):
            to_chip(e).wait_recv()
            block_add(own_ref.at[e], mine.at[e, chip], got_b.at[e], quarter)

        pick_copy = lambda k, target: remote(
            p_ref.at[target], op_ref.at[ring.me], p_send.at[k], p_recv.at[k], wide=target
        )
        for e in range(experts):
            for c in to_core(e):
                c.start()
            for c in load(e):
                c.start()
        own_pick = pltpu.make_async_copy(p_ref.at[ring.me], op_ref.at[ring.me], p_own)
        own_pick.start()
        for k, target in enumerate(others):
            pick_copy(k, target).start()

        def put(o_ref):
            def finish(row, size, got):
                o_ref[pl.ds(row, size)] = got.astype(o_ref.dtype)
            return finish

        b_steps = scatter_steps(ring, b_ref, *b_scr, put(ob_ref))
        c_steps = scatter_steps(ring, c_ref, *c_scr, put(oc_ref))
        queue = [(expert_first, e) for e in range(experts)]
        later = [(expert_last, e) for e in range(experts)]
        number = 0
        for steps in (b_steps, c_steps):
            for _ in steps:
                number += 1
                if queue:
                    job, e = queue.pop(0)
                    job(e)
                elif later and number % 3 == 0:
                    job, e = later.pop(0)
                    job(e)
        for job, e in queue + later:
            job(e)
        for e in range(experts):
            for c in to_core(e):
                c.wait_send()
            to_chip(e).wait_send()
        for k, target in enumerate(others):
            sender = (ring.me - (k + 1) + count) % count
            remote(
                p_ref.at[sender], op_ref.at[sender], p_send.at[k], p_recv.at[k], wide=target
            ).wait_recv()
            pick_copy(k, target).wait_send()
        own_pick.wait()

    vmem = pl.BlockSpec(memory_space=pltpu.VMEM)
    far = pl.BlockSpec(memory_space=pl.ANY)
    out_shape = [
        jax.ShapeDtypeStruct((rows, cols), F32),
        jax.ShapeDtypeStruct(picks.shape, F32),
        jax.ShapeDtypeStruct((rows, cols), F32),
    ]
    scratch = scatter_scratch(count, rows, cols) + scatter_scratch(count, rows, cols) + [
        pltpu.SemaphoreType.DMA((count - 1,)),
        pltpu.SemaphoreType.DMA((count - 1,)),
        pltpu.SemaphoreType.DMA,
    ]
    if paired:
        out_shape.append(jax.ShapeDtypeStruct((experts, quarter, cols), BF))
        scratch += [
            pltpu.VMEM((experts, 2, quarter, cols), BF),
            pltpu.VMEM((experts, 2, quarter, cols), BF),
            pltpu.VMEM((experts, quarter, cols), BF),
            pltpu.SemaphoreType.DMA((experts, 2, 2)),
            pltpu.SemaphoreType.DMA((experts, 2, 2)),
            pltpu.SemaphoreType.DMA((experts, 2, 2)),
            pltpu.SemaphoreType.DMA((experts,)),
            pltpu.SemaphoreType.DMA((experts,)),
        ]
    return pl.pallas_call(
        kernel,
        out_shape=out_shape,
        in_specs=[vmem] * 3 + [far] * (2 * pairs),
        out_specs=[vmem] * len(out_shape),
        scratch_shapes=scratch,
        compiler_params=pltpu.CompilerParams(
            collective_id=cid, has_side_effects=True, vmem_limit_bytes=56 * 2**20
        ),
    )(back, picks, expert_part, *up_grads, *down_grads)

def last_kernel(packed, own, shapes, cid):
    count, rows, cols = packed.shape
    paired = own is not None
    if paired:
        experts, quarter, width = own.shape
        up_shape, down_shape = shapes
        quarter_up, quarter_down = up_shape[1] // 4, down_shape[1] // 4

    def kernel(*refs):
        refs = list(refs)
        take = lambda number: [refs.pop(0) for _ in range(number)]
        (p_ref,) = take(1)
        if paired:
            (own_ref,) = take(1)
        (o_ref,) = take(1)
        if paired:
            up_ref, down_ref = take(2)
        s_scr, g_scr = take(3), take(2)
        if paired:
            c_send, c_recv, x_send, x_recv, f_send, f_recv, l_sem = take(7)
        ring = Ring(count)
        here = lax.axis_index("narrow")
        chip, core = here // 2, here % 2
        core_peer = 2 * chip + 1 - core
        chip_peer = 2 * (1 - chip) + core
        greet(list(ring.peers), [core_peer, chip_peer] if paired else [])

        def places(e, owner):
            return (
                (own_ref.at[e, pl.ds(0, quarter_up)], up_ref.at[e, pl.ds(owner * quarter_up, quarter_up)]),
                (own_ref.at[e, pl.ds(quarter_up, quarter_down)], down_ref.at[e, pl.ds(owner * quarter_down, quarter_down)]),
            )

        def send(e, sems, peer):
            return [
                remote(src, dst, sems[0].at[e, k], sems[1].at[e, k], narrow=peer)
                for k, (src, dst) in enumerate(places(e, here))
            ]

        def forward(e, owner, sems, peer):
            return [
                remote(dst, dst, sems[0].at[e, k], sems[1].at[e, k], narrow=peer)
                for k, (src, dst) in enumerate(places(e, owner))
            ]

        core_sems, chip_sems, far_sems = ((c_send, c_recv), (x_send, x_recv), (f_send, f_recv)) if paired else (None,) * 3

        def own_copy(e):
            return [
                pltpu.make_async_copy(src, dst, l_sem.at[e, k])
                for k, (src, dst) in enumerate(places(e, here))
            ]

        def pass_on(e):
            for c in forward(e, chip_peer, chip_sems, chip_peer):
                c.wait_recv()
            for c in forward(e, chip_peer, far_sems, core_peer):
                c.start()

        experts_here = experts if paired else 0
        for e in range(experts_here):
            for c in send(e, chip_sems, chip_peer):
                c.start()
        for e in range(experts_here):
            for c in send(e, core_sems, core_peer) + own_copy(e):
                c.start()

        def finish(row, size, got):
            o_ref[ring.me, pl.ds(row, size)] = got.astype(BF)

        waiting = list(range(experts_here))
        number = 0
        for steps in (scatter_steps(ring, p_ref, *s_scr, finish), gather_steps(ring, o_ref, *g_scr)):
            for _ in steps:
                number += 1
                if waiting and number % 4 == 0:
                    pass_on(waiting.pop(0))
        for e in waiting:
            pass_on(e)
        for e in range(experts_here):
            for c in own_copy(e):
                c.wait()
            for c in send(e, chip_sems, chip_peer) + send(e, core_sems, core_peer):
                c.wait_send()
            for c in forward(e, core_peer, core_sems, core_peer):
                c.wait_recv()
            far_owner = 2 * (1 - chip) + 1 - core
            for c in forward(e, chip_peer, far_sems, core_peer):
                c.wait_send()
            for c in forward(e, far_owner, far_sems, core_peer):
                c.wait_recv()

    vmem = pl.BlockSpec(memory_space=pltpu.VMEM)
    far = pl.BlockSpec(memory_space=pl.ANY)
    out_shape = [jax.ShapeDtypeStruct(packed.shape, BF)]
    operands = [packed]
    scratch = scatter_scratch(count, rows, cols) + gather_scratch(count)
    if paired:
        out_shape += [jax.ShapeDtypeStruct(s, BF) for s in shapes]
        operands.append(own)
        scratch += [pltpu.SemaphoreType.DMA((experts, 2))] * 7
    return pl.pallas_call(
        kernel,
        out_shape=out_shape,
        in_specs=[vmem] + [far] * (len(operands) - 1),
        out_specs=[vmem] + [far] * (len(out_shape) - 1),
        scratch_shapes=scratch,
        compiler_params=pltpu.CompilerParams(
            collective_id=cid, has_side_effects=True, vmem_limit_bytes=40 * 2**20
        ),
    )(*operands)


TILE = 256

def nt(a, b):
    return lax.dot_general(a, b, (((1,), (1,)), ((), ())), preferred_element_type=F32)

def tn(a, b):
    return lax.dot_general(a, b, (((0,), (0,)), ((), ())), preferred_element_type=F32)

def nn(a, b):
    return jnp.dot(a, b, preferred_element_type=F32)

def expert_pair(offsets, entry_all, grad_all, slots, slots_turned, gates, w_gate_up, w_down, earlier, first, pair, capacity):
    count, tokens, width = entry_all.shape
    ffe = w_down.shape[1]
    local = w_down.shape[0]
    room = count * capacity + TILE
    most = count * capacity // TILE
    adding = earlier is not None

    def kernel(off_ref, e_ref, g_ref, s_ref, st_ref, gate_ref, wgu_ref, wd_ref, *rest):
        if adding:
            pc_ref, pb_ref = rest[:2]
            rest = rest[2:]
        c_ref, b_ref, pick_ref, dgu_ref, dd_ref, x_s, s_s, act_s, pg_s, cr_s, bk_s, gcol, pcol, sems = rest
        e = pl.program_id(0)
        if adding:
            fetch = [
                pltpu.make_async_copy(pc_ref, c_ref, sems.at[0]),
                pltpu.make_async_copy(pb_ref, b_ref, sems.at[1]),
            ]

        @pl.when(e == 0)
        def _():
            if adding:
                for f in fetch:
                    f.start()
            cr_s[...] = jnp.zeros_like(cr_s)
            bk_s[...] = jnp.zeros_like(bk_s)
            pcol[...] = jnp.zeros_like(pcol)

        def start_of(expert, b):
            return pl.multiple_of(off_ref[(first + expert) * (count + 1) + b], 16)

        places = lax.broadcasted_iota(jnp.int32, (capacity, tokens), 0)
        for b in range(count):
            pick_out = places == s_ref[first + e, b : b + 1, :]
            chosen = jnp.where(pick_out, 1.0, 0.0).astype(BF)
            span = pl.ds(start_of(e, b), capacity)
            x_s[span] = nn(chosen, e_ref[b]).astype(BF)
            s_s[span] = nn(chosen, g_ref[b]).astype(BF)
            gate_col = jnp.sum(
                jnp.where(pick_out, gate_ref[first + e, b : b + 1, :], 0.0), axis=1, keepdims=True
            )
            gcol[span] = jnp.broadcast_to(gate_col, (capacity, 128))
        total = start_of(e, count)
        tail = pl.ds(total, TILE)
        x_s[tail] = jnp.zeros((TILE, width), BF)
        s_s[tail] = jnp.zeros((TILE, width), BF)
        gcol[tail] = jnp.zeros((TILE, 128), F32)
        tiles = (total + TILE - 1) // TILE

        def step(i, carry):
            rows = pl.ds(pl.multiple_of(i * TILE, TILE), TILE)
            pre = nn(x_s[rows], wgu_ref[0])
            gate_part = pre[:, :ffe]
            up_part = pre[:, ffe:]
            sig = jax.nn.sigmoid(gate_part)
            swish = gate_part * sig
            act = (swish * up_part).astype(BF)
            act_s[rows] = act
            result = nn(act, wd_ref[0]).astype(BF).astype(F32)
            grad_rows = s_s[rows].astype(F32)
            gate = gcol[rows][:, :1]
            pcol[rows] = jnp.broadcast_to(
                jnp.sum(result * grad_rows, axis=1, keepdims=True), (TILE, 128)
            )
            cr_s[e, rows] = (gate * result).astype(BF)
            slot_grad = (gate * grad_rows).astype(BF)
            s_s[rows] = slot_grad
            act_grad = nt(slot_grad, wd_ref[0])
            gate_grad = act_grad * up_part * sig * (1.0 + gate_part * (1.0 - sig))
            pre_grad = jnp.concatenate([gate_grad, act_grad * swish], axis=1).astype(BF)
            pg_s[rows] = pre_grad
            bk_s[e, rows] = nt(pre_grad, wgu_ref[0]).astype(BF)
            return carry

        lax.fori_loop(0, tiles, step, 0)
        for b in range(count):
            pick_out = places == s_ref[first + e, b : b + 1, :]
            span = pl.ds(start_of(e, b), capacity)
            pick_ref[0, b : b + 1, :] = jnp.sum(
                jnp.where(pick_out, pcol[span][:, :1], 0.0), axis=0, keepdims=True
            )

        @pl.when(tiles == 0)
        def _():
            dgu_ref[...] = jnp.zeros_like(dgu_ref)
            dd_ref[...] = jnp.zeros_like(dd_ref)

        block = 256
        for k in range(1, most + 1):

            @pl.when(tiles == k)
            def _(k=k):
                def columns(j, carry):
                    cols = pl.ds(pl.multiple_of(j * block, block), block)
                    dgu_ref[0, :, cols] = tn(x_s[: k * TILE], pg_s[: k * TILE, cols]).astype(BF)
                    dd_ref[0, :, cols] = tn(act_s[: k * TILE], s_s[: k * TILE, cols]).astype(BF)
                    return carry

                lax.fori_loop(0, width // block, columns, 0)

        @pl.when(e == pair - 1)
        def _():
            if adding:
                for f in fetch:
                    f.wait()
            across = lax.broadcasted_iota(jnp.int32, (tokens, capacity), 1)
            for b in range(count):
                sum_c = sum_b = None
                for x in range(pair):
                    back = jnp.where(across == st_ref[b][:, first + x : first + x + 1], 1.0, 0.0).astype(BF)
                    span = pl.ds(start_of(x, b), capacity)
                    one_c, one_b = nn(back, cr_s[x, span]), nn(back, bk_s[x, span])
                    sum_c = one_c if sum_c is None else sum_c + one_c
                    sum_b = one_b if sum_b is None else sum_b + one_b
                if adding:
                    sum_c = sum_c + c_ref[b].astype(F32)
                    sum_b = sum_b + b_ref[b].astype(F32)
                c_ref[b] = sum_c.astype(BF)
                b_ref[b] = sum_b.astype(BF)

    once = pl.Buffered(1)
    whole = lambda shape: pl.BlockSpec(shape, lambda e, off: (0,) * len(shape), pipeline_mode=once)
    any_space = pl.BlockSpec(memory_space=pl.ANY)
    cube = (count, tokens, width)
    in_specs = [
        whole(cube), whole(cube), whole(slots.shape), whole(slots_turned.shape), whole(gates.shape),
        pl.BlockSpec((1, width, 2 * ffe), lambda e, off: (first + e, 0, 0)),
        pl.BlockSpec((1, ffe, width), lambda e, off: (first + e, 0, 0)),
    ]
    operands = [entry_all, grad_all, slots, slots_turned, gates, w_gate_up, w_down]
    if adding:
        in_specs += [any_space, any_space]
        operands += list(earlier)
    return pl.pallas_call(
        kernel,
        grid_spec=pltpu.PrefetchScalarGridSpec(
            num_scalar_prefetch=1,
            grid=(pair,),
            in_specs=in_specs,
            out_specs=[
                whole(cube), whole(cube),
                pl.BlockSpec((1, count, tokens), lambda e, off: (e, 0, 0)),
                pl.BlockSpec((1, width, 2 * ffe), lambda e, off: (e, 0, 0)),
                pl.BlockSpec((1, ffe, width), lambda e, off: (e, 0, 0)),
            ],
            scratch_shapes=[
                pltpu.VMEM((room, width), BF),
                pltpu.VMEM((room, width), BF),
                pltpu.VMEM((room, ffe), BF),
                pltpu.VMEM((room, 2 * ffe), BF),
                pltpu.VMEM((pair, room, width), BF),
                pltpu.VMEM((pair, room, width), BF),
                pltpu.VMEM((room, 128), F32),
                pltpu.VMEM((room, 128), F32),
                pltpu.SemaphoreType.DMA((2,)),
            ],
        ),
        out_shape=[
            jax.ShapeDtypeStruct(cube, BF),
            jax.ShapeDtypeStruct(cube, BF),
            jax.ShapeDtypeStruct((pair, count, tokens), F32),
            jax.ShapeDtypeStruct((pair, width, 2 * ffe), BF),
            jax.ShapeDtypeStruct((pair, ffe, width), BF),
        ],
        compiler_params=pltpu.CompilerParams(
            dimension_semantics=("arbitrary",), vmem_limit_bytes=60 * 2**20
        ),
        cost_estimate=pl.CostEstimate(
            flops=pair * count * capacity * 6 * width * ffe * 3, bytes_accessed=40 * 2**20, transcendentals=0
        ),
    )(offsets, *operands)


def local(
    hidden,
    lengths,
    routes,
    cotangent,
    attn_gain,
    w_query,
    w_key,
    w_value,
    w_out,
    moe_gain,
    w_router,
    w_gate_up,
    w_down,
):
    rows_here = hidden.shape[1]
    width = hidden.shape[2]
    wide = lax.axis_size("wide")
    seq_len = rows_here * lax.axis_size("narrow")
    head_dim = HEAD_DIM
    group_size = HEADS // KV_HEADS
    kv_here = w_key.shape[1] // head_dim
    query_cols = kv_here * group_size * head_dim
    key_cols = kv_here * head_dim
    scaling = head_dim ** (-0.5)
    block_rows = min(512, seq_len)
    block_count = seq_len // block_rows
    length_here = lengths[0]
    offset = lax.axis_index("narrow") * rows_here
    local_places = offset + jnp.arange(rows_here, dtype=jnp.int32)
    valid = (local_places < length_here).astype(jnp.float32)[:, None]
    grad_all = lax.all_gather(cotangent[0], "wide", axis=0)
    picks = routes.shape[2]
    expert_total = w_router.shape[1]
    expert_here = w_gate_up.shape[0]
    first_expert = lax.axis_index("wide") * expert_here
    capacity = 2 * rows_here * picks // expert_total
    labels = jnp.concatenate(
        [routes[0].T, jnp.broadcast_to(lengths[0], (1, rows_here)).astype(jnp.int32)], axis=0
    )
    labels_all = lax.all_gather(labels, "wide", axis=0)
    routes_all = labels_all[:, :picks]
    valid_all = local_places[None, None, :] < labels_all[:, picks:]
    experts = jnp.arange(expert_total, dtype=jnp.int32)
    member_all = jnp.any(routes_all[:, :, None, :] == experts[None, None, :, None], axis=1)
    member_here = lax.dynamic_slice_in_dim(member_all, first_expert, expert_here, 1) & valid_all
    upper = jnp.triu(jnp.ones((rows_here, rows_here), BF))
    reached = jnp.einsum(
        "bet,ts->bes", member_here.astype(BF), upper, preferred_element_type=F32
    ).astype(jnp.int32)
    slots = jnp.where(member_here, reached - 1, -1).transpose(1, 0, 2)
    slots_turned = slots.transpose(1, 2, 0)
    padded = (reached[:, :, -1].T + 15) // 16 * 16
    offsets = jnp.concatenate(
        [jnp.zeros((expert_here, 1), jnp.int32), jnp.cumsum(padded, axis=1)], axis=1
    ).reshape(-1)

    source = hidden[0].astype(jnp.float32)
    normed, scale_one = norm_forward(source, attn_gain)
    normed_low = normed.astype(jnp.bfloat16)
    whole = lax.all_gather(normed_low, "narrow", axis=0, tiled=True)
    w_qkv = jnp.concatenate([w_query, w_key, w_value], axis=1)
    projected = jnp.dot(whole, w_qkv, preferred_element_type=jnp.float32)
    cosine, sine_part = rope_tables(seq_len, head_dim)
    query_rot = turn(
        projected[:, :query_cols].reshape(seq_len, kv_here, group_size, head_dim),
        cosine,
        sine_part,
        1.0,
    )
    key_rot = turn(
        projected[:, query_cols : query_cols + key_cols].reshape(seq_len, kv_here, head_dim),
        cosine,
        sine_part,
        1.0,
    )
    queries = (
        query_rot.astype(jnp.bfloat16)
        .reshape(block_count, block_rows, kv_here, group_size, head_dim)
        .transpose(0, 2, 3, 1, 4)
    )
    keys_low = key_rot.astype(jnp.bfloat16).transpose(1, 0, 2)
    values_low = (
        projected[:, query_cols + key_cols :]
        .astype(jnp.bfloat16)
        .reshape(seq_len, kv_here, head_dim)
        .transpose(1, 0, 2)
    )
    context, log_sums = attend_forward(queries, keys_low, values_low, length_here, scaling)
    context_rows = context.transpose(0, 3, 1, 2, 4).reshape(seq_len, query_cols)
    attn_part = lax.psum_scatter(
        jnp.dot(context_rows, w_out, preferred_element_type=jnp.float32).astype(jnp.bfloat16),
        "narrow",
        scatter_dimension=0,
        tiled=True,
    ).astype(jnp.float32)
    mixed = source + attn_part
    normed_two, scale_two = norm_forward(mixed, moe_gain)
    entry = normed_two.astype(jnp.bfloat16)

    entry_all = ring_gather(entry, wide, 1)
    logits = jnp.einsum("btd,de->bet", entry_all, w_router, preferred_element_type=F32)
    masked = jnp.where(member_all, logits, -jnp.inf)
    raised = jnp.exp(masked - jnp.max(masked, axis=1, keepdims=True))
    shares_all = raised / jnp.sum(raised, axis=1, keepdims=True)
    gates = (
        lax.dynamic_slice_in_dim(shares_all, first_expert, expert_here, 1) * valid_all.astype(F32)
    ).transpose(1, 0, 2)
    pair = min(2, expert_here)
    earlier, pick_parts, weight_parts = None, [], []
    for first in range(0, expert_here, pair):
        expert_part, back_part, pick_part, up_part, down_part = expert_pair(
            offsets, entry_all, grad_all, slots, slots_turned, gates, w_gate_up, w_down,
            earlier, first, pair, capacity,
        )
        earlier = (expert_part, back_part)
        pick_parts.append(pick_part)
        weight_parts.append((up_part, down_part))
    picks_out = jnp.concatenate(pick_parts, axis=0).transpose(1, 0, 2)
    paired = lax.axis_size("narrow") == 4
    ups = [p[0] for p in weight_parts]
    downs = [p[1] for p in weight_parts]
    entry_home, pick_home, expert_sum, *own = home_kernel(
        back_part, picks_out, expert_part, ups if paired else [], downs if paired else [], 2
    )
    pick_home = pick_home.reshape(expert_total, rows_here)
    output_rows = (valid * (mixed + expert_sum)).astype(jnp.bfloat16)
    grad_rows_here = cotangent[0].astype(jnp.float32) * valid

    shares = lax.dynamic_index_in_dim(shares_all, lax.axis_index("wide"), 0, keepdims=False)
    logit_grad = shares * (pick_home - jnp.sum(shares * pick_home, axis=0, keepdims=True))
    router_grad = lax.dot_general(
        entry.astype(jnp.float32), logit_grad, (((0,), (1,)), ((), ())), precision=HIGHEST
    )
    entry_grad = entry_home + lax.dot_general(
        logit_grad, w_router.astype(jnp.float32), (((0,), (1,)), ((), ())), precision=HIGHEST
    )
    mixed_from_norm, gain_two_grad = norm_backward(mixed, scale_two, moe_gain, entry_grad)
    mixed_grad = grad_rows_here + mixed_from_norm
    attn_grad_low = mixed_grad.astype(jnp.bfloat16)
    grad_whole = lax.all_gather(attn_grad_low, "narrow", axis=0, tiled=True)
    context_grad = lax.dot_general(
        grad_whole, w_out, (((1,), (1,)), ((), ())), preferred_element_type=jnp.float32
    ).astype(jnp.bfloat16)
    out_grad = lax.dot_general(
        context_rows, grad_whole, (((0,), (0,)), ((), ())), preferred_element_type=jnp.float32
    )
    context_blocks = context_grad.reshape(
        block_count, block_rows, kv_here, group_size, head_dim
    ).transpose(0, 2, 3, 1, 4)
    query_grad, key_grad, value_grad = attend_backward(
        queries, keys_low, values_low, context_blocks, log_sums, length_here, scaling
    )
    query_rows = turn(
        query_grad.transpose(0, 3, 1, 2, 4).reshape(seq_len, kv_here, group_size, head_dim),
        cosine,
        sine_part,
        -1.0,
    )
    key_rows = turn(key_grad.transpose(1, 0, 2), cosine, sine_part, -1.0)
    value_rows = value_grad.transpose(1, 0, 2)
    qkv_grad = jnp.concatenate(
        [
            query_rows.reshape(seq_len, query_cols),
            key_rows.reshape(seq_len, key_cols),
            value_rows.reshape(seq_len, key_cols),
        ],
        axis=1,
    ).astype(jnp.bfloat16)
    qkv_weight_grad = lax.dot_general(
        whole, qkv_grad, (((0,), (0,)), ((), ())), preferred_element_type=jnp.float32
    )
    normed_grad = lax.psum_scatter(
        lax.dot_general(
            qkv_grad, w_qkv, (((1,), (1,)), ((), ())), preferred_element_type=jnp.float32
        ).astype(jnp.bfloat16),
        "narrow",
        scatter_dimension=0,
        tiled=True,
    ).astype(jnp.float32)
    source_from_norm, gain_one_grad = norm_backward(source, scale_one, attn_gain, normed_grad)
    grad_input = (mixed_grad + source_from_norm).astype(jnp.bfloat16)
    gain_one_grad = jnp.sum(qkv_weight_grad * w_qkv.astype(F32), axis=1) / attn_gain
    small = jnp.concatenate(
        [router_grad.T, gain_one_grad[None], gain_two_grad[None], jnp.zeros((14, width), F32)], axis=0
    )
    small = lax.psum(small.astype(BF), "narrow").astype(F32)
    lanes = query_cols + 2 * key_cols
    rows_of = lambda array: [array[:, i : i + lanes] for i in range(0, width, lanes)]
    flat = jnp.concatenate([qkv_weight_grad, *rows_of(out_grad), *rows_of(small)], axis=0).astype(BF)
    block = -(-flat.shape[0] // (32 * wide)) * 32
    packed = jnp.pad(flat, ((0, block * wide - flat.shape[0]), (0, 0))).reshape(wide, block, lanes)
    summed, *expert_grads = last_kernel(
        packed, own[0] if paired else None, (w_gate_up.shape, w_down.shape), 3
    )
    if paired:
        gate_up_grad, down_grad = expert_grads[0].astype(F32), expert_grads[1].astype(F32)
    else:
        gate_up_grad = lax.psum(jnp.concatenate(ups, axis=0), "narrow").astype(F32)
        down_grad = lax.psum(jnp.concatenate(downs, axis=0), "narrow").astype(F32)
    summed = summed.reshape(wide * block, lanes).astype(F32)
    qkv_weight_grad = summed[:width]
    blocks_of = lambda start, rows: jnp.concatenate(
        [summed[start + i * rows : start + (i + 1) * rows] for i in range(width // lanes)], axis=1
    )
    out_grad = blocks_of(width, query_cols)
    small = blocks_of(width + query_cols * (width // lanes), small.shape[0])
    router_grad = small[:expert_total].T
    gain_one_grad = small[expert_total]
    gain_two_grad = small[expert_total + 1]
    query_weight_grad = qkv_weight_grad[:, :query_cols]
    key_weight_grad = qkv_weight_grad[:, query_cols : query_cols + key_cols]
    value_weight_grad = qkv_weight_grad[:, query_cols + key_cols :]
    return (
        output_rows[None],
        grad_input[None],
        gain_one_grad,
        query_weight_grad,
        key_weight_grad,
        value_weight_grad,
        out_grad,
        gain_two_grad,
        router_grad,
        gate_up_grad,
        down_grad,
    )


def solution(mesh):
    in_specs = (
        P("wide", "narrow", None),
        P("wide"),
        P("wide", "narrow", None),
        P("wide", "narrow", None),
        P(),
        P(None, "narrow"),
        P(None, "narrow"),
        P(None, "narrow"),
        P("narrow", None),
        P(),
        P(),
        P("wide", None, None),
        P("wide", None, None),
    )
    out_specs = (
        P("wide", "narrow", None),
        P("wide", "narrow", None),
        P(),
        P(None, "narrow"),
        P(None, "narrow"),
        P(None, "narrow"),
        P("narrow", None),
        P(),
        P(),
        P("wide", None, None),
        P("wide", None, None),
    )
    return jax.shard_map(local, mesh=mesh, in_specs=in_specs, out_specs=out_specs, check_vma=False)
```

```python
import jax
import jax.numpy as jnp
from jax import lax
from jax.experimental import pallas as pl
from jax.experimental.pallas import tpu as pltpu
from jax.sharding import PartitionSpec as P

HEADS = 16
KV_HEADS = 8
HEAD_DIM = 64
BF = jnp.bfloat16
F32 = jnp.float32
MESH = pl.DeviceIdType.MESH
EPSILON = 1e-06
THETA = 10000.0
HIGHEST = lax.Precision.HIGHEST


def rope_tables(count, head_dim):
    half_dim = head_dim // 2
    inverse = THETA ** (-jnp.arange(half_dim, dtype=jnp.float32) * 2.0 / head_dim)
    angles = jnp.arange(count, dtype=jnp.float32)[:, None] * inverse[None, :]
    return (jnp.cos(angles), jnp.sin(angles))


def turn(values, cosine, sine_part, direction):
    half_dim = values.shape[-1] // 2
    shape_here = (cosine.shape[0],) + (1,) * (values.ndim - 2) + (half_dim,)
    cosine = cosine.reshape(shape_here)
    sine_part = direction * sine_part.reshape(shape_here)
    first = values[..., :half_dim]
    second = values[..., half_dim:]
    return jnp.concatenate(
        [first * cosine - second * sine_part, second * cosine + first * sine_part], axis=-1
    )


def norm_forward(values, gain):
    scaling = lax.rsqrt(jnp.mean(values * values, axis=-1, keepdims=True) + EPSILON)
    return (values * scaling * gain, scaling)


def norm_backward(values, scaling, gain, incoming):
    unit_values = values * scaling
    gain_grad = jnp.sum(incoming * unit_values, axis=0)
    inner = incoming * gain
    input_grad = scaling * (
        inner - unit_values * jnp.mean(inner * unit_values, axis=-1, keepdims=True)
    )
    return (input_grad, gain_grad)


def visible(start, block_rows, key_places, length_here):
    query_places = start + jnp.arange(block_rows, dtype=jnp.int32)
    return (key_places[None, :] <= query_places[:, None]) & (key_places[None, :] < length_here)


def attend_forward(queries, keys_low, values_low, length_here, scaling):
    key_places = jnp.arange(keys_low.shape[1], dtype=jnp.int32)
    block_rows = queries.shape[3]

    def one_block(inputs):
        query_block, start = inputs
        scores = (
            jnp.einsum("kgqd,ksd->kgqs", query_block, keys_low, preferred_element_type=jnp.float32)
            * scaling
        )
        scores = jnp.where(visible(start, block_rows, key_places, length_here), scores, -1e30)
        highest = jnp.max(scores, axis=-1, keepdims=True)
        weights = jnp.exp(scores - highest)
        totals = jnp.sum(weights, axis=-1, keepdims=True)
        chances = (weights / totals).astype(jnp.bfloat16)
        context = jnp.einsum(
            "kgqs,ksd->kgqd", chances, values_low, preferred_element_type=jnp.float32
        )
        return (context.astype(jnp.bfloat16), (highest + jnp.log(totals))[..., 0])

    starts = jnp.arange(queries.shape[0], dtype=jnp.int32) * block_rows
    return lax.map(one_block, (queries, starts))


def attend_backward(queries, keys_low, values_low, context_grad, log_sums, length_here, scaling):
    key_places = jnp.arange(keys_low.shape[1], dtype=jnp.int32)
    block_rows = queries.shape[3]

    def one_block(carry, inputs):
        key_grad, value_grad = carry
        query_block, grad_block, sum_block, start = inputs
        scores = (
            jnp.einsum("kgqd,ksd->kgqs", query_block, keys_low, preferred_element_type=jnp.float32)
            * scaling
        )
        allowed = visible(start, block_rows, key_places, length_here)
        scores = jnp.where(allowed, scores, -1e30)
        chances = jnp.where(allowed, jnp.exp(scores - sum_block[..., None]), 0.0)
        chance_grad = jnp.einsum(
            "kgqd,ksd->kgqs", grad_block, values_low, preferred_element_type=jnp.float32
        )
        inner = jnp.sum(chances * chance_grad, axis=-1, keepdims=True)
        score_grad = (chances * (chance_grad - inner)).astype(jnp.bfloat16)
        query_grad = (
            jnp.einsum("kgqs,ksd->kgqd", score_grad, keys_low, preferred_element_type=jnp.float32)
            * scaling
        )
        key_grad = (
            key_grad
            + jnp.einsum(
                "kgqs,kgqd->ksd", score_grad, query_block, preferred_element_type=jnp.float32
            )
            * scaling
        )
        value_grad = value_grad + jnp.einsum(
            "kgqs,kgqd->ksd",
            chances.astype(jnp.bfloat16),
            grad_block,
            preferred_element_type=jnp.float32,
        )
        return ((key_grad, value_grad), query_grad)

    starts = jnp.arange(queries.shape[0], dtype=jnp.int32) * block_rows
    zeros = jnp.zeros(keys_low.shape, jnp.float32)
    (key_grad, value_grad), query_grad = lax.scan(
        one_block, (zeros, zeros), (queries, context_grad, log_sums, starts)
    )
    return (query_grad, key_grad, value_grad)


def ring_place(index, count):
    half = index // 2
    odd = index % 2
    return (1 - odd) * half + odd * (count - 1 - half)

def ring_index(place, count):
    odd = place // (count // 2)
    half = (1 - odd) * place + odd * (count - 1 - place)
    return 2 * half + odd


def add_low(one, two):
    return (one.astype(F32) + two.astype(F32)).astype(BF)

class Ring:
    def __init__(self, count):
        self.count = count
        self.me = lax.axis_index("wide")
        self.place = ring_place(self.me, count)
        self.peers = (self.at(1), self.at(-1))

    def at(self, shift):
        return ring_index((self.place + shift + 2 * self.count) % self.count, self.count)

def greet(wide_peers, narrow_peers):
    barrier = pltpu.get_barrier_semaphore()
    for peer in wide_peers:
        pl.semaphore_signal(barrier, inc=1, device_id={"wide": peer}, device_id_type=MESH)
    for peer in narrow_peers:
        pl.semaphore_signal(barrier, inc=1, device_id={"narrow": peer}, device_id_type=MESH)
    pl.semaphore_wait(barrier, len(wide_peers) + len(narrow_peers))

def remote(source, target, send, recv, **device):
    return pltpu.make_async_remote_copy(
        src_ref=source, dst_ref=target, send_sem=send, recv_sem=recv,
        device_id=device, device_id_type=MESH,
    )

def cuts(rows):
    first = (rows // 2 + 15) // 16 * 16
    return ((0, first), (first, rows - first))

def scatter_steps(ring, p_ref, held, send_sem, recv_sem, finish):
    count = ring.count
    lane = p_ref.shape[1] // 2

    def copy(way, step, k):
        sign = 1 if way == 0 else -1
        start, size = cuts(lane)[k]
        src = (
            p_ref.at[ring.at(-sign), pl.ds(way * lane + start, size)]
            if step == 0
            else held.at[way, step - 1, pl.ds(start, size)]
        )
        return remote(
            src, held.at[way, step, pl.ds(start, size)],
            send_sem.at[way, step, k], recv_sem.at[way, step, k], wide=ring.peers[way],
        )

    for step in range(count - 1):
        for k in range(2):
            for way in range(2):
                sign = 1 if way == 0 else -1
                start, size = cuts(lane)[k]
                if step > 0:
                    copy(way, step - 1, k).wait_recv()
                    span = pl.ds(start, size)
                    mine = p_ref[ring.at(-sign * (1 + step)), pl.ds(way * lane + start, size)]
                    held[way, step - 1, span] = add_low(held[way, step - 1, span], mine)
                copy(way, step, k).start()
        yield
    for k in range(2):
        for way in range(2):
            start, size = cuts(lane)[k]
            copy(way, count - 2, k).wait_recv()
            row = way * lane + start
            finish(
                row, size,
                held[way, count - 2, pl.ds(start, size)].astype(F32)
                + p_ref[ring.me, pl.ds(row, size)].astype(F32),
            )
    for step in range(count - 1):
        for k in range(2):
            for way in range(2):
                copy(way, step, k).wait_send()
    yield

def gather_steps(ring, o_ref, send_sem, recv_sem, own=None):
    count = ring.count
    hops = count // 2
    rows = o_ref.shape[1]
    live = lambda way, hop, k: hop < hops - 1 or k == way

    def copy(way, hop, k, shift):
        sign = 1 if way == 0 else -1
        start, size = cuts(rows)[k]
        block = o_ref.at[ring.at(-sign * (hop + shift)), pl.ds(start, size)]
        from_own = own is not None and hop == 0 and shift == 0
        return remote(
            own.at[pl.ds(start, size)] if from_own else block, block, send_sem.at[way, hop, k], recv_sem.at[way, hop, k], wide=ring.peers[way]
        )

    for hop in range(hops):
        for k in range(2):
            for way in range(2):
                if live(way, hop, k):
                    if hop > 0:
                        copy(way, hop - 1, k, 1).wait_recv()
                    copy(way, hop, k, 0).start()
        yield
    for hop in range(hops):
        for k in range(2):
            for way in range(2):
                if live(way, hop, k) and not (hop + 1 < hops and live(way, hop + 1, k)):
                    copy(way, hop, k, 1).wait_recv()
    for hop in range(hops):
        for k in range(2):
            for way in range(2):
                if live(way, hop, k):
                    copy(way, hop, k, 0).wait_send()
    yield

def scatter_scratch(count, rows, cols):
    return [
        pltpu.VMEM((2, count - 1, rows // 2, cols), BF),
        pltpu.SemaphoreType.DMA((2, count - 1, 2)),
        pltpu.SemaphoreType.DMA((2, count - 1, 2)),
    ]

def gather_scratch(count):
    return [pltpu.SemaphoreType.DMA((2, count // 2, 2)), pltpu.SemaphoreType.DMA((2, count // 2, 2))]

def run(*makers):
    live = list(makers)
    while live:
        for one in list(live):
            if next(one, "end") == "end":
                live.remove(one)

def block_add(out, one, two, rows):
    def step(i, carry):
        span = pl.ds(pl.multiple_of(i * 128, 128), 128)
        out[span] = add_low(one[span], two[span])
        return carry
    lax.fori_loop(0, rows // 128, step, 0)

def home_kernel(back, picks, up_grads, down_grads, cid):
    count, rows, cols = back.shape
    paired = len(up_grads) > 0
    pairs = len(up_grads)
    each = up_grads[0].shape[0] if paired else 0
    experts = pairs * each
    quarter_up = up_grads[0].shape[1] // 4 if paired else 0
    quarter_down = down_grads[0].shape[1] // 4 if paired else 0
    quarter = quarter_up + quarter_down

    def kernel(*refs):
        refs = list(refs)
        take = lambda number: [refs.pop(0) for _ in range(number)]
        b_ref, p_ref = take(2)
        up_refs, down_refs = take(pairs), take(pairs)
        ob_ref, op_ref = take(2)
        if paired:
            (own_ref,) = take(1)
        b_scr = take(3)
        p_send, p_recv, p_own = take(3)
        if paired:
            got_a, mine, got_b, a_send, a_recv, l_sem, x_send, x_recv = take(8)
        ring = Ring(count)
        here = lax.axis_index("narrow")
        chip, core = here // 2, here % 2
        others = [(ring.me + shift) % count for shift in range(1, count)]
        core_peer = 2 * chip + 1 - core
        chip_peer = 2 * (1 - chip) + core
        greet(others, [core_peer, chip_peer] if paired else [])

        def piece_refs(expert, owner):
            up, down = up_refs[expert // each], down_refs[expert // each]
            return (
                (up.at[expert % each, pl.ds(owner * quarter_up, quarter_up)], 0, quarter_up),
                (down.at[expert % each, pl.ds(owner * quarter_down, quarter_down)], quarter_up, quarter_down),
            )

        def to_core(e):
            return [
                remote(src, got_a.at[e, x, pl.ds(start, size)], a_send.at[e, x, k], a_recv.at[e, x, k], narrow=core_peer)
                for x in range(2)
                for k, (src, start, size) in enumerate(piece_refs(e, 2 * x + 1 - core))
            ]

        def load(e):
            return [
                pltpu.make_async_copy(src, mine.at[e, x, pl.ds(start, size)], l_sem.at[e, x, k])
                for x in range(2)
                for k, (src, start, size) in enumerate(piece_refs(e, 2 * x + core))
            ]

        def to_chip(e):
            return remote(mine.at[e, 1 - chip], got_b.at[e], x_send.at[e], x_recv.at[e], narrow=chip_peer)

        def expert_first(e):
            for c in to_core(e):
                c.wait_recv()
            for c in load(e):
                c.wait()
            block_add(mine.at[e, 1 - chip], mine.at[e, 1 - chip], got_a.at[e, 1 - chip], quarter)
            to_chip(e).start()
            block_add(mine.at[e, chip], mine.at[e, chip], got_a.at[e, chip], quarter)

        def expert_last(e):
            to_chip(e).wait_recv()
            block_add(own_ref.at[e], mine.at[e, chip], got_b.at[e], quarter)

        pick_copy = lambda k, target: remote(
            p_ref.at[target], op_ref.at[ring.me], p_send.at[k], p_recv.at[k], wide=target
        )
        for e in range(experts):
            for c in to_core(e):
                c.start()
            for c in load(e):
                c.start()
        own_pick = pltpu.make_async_copy(p_ref.at[ring.me], op_ref.at[ring.me], p_own)
        own_pick.start()
        for k, target in enumerate(others):
            pick_copy(k, target).start()

        def put(o_ref):
            def finish(row, size, got):
                o_ref[pl.ds(row, size)] = got.astype(o_ref.dtype)
            return finish

        b_steps = scatter_steps(ring, b_ref, *b_scr, put(ob_ref))
        queue = [(expert_first, e) for e in range(experts)]
        later = [(expert_last, e) for e in range(experts)]
        for number, _ in enumerate(b_steps):
            if queue:
                job, e = queue.pop(0)
                job(e)
            elif later and number % 2 == 1:
                job, e = later.pop(0)
                job(e)
        for job, e in queue + later:
            job(e)
        for e in range(experts):
            for c in to_core(e):
                c.wait_send()
            to_chip(e).wait_send()
        for k, target in enumerate(others):
            sender = (ring.me - (k + 1) + count) % count
            remote(
                p_ref.at[sender], op_ref.at[sender], p_send.at[k], p_recv.at[k], wide=target
            ).wait_recv()
            pick_copy(k, target).wait_send()
        own_pick.wait()

    vmem = pl.BlockSpec(memory_space=pltpu.VMEM)
    far = pl.BlockSpec(memory_space=pl.ANY)
    out_shape = [
        jax.ShapeDtypeStruct((rows, cols), F32),
        jax.ShapeDtypeStruct(picks.shape, F32),
    ]
    scratch = scatter_scratch(count, rows, cols) + [
        pltpu.SemaphoreType.DMA((count - 1,)),
        pltpu.SemaphoreType.DMA((count - 1,)),
        pltpu.SemaphoreType.DMA,
    ]
    if paired:
        out_shape.append(jax.ShapeDtypeStruct((experts, quarter, cols), BF))
        scratch += [
            pltpu.VMEM((experts, 2, quarter, cols), BF),
            pltpu.VMEM((experts, 2, quarter, cols), BF),
            pltpu.VMEM((experts, quarter, cols), BF),
            pltpu.SemaphoreType.DMA((experts, 2, 2)),
            pltpu.SemaphoreType.DMA((experts, 2, 2)),
            pltpu.SemaphoreType.DMA((experts, 2, 2)),
            pltpu.SemaphoreType.DMA((experts,)),
            pltpu.SemaphoreType.DMA((experts,)),
        ]
    return pl.pallas_call(
        kernel,
        out_shape=out_shape,
        in_specs=[vmem] * 2 + [far] * (2 * pairs),
        out_specs=[vmem] * len(out_shape),
        scratch_shapes=scratch,
        compiler_params=pltpu.CompilerParams(
            collective_id=cid, has_side_effects=True, vmem_limit_bytes=56 * 2**20
        ),
    )(back, picks, *up_grads, *down_grads)


def nt(a, b):
    return lax.dot_general(a, b, (((1,), (1,)), ((), ())), preferred_element_type=F32)

def tn(a, b):
    return lax.dot_general(a, b, (((0,), (0,)), ((), ())), preferred_element_type=F32)

def nn(a, b):
    return jnp.dot(a, b, preferred_element_type=F32)

LANES = 128

def lane_of(shape):
    return lax.broadcasted_iota(jnp.int32, shape, len(shape) - 1)

def turn_lanes(values, cosine, signed_sine):
    low = lane_of(values.shape) % HEAD_DIM < HEAD_DIM // 2
    swapped = jnp.where(
        low,
        pltpu.roll(values, LANES - HEAD_DIM // 2, 1),
        pltpu.roll(values, HEAD_DIM // 2, 1),
    )
    return values * cosine + swapped * signed_sine

def doubled(tile, head):
    other = pltpu.roll(tile, HEAD_DIM, 1)
    low = lane_of(tile.shape) < HEAD_DIM
    return jnp.where(low, tile, other) if head == 0 else jnp.where(low, other, tile)

def stacked(tile):
    low = lane_of(tile.shape) < HEAD_DIM
    zero = jnp.zeros_like(tile)
    return jnp.concatenate([jnp.where(low, tile, zero), jnp.where(low, zero, tile)], axis=0)

def unstacked(turned):
    full = turned.T
    rows = full.shape[0] // 2
    return jnp.where(lane_of((rows, LANES)) < HEAD_DIM, full[:rows], full[rows:])

def masked_scores(keys, queries, key_start, query_start, length, causal):
    scores = nt(keys, queries) * HEAD_DIM ** (-0.5)
    half = queries.shape[0] // 2
    key_at = key_start + lax.broadcasted_iota(jnp.int32, scores.shape, 0)
    allowed = key_at < length
    if causal:
        query_at = query_start + lane_of(scores.shape) % half
        allowed = allowed & (key_at <= query_at)
    return jnp.where(allowed, scores, -1e30)

class Corner:
    def __init__(self):
        self.here = lax.axis_index("narrow")
        self.chip, self.core = self.here // 2, self.here % 2
        self.core_peer = 2 * self.chip + 1 - self.core
        self.chip_peer = 2 * (1 - self.chip) + self.core
        self.far_peer = 2 * (1 - self.chip) + 1 - self.core

class Share:
    def __init__(self, corner, ref, send, recv):
        self.corner, self.ref, self.sems = corner, ref, (send, recv)

    def copy(self, kind, k, owner, peer):
        start, size = cuts(self.ref.shape[1])[k]
        block = self.ref.at[owner, pl.ds(start, size)]
        return remote(block, block, self.sems[0].at[kind, k], self.sems[1].at[kind, k], narrow=peer)

    def start(self):
        c = self.corner
        for k in range(2):
            self.copy(1, k, c.here, c.chip_peer).start()
        for k in range(2):
            self.copy(0, k, c.here, c.core_peer).start()

    def wait_core(self):
        c = self.corner
        for k in range(2):
            self.copy(0, k, c.core_peer, c.core_peer).wait_recv()

    def wait_chip(self):
        c = self.corner
        for k in range(2):
            self.copy(1, k, c.chip_peer, c.chip_peer).wait_recv()
            self.copy(2, k, c.chip_peer, c.core_peer).start()

    def wait_far(self):
        c = self.corner
        for k in range(2):
            self.copy(2, k, c.far_peer, c.core_peer).wait_recv()

    def drain(self):
        c = self.corner
        for k in range(2):
            self.copy(0, k, c.here, c.core_peer).wait_send()
            self.copy(1, k, c.here, c.chip_peer).wait_send()
            self.copy(2, k, c.chip_peer, c.core_peer).wait_send()

    scratch = lambda: [pltpu.SemaphoreType.DMA((3, 2)), pltpu.SemaphoreType.DMA((3, 2))]

class Fold:
    def __init__(self, corner, out_c, got_c, out_x, got_x, held, c_send, c_recv, x_send, x_recv):
        self.corner, self.held = corner, held
        self.out_c, self.got_c, self.out_x, self.got_x = out_c, got_c, out_x, got_x
        self.sems = (c_send, c_recv, x_send, x_recv)

    def to_core(self, x):
        return remote(
            self.out_c.at[x], self.got_c.at[x], self.sems[0].at[x], self.sems[1].at[x],
            narrow=self.corner.core_peer,
        )

    def to_chip(self):
        return remote(self.out_x, self.got_x, self.sems[2], self.sems[3], narrow=self.corner.chip_peer)

    def give(self, block, part):
        x, c = block // 2, block % 2

        @pl.when(self.corner.core != c)
        def _():
            self.out_c[x] = part.astype(BF)
            self.to_core(x).start()

        @pl.when(self.corner.core == c)
        def _():
            self.held[x] = part

    def settle(self, block):
        x, c = block // 2, block % 2

        @pl.when(self.corner.core == c)
        def _():
            self.to_core(x).wait_recv()

            @pl.when(self.corner.chip != x)
            def _():
                self.out_x[...] = (self.held[x] + self.got_c[x].astype(F32)).astype(BF)
                self.to_chip().start()

    def total(self):
        chip = self.corner.chip
        near = self.held[chip] + self.got_c[chip].astype(F32)
        self.to_chip().wait_recv()
        return near + self.got_x[...].astype(F32)

    def drain(self):
        for x in range(2):
            self.to_core(x).wait_send()
        self.to_chip().wait_send()

    def scratch(rows, cols):
        return [
            pltpu.VMEM((2, rows, cols), BF),
            pltpu.VMEM((2, rows, cols), BF),
            pltpu.VMEM((rows, cols), BF),
            pltpu.VMEM((rows, cols), BF),
            pltpu.VMEM((2, rows, cols), F32),
            pltpu.SemaphoreType.DMA((2,)),
            pltpu.SemaphoreType.DMA((2,)),
            pltpu.SemaphoreType.DMA,
            pltpu.SemaphoreType.DMA,
        ]

def front_kernel(hidden, cotangent, labels, length, attn_gain, w_qkv, w_out, moe_gain, router_turned, cosine, sine, count, experts_here, picks, cid):
    rows, width = hidden.shape
    seq = 4 * rows
    query_cols, key_cols = w_out.shape[0], (w_qkv.shape[1] - w_out.shape[0]) // 2
    kv_here = key_cols // HEAD_DIM
    experts = router_turned.shape[0]

    def kernel(*refs):
        refs = list(refs)
        take = lambda number: [refs.pop(0) for _ in range(number)]
        h_ref, cot_ref, lab_ref, len_ref, g1_ref, wqkv_ref, wout_ref, g2_ref, wr_ref, cos_ref, sin_ref = take(11)
        ea_ref, ga_ref, whole_ref, q_ref, k_ref, v_ref, ctx_ref, lse_ref, mixed_ref, slots_ref, gates_ref, shares_ref, offs_ref = take(13)
        kd, vd, s_scr, p_scr, lab_all = take(5)
        share = take(2)
        fold = take(9)
        g_scr, e_scr = take(2), take(2)
        l_send, l_recv, own_sem = take(3)
        ring, corner = Ring(count), Corner()
        others = [(ring.me + shift) % count for shift in range(1, count)]
        greet(others, [corner.core_peer, corner.chip_peer])
        length_here = len_ref[0]

        g_ring = gather_steps(ring, ga_ref, *g_scr, own=cot_ref)
        next(g_ring)
        own_grad = pltpu.make_async_copy(cot_ref, ga_ref.at[ring.me], own_sem)
        own_grad.start()
        label_copy = lambda k, target: remote(
            lab_ref, lab_all.at[ring.me], l_send.at[k], l_recv.at[k], wide=target
        )
        for k, target in enumerate(others):
            label_copy(k, target).start()
        lab_all[ring.me] = lab_ref[...]

        source = h_ref[...].astype(F32)
        scale = lax.rsqrt(jnp.mean(source * source, axis=1, keepdims=True) + EPSILON)
        whole_ref[corner.here] = (source * scale * g1_ref[...]).astype(BF)
        sharing = Share(corner, whole_ref, *share)
        sharing.start()

        def project(block):
            span = pl.ds(pl.multiple_of(block * rows, rows), rows)
            lin = nn(whole_ref[block], wqkv_ref[...])
            cos, sin = cos_ref[span], sin_ref[span]
            for t in range(kv_here):
                lanes = slice(t * LANES, (t + 1) * LANES)
                q_ref[span, lanes] = turn_lanes(lin[:, lanes], cos, sin).astype(BF)
            keys = turn_lanes(lin[:, query_cols : query_cols + key_cols], cos, sin)
            values = lin[:, query_cols + key_cols :]
            k_ref[span] = keys.astype(BF)
            v_ref[span] = values.astype(BF)
            for t in range(kv_here):
                kd[t, span] = doubled(keys, t).astype(BF)
                vd[t, span] = doubled(values, t).astype(BF)

        project(corner.here)
        sharing.wait_core()
        project(corner.core_peer)

        for k, target in enumerate(others):
            sender = (ring.me - (k + 1) + count) % count
            remote(lab_ref, lab_all.at[sender], l_send.at[k], l_recv.at[k], wide=target).wait_recv()
        places = corner.here * rows + lane_of((1, rows))
        first = ring.me * experts_here
        upper = jnp.where(
            lax.broadcasted_iota(jnp.int32, (rows, rows), 0) <= lane_of((rows, rows)), 1.0, 0.0
        ).astype(BF)

        def belongs(block, expert_rows):
            found = lab_all[block, 0:1] == expert_rows
            for k in range(1, picks):
                found = found | (lab_all[block, k : k + 1] == expert_rows)
            return found

        local_rows = lax.broadcasted_iota(jnp.int32, (8, rows), 0)
        own_rows = jnp.where(local_rows < experts_here, first + local_rows, -1)
        at = jnp.zeros((8, 1), jnp.int32)
        lane = lane_of((8, LANES))
        starts = jnp.zeros((8, LANES), jnp.int32)
        for b in range(count):
            mine = jnp.where(belongs(b, own_rows) & (places < lab_all[b, picks : picks + 1]), 1.0, 0.0)
            reached = nn(mine.astype(BF), upper)
            slots_ref[b] = jnp.where(mine > 0.0, reached, 0.0).astype(jnp.int32) - 1
            starts = jnp.where(lane == b, at, starts)
            filled = jnp.max(reached, axis=1, keepdims=True).astype(jnp.int32)
            at = at + (filled + 15) // 16 * 16
        offs_ref[...] = jnp.where(lane == count, at, starts)

        sharing.wait_chip()
        project(corner.chip_peer)
        next(g_ring)
        sharing.wait_far()
        project(corner.far_peer)

        folding = Fold(corner, *fold)
        before = None
        for block in (3, 2, 1, 0):
            span = pl.ds(block * rows, rows)
            for t in range(kv_here):
                lanes = slice(t * LANES, (t + 1) * LANES)
                queries = stacked(q_ref[span, lanes])
                highest = None
                for b in range(block + 1):
                    keys = pl.ds(b * rows, rows)
                    scores = masked_scores(kd[t, keys], queries, b * rows, block * rows, length_here, b == block)
                    s_scr[keys] = scores
                    top = jnp.max(scores, axis=0, keepdims=True)
                    highest = top if highest is None else jnp.maximum(highest, top)
                total = None
                for b in range(block + 1):
                    keys = pl.ds(b * rows, rows)
                    weights = jnp.exp(s_scr[keys] - highest)
                    p_scr[keys] = weights.astype(BF)
                    one = jnp.sum(weights, axis=0, keepdims=True)
                    total = one if total is None else total + one
                keys = pl.ds(0, (block + 1) * rows)
                context = tn(vd[t, keys], p_scr[keys]) / total
                ctx_ref[span, lanes] = unstacked(context).astype(BF)
                lse_ref[t * 4 + block : t * 4 + block + 1] = highest + jnp.log(total)
            folding.give(block, nn(ctx_ref[span], wout_ref[...]))
            if before is not None:
                folding.settle(before)
            before = block
            if block in (3, 1):
                next(g_ring)
        folding.settle(before)
        mixed = source + folding.total()
        mixed_ref[...] = mixed
        scale = lax.rsqrt(jnp.mean(mixed * mixed, axis=1, keepdims=True) + EPSILON)
        ea_ref[ring.me] = (mixed * scale * g2_ref[...]).astype(BF)

        every = lax.broadcasted_iota(jnp.int32, (experts, rows), 0)

        def gate(block, home):
            logits = nt(wr_ref[...], ea_ref[block])
            member = belongs(block, every)
            masked = jnp.where(member, logits, -jnp.inf)
            raised = jnp.exp(masked - jnp.max(masked, axis=0, keepdims=True))
            shares = raised / jnp.sum(raised, axis=0, keepdims=True)
            if home:
                shares_ref[...] = shares
            kept = jnp.where(places < lab_all[block, picks : picks + 1], shares, 0.0)
            own = jnp.zeros((8, rows), F32)
            for e in range(experts_here):
                row = jnp.sum(jnp.where(every == first + e, kept, 0.0), axis=0, keepdims=True)
                own = jnp.where(local_rows == e, row, own)
            gates_ref[block] = own

        hops = count // 2
        for hop, _ in enumerate(gather_steps(ring, ea_ref, *e_scr)):
            if hop == 0:
                gate(ring.me, True)
                for _ in g_ring:
                    pass
            elif hop < hops - 1:
                gate(ring.at(hop), False)
                gate(ring.at(-hop), False)
        for shift in range(hops - 1, hops + 1):
            gate(ring.at(shift), False)
            if shift < hops:
                gate(ring.at(-shift), False)
        for k, target in enumerate(others):
            label_copy(k, target).wait_send()
        own_grad.wait()
        sharing.drain()
        folding.drain()

    vmem = pl.BlockSpec(memory_space=pltpu.VMEM)
    far = pl.BlockSpec(memory_space=pl.ANY)
    shape = jax.ShapeDtypeStruct
    out_shape = [
        shape((count, rows, width), BF),
        shape((count, rows, width), BF),
        shape((4, rows, width), BF),
        shape((seq, query_cols), BF),
        shape((seq, key_cols), BF),
        shape((seq, key_cols), BF),
        shape((seq, query_cols), BF),
        shape((8, 2 * rows), F32),
        shape((rows, width), F32),
        shape((count, 8, rows), jnp.int32),
        shape((count, 8, rows), F32),
        shape((experts, rows), F32),
        shape((8, LANES), jnp.int32),
    ]
    scratch = [
        pltpu.VMEM((kv_here, seq, LANES), BF),
        pltpu.VMEM((kv_here, seq, LANES), BF),
        pltpu.VMEM((seq, 2 * rows), F32),
        pltpu.VMEM((seq, 2 * rows), BF),
        pltpu.VMEM((count,) + labels.shape, jnp.int32),
        *Share.scratch(),
        *Fold.scratch(rows, width),
        *gather_scratch(count),
        *gather_scratch(count),
        pltpu.SemaphoreType.DMA((count - 1,)),
        pltpu.SemaphoreType.DMA((count - 1,)),
        pltpu.SemaphoreType.DMA,
    ]
    return pl.pallas_call(
        kernel,
        out_shape=out_shape,
        in_specs=[vmem, far, vmem, pl.BlockSpec(memory_space=pltpu.SMEM)] + [vmem] * 7,
        out_specs=[vmem, far] + [vmem] * (len(out_shape) - 2),
        scratch_shapes=scratch,
        compiler_params=pltpu.CompilerParams(
            collective_id=cid, has_side_effects=True, vmem_limit_bytes=56 * 2**20
        ),
    )(hidden, cotangent, labels, length, attn_gain, w_qkv, w_out, moe_gain, router_turned, cosine, sine)


TILE = 256

def expert_pair(offsets, entry_all, grad_all, slots, gates, w_gate_up, w_down, earlier, first, pair, capacity):
    count, tokens, width = entry_all.shape
    ffe = w_down.shape[1]
    local = w_down.shape[0]
    room = count * capacity + TILE
    most = count * capacity // TILE
    adding = earlier is not None

    def kernel(off_ref, e_ref, g_ref, s_ref, gate_ref, wgu_ref, wd_ref, *rest):
        if adding:
            pc_ref, pb_ref = rest[:2]
            rest = rest[2:]
        c_ref, b_ref, pick_ref, dgu_ref, dd_ref, x_s, s_s, act_s, pg_s, cr_s, bk_s, gcol, pcol, sems = rest
        e = pl.program_id(0)
        if adding:
            fetch = [
                pltpu.make_async_copy(pc_ref, c_ref, sems.at[0]),
                pltpu.make_async_copy(pb_ref, b_ref, sems.at[1]),
            ]

        @pl.when(e == 0)
        def _():
            if adding:
                for f in fetch:
                    f.start()
            cr_s[...] = jnp.zeros_like(cr_s)
            bk_s[...] = jnp.zeros_like(bk_s)
            pcol[...] = jnp.zeros_like(pcol)

        def start_of(expert, b):
            return pl.multiple_of(off_ref[(first + expert) * 128 + b], 16)

        places = lax.broadcasted_iota(jnp.int32, (capacity, tokens), 0)
        for b in range(count):
            pick_out = places == s_ref[b, pl.ds(first + e, 1), :]
            chosen = jnp.where(pick_out, 1.0, 0.0).astype(BF)
            span = pl.ds(start_of(e, b), capacity)
            x_s[span] = nn(chosen, e_ref[b]).astype(BF)
            s_s[span] = nn(chosen, g_ref[b]).astype(BF)
            gate_col = jnp.sum(
                jnp.where(pick_out, gate_ref[b, pl.ds(first + e, 1), :], 0.0), axis=1, keepdims=True
            )
            gcol[span] = jnp.broadcast_to(gate_col, (capacity, 128))
        total = start_of(e, count)
        tail = pl.ds(total, TILE)
        x_s[tail] = jnp.zeros((TILE, width), BF)
        s_s[tail] = jnp.zeros((TILE, width), BF)
        gcol[tail] = jnp.zeros((TILE, 128), F32)
        tiles = (total + TILE - 1) // TILE

        def step(i, carry):
            rows = pl.ds(pl.multiple_of(i * TILE, TILE), TILE)
            pre = nn(x_s[rows], wgu_ref[0])
            gate_part = pre[:, :ffe]
            up_part = pre[:, ffe:]
            sig = jax.nn.sigmoid(gate_part)
            swish = gate_part * sig
            act = (swish * up_part).astype(BF)
            act_s[rows] = act
            result = nn(act, wd_ref[0]).astype(BF).astype(F32)
            grad_rows = s_s[rows].astype(F32)
            gate = gcol[rows][:, :1]
            pcol[rows] = jnp.broadcast_to(
                jnp.sum(result * grad_rows, axis=1, keepdims=True), (TILE, 128)
            )
            cr_s[e, rows] = (gate * result).astype(BF)
            slot_grad = (gate * grad_rows).astype(BF)
            s_s[rows] = slot_grad
            act_grad = nt(slot_grad, wd_ref[0])
            gate_grad = act_grad * up_part * sig * (1.0 + gate_part * (1.0 - sig))
            pre_grad = jnp.concatenate([gate_grad, act_grad * swish], axis=1).astype(BF)
            pg_s[rows] = pre_grad
            bk_s[e, rows] = nt(pre_grad, wgu_ref[0]).astype(BF)
            return carry

        lax.fori_loop(0, tiles, step, 0)
        for b in range(count):
            pick_out = places == s_ref[b, pl.ds(first + e, 1), :]
            span = pl.ds(start_of(e, b), capacity)
            pick_ref[0, b : b + 1, :] = jnp.sum(
                jnp.where(pick_out, pcol[span][:, :1], 0.0), axis=0, keepdims=True
            )

        @pl.when(tiles == 0)
        def _():
            dgu_ref[...] = jnp.zeros_like(dgu_ref)
            dd_ref[...] = jnp.zeros_like(dd_ref)

        block = 256
        for k in range(1, most + 1):

            @pl.when(tiles == k)
            def _(k=k):
                def columns(j, carry):
                    cols = pl.ds(pl.multiple_of(j * block, block), block)
                    dgu_ref[0, :, cols] = tn(x_s[: k * TILE], pg_s[: k * TILE, cols]).astype(BF)
                    dd_ref[0, :, cols] = tn(act_s[: k * TILE], s_s[: k * TILE, cols]).astype(BF)
                    return carry

                lax.fori_loop(0, width // block, columns, 0)

        @pl.when(e == pair - 1)
        def _():
            if adding:
                for f in fetch:
                    f.wait()
            for b in range(count):
                sum_c = sum_b = None
                for x in range(pair):
                    chosen = jnp.where(places == s_ref[b, first + x : first + x + 1, :], 1.0, 0.0).astype(BF)
                    span = pl.ds(start_of(x, b), capacity)
                    one_c, one_b = tn(chosen, cr_s[x, span]), tn(chosen, bk_s[x, span])
                    sum_c = one_c if sum_c is None else sum_c + one_c
                    sum_b = one_b if sum_b is None else sum_b + one_b
                if adding:
                    sum_c = sum_c + c_ref[b].astype(F32)
                    sum_b = sum_b + b_ref[b].astype(F32)
                c_ref[b] = sum_c.astype(BF)
                b_ref[b] = sum_b.astype(BF)

    once = pl.Buffered(1)
    whole = lambda shape: pl.BlockSpec(shape, lambda e, off: (0,) * len(shape), pipeline_mode=once)
    any_space = pl.BlockSpec(memory_space=pl.ANY)
    cube = (count, tokens, width)
    in_specs = [
        whole(cube), whole(cube), whole(slots.shape), whole(gates.shape),
        pl.BlockSpec((1, width, 2 * ffe), lambda e, off: (first + e, 0, 0)),
        pl.BlockSpec((1, ffe, width), lambda e, off: (first + e, 0, 0)),
    ]
    operands = [entry_all, grad_all, slots, gates, w_gate_up, w_down]
    if adding:
        in_specs += [any_space, any_space]
        operands += list(earlier)
    return pl.pallas_call(
        kernel,
        grid_spec=pltpu.PrefetchScalarGridSpec(
            num_scalar_prefetch=1,
            grid=(pair,),
            in_specs=in_specs,
            out_specs=[
                whole(cube), whole(cube),
                pl.BlockSpec((1, count, tokens), lambda e, off: (e, 0, 0)),
                pl.BlockSpec((1, width, 2 * ffe), lambda e, off: (e, 0, 0)),
                pl.BlockSpec((1, ffe, width), lambda e, off: (e, 0, 0)),
            ],
            scratch_shapes=[
                pltpu.VMEM((room, width), BF),
                pltpu.VMEM((room, width), BF),
                pltpu.VMEM((room, ffe), BF),
                pltpu.VMEM((room, 2 * ffe), BF),
                pltpu.VMEM((pair, room, width), BF),
                pltpu.VMEM((pair, room, width), BF),
                pltpu.VMEM((room, 128), F32),
                pltpu.VMEM((room, 128), F32),
                pltpu.SemaphoreType.DMA((2,)),
            ],
        ),
        out_shape=[
            jax.ShapeDtypeStruct(cube, BF),
            jax.ShapeDtypeStruct(cube, BF),
            jax.ShapeDtypeStruct((pair, count, tokens), F32),
            jax.ShapeDtypeStruct((pair, width, 2 * ffe), BF),
            jax.ShapeDtypeStruct((pair, ffe, width), BF),
        ],
        compiler_params=pltpu.CompilerParams(
            dimension_semantics=("arbitrary",), vmem_limit_bytes=60 * 2**20
        ),
        cost_estimate=pl.CostEstimate(
            flops=pair * count * capacity * 6 * width * ffe * 3, bytes_accessed=40 * 2**20, transcendentals=0
        ),
    )(offsets, *operands)


def tail_kernel(entry_home, pick_home, shares, router_turned, mixed, cotangent, hidden, length, attn_gain, moe_gain, w_qkv, w_qkv_turned, w_out, queries, keys, values, context, whole, lse, cosine, sine, expert_part, own, shapes, cid):
    count, rows, width = expert_part.shape
    seq = 4 * rows
    query_cols, key_cols = w_out.shape[0], (w_qkv.shape[1] - w_out.shape[0]) // 2
    cols = w_qkv.shape[1]
    kv_here = key_cols // HEAD_DIM
    experts_all = router_turned.shape[0]
    small_rows = (experts_all + 2 + 15) // 16 * 16
    block = -(-(cols + query_cols + small_rows) // (32 * count)) * 32
    experts, quarter, _ = own.shape
    up_shape, down_shape = shapes
    quarter_up, quarter_down = up_shape[1] // 4, down_shape[1] // 4
    base = [0, rows, 3 * rows, 6 * rows]
    small_at = cols + query_cols

    def kernel(*refs):
        refs = list(refs)
        take = lambda number: [refs.pop(0) for _ in range(number)]
        eh_ref, pick_ref, shares_ref, wr_ref, mixed_ref, cot_ref, h_ref, len_ref, g1_ref, g2_ref = take(10)
        wqkv_ref, wt_ref, wout_ref, q_ref, k_ref, v_ref, ctx_ref, whole_ref, lse_ref, cos_ref, sin_ref = take(11)
        c_ref, own_ref = take(2)
        out_ref, gh_ref, sum_ref, up_ref, down_ref = take(5)
        gw, mg_s, kd, vd, p_all, dp_scr, ds_scr, dctx, dk, dv, qg, packed, small_got, expert_sum = take(14)
        share, fold = take(2), take(9)
        c_scr, s_scr, g_scr = take(3), take(3), take(2)
        sm_send, sm_recv = take(2)
        c_send, c_recv, x_send, x_recv, f_send, f_recv, l_sem = take(7)
        ring, corner = Ring(count), Corner()
        greet(list(ring.peers), [corner.core_peer, corner.chip_peer, corner.far_peer])
        length_here = len_ref[0]

        def put(row, size, got):
            expert_sum[pl.ds(row, size)] = got

        c_ring = scatter_steps(ring, c_ref, *c_scr, put)
        next(c_ring)

        def places(e, owner):
            return (
                (own_ref.at[e, pl.ds(0, quarter_up)], up_ref.at[e, pl.ds(owner * quarter_up, quarter_up)]),
                (own_ref.at[e, pl.ds(quarter_up, quarter_down)], down_ref.at[e, pl.ds(owner * quarter_down, quarter_down)]),
            )

        def send(e, sems, peer):
            return [
                remote(src, dst, sems[0].at[e, k], sems[1].at[e, k], narrow=peer)
                for k, (src, dst) in enumerate(places(e, corner.here))
            ]

        def forward(e, owner, sems):
            return [
                remote(dst, dst, sems[0].at[e, k], sems[1].at[e, k], narrow=corner.core_peer)
                for k, (src, dst) in enumerate(places(e, owner))
            ]

        core_sems, chip_sems, far_sems = (c_send, c_recv), (x_send, x_recv), (f_send, f_recv)

        def own_copy(e):
            return [
                pltpu.make_async_copy(src, dst, l_sem.at[e, k])
                for k, (src, dst) in enumerate(places(e, corner.here))
            ]

        def send_out(e):
            for c in send(e, chip_sems, corner.chip_peer):
                c.start()

        def pass_on(e):
            for c in forward(e, corner.chip_peer, chip_sems):
                c.wait_recv()
            for c in forward(e, corner.chip_peer, far_sems):
                c.start()

        picked, held_shares = pick_ref[...], shares_ref[...]
        logit_grad = held_shares * (picked - jnp.sum(held_shares * picked, axis=0, keepdims=True))
        high = logit_grad.astype(BF)
        low = (logit_grad - high.astype(F32)).astype(BF)
        entry_grad = eh_ref[...] + (tn(high, wr_ref[...]) + tn(low, wr_ref[...]))
        mixed_here = mixed_ref[...]
        scale = lax.rsqrt(jnp.mean(mixed_here * mixed_here, axis=1, keepdims=True) + EPSILON)
        unit = mixed_here * scale
        inner = entry_grad * g2_ref[...]
        from_norm = scale * (inner - unit * jnp.mean(inner * unit, axis=1, keepdims=True))
        at = corner.here * rows + lax.broadcasted_iota(jnp.int32, (rows, 1), 0)
        valid = jnp.where(at < length_here, 1.0, 0.0)
        mixed_grad = valid * cot_ref[...].astype(F32) + from_norm
        mg_s[...] = mixed_grad
        gw[corner.here] = mixed_grad.astype(BF)
        sharing = Share(corner, gw, *share)
        sharing.start()
        for e in range(experts):
            for c in send(e, core_sems, corner.core_peer) + own_copy(e):
                c.start()
        entry = (unit * g2_ref[...]).astype(BF)
        router_grad = nn(high, entry) + nn(low, entry)
        gain_two = jnp.sum(entry_grad * unit, axis=0, keepdims=True)

        for t in range(kv_here):
            kd[t] = doubled(k_ref[...].astype(F32), t).astype(BF)
            vd[t] = doubled(v_ref[...].astype(F32), t).astype(BF)

        def chances(b):
            for t in range(kv_here):
                lanes = slice(t * LANES, (t + 1) * LANES)
                stack = stacked(q_ref[pl.ds(b * rows, rows), lanes])
                log_sum = lse_ref[t * 4 + b : t * 4 + b + 1]
                for kb in range(b + 1):
                    scores = masked_scores(
                        kd[t, pl.ds(kb * rows, rows)], stack, kb * rows, b * rows, length_here, kb == b
                    )
                    p_all[t, pl.ds(base[b] + kb * rows, rows)] = jnp.exp(scores - log_sum).astype(BF)

        def pull(owner):
            dctx[owner] = nt(gw[owner], wout_ref[...]).astype(BF)

        pull(corner.here)
        chances(3)
        next(c_ring)
        sharing.wait_core()
        pull(corner.core_peer)
        chances(2)
        next(c_ring)
        chances(1)
        chances(0)
        sharing.wait_chip()
        send_out(0)
        pull(corner.chip_peer)
        sharing.wait_far()
        pull(corner.far_peer)
        dk[...] = jnp.zeros_like(dk)
        dv[...] = jnp.zeros_like(dv)

        folding = Fold(corner, *fold)
        before = None
        for b in (3, 2, 1, 0):
            span = pl.ds(b * rows, rows)
            cos, sin = cos_ref[span], sin_ref[span]
            for t in range(kv_here):
                lanes = slice(t * LANES, (t + 1) * LANES)
                stack = stacked(q_ref[span, lanes])
                grad_stack = stacked(dctx[b, :, lanes])
                inner = None
                for kb in range(b + 1):
                    chance = p_all[t, pl.ds(base[b] + kb * rows, rows)]
                    grad = nt(vd[t, pl.ds(kb * rows, rows)], grad_stack)
                    dp_scr[pl.ds(kb * rows, rows)] = grad
                    one = jnp.sum(chance.astype(F32) * grad, axis=0, keepdims=True)
                    inner = one if inner is None else inner + one
                for kb in range(b + 1):
                    key_span = pl.ds(kb * rows, rows)
                    chance = p_all[t, pl.ds(base[b] + kb * rows, rows)]
                    score_grad = (chance.astype(F32) * (dp_scr[key_span] - inner)).astype(BF)
                    ds_scr[key_span] = score_grad
                    dk[t, key_span] += nn(score_grad, stack)
                    dv[t, key_span] += nn(chance, grad_stack)
                every = pl.ds(0, (b + 1) * rows)
                query_grad = unstacked(tn(kd[t, every], ds_scr[every])) * HEAD_DIM ** (-0.5)
                qg[span, lanes] = turn_lanes(query_grad, cos, -sin).astype(BF)
            low_lanes = lane_of((rows, LANES)) < HEAD_DIM
            both = lambda ref, t: ref[t, span] + pltpu.roll(ref[t, span], HEAD_DIM, 1)
            key_grad = jnp.where(low_lanes, both(dk, 0), both(dk, 1)) * HEAD_DIM ** (-0.5)
            qg[span, query_cols : query_cols + key_cols] = turn_lanes(key_grad, cos, -sin).astype(BF)
            qg[span, query_cols + key_cols :] = jnp.where(low_lanes, both(dv, 0), both(dv, 1)).astype(BF)
            folding.give(b, nt(qg[span], wqkv_ref[...]))
            if before is not None:
                folding.settle(before)
            before = b
            next(c_ring)
            if b == 1:
                send_out(1)
        folding.settle(before)

        def store(row, value):
            for start in range(0, value.shape[0], 16):
                size = min(16, value.shape[0] - start)
                at_row = row + start
                packed[at_row // block, pl.ds(at_row % block, size)] = value[start : start + size].astype(BF)

        weight_grad = tn(qg[...], whole_ref[...])
        gain_one = jnp.sum(weight_grad * wt_ref[...].astype(F32), axis=0, keepdims=True) / g1_ref[...]
        small_here = jnp.concatenate(
            [router_grad, gain_one, gain_two, jnp.zeros((small_rows - experts_all - 2, width), F32)], axis=0
        )
        small_got[3] = small_here.astype(BF)
        small_copy = lambda k, peer: remote(
            small_got.at[3], small_got.at[k], sm_send.at[k], sm_recv.at[k], narrow=peer
        )
        peers = (corner.core_peer, corner.chip_peer, corner.far_peer)
        for k, peer in enumerate(peers):
            small_copy(k, peer).start()
        store(0, weight_grad)
        store(cols, tn(ctx_ref[...], gw[...].reshape(seq, width)))
        rest = small_at + small_rows
        store(rest, jnp.zeros((count * block - rest, width), F32))
        for k, peer in enumerate(peers):
            small_copy(k, peer).wait_recv()
        store(small_at, small_here + sum(small_got[k].astype(F32) for k in range(3)))

        def finish(row, size, got):
            sum_ref[ring.me, pl.ds(row, size)] = got.astype(BF)

        sums = scatter_steps(ring, packed, *s_scr, finish)
        next(sums)
        pass_on(0)
        send_out(2)
        normed_grad = folding.total()
        source = h_ref[...].astype(F32)
        scale = lax.rsqrt(jnp.mean(source * source, axis=1, keepdims=True) + EPSILON)
        unit = source * scale
        inner = normed_grad * g1_ref[...]
        from_norm = scale * (inner - unit * jnp.mean(inner * unit, axis=1, keepdims=True))
        gh_ref[...] = (mg_s[...] + from_norm).astype(BF)
        send_out(3)
        next(sums)
        for _ in c_ring:
            next(sums, None)
        out_ref[...] = (valid * (mixed_here + expert_sum[...])).astype(BF)
        for _ in sums:
            pass
        pass_on(1)
        gathers = gather_steps(ring, sum_ref, *g_scr)
        next(gathers)
        next(gathers)
        pass_on(2)
        for _ in gathers:
            pass
        pass_on(3)
        for k, peer in enumerate(peers):
            small_copy(k, peer).wait_send()
        for e in range(experts):
            for c in own_copy(e):
                c.wait()
            for c in send(e, chip_sems, corner.chip_peer) + send(e, core_sems, corner.core_peer):
                c.wait_send()
            for c in forward(e, corner.core_peer, core_sems):
                c.wait_recv()
            for c in forward(e, corner.chip_peer, far_sems):
                c.wait_send()
            for c in forward(e, corner.far_peer, far_sems):
                c.wait_recv()
        sharing.drain()
        folding.drain()

    vmem = pl.BlockSpec(memory_space=pltpu.VMEM)
    far = pl.BlockSpec(memory_space=pl.ANY)
    shape = jax.ShapeDtypeStruct
    out_shape = [
        shape((rows, width), BF),
        shape((rows, width), BF),
        shape((count, block, width), BF),
        shape(up_shape, BF),
        shape(down_shape, BF),
    ]
    scratch = [
        pltpu.VMEM((4, rows, width), BF),
        pltpu.VMEM((rows, width), F32),
        pltpu.VMEM((kv_here, seq, LANES), BF),
        pltpu.VMEM((kv_here, seq, LANES), BF),
        pltpu.VMEM((kv_here, 10 * rows, 2 * rows), BF),
        pltpu.VMEM((seq, 2 * rows), F32),
        pltpu.VMEM((seq, 2 * rows), BF),
        pltpu.VMEM((4, rows, query_cols), BF),
        pltpu.VMEM((kv_here, seq, LANES), F32),
        pltpu.VMEM((kv_here, seq, LANES), F32),
        pltpu.VMEM((seq, cols), BF),
        pltpu.VMEM((count, block, width), BF),
        pltpu.VMEM((4, small_rows, width), BF),
        pltpu.VMEM((rows, width), F32),
        *Share.scratch(),
        *Fold.scratch(rows, width),
        *scatter_scratch(count, rows, width),
        *scatter_scratch(count, block, width),
        *gather_scratch(count),
        pltpu.SemaphoreType.DMA((3,)),
        pltpu.SemaphoreType.DMA((3,)),
    ] + [pltpu.SemaphoreType.DMA((experts, 2))] * 7
    return pl.pallas_call(
        kernel,
        out_shape=out_shape,
        in_specs=[vmem] * 7 + [pl.BlockSpec(memory_space=pltpu.SMEM)] + [vmem] * 15,
        out_specs=[vmem] * 3 + [far] * 2,
        scratch_shapes=scratch,
        compiler_params=pltpu.CompilerParams(
            collective_id=cid, has_side_effects=True, vmem_limit_bytes=62 * 2**20
        ),
    )(entry_home, pick_home, shares, router_turned, mixed, cotangent, hidden, length, attn_gain, moe_gain,
      w_qkv, w_qkv_turned, w_out, queries, keys, values, context, whole, lse, cosine, sine, expert_part, own)


def local_general(
    hidden,
    lengths,
    routes,
    cotangent,
    attn_gain,
    w_query,
    w_key,
    w_value,
    w_out,
    moe_gain,
    w_router,
    w_gate_up,
    w_down,
):
    rows_here = hidden.shape[1]
    width = hidden.shape[2]
    seq_len = rows_here * lax.axis_size("narrow")
    head_dim = HEAD_DIM
    group_size = HEADS // KV_HEADS
    kv_here = w_key.shape[1] // head_dim
    query_cols = kv_here * group_size * head_dim
    key_cols = kv_here * head_dim
    scaling = head_dim ** (-0.5)
    block_rows = min(512, seq_len)
    block_count = seq_len // block_rows
    length_here = lengths[0]
    offset = lax.axis_index("narrow") * rows_here
    local_places = offset + jnp.arange(rows_here, dtype=jnp.int32)
    valid = (local_places < length_here).astype(jnp.float32)[:, None]
    source = hidden[0].astype(jnp.float32)
    normed, scale_one = norm_forward(source, attn_gain)
    normed_low = normed.astype(jnp.bfloat16)
    whole = lax.all_gather(normed_low, "narrow", axis=0, tiled=True)
    w_qkv = jnp.concatenate([w_query, w_key, w_value], axis=1)
    projected = jnp.dot(whole, w_qkv, preferred_element_type=jnp.float32)
    cosine, sine_part = rope_tables(seq_len, head_dim)
    query_rot = turn(
        projected[:, :query_cols].reshape(seq_len, kv_here, group_size, head_dim),
        cosine,
        sine_part,
        1.0,
    )
    key_rot = turn(
        projected[:, query_cols : query_cols + key_cols].reshape(seq_len, kv_here, head_dim),
        cosine,
        sine_part,
        1.0,
    )
    queries = (
        query_rot.astype(jnp.bfloat16)
        .reshape(block_count, block_rows, kv_here, group_size, head_dim)
        .transpose(0, 2, 3, 1, 4)
    )
    keys_low = key_rot.astype(jnp.bfloat16).transpose(1, 0, 2)
    values_low = (
        projected[:, query_cols + key_cols :]
        .astype(jnp.bfloat16)
        .reshape(seq_len, kv_here, head_dim)
        .transpose(1, 0, 2)
    )
    context, log_sums = attend_forward(queries, keys_low, values_low, length_here, scaling)
    context_rows = context.transpose(0, 3, 1, 2, 4).reshape(seq_len, query_cols)
    piece = context_rows
    attn_part = lax.psum_scatter(
        jnp.dot(piece, w_out, preferred_element_type=jnp.float32).astype(jnp.bfloat16),
        "narrow",
        scatter_dimension=0,
        tiled=True,
    ).astype(jnp.float32)
    mixed = source + attn_part
    normed_two, scale_two = norm_forward(mixed, moe_gain)
    entry = normed_two.astype(jnp.bfloat16)
    logits = jnp.dot(entry, w_router, preferred_element_type=jnp.float32)
    route_here = routes[0]
    tokens_here, picks = route_here.shape
    expert_total = w_router.shape[1]
    capacity = 2 * tokens_here * picks // expert_total
    member = (
        route_here[:, :, None] == jnp.arange(expert_total, dtype=jnp.int32)[None, None, :]
    ).astype(jnp.int32)
    flat_member = member.reshape(tokens_here * picks, expert_total)
    earlier = jnp.cumsum(flat_member, axis=0) - flat_member
    slot_index = jnp.sum(earlier * flat_member, axis=1)
    places = route_here.reshape(-1) * capacity + slot_index
    member_float = member.astype(jnp.float32)
    chosen = jnp.einsum("tke,te->tk", member_float, logits, precision=HIGHEST)
    highest = jnp.max(chosen, axis=-1, keepdims=True)
    raised = jnp.exp(chosen - highest)
    shares = raised / jnp.sum(raised, axis=-1, keepdims=True)
    gates = shares * valid
    outgoing = (
        jnp.zeros((expert_total * capacity, width), jnp.bfloat16)
        .at[places]
        .set(jnp.repeat(entry, picks, axis=0))
    )
    received = lax.all_to_all(
        outgoing.reshape(expert_total, capacity, width),
        "wide",
        split_axis=0,
        concat_axis=1,
        tiled=True,
    )
    expert_pre = jnp.einsum("erd,edf->erf", received, w_gate_up, preferred_element_type=jnp.float32)
    ffe_width = w_down.shape[1]
    gate_part = expert_pre[..., :ffe_width]
    up_part = expert_pre[..., ffe_width:]
    sigmoid_gate = jax.nn.sigmoid(gate_part)
    swish = gate_part * sigmoid_gate
    act_low = (swish * up_part).astype(jnp.bfloat16)
    expert_result = jnp.einsum(
        "erf,efd->erd", act_low, w_down, preferred_element_type=jnp.float32
    ).astype(jnp.bfloat16)
    returned = lax.all_to_all(expert_result, "wide", split_axis=1, concat_axis=0, tiled=True)
    picked = returned.reshape(expert_total * capacity, width)[places].reshape(
        tokens_here, picks, width
    )
    expert_sum = jnp.einsum("tk,tkd->td", gates, picked, precision=HIGHEST)
    output_rows = (valid * (mixed + expert_sum)).astype(jnp.bfloat16)
    grad_rows_here = cotangent[0].astype(jnp.float32) * valid
    slot_grad = (gates[:, :, None] * grad_rows_here[:, None, :]).astype(jnp.bfloat16)
    grad_outgoing = (
        jnp.zeros((expert_total * capacity, width), jnp.bfloat16)
        .at[places]
        .set(slot_grad.reshape(tokens_here * picks, width))
    )
    grad_received = lax.all_to_all(
        grad_outgoing.reshape(expert_total, capacity, width),
        "wide",
        split_axis=0,
        concat_axis=1,
        tiled=True,
    )
    act_grad = jnp.einsum("erd,efd->erf", grad_received, w_down, preferred_element_type=jnp.float32)
    down_grad = jnp.einsum(
        "erf,erd->efd", act_low, grad_received, preferred_element_type=jnp.float32
    )
    gate_grad = act_grad * up_part * sigmoid_gate * (1.0 + gate_part * (1.0 - sigmoid_gate))
    pre_grad = jnp.concatenate([gate_grad, act_grad * swish], axis=-1).astype(jnp.bfloat16)
    gate_up_grad = jnp.einsum(
        "erd,erf->edf", received, pre_grad, preferred_element_type=jnp.float32
    )
    entry_back = jnp.einsum(
        "erf,edf->erd", pre_grad, w_gate_up, preferred_element_type=jnp.float32
    ).astype(jnp.bfloat16)
    entry_home = lax.all_to_all(entry_back, "wide", split_axis=1, concat_axis=0, tiled=True)
    entry_rows = entry_home.reshape(expert_total * capacity, width)[places].reshape(
        tokens_here, picks, width
    )
    entry_grad = jnp.sum(entry_rows, axis=1, dtype=jnp.float32)
    pick_grad = jnp.einsum("td,tkd->tk", grad_rows_here, picked, precision=HIGHEST) * valid
    chosen_grad = shares * (pick_grad - jnp.sum(shares * pick_grad, axis=-1, keepdims=True))
    logit_grad = jnp.einsum("tk,tke->te", chosen_grad, member_float, precision=HIGHEST)
    router_grad = lax.dot_general(
        entry.astype(jnp.float32), logit_grad, (((0,), (0,)), ((), ())), precision=HIGHEST
    )
    entry_grad = entry_grad + lax.dot_general(
        logit_grad, w_router.astype(jnp.float32), (((1,), (1,)), ((), ())), precision=HIGHEST
    )
    mixed_from_norm, gain_two_grad = norm_backward(mixed, scale_two, moe_gain, entry_grad)
    mixed_grad = grad_rows_here + mixed_from_norm
    attn_grad_low = mixed_grad.astype(jnp.bfloat16)
    grad_whole = lax.all_gather(attn_grad_low, "narrow", axis=0, tiled=True)
    context_grad = lax.dot_general(
        grad_whole, w_out, (((1,), (1,)), ((), ())), preferred_element_type=jnp.float32
    ).astype(jnp.bfloat16)
    out_grad = lax.dot_general(
        context_rows, grad_whole, (((0,), (0,)), ((), ())), preferred_element_type=jnp.float32
    )
    context_blocks = context_grad.reshape(
        block_count, block_rows, kv_here, group_size, head_dim
    ).transpose(0, 2, 3, 1, 4)
    query_grad, key_grad, value_grad = attend_backward(
        queries, keys_low, values_low, context_blocks, log_sums, length_here, scaling
    )
    query_rows = turn(
        query_grad.transpose(0, 3, 1, 2, 4).reshape(seq_len, kv_here, group_size, head_dim),
        cosine,
        sine_part,
        -1.0,
    )
    key_rows = turn(key_grad.transpose(1, 0, 2), cosine, sine_part, -1.0)
    value_rows = value_grad.transpose(1, 0, 2)
    qkv_grad = jnp.concatenate(
        [
            query_rows.reshape(seq_len, query_cols),
            key_rows.reshape(seq_len, key_cols),
            value_rows.reshape(seq_len, key_cols),
        ],
        axis=1,
    ).astype(jnp.bfloat16)
    qkv_weight_grad = lax.dot_general(
        whole, qkv_grad, (((0,), (0,)), ((), ())), preferred_element_type=jnp.float32
    )
    piece = qkv_grad
    normed_grad = lax.psum_scatter(
        lax.dot_general(
            piece, w_qkv, (((1,), (1,)), ((), ())), preferred_element_type=jnp.float32
        ).astype(jnp.bfloat16),
        "narrow",
        scatter_dimension=0,
        tiled=True,
    ).astype(jnp.float32)
    source_from_norm, gain_one_grad = norm_backward(source, scale_one, attn_gain, normed_grad)
    grad_input = (mixed_grad + source_from_norm).astype(jnp.bfloat16)
    gate_up_grad, down_grad, router_grad, gain_one_grad, gain_two_grad = (
        lax.psum(gate_up_grad.astype(jnp.bfloat16), "narrow").astype(jnp.float32),
        lax.psum(down_grad.astype(jnp.bfloat16), "narrow").astype(jnp.float32),
        lax.psum(router_grad.astype(jnp.bfloat16), "narrow").astype(jnp.float32),
        lax.psum(gain_one_grad.astype(jnp.bfloat16), "narrow").astype(jnp.float32),
        lax.psum(gain_two_grad.astype(jnp.bfloat16), "narrow").astype(jnp.float32),
    )
    qkv_weight_grad, out_grad, router_grad, gain_one_grad, gain_two_grad = (
        lax.psum(qkv_weight_grad.astype(jnp.bfloat16), "wide").astype(jnp.float32),
        lax.psum(out_grad.astype(jnp.bfloat16), "wide").astype(jnp.float32),
        lax.psum(router_grad.astype(jnp.bfloat16), "wide").astype(jnp.float32),
        lax.psum(gain_one_grad.astype(jnp.bfloat16), "wide").astype(jnp.float32),
        lax.psum(gain_two_grad.astype(jnp.bfloat16), "wide").astype(jnp.float32),
    )
    query_weight_grad = qkv_weight_grad[:, :query_cols]
    key_weight_grad = qkv_weight_grad[:, query_cols : query_cols + key_cols]
    value_weight_grad = qkv_weight_grad[:, query_cols + key_cols :]
    return (
        output_rows[None],
        grad_input[None],
        gain_one_grad,
        query_weight_grad,
        key_weight_grad,
        value_weight_grad,
        out_grad,
        gain_two_grad,
        router_grad,
        gate_up_grad,
        down_grad,
    )


def local(
    hidden,
    lengths,
    routes,
    cotangent,
    attn_gain,
    w_query,
    w_key,
    w_value,
    w_out,
    moe_gain,
    w_router,
    w_gate_up,
    w_down,
):
    kv_here = w_key.shape[1] // HEAD_DIM
    rows, width = hidden.shape[1:]
    if lax.axis_size("narrow") != 4 or kv_here != 2 or rows != 256:
        return local_general(
            hidden, lengths, routes, cotangent, attn_gain, w_query, w_key, w_value, w_out,
            moe_gain, w_router, w_gate_up, w_down,
        )
    count = lax.axis_size("wide")
    picks = routes.shape[2]
    expert_total = w_router.shape[1]
    expert_here = w_gate_up.shape[0]
    capacity = 2 * rows * picks // expert_total
    query_cols, key_cols = w_query.shape[1], w_key.shape[1]
    labels = jnp.concatenate(
        [routes[0].T, jnp.broadcast_to(lengths, (8, rows)).astype(jnp.int32)], axis=0
    )
    cosine, sine = rope_tables(4 * rows, HEAD_DIM)
    cosine = jnp.concatenate([cosine] * 4, axis=1)
    sine = jnp.concatenate([-sine, sine] * 2, axis=1)
    w_qkv = jnp.concatenate([w_query, w_key, w_value], axis=1)
    router_turned = w_router.T
    gain_one, gain_two = attn_gain[None], moe_gain[None]
    entry_all, grad_all, whole, queries, keys, values, context, lse, mixed, slots, gates, shares, offsets = front_kernel(
        hidden[0], cotangent[0], labels, lengths, gain_one, w_qkv, w_out, gain_two, router_turned,
        cosine, sine, count, expert_here, picks, 1,
    )
    offsets = offsets.reshape(-1)
    earlier, pick_parts, ups, downs = None, [], [], []
    pair = 2
    for first in range(0, expert_here, pair):
        expert_part, back_part, pick_part, up_part, down_part = expert_pair(
            offsets, entry_all, grad_all, slots, gates, w_gate_up, w_down, earlier, first, pair, capacity
        )
        earlier = (expert_part, back_part)
        pick_parts.append(pick_part)
        ups.append(up_part)
        downs.append(down_part)
    picks_out = jnp.concatenate(pick_parts, axis=0).transpose(1, 0, 2)
    entry_home, pick_home, own = home_kernel(back_part, picks_out, ups, downs, 2)
    out, grad_hidden, summed, up_grad, down_grad = tail_kernel(
        entry_home, pick_home.reshape(expert_total, rows), shares, router_turned, mixed, cotangent[0],
        hidden[0], lengths, gain_one, gain_two, w_qkv, w_qkv.T, w_out, queries, keys, values, context,
        whole.reshape(4 * rows, width), lse, cosine, sine, expert_part, own,
        (w_gate_up.shape, w_down.shape), 3,
    )
    summed = summed.reshape(-1, width).astype(F32)
    cols = query_cols + 2 * key_cols
    turned = summed[:cols].T
    small = summed[cols + query_cols :]
    return (
        out[None],
        grad_hidden[None],
        small[expert_total],
        turned[:, :query_cols],
        turned[:, query_cols : query_cols + key_cols],
        turned[:, query_cols + key_cols :],
        summed[cols : cols + query_cols],
        small[expert_total + 1],
        small[:expert_total].T,
        up_grad.astype(F32),
        down_grad.astype(F32),
    )


def solution(mesh):
    in_specs = (
        P("wide", "narrow", None),
        P("wide"),
        P("wide", "narrow", None),
        P("wide", "narrow", None),
        P(),
        P(None, "narrow"),
        P(None, "narrow"),
        P(None, "narrow"),
        P("narrow", None),
        P(),
        P(),
        P("wide", None, None),
        P("wide", None, None),
    )
    out_specs = (
        P("wide", "narrow", None),
        P("wide", "narrow", None),
        P(),
        P(None, "narrow"),
        P(None, "narrow"),
        P(None, "narrow"),
        P("narrow", None),
        P(),
        P(),
        P("wide", None, None),
        P("wide", None, None),
    )
    return jax.shard_map(local, mesh=mesh, in_specs=in_specs, out_specs=out_specs, check_vma=False)
```

```python
import jax
import jax.numpy as jnp
from jax import lax
from jax.experimental import pallas as pl
from jax.experimental.pallas import tpu as pltpu
from jax.sharding import PartitionSpec as P

HEADS = 16
KV_HEADS = 8
HEAD_DIM = 64
BF = jnp.bfloat16
F32 = jnp.float32
MESH = pl.DeviceIdType.MESH
EPSILON = 1e-06
THETA = 10000.0
HIGHEST = lax.Precision.HIGHEST


def rope_tables(count, head_dim):
    half_dim = head_dim // 2
    inverse = THETA ** (-jnp.arange(half_dim, dtype=jnp.float32) * 2.0 / head_dim)
    angles = jnp.arange(count, dtype=jnp.float32)[:, None] * inverse[None, :]
    return (jnp.cos(angles), jnp.sin(angles))


def turn(values, cosine, sine_part, direction):
    half_dim = values.shape[-1] // 2
    shape_here = (cosine.shape[0],) + (1,) * (values.ndim - 2) + (half_dim,)
    cosine = cosine.reshape(shape_here)
    sine_part = direction * sine_part.reshape(shape_here)
    first = values[..., :half_dim]
    second = values[..., half_dim:]
    return jnp.concatenate(
        [first * cosine - second * sine_part, second * cosine + first * sine_part], axis=-1
    )


def norm_forward(values, gain):
    scaling = lax.rsqrt(jnp.mean(values * values, axis=-1, keepdims=True) + EPSILON)
    return (values * scaling * gain, scaling)


def norm_backward(values, scaling, gain, incoming):
    unit_values = values * scaling
    gain_grad = jnp.sum(incoming * unit_values, axis=0)
    inner = incoming * gain
    input_grad = scaling * (
        inner - unit_values * jnp.mean(inner * unit_values, axis=-1, keepdims=True)
    )
    return (input_grad, gain_grad)


def visible(start, block_rows, key_places, length_here):
    query_places = start + jnp.arange(block_rows, dtype=jnp.int32)
    return (key_places[None, :] <= query_places[:, None]) & (key_places[None, :] < length_here)


def attend_forward(queries, keys_low, values_low, length_here, scaling):
    key_places = jnp.arange(keys_low.shape[1], dtype=jnp.int32)
    block_rows = queries.shape[3]

    def one_block(inputs):
        query_block, start = inputs
        scores = (
            jnp.einsum("kgqd,ksd->kgqs", query_block, keys_low, preferred_element_type=jnp.float32)
            * scaling
        )
        scores = jnp.where(visible(start, block_rows, key_places, length_here), scores, -1e30)
        highest = jnp.max(scores, axis=-1, keepdims=True)
        weights = jnp.exp(scores - highest)
        totals = jnp.sum(weights, axis=-1, keepdims=True)
        chances = (weights / totals).astype(jnp.bfloat16)
        context = jnp.einsum(
            "kgqs,ksd->kgqd", chances, values_low, preferred_element_type=jnp.float32
        )
        return (context.astype(jnp.bfloat16), (highest + jnp.log(totals))[..., 0])

    starts = jnp.arange(queries.shape[0], dtype=jnp.int32) * block_rows
    return lax.map(one_block, (queries, starts))


def attend_backward(queries, keys_low, values_low, context_grad, log_sums, length_here, scaling):
    key_places = jnp.arange(keys_low.shape[1], dtype=jnp.int32)
    block_rows = queries.shape[3]

    def one_block(carry, inputs):
        key_grad, value_grad = carry
        query_block, grad_block, sum_block, start = inputs
        scores = (
            jnp.einsum("kgqd,ksd->kgqs", query_block, keys_low, preferred_element_type=jnp.float32)
            * scaling
        )
        allowed = visible(start, block_rows, key_places, length_here)
        scores = jnp.where(allowed, scores, -1e30)
        chances = jnp.where(allowed, jnp.exp(scores - sum_block[..., None]), 0.0)
        chance_grad = jnp.einsum(
            "kgqd,ksd->kgqs", grad_block, values_low, preferred_element_type=jnp.float32
        )
        inner = jnp.sum(chances * chance_grad, axis=-1, keepdims=True)
        score_grad = (chances * (chance_grad - inner)).astype(jnp.bfloat16)
        query_grad = (
            jnp.einsum("kgqs,ksd->kgqd", score_grad, keys_low, preferred_element_type=jnp.float32)
            * scaling
        )
        key_grad = (
            key_grad
            + jnp.einsum(
                "kgqs,kgqd->ksd", score_grad, query_block, preferred_element_type=jnp.float32
            )
            * scaling
        )
        value_grad = value_grad + jnp.einsum(
            "kgqs,kgqd->ksd",
            chances.astype(jnp.bfloat16),
            grad_block,
            preferred_element_type=jnp.float32,
        )
        return ((key_grad, value_grad), query_grad)

    starts = jnp.arange(queries.shape[0], dtype=jnp.int32) * block_rows
    zeros = jnp.zeros(keys_low.shape, jnp.float32)
    (key_grad, value_grad), query_grad = lax.scan(
        one_block, (zeros, zeros), (queries, context_grad, log_sums, starts)
    )
    return (query_grad, key_grad, value_grad)


def ring_place(index, count):
    half = index // 2
    odd = index % 2
    return (1 - odd) * half + odd * (count - 1 - half)

def ring_index(place, count):
    odd = place // (count // 2)
    half = (1 - odd) * place + odd * (count - 1 - place)
    return 2 * half + odd


def add_low(one, two):
    return (one.astype(F32) + two.astype(F32)).astype(BF)

class Ring:
    def __init__(self, count):
        self.count = count
        self.me = lax.axis_index("wide")
        self.place = ring_place(self.me, count)
        self.peers = (self.at(1), self.at(-1))

    def at(self, shift):
        return ring_index((self.place + shift + 2 * self.count) % self.count, self.count)

def greet(wide_peers, narrow_peers):
    barrier = pltpu.get_barrier_semaphore()
    for peer in wide_peers:
        pl.semaphore_signal(barrier, inc=1, device_id={"wide": peer}, device_id_type=MESH)
    for peer in narrow_peers:
        pl.semaphore_signal(barrier, inc=1, device_id={"narrow": peer}, device_id_type=MESH)
    pl.semaphore_wait(barrier, len(wide_peers) + len(narrow_peers))

def remote(source, target, send, recv, **device):
    return pltpu.make_async_remote_copy(
        src_ref=source, dst_ref=target, send_sem=send, recv_sem=recv,
        device_id=device, device_id_type=MESH,
    )

def cuts(rows):
    first = (rows // 2 + 15) // 16 * 16
    return ((0, first), (first, rows - first))

def scatter_steps(ring, p_ref, held, send_sem, recv_sem, finish):
    count = ring.count
    lane = p_ref.shape[1] // 2

    def copy(way, step, k):
        sign = 1 if way == 0 else -1
        start, size = cuts(lane)[k]
        src = (
            p_ref.at[ring.at(-sign), pl.ds(way * lane + start, size)]
            if step == 0
            else held.at[way, step - 1, pl.ds(start, size)]
        )
        return remote(
            src, held.at[way, step, pl.ds(start, size)],
            send_sem.at[way, step, k], recv_sem.at[way, step, k], wide=ring.peers[way],
        )

    for step in range(count - 1):
        for k in range(2):
            for way in range(2):
                sign = 1 if way == 0 else -1
                start, size = cuts(lane)[k]
                if step > 0:
                    copy(way, step - 1, k).wait_recv()
                    span = pl.ds(start, size)
                    mine = p_ref[ring.at(-sign * (1 + step)), pl.ds(way * lane + start, size)]
                    held[way, step - 1, span] = add_low(held[way, step - 1, span], mine)
                copy(way, step, k).start()
        yield
    for k in range(2):
        for way in range(2):
            start, size = cuts(lane)[k]
            copy(way, count - 2, k).wait_recv()
            row = way * lane + start
            finish(
                row, size,
                held[way, count - 2, pl.ds(start, size)].astype(F32)
                + p_ref[ring.me, pl.ds(row, size)].astype(F32),
            )
    for step in range(count - 1):
        for k in range(2):
            for way in range(2):
                copy(way, step, k).wait_send()
    yield

def gather_steps(ring, o_ref, send_sem, recv_sem, own=None):
    count = ring.count
    hops = count // 2
    rows = o_ref.shape[1]
    live = lambda way, hop, k: hop < hops - 1 or k == way

    def copy(way, hop, k, shift):
        sign = 1 if way == 0 else -1
        start, size = cuts(rows)[k]
        block = o_ref.at[ring.at(-sign * (hop + shift)), pl.ds(start, size)]
        from_own = own is not None and hop == 0 and shift == 0
        return remote(
            own.at[pl.ds(start, size)] if from_own else block, block, send_sem.at[way, hop, k], recv_sem.at[way, hop, k], wide=ring.peers[way]
        )

    for hop in range(hops):
        for k in range(2):
            for way in range(2):
                if hop > 0:
                    copy(way, hop - 1, k, 1).wait_recv()
                if live(way, hop, k):
                    copy(way, hop, k, 0).start()
        yield
    for k in range(2):
        for way in range(2):
            if live(way, hops - 1, k):
                copy(way, hops - 1, k, 1).wait_recv()
    for hop in range(hops):
        for k in range(2):
            for way in range(2):
                if live(way, hop, k):
                    copy(way, hop, k, 0).wait_send()
    yield

def scatter_scratch(count, rows, cols):
    return [
        pltpu.VMEM((2, count - 1, rows // 2, cols), BF),
        pltpu.SemaphoreType.DMA((2, count - 1, 2)),
        pltpu.SemaphoreType.DMA((2, count - 1, 2)),
    ]

def gather_scratch(count):
    return [pltpu.SemaphoreType.DMA((2, count // 2, 2)), pltpu.SemaphoreType.DMA((2, count // 2, 2))]

def run(*makers):
    live = list(makers)
    while live:
        for one in list(live):
            if next(one, "end") == "end":
                live.remove(one)

def block_add(out, one, two, rows):
    def step(i, carry):
        span = pl.ds(pl.multiple_of(i * 128, 128), 128)
        out[span] = add_low(one[span], two[span])
        return carry
    lax.fori_loop(0, rows // 128, step, 0)


def nt(a, b):
    return lax.dot_general(a, b, (((1,), (1,)), ((), ())), preferred_element_type=F32)

def tn(a, b):
    return lax.dot_general(a, b, (((0,), (0,)), ((), ())), preferred_element_type=F32)

def nn(a, b):
    return jnp.dot(a, b, preferred_element_type=F32)

LANES = 128

def lane_of(shape):
    return lax.broadcasted_iota(jnp.int32, shape, len(shape) - 1)

def turn_lanes(values, cosine, signed_sine):
    low = lane_of(values.shape) % HEAD_DIM < HEAD_DIM // 2
    swapped = jnp.where(
        low,
        pltpu.roll(values, LANES - HEAD_DIM // 2, 1),
        pltpu.roll(values, HEAD_DIM // 2, 1),
    )
    return values * cosine + swapped * signed_sine

def doubled(tile, head):
    other = pltpu.roll(tile, HEAD_DIM, 1)
    low = lane_of(tile.shape) < HEAD_DIM
    return jnp.where(low, tile, other) if head == 0 else jnp.where(low, other, tile)

def stacked(tile):
    low = lane_of(tile.shape) < HEAD_DIM
    zero = jnp.zeros_like(tile)
    return jnp.concatenate([jnp.where(low, tile, zero), jnp.where(low, zero, tile)], axis=0)

def unstacked(turned):
    full = turned.T
    rows = full.shape[0] // 2
    return jnp.where(lane_of((rows, LANES)) < HEAD_DIM, full[:rows], full[rows:])

def masked_scores(keys, queries, key_start, query_start, length, causal):
    scores = nt(keys, queries) * HEAD_DIM ** (-0.5)
    half = queries.shape[0] // 2
    key_at = key_start + lax.broadcasted_iota(jnp.int32, scores.shape, 0)
    allowed = key_at < length
    if causal:
        query_at = query_start + lane_of(scores.shape) % half
        allowed = allowed & (key_at <= query_at)
    return jnp.where(allowed, scores, -1e30)

class Corner:
    def __init__(self):
        self.here = lax.axis_index("narrow")
        self.chip, self.core = self.here // 2, self.here % 2
        self.core_peer = 2 * self.chip + 1 - self.core
        self.chip_peer = 2 * (1 - self.chip) + self.core
        self.far_peer = 2 * (1 - self.chip) + 1 - self.core

class Share:
    def __init__(self, corner, ref, send, recv):
        self.corner, self.ref, self.sems = corner, ref, (send, recv)

    def copy(self, kind, k, owner, peer):
        start, size = cuts(self.ref.shape[1])[k]
        block = self.ref.at[owner, pl.ds(start, size)]
        return remote(block, block, self.sems[0].at[kind, k], self.sems[1].at[kind, k], narrow=peer)

    def start(self):
        c = self.corner
        for k in range(2):
            self.copy(1, k, c.here, c.chip_peer).start()
        for k in range(2):
            self.copy(0, k, c.here, c.core_peer).start()

    def wait_core(self):
        c = self.corner
        for k in range(2):
            self.copy(0, k, c.core_peer, c.core_peer).wait_recv()

    def wait_chip(self):
        c = self.corner
        for k in range(2):
            self.copy(1, k, c.chip_peer, c.chip_peer).wait_recv()
            self.copy(2, k, c.chip_peer, c.core_peer).start()

    def wait_far(self):
        c = self.corner
        for k in range(2):
            self.copy(2, k, c.far_peer, c.core_peer).wait_recv()

    def drain(self):
        c = self.corner
        for k in range(2):
            self.copy(0, k, c.here, c.core_peer).wait_send()
            self.copy(1, k, c.here, c.chip_peer).wait_send()
            self.copy(2, k, c.chip_peer, c.core_peer).wait_send()

    scratch = lambda: [pltpu.SemaphoreType.DMA((3, 2)), pltpu.SemaphoreType.DMA((3, 2))]

class Fold:
    def __init__(self, corner, out_c, got_c, out_x, got_x, held, c_send, c_recv, x_send, x_recv):
        self.corner, self.held = corner, held
        self.out_c, self.got_c, self.out_x, self.got_x = out_c, got_c, out_x, got_x
        self.sems = (c_send, c_recv, x_send, x_recv)

    def to_core(self, x):
        return remote(
            self.out_c.at[x], self.got_c.at[x], self.sems[0].at[x], self.sems[1].at[x],
            narrow=self.corner.core_peer,
        )

    def to_chip(self):
        return remote(self.out_x, self.got_x, self.sems[2], self.sems[3], narrow=self.corner.chip_peer)

    def give(self, block, part):
        x, c = block // 2, block % 2

        @pl.when(self.corner.core != c)
        def _():
            self.out_c[x] = part.astype(BF)
            self.to_core(x).start()

        @pl.when(self.corner.core == c)
        def _():
            self.held[x] = part

    def settle(self, block):
        x, c = block // 2, block % 2

        @pl.when(self.corner.core == c)
        def _():
            self.to_core(x).wait_recv()

            @pl.when(self.corner.chip != x)
            def _():
                self.out_x[...] = (self.held[x] + self.got_c[x].astype(F32)).astype(BF)
                self.to_chip().start()

    def total(self):
        chip = self.corner.chip
        near = self.held[chip] + self.got_c[chip].astype(F32)
        self.to_chip().wait_recv()
        return near + self.got_x[...].astype(F32)

    def drain(self):
        for x in range(2):
            self.to_core(x).wait_send()
        self.to_chip().wait_send()

    def scratch(rows, cols):
        return [
            pltpu.VMEM((2, rows, cols), BF),
            pltpu.VMEM((2, rows, cols), BF),
            pltpu.VMEM((rows, cols), BF),
            pltpu.VMEM((rows, cols), BF),
            pltpu.VMEM((2, rows, cols), F32),
            pltpu.SemaphoreType.DMA((2,)),
            pltpu.SemaphoreType.DMA((2,)),
            pltpu.SemaphoreType.DMA,
            pltpu.SemaphoreType.DMA,
        ]

def front_kernel(hidden, cotangent, labels, length, attn_gain, w_qkv, w_out, moe_gain, cosine, sine, count, experts_here, picks, cid):
    rows, width = hidden.shape
    seq = 4 * rows
    query_cols, key_cols = w_out.shape[0], (w_qkv.shape[1] - w_out.shape[0]) // 2
    kv_here = key_cols // HEAD_DIM

    def kernel(*refs):
        refs = list(refs)
        take = lambda number: [refs.pop(0) for _ in range(number)]
        h_ref, cot_ref, lab_ref, len_ref, g1_ref, wqkv_ref, wout_ref, g2_ref, cos_ref, sin_ref = take(10)
        en_ref, ga_ref, whole_ref, q_ref, k_ref, v_ref, ctx_ref, lse_ref, mixed_ref, slots_ref, lab_all = take(11)
        kd, vd, s_scr, p_scr = take(4)
        share = take(2)
        fold = take(9)
        g_scr = take(2)
        l_send, l_recv, own_sem = take(3)
        ring, corner = Ring(count), Corner()
        others = [(ring.me + shift) % count for shift in range(1, count)]
        greet(others, [corner.core_peer, corner.chip_peer])
        length_here = len_ref[0]

        g_ring = gather_steps(ring, ga_ref, *g_scr, own=cot_ref)
        next(g_ring)
        own_grad = pltpu.make_async_copy(cot_ref, ga_ref.at[ring.me], own_sem)
        own_grad.start()
        label_copy = lambda k, target: remote(
            lab_ref, lab_all.at[ring.me], l_send.at[k], l_recv.at[k], wide=target
        )
        for k, target in enumerate(others):
            label_copy(k, target).start()
        lab_all[ring.me] = lab_ref[...]

        source = h_ref[...].astype(F32)
        scale = lax.rsqrt(jnp.mean(source * source, axis=1, keepdims=True) + EPSILON)
        whole_ref[corner.here] = (source * scale * g1_ref[...]).astype(BF)
        sharing = Share(corner, whole_ref, *share)
        sharing.start()

        def project(block):
            span = pl.ds(pl.multiple_of(block * rows, rows), rows)
            lin = nn(whole_ref[block], wqkv_ref[...])
            cos, sin = cos_ref[span], sin_ref[span]
            for t in range(kv_here):
                lanes = slice(t * LANES, (t + 1) * LANES)
                q_ref[span, lanes] = turn_lanes(lin[:, lanes], cos, sin).astype(BF)
            keys = turn_lanes(lin[:, query_cols : query_cols + key_cols], cos, sin)
            values = lin[:, query_cols + key_cols :]
            k_ref[span] = keys.astype(BF)
            v_ref[span] = values.astype(BF)
            for t in range(kv_here):
                kd[t, span] = doubled(keys, t).astype(BF)
                vd[t, span] = doubled(values, t).astype(BF)

        project(corner.here)
        sharing.wait_core()
        project(corner.core_peer)

        for k, target in enumerate(others):
            sender = (ring.me - (k + 1) + count) % count
            remote(lab_ref, lab_all.at[sender], l_send.at[k], l_recv.at[k], wide=target).wait_recv()
        places = corner.here * rows + lane_of((1, rows))
        first = ring.me * experts_here
        upper = jnp.where(
            lax.broadcasted_iota(jnp.int32, (rows, rows), 0) <= lane_of((rows, rows)), 1.0, 0.0
        ).astype(BF)

        def belongs(block, expert_rows):
            found = lab_all[block, 0:1] == expert_rows
            for k in range(1, picks):
                found = found | (lab_all[block, k : k + 1] == expert_rows)
            return found

        local_rows = lax.broadcasted_iota(jnp.int32, (8, rows), 0)
        own_rows = jnp.where(local_rows < experts_here, first + local_rows, -1)
        for b in range(count):
            mine = jnp.where(belongs(b, own_rows) & (places < lab_all[b, picks : picks + 1]), 1.0, 0.0)
            reached = nn(mine.astype(BF), upper)
            slots_ref[b] = jnp.where(mine > 0.0, reached, 0.0).astype(jnp.int32) - 1

        sharing.wait_chip()
        project(corner.chip_peer)
        next(g_ring)
        sharing.wait_far()
        project(corner.far_peer)

        folding = Fold(corner, *fold)
        before = None
        for block in (3, 2, 1, 0):
            span = pl.ds(block * rows, rows)
            for t in range(kv_here):
                lanes = slice(t * LANES, (t + 1) * LANES)
                queries = stacked(q_ref[span, lanes])
                highest = None
                for b in range(block + 1):
                    keys = pl.ds(b * rows, rows)
                    scores = masked_scores(kd[t, keys], queries, b * rows, block * rows, length_here, b == block)
                    s_scr[keys] = scores
                    top = jnp.max(scores, axis=0, keepdims=True)
                    highest = top if highest is None else jnp.maximum(highest, top)
                total = None
                for b in range(block + 1):
                    keys = pl.ds(b * rows, rows)
                    weights = jnp.exp(s_scr[keys] - highest)
                    p_scr[keys] = weights.astype(BF)
                    one = jnp.sum(weights, axis=0, keepdims=True)
                    total = one if total is None else total + one
                keys = pl.ds(0, (block + 1) * rows)
                context = tn(vd[t, keys], p_scr[keys]) / total
                ctx_ref[span, lanes] = unstacked(context).astype(BF)
                lse_ref[t * 4 + block : t * 4 + block + 1] = highest + jnp.log(total)
            folding.give(block, nn(ctx_ref[span], wout_ref[...]))
            if before is not None:
                folding.settle(before)
            before = block
            if block in (3, 1):
                next(g_ring)
        folding.settle(before)
        mixed = source + folding.total()
        mixed_ref[...] = mixed
        scale = lax.rsqrt(jnp.mean(mixed * mixed, axis=1, keepdims=True) + EPSILON)
        en_ref[...] = (mixed * scale * g2_ref[...]).astype(BF)
        for _ in g_ring:
            pass
        for k, target in enumerate(others):
            label_copy(k, target).wait_send()
        own_grad.wait()
        sharing.drain()
        folding.drain()

    vmem = pl.BlockSpec(memory_space=pltpu.VMEM)
    far = pl.BlockSpec(memory_space=pl.ANY)
    shape = jax.ShapeDtypeStruct
    out_shape = [
        shape((rows, width), BF),
        shape((count, rows, width), BF),
        shape((4, rows, width), BF),
        shape((seq, query_cols), BF),
        shape((seq, key_cols), BF),
        shape((seq, key_cols), BF),
        shape((seq, query_cols), BF),
        shape((8, 2 * rows), F32),
        shape((rows, width), F32),
        shape((count, 8, rows), jnp.int32),
        shape((count,) + labels.shape, jnp.int32),
    ]
    scratch = [
        pltpu.VMEM((kv_here, seq, LANES), BF),
        pltpu.VMEM((kv_here, seq, LANES), BF),
        pltpu.VMEM((seq, 2 * rows), F32),
        pltpu.VMEM((seq, 2 * rows), BF),
        *Share.scratch(),
        *Fold.scratch(rows, width),
        *gather_scratch(count),
        pltpu.SemaphoreType.DMA((count - 1,)),
        pltpu.SemaphoreType.DMA((count - 1,)),
        pltpu.SemaphoreType.DMA,
    ]
    return pl.pallas_call(
        kernel,
        out_shape=out_shape,
        in_specs=[vmem, far, vmem, pl.BlockSpec(memory_space=pltpu.SMEM)] + [vmem] * 6,
        out_specs=[vmem, far] + [vmem] * (len(out_shape) - 2),
        scratch_shapes=scratch,
        compiler_params=pltpu.CompilerParams(
            collective_id=cid, has_side_effects=True, vmem_limit_bytes=56 * 2**20
        ),
    )(hidden, cotangent, labels, length, attn_gain, w_qkv, w_out, moe_gain, cosine, sine)


def middle_kernel(entry, grad_all, labels_all, slots, router_turned, w_gate_up, w_down, capacity, picks, cid):
    rows, width = entry.shape
    count = grad_all.shape[0]
    experts_here, _, ffe2 = w_gate_up.shape
    ffe = ffe2 // 2
    experts = router_turned.shape[0]
    hops = count // 2
    shifts = [0] + [s for hop in range(1, hops) for s in (hop, -hop)] + [hops]
    room = count * capacity
    quarter_up, quarter_down = width // 4, ffe // 4
    quarter = quarter_up + quarter_down

    def kernel(*refs):
        refs = list(refs)
        take = lambda number: [refs.pop(0) for _ in range(number)]
        en_ref, ga_far, lab_all, slots_ref, wr_ref, wgu_far, wd_far = take(7)
        ob_ref, op_ref, c_far, own_far, shares_ref = take(5)
        wgu, wd, e_buf, g_buf, pg, act_s, x_s, s_s, b_buf, c_slot, got_a, got_b, gates, pick_buf = take(14)
        held = take(3)
        e_scr = take(2)
        w_sem, g_sem, c_sem, p_send, p_recv, a_send, a_recv, x_send, x_recv, o_sem = take(10)
        ring, corner = Ring(count), Corner()
        others = [(ring.me + shift) % count for shift in range(1, count)]
        greet(others, [corner.core_peer, corner.chip_peer])

        def weights(e):
            return [
                pltpu.make_async_copy(wgu_far.at[e], wgu.at[e], w_sem.at[0, e]),
                pltpu.make_async_copy(wd_far.at[e], wd.at[e], w_sem.at[1, e]),
            ]

        def grads(p):
            block = ring.at(shifts[p])
            return pltpu.make_async_copy(ga_far.at[block], g_buf.at[block], g_sem.at[p])

        e_buf[ring.me] = en_ref[...]
        e_ring = gather_steps(ring, e_buf, *e_scr)
        next(e_ring)
        for e in range(experts_here):
            for c in weights(e):
                c.start()
            if e == 0:
                for p in range(count):
                    grads(p).start()

        places = corner.here * rows + lane_of((1, rows))
        first = ring.me * experts_here
        every = lax.broadcasted_iota(jnp.int32, (experts, rows), 0)
        local_rows = lax.broadcasted_iota(jnp.int32, (8, rows), 0)
        slot_rows = lax.broadcasted_iota(jnp.int32, (capacity, rows), 0)

        def gate(block, home):
            logits = nt(wr_ref[...], e_buf[block])
            member = lab_all[block, 0:1] == every
            for k in range(1, picks):
                member = member | (lab_all[block, k : k + 1] == every)
            masked = jnp.where(member, logits, -jnp.inf)
            raised = jnp.exp(masked - jnp.max(masked, axis=0, keepdims=True))
            shares = raised / jnp.sum(raised, axis=0, keepdims=True)
            if home:
                shares_ref[...] = shares
            kept = jnp.where(places < lab_all[block, picks : picks + 1], shares, 0.0)
            own = jnp.zeros((8, rows), F32)
            for e in range(experts_here):
                row = jnp.sum(jnp.where(every == first + e, kept, 0.0), axis=0, keepdims=True)
                own = jnp.where(local_rows == e, row, own)
            gates[block] = own

        def pick_rows(block, e):
            return slot_rows == slots_ref[block, pl.ds(e, 1), :]

        def gather_rows(block, e):
            found = pick_rows(block, e)
            chosen = jnp.where(found, 1.0, 0.0).astype(BF)
            gate_col = jnp.sum(jnp.where(found, gates[block, pl.ds(e, 1), :], 0.0), axis=1, keepdims=True)
            return found, nn(chosen, e_buf[block]).astype(BF), nn(chosen, g_buf[block]), gate_col

        def tile(numbers, await_weights):
            blocks = [ring.at(shifts[p]) for p in numbers]
            size = len(numbers) * capacity
            start = numbers[0] * capacity
            for p in numbers:
                grads(p).wait()

            def one(e, carry):
                if await_weights:
                    for c in weights(e):
                        c.wait()
                parts = [gather_rows(block, e) for block in blocks]
                entries = jnp.concatenate([p[1] for p in parts], axis=0)
                grad_rows = jnp.concatenate([p[2] for p in parts], axis=0)
                gate_col = jnp.concatenate([p[3] for p in parts], axis=0)
                slot_grad = (gate_col * grad_rows).astype(BF)
                act_grad = nt(slot_grad, wd[e])
                pre = nn(entries, wgu[e])
                gate_part = pre[:, :ffe]
                up_part = pre[:, ffe:]
                sig = jax.nn.sigmoid(gate_part)
                swish = gate_part * sig
                act = (swish * up_part).astype(BF)
                act_s[e, pl.ds(start, size)] = act
                result = nn(act, wd[e]).astype(BF).astype(F32)
                gate_grad = act_grad * up_part * sig * (1.0 + gate_part * (1.0 - sig))
                pre_grad = jnp.concatenate([gate_grad, act_grad * swish], axis=1).astype(BF)
                pg[e, pl.ds(start, size)] = pre_grad
                here = pl.ds(pl.multiple_of(e * 2 * capacity, 2 * capacity), size)
                s_s[here] = nt(pre_grad, wgu[e]).astype(BF)
                x_s[here] = (gate_col * result).astype(BF)
                pick_col = jnp.sum(result * grad_rows, axis=1, keepdims=True)
                for i, block in enumerate(blocks):
                    row = jnp.sum(
                        jnp.where(parts[i][0], pick_col[i * capacity : (i + 1) * capacity], 0.0),
                        axis=0, keepdims=True,
                    )
                    pick_buf[block] = jnp.where(local_rows == e, row, pick_buf[block])
                return carry

            lax.fori_loop(0, experts_here, one, 0)
            for i, block in enumerate(blocks):
                chosen = jnp.concatenate(
                    [jnp.where(pick_rows(block, e), 1.0, 0.0).astype(BF) for e in range(experts_here)], axis=0
                )
                windows = [pl.ds((2 * e + i) * capacity, capacity) for e in range(experts_here)]
                number = numbers[i]
                slot = number % 2
                if number >= 2:
                    results(number - 2).wait()
                c_slot[slot] = tn(chosen, jnp.concatenate([x_s[w] for w in windows], axis=0)).astype(BF)
                results(number).start()
                b_buf[block] = tn(chosen, jnp.concatenate([s_s[w] for w in windows], axis=0)).astype(BF)

        def results(number):
            return pltpu.make_async_copy(
                c_slot.at[number % 2], c_far.at[ring.at(shifts[number])], c_sem.at[number]
            )

        def put(row, size, got):
            ob_ref[pl.ds(row, size)] = got

        b_ring = scatter_steps(ring, b_buf, *held, put)
        pick_buf[...] = jnp.zeros_like(pick_buf)
        gate(ring.me, True)
        tile([0], True)
        for hop in range(1, hops):
            next(e_ring)
            gate(ring.at(hop), False)
            gate(ring.at(-hop), False)
            tile([2 * hop - 1, 2 * hop], False)
            next(b_ring)
        for _ in e_ring:
            pass
        gate(ring.at(hops), False)
        tile([count - 1], False)
        next(b_ring)
        pick_copy = lambda k, target: remote(
            pick_buf.at[target], op_ref.at[ring.me], p_send.at[k], p_recv.at[k], wide=target
        )
        for k, target in enumerate(others):
            pick_copy(k, target).start()
        op_ref[ring.me] = pick_buf[ring.me]

        def weight_grads(e):
            for p in range(count):
                _, entries, grad_rows, gate_col = gather_rows(ring.at(shifts[p]), e)
                span = pl.ds(p * capacity, capacity)
                x_s[span] = entries
                s_s[span] = (gate_col * grad_rows).astype(BF)

            def columns(j, carry):
                cols = pl.ds(pl.multiple_of(j * 256, 256), 256)
                wgu[e, :, cols] = tn(x_s[...], pg[e, :, cols]).astype(BF)
                wd[e, :, cols] = tn(act_s[e], s_s[:, cols]).astype(BF)
                return carry

            lax.fori_loop(0, width // 256, columns, 0)

        def pieces(e, owner):
            return (
                (wgu.at[e, pl.ds(owner * quarter_up, quarter_up)], 0, quarter_up),
                (wd.at[e, pl.ds(owner * quarter_down, quarter_down)], quarter_up, quarter_down),
            )

        def to_core(e):
            return [
                remote(src, got_a.at[e, x, pl.ds(start, size)], a_send.at[e, x, k], a_recv.at[e, x, k], narrow=corner.core_peer)
                for x in range(2)
                for k, (src, start, size) in enumerate(pieces(e, 2 * x + 1 - corner.core))
            ]

        def to_chip(e):
            return [
                remote(src, got_b.at[e, pl.ds(start, size)], x_send.at[e, k], x_recv.at[e, k], narrow=corner.chip_peer)
                for k, (src, start, size) in enumerate(pieces(e, 2 * (1 - corner.chip) + corner.core))
            ]

        def own_out(e):
            return [
                pltpu.make_async_copy(src, own_far.at[e, pl.ds(start, size)], o_sem.at[e, k])
                for k, (src, start, size) in enumerate(pieces(e, corner.here))
            ]

        def send_core(e):
            for c in to_core(e):
                c.start()

        def first_sum(e):
            for c in to_core(e):
                c.wait_recv()
            for x in (1 - corner.chip, corner.chip):
                for src, start, size in pieces(e, 2 * x + corner.core):
                    block_add(src, src, got_a.at[e, x, pl.ds(start, size)], size)
                if x is not corner.chip:
                    for c in to_chip(e):
                        c.start()

        def last_sum(e):
            for c in to_chip(e):
                c.wait_recv()
            for src, start, size in pieces(e, corner.here):
                block_add(src, src, got_b.at[e, pl.ds(start, size)], size)
            for c in own_out(e):
                c.start()

        for e in range(experts_here):
            weight_grads(e)
            send_core(e)
            if e > 0:
                first_sum(e - 1)
            if e < experts_here - 1:
                next(b_ring)
        first_sum(experts_here - 1)
        for _ in b_ring:
            pass
        for e in range(experts_here):
            last_sum(e)
        for e in range(experts_here):
            for c in to_core(e) + to_chip(e):
                c.wait_send()
            for c in own_out(e):
                c.wait()
        for number in range(max(0, count - 2), count):
            results(number).wait()
        for k, target in enumerate(others):
            sender = (ring.me - (k + 1) + count) % count
            remote(
                pick_buf.at[sender], op_ref.at[sender], p_send.at[k], p_recv.at[k], wide=target
            ).wait_recv()
            pick_copy(k, target).wait_send()

    vmem = pl.BlockSpec(memory_space=pltpu.VMEM)
    far = pl.BlockSpec(memory_space=pl.ANY)
    shape = jax.ShapeDtypeStruct
    out_shape = [
        shape((rows, width), F32),
        shape((count, 8, rows), F32),
        shape((count, rows, width), BF),
        shape((experts_here, quarter, width), BF),
        shape((experts, rows), F32),
    ]
    dma = pltpu.SemaphoreType.DMA
    scratch = [
        pltpu.VMEM(w_gate_up.shape, BF),
        pltpu.VMEM(w_down.shape, BF),
        pltpu.VMEM((count, rows, width), BF),
        pltpu.VMEM((count, rows, width), BF),
        pltpu.VMEM((experts_here, room, 2 * ffe), BF),
        pltpu.VMEM((experts_here, room, ffe), BF),
        pltpu.VMEM((room, width), BF),
        pltpu.VMEM((room, width), BF),
        pltpu.VMEM((count, rows, width), BF),
        pltpu.VMEM((2, rows, width), BF),
        pltpu.VMEM((experts_here, 2, quarter, width), BF),
        pltpu.VMEM((experts_here, quarter, width), BF),
        pltpu.VMEM((count, 8, rows), F32),
        pltpu.VMEM((count, 8, rows), F32),
        *scatter_scratch(count, rows, width),
        *gather_scratch(count),
        dma((2, experts_here)), dma((count,)), dma((count,)),
        dma((count - 1,)), dma((count - 1,)),
        dma((experts_here, 2, 2)), dma((experts_here, 2, 2)),
        dma((experts_here, 2)), dma((experts_here, 2)), dma((experts_here, 2)),
    ]
    return pl.pallas_call(
        kernel,
        out_shape=out_shape,
        in_specs=[vmem, far, vmem, vmem, vmem, far, far],
        out_specs=[vmem, vmem, far, far, vmem],
        scratch_shapes=scratch,
        compiler_params=pltpu.CompilerParams(
            collective_id=cid, has_side_effects=True, vmem_limit_bytes=63 * 2**20
        ),
    )(entry, grad_all, labels_all, slots, router_turned, w_gate_up, w_down)


def tail_kernel(entry_home, pick_home, shares, router_turned, mixed, cotangent, hidden, length, attn_gain, moe_gain, w_qkv, w_qkv_turned, w_out, queries, keys, values, context, whole, lse, cosine, sine, expert_part, own, shapes, cid):
    count, rows, width = expert_part.shape
    seq = 4 * rows
    query_cols, key_cols = w_out.shape[0], (w_qkv.shape[1] - w_out.shape[0]) // 2
    cols = w_qkv.shape[1]
    kv_here = key_cols // HEAD_DIM
    experts_all = router_turned.shape[0]
    small_rows = (experts_all + 2 + 15) // 16 * 16
    block = -(-(cols + query_cols + small_rows) // (32 * count)) * 32
    experts, quarter, _ = own.shape
    up_shape, down_shape = shapes
    quarter_up, quarter_down = up_shape[1] // 4, down_shape[1] // 4
    base = [0, rows, 3 * rows, 6 * rows]
    small_at = cols + query_cols

    def kernel(*refs):
        refs = list(refs)
        take = lambda number: [refs.pop(0) for _ in range(number)]
        eh_ref, pick_ref, shares_ref, wr_ref, mixed_ref, cot_ref, h_ref, len_ref, g1_ref, g2_ref = take(10)
        wqkv_ref, wt_ref, wout_ref, q_ref, k_ref, v_ref, ctx_ref, whole_ref, lse_ref, cos_ref, sin_ref = take(11)
        c_far, own_ref = take(2)
        out_ref, gh_ref, sum_ref, up_ref, down_ref = take(5)
        gw, mg_s, kd, vd, p_all, dp_scr, ds_scr, dctx, dk, dv, qg, packed, small_got, expert_sum, c_ref = take(15)
        share, fold = take(2), take(9)
        (c_sem,) = take(1)
        c_scr, s_scr, g_scr = take(3), take(3), take(2)
        sm_send, sm_recv = take(2)
        c_send, c_recv, x_send, x_recv, f_send, f_recv, l_sem = take(7)
        ring, corner = Ring(count), Corner()
        greet(list(ring.peers), [corner.core_peer, corner.chip_peer, corner.far_peer])
        length_here = len_ref[0]

        def put(row, size, got):
            expert_sum[pl.ds(row, size)] = got

        c_load = pltpu.make_async_copy(c_far, c_ref, c_sem)
        c_load.start()
        c_ring = scatter_steps(ring, c_ref, *c_scr, put)

        def places(e, owner):
            return (
                (own_ref.at[e, pl.ds(0, quarter_up)], up_ref.at[e, pl.ds(owner * quarter_up, quarter_up)]),
                (own_ref.at[e, pl.ds(quarter_up, quarter_down)], down_ref.at[e, pl.ds(owner * quarter_down, quarter_down)]),
            )

        def send(e, sems, peer):
            return [
                remote(src, dst, sems[0].at[e, k], sems[1].at[e, k], narrow=peer)
                for k, (src, dst) in enumerate(places(e, corner.here))
            ]

        def forward(e, owner, sems):
            return [
                remote(dst, dst, sems[0].at[e, k], sems[1].at[e, k], narrow=corner.core_peer)
                for k, (src, dst) in enumerate(places(e, owner))
            ]

        core_sems, chip_sems, far_sems = (c_send, c_recv), (x_send, x_recv), (f_send, f_recv)

        def own_copy(e):
            return [
                pltpu.make_async_copy(src, dst, l_sem.at[e, k])
                for k, (src, dst) in enumerate(places(e, corner.here))
            ]

        def send_out(e):
            for c in send(e, chip_sems, corner.chip_peer):
                c.start()

        def pass_on(e):
            for c in forward(e, corner.chip_peer, chip_sems):
                c.wait_recv()
            for c in forward(e, corner.chip_peer, far_sems):
                c.start()

        picked, held_shares = pick_ref[...], shares_ref[...]
        logit_grad = held_shares * (picked - jnp.sum(held_shares * picked, axis=0, keepdims=True))
        high = logit_grad.astype(BF)
        low = (logit_grad - high.astype(F32)).astype(BF)
        entry_grad = eh_ref[...] + (tn(high, wr_ref[...]) + tn(low, wr_ref[...]))
        mixed_here = mixed_ref[...]
        scale = lax.rsqrt(jnp.mean(mixed_here * mixed_here, axis=1, keepdims=True) + EPSILON)
        unit = mixed_here * scale
        inner = entry_grad * g2_ref[...]
        from_norm = scale * (inner - unit * jnp.mean(inner * unit, axis=1, keepdims=True))
        at = corner.here * rows + lax.broadcasted_iota(jnp.int32, (rows, 1), 0)
        valid = jnp.where(at < length_here, 1.0, 0.0)
        mixed_grad = valid * cot_ref[...].astype(F32) + from_norm
        mg_s[...] = mixed_grad
        gw[corner.here] = mixed_grad.astype(BF)
        sharing = Share(corner, gw, *share)
        sharing.start()
        for e in range(experts):
            for c in send(e, core_sems, corner.core_peer) + own_copy(e):
                c.start()
        entry = (unit * g2_ref[...]).astype(BF)
        router_grad = nn(high, entry) + nn(low, entry)
        gain_two = jnp.sum(entry_grad * unit, axis=0, keepdims=True)

        for t in range(kv_here):
            kd[t] = doubled(k_ref[...].astype(F32), t).astype(BF)
            vd[t] = doubled(v_ref[...].astype(F32), t).astype(BF)

        def chances(b):
            for t in range(kv_here):
                lanes = slice(t * LANES, (t + 1) * LANES)
                stack = stacked(q_ref[pl.ds(b * rows, rows), lanes])
                log_sum = lse_ref[t * 4 + b : t * 4 + b + 1]
                for kb in range(b + 1):
                    scores = masked_scores(
                        kd[t, pl.ds(kb * rows, rows)], stack, kb * rows, b * rows, length_here, kb == b
                    )
                    p_all[t, pl.ds(base[b] + kb * rows, rows)] = jnp.exp(scores - log_sum).astype(BF)

        def pull(owner):
            dctx[owner] = nt(gw[owner], wout_ref[...]).astype(BF)

        pull(corner.here)
        c_load.wait()
        next(c_ring)
        chances(3)
        next(c_ring)
        sharing.wait_core()
        pull(corner.core_peer)
        chances(2)
        next(c_ring)
        chances(1)
        chances(0)
        sharing.wait_chip()
        send_out(0)
        pull(corner.chip_peer)
        sharing.wait_far()
        pull(corner.far_peer)
        dk[...] = jnp.zeros_like(dk)
        dv[...] = jnp.zeros_like(dv)

        folding = Fold(corner, *fold)
        before = None
        for b in (3, 2, 1, 0):
            span = pl.ds(b * rows, rows)
            cos, sin = cos_ref[span], sin_ref[span]
            for t in range(kv_here):
                lanes = slice(t * LANES, (t + 1) * LANES)
                stack = stacked(q_ref[span, lanes])
                grad_stack = stacked(dctx[b, :, lanes])
                inner = None
                for kb in range(b + 1):
                    chance = p_all[t, pl.ds(base[b] + kb * rows, rows)]
                    grad = nt(vd[t, pl.ds(kb * rows, rows)], grad_stack)
                    dp_scr[pl.ds(kb * rows, rows)] = grad
                    one = jnp.sum(chance.astype(F32) * grad, axis=0, keepdims=True)
                    inner = one if inner is None else inner + one
                for kb in range(b + 1):
                    key_span = pl.ds(kb * rows, rows)
                    chance = p_all[t, pl.ds(base[b] + kb * rows, rows)]
                    score_grad = (chance.astype(F32) * (dp_scr[key_span] - inner)).astype(BF)
                    ds_scr[key_span] = score_grad
                    dk[t, key_span] += nn(score_grad, stack)
                    dv[t, key_span] += nn(chance, grad_stack)
                every = pl.ds(0, (b + 1) * rows)
                query_grad = unstacked(tn(kd[t, every], ds_scr[every])) * HEAD_DIM ** (-0.5)
                qg[span, lanes] = turn_lanes(query_grad, cos, -sin).astype(BF)
            low_lanes = lane_of((rows, LANES)) < HEAD_DIM
            both = lambda ref, t: ref[t, span] + pltpu.roll(ref[t, span], HEAD_DIM, 1)
            key_grad = jnp.where(low_lanes, both(dk, 0), both(dk, 1)) * HEAD_DIM ** (-0.5)
            qg[span, query_cols : query_cols + key_cols] = turn_lanes(key_grad, cos, -sin).astype(BF)
            qg[span, query_cols + key_cols :] = jnp.where(low_lanes, both(dv, 0), both(dv, 1)).astype(BF)
            folding.give(b, nt(qg[span], wqkv_ref[...]))
            if before is not None:
                folding.settle(before)
            before = b
            next(c_ring)
            if b == 1:
                send_out(1)
        folding.settle(before)

        def store(row, value):
            for start in range(0, value.shape[0], 16):
                size = min(16, value.shape[0] - start)
                at_row = row + start
                packed[at_row // block, pl.ds(at_row % block, size)] = value[start : start + size].astype(BF)

        weight_grad = tn(qg[...], whole_ref[...])
        gain_one = jnp.sum(weight_grad * wt_ref[...].astype(F32), axis=0, keepdims=True) / g1_ref[...]
        small_here = jnp.concatenate(
            [router_grad, gain_one, gain_two, jnp.zeros((small_rows - experts_all - 2, width), F32)], axis=0
        )
        small_got[3] = small_here.astype(BF)
        small_copy = lambda k, peer: remote(
            small_got.at[3], small_got.at[k], sm_send.at[k], sm_recv.at[k], narrow=peer
        )
        peers = (corner.core_peer, corner.chip_peer, corner.far_peer)
        for k, peer in enumerate(peers):
            small_copy(k, peer).start()
        store(0, weight_grad)
        store(cols, tn(ctx_ref[...], gw[...].reshape(seq, width)))
        rest = small_at + small_rows
        store(rest, jnp.zeros((count * block - rest, width), F32))
        for k, peer in enumerate(peers):
            small_copy(k, peer).wait_recv()
        store(small_at, small_here + sum(small_got[k].astype(F32) for k in range(3)))

        def finish(row, size, got):
            sum_ref[ring.me, pl.ds(row, size)] = got.astype(BF)

        sums = scatter_steps(ring, packed, *s_scr, finish)
        next(sums)
        pass_on(0)
        send_out(2)
        normed_grad = folding.total()
        source = h_ref[...].astype(F32)
        scale = lax.rsqrt(jnp.mean(source * source, axis=1, keepdims=True) + EPSILON)
        unit = source * scale
        inner = normed_grad * g1_ref[...]
        from_norm = scale * (inner - unit * jnp.mean(inner * unit, axis=1, keepdims=True))
        gh_ref[...] = (mg_s[...] + from_norm).astype(BF)
        send_out(3)
        next(sums)
        for _ in c_ring:
            next(sums, None)
        out_ref[...] = (valid * (mixed_here + expert_sum[...])).astype(BF)
        for _ in sums:
            pass
        pass_on(1)
        gathers = gather_steps(ring, sum_ref, *g_scr)
        next(gathers)
        next(gathers)
        pass_on(2)
        for _ in gathers:
            pass
        pass_on(3)
        for k, peer in enumerate(peers):
            small_copy(k, peer).wait_send()
        for e in range(experts):
            for c in own_copy(e):
                c.wait()
            for c in send(e, chip_sems, corner.chip_peer) + send(e, core_sems, corner.core_peer):
                c.wait_send()
            for c in forward(e, corner.core_peer, core_sems):
                c.wait_recv()
            for c in forward(e, corner.chip_peer, far_sems):
                c.wait_send()
            for c in forward(e, corner.far_peer, far_sems):
                c.wait_recv()
        sharing.drain()
        folding.drain()

    vmem = pl.BlockSpec(memory_space=pltpu.VMEM)
    far = pl.BlockSpec(memory_space=pl.ANY)
    shape = jax.ShapeDtypeStruct
    out_shape = [
        shape((rows, width), BF),
        shape((rows, width), BF),
        shape((count, block, width), BF),
        shape(up_shape, BF),
        shape(down_shape, BF),
    ]
    scratch = [
        pltpu.VMEM((4, rows, width), BF),
        pltpu.VMEM((rows, width), F32),
        pltpu.VMEM((kv_here, seq, LANES), BF),
        pltpu.VMEM((kv_here, seq, LANES), BF),
        pltpu.VMEM((kv_here, 10 * rows, 2 * rows), BF),
        pltpu.VMEM((seq, 2 * rows), F32),
        pltpu.VMEM((seq, 2 * rows), BF),
        pltpu.VMEM((4, rows, query_cols), BF),
        pltpu.VMEM((kv_here, seq, LANES), F32),
        pltpu.VMEM((kv_here, seq, LANES), F32),
        pltpu.VMEM((seq, cols), BF),
        pltpu.VMEM((count, block, width), BF),
        pltpu.VMEM((4, small_rows, width), BF),
        pltpu.VMEM((rows, width), F32),
        pltpu.VMEM((count, rows, width), BF),
        *Share.scratch(),
        *Fold.scratch(rows, width),
        pltpu.SemaphoreType.DMA,
        *scatter_scratch(count, rows, width),
        *scatter_scratch(count, block, width),
        *gather_scratch(count),
        pltpu.SemaphoreType.DMA((3,)),
        pltpu.SemaphoreType.DMA((3,)),
    ] + [pltpu.SemaphoreType.DMA((experts, 2))] * 7
    return pl.pallas_call(
        kernel,
        out_shape=out_shape,
        in_specs=[vmem] * 7 + [pl.BlockSpec(memory_space=pltpu.SMEM)] + [vmem] * 13 + [far] * 2,
        out_specs=[vmem] * 3 + [far] * 2,
        scratch_shapes=scratch,
        compiler_params=pltpu.CompilerParams(
            collective_id=cid, has_side_effects=True, vmem_limit_bytes=62 * 2**20
        ),
    )(entry_home, pick_home, shares, router_turned, mixed, cotangent, hidden, length, attn_gain, moe_gain,
      w_qkv, w_qkv_turned, w_out, queries, keys, values, context, whole, lse, cosine, sine, expert_part, own)


def local_general(
    hidden,
    lengths,
    routes,
    cotangent,
    attn_gain,
    w_query,
    w_key,
    w_value,
    w_out,
    moe_gain,
    w_router,
    w_gate_up,
    w_down,
):
    rows_here = hidden.shape[1]
    width = hidden.shape[2]
    seq_len = rows_here * lax.axis_size("narrow")
    head_dim = HEAD_DIM
    group_size = HEADS // KV_HEADS
    kv_here = w_key.shape[1] // head_dim
    query_cols = kv_here * group_size * head_dim
    key_cols = kv_here * head_dim
    scaling = head_dim ** (-0.5)
    block_rows = min(512, seq_len)
    block_count = seq_len // block_rows
    length_here = lengths[0]
    offset = lax.axis_index("narrow") * rows_here
    local_places = offset + jnp.arange(rows_here, dtype=jnp.int32)
    valid = (local_places < length_here).astype(jnp.float32)[:, None]
    source = hidden[0].astype(jnp.float32)
    normed, scale_one = norm_forward(source, attn_gain)
    normed_low = normed.astype(jnp.bfloat16)
    whole = lax.all_gather(normed_low, "narrow", axis=0, tiled=True)
    w_qkv = jnp.concatenate([w_query, w_key, w_value], axis=1)
    projected = jnp.dot(whole, w_qkv, preferred_element_type=jnp.float32)
    cosine, sine_part = rope_tables(seq_len, head_dim)
    query_rot = turn(
        projected[:, :query_cols].reshape(seq_len, kv_here, group_size, head_dim),
        cosine,
        sine_part,
        1.0,
    )
    key_rot = turn(
        projected[:, query_cols : query_cols + key_cols].reshape(seq_len, kv_here, head_dim),
        cosine,
        sine_part,
        1.0,
    )
    queries = (
        query_rot.astype(jnp.bfloat16)
        .reshape(block_count, block_rows, kv_here, group_size, head_dim)
        .transpose(0, 2, 3, 1, 4)
    )
    keys_low = key_rot.astype(jnp.bfloat16).transpose(1, 0, 2)
    values_low = (
        projected[:, query_cols + key_cols :]
        .astype(jnp.bfloat16)
        .reshape(seq_len, kv_here, head_dim)
        .transpose(1, 0, 2)
    )
    context, log_sums = attend_forward(queries, keys_low, values_low, length_here, scaling)
    context_rows = context.transpose(0, 3, 1, 2, 4).reshape(seq_len, query_cols)
    piece = context_rows
    attn_part = lax.psum_scatter(
        jnp.dot(piece, w_out, preferred_element_type=jnp.float32).astype(jnp.bfloat16),
        "narrow",
        scatter_dimension=0,
        tiled=True,
    ).astype(jnp.float32)
    mixed = source + attn_part
    normed_two, scale_two = norm_forward(mixed, moe_gain)
    entry = normed_two.astype(jnp.bfloat16)
    logits = jnp.dot(entry, w_router, preferred_element_type=jnp.float32)
    route_here = routes[0]
    tokens_here, picks = route_here.shape
    expert_total = w_router.shape[1]
    capacity = 2 * tokens_here * picks // expert_total
    member = (
        route_here[:, :, None] == jnp.arange(expert_total, dtype=jnp.int32)[None, None, :]
    ).astype(jnp.int32)
    flat_member = member.reshape(tokens_here * picks, expert_total)
    earlier = jnp.cumsum(flat_member, axis=0) - flat_member
    slot_index = jnp.sum(earlier * flat_member, axis=1)
    places = route_here.reshape(-1) * capacity + slot_index
    member_float = member.astype(jnp.float32)
    chosen = jnp.einsum("tke,te->tk", member_float, logits, precision=HIGHEST)
    highest = jnp.max(chosen, axis=-1, keepdims=True)
    raised = jnp.exp(chosen - highest)
    shares = raised / jnp.sum(raised, axis=-1, keepdims=True)
    gates = shares * valid
    outgoing = (
        jnp.zeros((expert_total * capacity, width), jnp.bfloat16)
        .at[places]
        .set(jnp.repeat(entry, picks, axis=0))
    )
    received = lax.all_to_all(
        outgoing.reshape(expert_total, capacity, width),
        "wide",
        split_axis=0,
        concat_axis=1,
        tiled=True,
    )
    expert_pre = jnp.einsum("erd,edf->erf", received, w_gate_up, preferred_element_type=jnp.float32)
    ffe_width = w_down.shape[1]
    gate_part = expert_pre[..., :ffe_width]
    up_part = expert_pre[..., ffe_width:]
    sigmoid_gate = jax.nn.sigmoid(gate_part)
    swish = gate_part * sigmoid_gate
    act_low = (swish * up_part).astype(jnp.bfloat16)
    expert_result = jnp.einsum(
        "erf,efd->erd", act_low, w_down, preferred_element_type=jnp.float32
    ).astype(jnp.bfloat16)
    returned = lax.all_to_all(expert_result, "wide", split_axis=1, concat_axis=0, tiled=True)
    picked = returned.reshape(expert_total * capacity, width)[places].reshape(
        tokens_here, picks, width
    )
    expert_sum = jnp.einsum("tk,tkd->td", gates, picked, precision=HIGHEST)
    output_rows = (valid * (mixed + expert_sum)).astype(jnp.bfloat16)
    grad_rows_here = cotangent[0].astype(jnp.float32) * valid
    slot_grad = (gates[:, :, None] * grad_rows_here[:, None, :]).astype(jnp.bfloat16)
    grad_outgoing = (
        jnp.zeros((expert_total * capacity, width), jnp.bfloat16)
        .at[places]
        .set(slot_grad.reshape(tokens_here * picks, width))
    )
    grad_received = lax.all_to_all(
        grad_outgoing.reshape(expert_total, capacity, width),
        "wide",
        split_axis=0,
        concat_axis=1,
        tiled=True,
    )
    act_grad = jnp.einsum("erd,efd->erf", grad_received, w_down, preferred_element_type=jnp.float32)
    down_grad = jnp.einsum(
        "erf,erd->efd", act_low, grad_received, preferred_element_type=jnp.float32
    )
    gate_grad = act_grad * up_part * sigmoid_gate * (1.0 + gate_part * (1.0 - sigmoid_gate))
    pre_grad = jnp.concatenate([gate_grad, act_grad * swish], axis=-1).astype(jnp.bfloat16)
    gate_up_grad = jnp.einsum(
        "erd,erf->edf", received, pre_grad, preferred_element_type=jnp.float32
    )
    entry_back = jnp.einsum(
        "erf,edf->erd", pre_grad, w_gate_up, preferred_element_type=jnp.float32
    ).astype(jnp.bfloat16)
    entry_home = lax.all_to_all(entry_back, "wide", split_axis=1, concat_axis=0, tiled=True)
    entry_rows = entry_home.reshape(expert_total * capacity, width)[places].reshape(
        tokens_here, picks, width
    )
    entry_grad = jnp.sum(entry_rows, axis=1, dtype=jnp.float32)
    pick_grad = jnp.einsum("td,tkd->tk", grad_rows_here, picked, precision=HIGHEST) * valid
    chosen_grad = shares * (pick_grad - jnp.sum(shares * pick_grad, axis=-1, keepdims=True))
    logit_grad = jnp.einsum("tk,tke->te", chosen_grad, member_float, precision=HIGHEST)
    router_grad = lax.dot_general(
        entry.astype(jnp.float32), logit_grad, (((0,), (0,)), ((), ())), precision=HIGHEST
    )
    entry_grad = entry_grad + lax.dot_general(
        logit_grad, w_router.astype(jnp.float32), (((1,), (1,)), ((), ())), precision=HIGHEST
    )
    mixed_from_norm, gain_two_grad = norm_backward(mixed, scale_two, moe_gain, entry_grad)
    mixed_grad = grad_rows_here + mixed_from_norm
    attn_grad_low = mixed_grad.astype(jnp.bfloat16)
    grad_whole = lax.all_gather(attn_grad_low, "narrow", axis=0, tiled=True)
    context_grad = lax.dot_general(
        grad_whole, w_out, (((1,), (1,)), ((), ())), preferred_element_type=jnp.float32
    ).astype(jnp.bfloat16)
    out_grad = lax.dot_general(
        context_rows, grad_whole, (((0,), (0,)), ((), ())), preferred_element_type=jnp.float32
    )
    context_blocks = context_grad.reshape(
        block_count, block_rows, kv_here, group_size, head_dim
    ).transpose(0, 2, 3, 1, 4)
    query_grad, key_grad, value_grad = attend_backward(
        queries, keys_low, values_low, context_blocks, log_sums, length_here, scaling
    )
    query_rows = turn(
        query_grad.transpose(0, 3, 1, 2, 4).reshape(seq_len, kv_here, group_size, head_dim),
        cosine,
        sine_part,
        -1.0,
    )
    key_rows = turn(key_grad.transpose(1, 0, 2), cosine, sine_part, -1.0)
    value_rows = value_grad.transpose(1, 0, 2)
    qkv_grad = jnp.concatenate(
        [
            query_rows.reshape(seq_len, query_cols),
            key_rows.reshape(seq_len, key_cols),
            value_rows.reshape(seq_len, key_cols),
        ],
        axis=1,
    ).astype(jnp.bfloat16)
    qkv_weight_grad = lax.dot_general(
        whole, qkv_grad, (((0,), (0,)), ((), ())), preferred_element_type=jnp.float32
    )
    piece = qkv_grad
    normed_grad = lax.psum_scatter(
        lax.dot_general(
            piece, w_qkv, (((1,), (1,)), ((), ())), preferred_element_type=jnp.float32
        ).astype(jnp.bfloat16),
        "narrow",
        scatter_dimension=0,
        tiled=True,
    ).astype(jnp.float32)
    source_from_norm, gain_one_grad = norm_backward(source, scale_one, attn_gain, normed_grad)
    grad_input = (mixed_grad + source_from_norm).astype(jnp.bfloat16)
    gate_up_grad, down_grad, router_grad, gain_one_grad, gain_two_grad = (
        lax.psum(gate_up_grad.astype(jnp.bfloat16), "narrow").astype(jnp.float32),
        lax.psum(down_grad.astype(jnp.bfloat16), "narrow").astype(jnp.float32),
        lax.psum(router_grad.astype(jnp.bfloat16), "narrow").astype(jnp.float32),
        lax.psum(gain_one_grad.astype(jnp.bfloat16), "narrow").astype(jnp.float32),
        lax.psum(gain_two_grad.astype(jnp.bfloat16), "narrow").astype(jnp.float32),
    )
    qkv_weight_grad, out_grad, router_grad, gain_one_grad, gain_two_grad = (
        lax.psum(qkv_weight_grad.astype(jnp.bfloat16), "wide").astype(jnp.float32),
        lax.psum(out_grad.astype(jnp.bfloat16), "wide").astype(jnp.float32),
        lax.psum(router_grad.astype(jnp.bfloat16), "wide").astype(jnp.float32),
        lax.psum(gain_one_grad.astype(jnp.bfloat16), "wide").astype(jnp.float32),
        lax.psum(gain_two_grad.astype(jnp.bfloat16), "wide").astype(jnp.float32),
    )
    query_weight_grad = qkv_weight_grad[:, :query_cols]
    key_weight_grad = qkv_weight_grad[:, query_cols : query_cols + key_cols]
    value_weight_grad = qkv_weight_grad[:, query_cols + key_cols :]
    return (
        output_rows[None],
        grad_input[None],
        gain_one_grad,
        query_weight_grad,
        key_weight_grad,
        value_weight_grad,
        out_grad,
        gain_two_grad,
        router_grad,
        gate_up_grad,
        down_grad,
    )


def local(
    hidden,
    lengths,
    routes,
    cotangent,
    attn_gain,
    w_query,
    w_key,
    w_value,
    w_out,
    moe_gain,
    w_router,
    w_gate_up,
    w_down,
):
    kv_here = w_key.shape[1] // HEAD_DIM
    rows, width = hidden.shape[1:]
    if lax.axis_size("narrow") != 4 or kv_here != 2 or rows != 256:
        return local_general(
            hidden, lengths, routes, cotangent, attn_gain, w_query, w_key, w_value, w_out,
            moe_gain, w_router, w_gate_up, w_down,
        )
    count = lax.axis_size("wide")
    picks = routes.shape[2]
    expert_total = w_router.shape[1]
    expert_here = w_gate_up.shape[0]
    capacity = 2 * rows * picks // expert_total
    query_cols, key_cols = w_query.shape[1], w_key.shape[1]
    labels = jnp.concatenate(
        [routes[0].T, jnp.broadcast_to(lengths, (8, rows)).astype(jnp.int32)], axis=0
    )
    cosine, sine = rope_tables(4 * rows, HEAD_DIM)
    cosine = jnp.concatenate([cosine] * 4, axis=1)
    sine = jnp.concatenate([-sine, sine] * 2, axis=1)
    w_qkv = jnp.concatenate([w_query, w_key, w_value], axis=1)
    router_turned = w_router.T
    gain_one, gain_two = attn_gain[None], moe_gain[None]
    entry, grad_all, whole, queries, keys, values, context, lse, mixed, slots, labels_all = front_kernel(
        hidden[0], cotangent[0], labels, lengths, gain_one, w_qkv, w_out, gain_two, cosine, sine,
        count, expert_here, picks, 1,
    )
    entry_home, pick_home, expert_part, own, shares = middle_kernel(
        entry, grad_all, labels_all, slots, router_turned, w_gate_up, w_down, capacity, picks, 2
    )
    pick_home = pick_home[:, :expert_here]
    out, grad_hidden, summed, up_grad, down_grad = tail_kernel(
        entry_home, pick_home.reshape(expert_total, rows), shares, router_turned, mixed, cotangent[0],
        hidden[0], lengths, gain_one, gain_two, w_qkv, w_qkv.T, w_out, queries, keys, values, context,
        whole.reshape(4 * rows, width), lse, cosine, sine, expert_part, own,
        (w_gate_up.shape, w_down.shape), 3,
    )
    summed = summed.reshape(-1, width).astype(F32)
    cols = query_cols + 2 * key_cols
    turned = summed[:cols].T
    small = summed[cols + query_cols :]
    return (
        out[None],
        grad_hidden[None],
        small[expert_total],
        turned[:, :query_cols],
        turned[:, query_cols : query_cols + key_cols],
        turned[:, query_cols + key_cols :],
        summed[cols : cols + query_cols],
        small[expert_total + 1],
        small[:expert_total].T,
        up_grad.astype(F32),
        down_grad.astype(F32),
    )


def solution(mesh):
    in_specs = (
        P("wide", "narrow", None),
        P("wide"),
        P("wide", "narrow", None),
        P("wide", "narrow", None),
        P(),
        P(None, "narrow"),
        P(None, "narrow"),
        P(None, "narrow"),
        P("narrow", None),
        P(),
        P(),
        P("wide", None, None),
        P("wide", None, None),
    )
    out_specs = (
        P("wide", "narrow", None),
        P("wide", "narrow", None),
        P(),
        P(None, "narrow"),
        P(None, "narrow"),
        P(None, "narrow"),
        P("narrow", None),
        P(),
        P(),
        P("wide", None, None),
        P("wide", None, None),
    )
    return jax.shard_map(local, mesh=mesh, in_specs=in_specs, out_specs=out_specs, check_vma=False)
```

```python
import jax
import numpy as np
import jax.numpy as jnp
from jax import lax
from jax.experimental import pallas as pl
from jax.experimental.pallas import tpu as pltpu
from jax.sharding import PartitionSpec as P

HEADS = 16
KV_HEADS = 8
HEAD_DIM = 64
BF = jnp.bfloat16
F32 = jnp.float32
MESH = pl.DeviceIdType.MESH
EPSILON = 1e-06
THETA = 10000.0
HIGHEST = lax.Precision.HIGHEST


def rope_tables(count, head_dim):
    half_dim = head_dim // 2
    inverse = THETA ** (-jnp.arange(half_dim, dtype=jnp.float32) * 2.0 / head_dim)
    angles = jnp.arange(count, dtype=jnp.float32)[:, None] * inverse[None, :]
    return (jnp.cos(angles), jnp.sin(angles))


def turn(values, cosine, sine_part, direction):
    half_dim = values.shape[-1] // 2
    shape_here = (cosine.shape[0],) + (1,) * (values.ndim - 2) + (half_dim,)
    cosine = cosine.reshape(shape_here)
    sine_part = direction * sine_part.reshape(shape_here)
    first = values[..., :half_dim]
    second = values[..., half_dim:]
    return jnp.concatenate(
        [first * cosine - second * sine_part, second * cosine + first * sine_part], axis=-1
    )


def norm_forward(values, gain):
    scaling = lax.rsqrt(jnp.mean(values * values, axis=-1, keepdims=True) + EPSILON)
    return (values * scaling * gain, scaling)


def norm_backward(values, scaling, gain, incoming):
    unit_values = values * scaling
    gain_grad = jnp.sum(incoming * unit_values, axis=0)
    inner = incoming * gain
    input_grad = scaling * (
        inner - unit_values * jnp.mean(inner * unit_values, axis=-1, keepdims=True)
    )
    return (input_grad, gain_grad)


def visible(start, block_rows, key_places, length_here):
    query_places = start + jnp.arange(block_rows, dtype=jnp.int32)
    return (key_places[None, :] <= query_places[:, None]) & (key_places[None, :] < length_here)


def attend_forward(queries, keys_low, values_low, length_here, scaling):
    key_places = jnp.arange(keys_low.shape[1], dtype=jnp.int32)
    block_rows = queries.shape[3]

    def one_block(inputs):
        query_block, start = inputs
        scores = (
            jnp.einsum("kgqd,ksd->kgqs", query_block, keys_low, preferred_element_type=jnp.float32)
            * scaling
        )
        scores = jnp.where(visible(start, block_rows, key_places, length_here), scores, -1e30)
        highest = jnp.max(scores, axis=-1, keepdims=True)
        weights = jnp.exp(scores - highest)
        totals = jnp.sum(weights, axis=-1, keepdims=True)
        chances = (weights / totals).astype(jnp.bfloat16)
        context = jnp.einsum(
            "kgqs,ksd->kgqd", chances, values_low, preferred_element_type=jnp.float32
        )
        return (context.astype(jnp.bfloat16), (highest + jnp.log(totals))[..., 0])

    starts = jnp.arange(queries.shape[0], dtype=jnp.int32) * block_rows
    return lax.map(one_block, (queries, starts))


def attend_backward(queries, keys_low, values_low, context_grad, log_sums, length_here, scaling):
    key_places = jnp.arange(keys_low.shape[1], dtype=jnp.int32)
    block_rows = queries.shape[3]

    def one_block(carry, inputs):
        key_grad, value_grad = carry
        query_block, grad_block, sum_block, start = inputs
        scores = (
            jnp.einsum("kgqd,ksd->kgqs", query_block, keys_low, preferred_element_type=jnp.float32)
            * scaling
        )
        allowed = visible(start, block_rows, key_places, length_here)
        scores = jnp.where(allowed, scores, -1e30)
        chances = jnp.where(allowed, jnp.exp(scores - sum_block[..., None]), 0.0)
        chance_grad = jnp.einsum(
            "kgqd,ksd->kgqs", grad_block, values_low, preferred_element_type=jnp.float32
        )
        inner = jnp.sum(chances * chance_grad, axis=-1, keepdims=True)
        score_grad = (chances * (chance_grad - inner)).astype(jnp.bfloat16)
        query_grad = (
            jnp.einsum("kgqs,ksd->kgqd", score_grad, keys_low, preferred_element_type=jnp.float32)
            * scaling
        )
        key_grad = (
            key_grad
            + jnp.einsum(
                "kgqs,kgqd->ksd", score_grad, query_block, preferred_element_type=jnp.float32
            )
            * scaling
        )
        value_grad = value_grad + jnp.einsum(
            "kgqs,kgqd->ksd",
            chances.astype(jnp.bfloat16),
            grad_block,
            preferred_element_type=jnp.float32,
        )
        return ((key_grad, value_grad), query_grad)

    starts = jnp.arange(queries.shape[0], dtype=jnp.int32) * block_rows
    zeros = jnp.zeros(keys_low.shape, jnp.float32)
    (key_grad, value_grad), query_grad = lax.scan(
        one_block, (zeros, zeros), (queries, context_grad, log_sums, starts)
    )
    return (query_grad, key_grad, value_grad)


def ring_place(index, count):
    half = index // 2
    odd = index % 2
    return (1 - odd) * half + odd * (count - 1 - half)

def ring_index(place, count):
    odd = place // (count // 2)
    half = (1 - odd) * place + odd * (count - 1 - place)
    return 2 * half + odd


def add_low(one, two):
    return (one.astype(F32) + two.astype(F32)).astype(BF)

class Ring:
    def __init__(self, count):
        self.count = count
        self.me = lax.axis_index("wide")
        self.place = ring_place(self.me, count)
        self.peers = (self.at(1), self.at(-1))

    def at(self, shift):
        return ring_index((self.place + shift + 2 * self.count) % self.count, self.count)

def greet(wide_peers, narrow_peers):
    barrier = pltpu.get_barrier_semaphore()
    for peer in wide_peers:
        pl.semaphore_signal(barrier, inc=1, device_id={"wide": peer}, device_id_type=MESH)
    for peer in narrow_peers:
        pl.semaphore_signal(barrier, inc=1, device_id={"narrow": peer}, device_id_type=MESH)
    pl.semaphore_wait(barrier, len(wide_peers) + len(narrow_peers))

def remote(source, target, send, recv, **device):
    return pltpu.make_async_remote_copy(
        src_ref=source, dst_ref=target, send_sem=send, recv_sem=recv,
        device_id=device, device_id_type=MESH,
    )

def cuts(rows):
    first = (rows // 2 + 15) // 16 * 16
    return ((0, first), (first, rows - first))

def scatter_steps(ring, p_ref, held, send_sem, recv_sem, finish):
    count = ring.count
    lane = p_ref.shape[1] // 2

    def copy(way, step, k):
        sign = 1 if way == 0 else -1
        start, size = cuts(lane)[k]
        src = (
            p_ref.at[ring.at(-sign), pl.ds(way * lane + start, size)]
            if step == 0
            else held.at[way, step - 1, pl.ds(start, size)]
        )
        return remote(
            src, held.at[way, step, pl.ds(start, size)],
            send_sem.at[way, step, k], recv_sem.at[way, step, k], wide=ring.peers[way],
        )

    for step in range(count - 1):
        for k in range(2):
            for way in range(2):
                sign = 1 if way == 0 else -1
                start, size = cuts(lane)[k]
                if step > 0:
                    copy(way, step - 1, k).wait_recv()
                    span = pl.ds(start, size)
                    mine = p_ref[ring.at(-sign * (1 + step)), pl.ds(way * lane + start, size)]
                    held[way, step - 1, span] = add_low(held[way, step - 1, span], mine)
                copy(way, step, k).start()
        yield
    for k in range(2):
        for way in range(2):
            start, size = cuts(lane)[k]
            copy(way, count - 2, k).wait_recv()
            row = way * lane + start
            finish(
                row, size,
                held[way, count - 2, pl.ds(start, size)].astype(F32)
                + p_ref[ring.me, pl.ds(row, size)].astype(F32),
            )
    for step in range(count - 1):
        for k in range(2):
            for way in range(2):
                copy(way, step, k).wait_send()
    yield

def gather_steps(ring, o_ref, send_sem, recv_sem, own=None):
    count = ring.count
    hops = count // 2
    rows = o_ref.shape[1]
    live = lambda way, hop, k: hop < hops - 1 or k == way

    def copy(way, hop, k, shift):
        sign = 1 if way == 0 else -1
        start, size = cuts(rows)[k]
        block = o_ref.at[ring.at(-sign * (hop + shift)), pl.ds(start, size)]
        from_own = own is not None and hop == 0 and shift == 0
        return remote(
            own.at[pl.ds(start, size)] if from_own else block, block, send_sem.at[way, hop, k], recv_sem.at[way, hop, k], wide=ring.peers[way]
        )

    for hop in range(hops):
        for k in range(2):
            for way in range(2):
                if hop > 0:
                    copy(way, hop - 1, k, 1).wait_recv()
                if live(way, hop, k):
                    copy(way, hop, k, 0).start()
        yield
    for k in range(2):
        for way in range(2):
            if live(way, hops - 1, k):
                copy(way, hops - 1, k, 1).wait_recv()
    for hop in range(hops):
        for k in range(2):
            for way in range(2):
                if live(way, hop, k):
                    copy(way, hop, k, 0).wait_send()
    yield

def scatter_scratch(count, rows, cols):
    return [
        pltpu.VMEM((2, count - 1, rows // 2, cols), BF),
        pltpu.SemaphoreType.DMA((2, count - 1, 2)),
        pltpu.SemaphoreType.DMA((2, count - 1, 2)),
    ]

def gather_scratch(count):
    return [pltpu.SemaphoreType.DMA((2, count // 2, 2)), pltpu.SemaphoreType.DMA((2, count // 2, 2))]

def run(*makers):
    live = list(makers)
    while live:
        for one in list(live):
            if next(one, "end") == "end":
                live.remove(one)

def block_add(out, one, two, rows):
    def step(i, carry):
        span = pl.ds(pl.multiple_of(i * 128, 128), 128)
        out[span] = add_low(one[span], two[span])
        return carry
    lax.fori_loop(0, rows // 128, step, 0)


def nt(a, b):
    return lax.dot_general(a, b, (((1,), (1,)), ((), ())), preferred_element_type=F32)

def tn(a, b):
    return lax.dot_general(a, b, (((0,), (0,)), ((), ())), preferred_element_type=F32)

def nn(a, b):
    return jnp.dot(a, b, preferred_element_type=F32)

LANES = 128

def lane_of(shape):
    return lax.broadcasted_iota(jnp.int32, shape, len(shape) - 1)

def turn_lanes(values, cosine, signed_sine):
    low = lane_of(values.shape) % HEAD_DIM < HEAD_DIM // 2
    swapped = jnp.where(
        low,
        pltpu.roll(values, LANES - HEAD_DIM // 2, 1),
        pltpu.roll(values, HEAD_DIM // 2, 1),
    )
    return values * cosine + swapped * signed_sine

def doubled(tile, head):
    other = pltpu.roll(tile, HEAD_DIM, 1)
    low = lane_of(tile.shape) < HEAD_DIM
    return jnp.where(low, tile, other) if head == 0 else jnp.where(low, other, tile)

def stacked(tile):
    low = lane_of(tile.shape) < HEAD_DIM
    zero = jnp.zeros_like(tile)
    return jnp.concatenate([jnp.where(low, tile, zero), jnp.where(low, zero, tile)], axis=0)

def unstacked(turned):
    full = turned.T
    rows = full.shape[0] // 2
    return jnp.where(lane_of((rows, LANES)) < HEAD_DIM, full[:rows], full[rows:])

def masked_scores(keys, queries, key_start, query_start, length, causal):
    scores = nt(keys, queries) * HEAD_DIM ** (-0.5)
    half = queries.shape[0] // 2
    key_at = key_start + lax.broadcasted_iota(jnp.int32, scores.shape, 0)
    allowed = key_at < length
    if causal:
        query_at = query_start + lane_of(scores.shape) % half
        allowed = allowed & (key_at <= query_at)
    return jnp.where(allowed, scores, -1e30)

class Corner:
    def __init__(self):
        self.here = lax.axis_index("narrow")
        self.chip, self.core = self.here // 2, self.here % 2
        self.core_peer = 2 * self.chip + 1 - self.core
        self.chip_peer = 2 * (1 - self.chip) + self.core
        self.far_peer = 2 * (1 - self.chip) + 1 - self.core

class Share:
    def __init__(self, corner, ref, send, recv):
        self.corner, self.ref, self.sems = corner, ref, (send, recv)

    def copy(self, kind, k, owner, peer):
        start, size = cuts(self.ref.shape[1])[k]
        block = self.ref.at[owner, pl.ds(start, size)]
        return remote(block, block, self.sems[0].at[kind, k], self.sems[1].at[kind, k], narrow=peer)

    def start(self):
        c = self.corner
        for k in range(2):
            self.copy(1, k, c.here, c.chip_peer).start()
        for k in range(2):
            self.copy(0, k, c.here, c.core_peer).start()

    def wait_core(self):
        c = self.corner
        for k in range(2):
            self.copy(0, k, c.core_peer, c.core_peer).wait_recv()

    def wait_chip(self):
        c = self.corner
        for k in range(2):
            self.copy(1, k, c.chip_peer, c.chip_peer).wait_recv()
            self.copy(2, k, c.chip_peer, c.core_peer).start()

    def wait_far(self):
        c = self.corner
        for k in range(2):
            self.copy(2, k, c.far_peer, c.core_peer).wait_recv()

    def drain(self):
        c = self.corner
        for k in range(2):
            self.copy(0, k, c.here, c.core_peer).wait_send()
            self.copy(1, k, c.here, c.chip_peer).wait_send()
            self.copy(2, k, c.chip_peer, c.core_peer).wait_send()

    scratch = lambda: [pltpu.SemaphoreType.DMA((3, 2)), pltpu.SemaphoreType.DMA((3, 2))]

class Fold:
    def __init__(self, corner, out_c, got_c, out_x, got_x, held, c_send, c_recv, x_send, x_recv):
        self.corner, self.held = corner, held
        self.out_c, self.got_c, self.out_x, self.got_x = out_c, got_c, out_x, got_x
        self.sems = (c_send, c_recv, x_send, x_recv)

    def to_core(self, x):
        return remote(
            self.out_c.at[x], self.got_c.at[x], self.sems[0].at[x], self.sems[1].at[x],
            narrow=self.corner.core_peer,
        )

    def to_chip(self):
        return remote(self.out_x, self.got_x, self.sems[2], self.sems[3], narrow=self.corner.chip_peer)

    def give(self, block, part):
        x, c = block // 2, block % 2

        @pl.when(self.corner.core != c)
        def _():
            self.out_c[x] = part.astype(BF)
            self.to_core(x).start()

        @pl.when(self.corner.core == c)
        def _():
            self.held[x] = part

    def settle(self, block):
        x, c = block // 2, block % 2

        @pl.when(self.corner.core == c)
        def _():
            self.to_core(x).wait_recv()

            @pl.when(self.corner.chip != x)
            def _():
                self.out_x[...] = (self.held[x] + self.got_c[x].astype(F32)).astype(BF)
                self.to_chip().start()

    def total(self):
        chip = self.corner.chip
        near = self.held[chip] + self.got_c[chip].astype(F32)
        self.to_chip().wait_recv()
        return near + self.got_x[...].astype(F32)

    def drain(self):
        for x in range(2):
            self.to_core(x).wait_send()
        self.to_chip().wait_send()

    def scratch(rows, cols):
        return [
            pltpu.VMEM((2, rows, cols), BF),
            pltpu.VMEM((2, rows, cols), BF),
            pltpu.VMEM((rows, cols), BF),
            pltpu.VMEM((rows, cols), BF),
            pltpu.VMEM((2, rows, cols), F32),
            pltpu.SemaphoreType.DMA((2,)),
            pltpu.SemaphoreType.DMA((2,)),
            pltpu.SemaphoreType.DMA,
            pltpu.SemaphoreType.DMA,
        ]

def front_kernel(hidden, cotangent, routes, length, attn_gain, w_query, w_key, w_value, w_out, moe_gain, cosine, sine, count, experts_here, cid):
    rows, width = hidden.shape
    seq = 4 * rows
    query_cols, key_cols = w_query.shape[1], w_key.shape[1]
    picks = routes.shape[1]
    kv_here = key_cols // HEAD_DIM

    def kernel(*refs):
        refs = list(refs)
        take = lambda number: [refs.pop(0) for _ in range(number)]
        h_ref, cot_ref, route_ref, len_ref, g1_ref, wq_far, wk_far, wv_far, wout_ref, g2_ref, cos_ref, sin_ref = take(12)
        en_ref, ga_ref, whole_ref, q_ref, k_ref, v_ref, ctx_ref, lse_ref, mixed_ref, slots_ref, lab_all = take(11)
        kd, vd, s_scr, p_scr, wqkv_ref, lab_ref = take(6)
        share = take(2)
        fold = take(9)
        g_scr = take(2)
        l_send, l_recv, own_sem, w_sem = take(4)
        ring, corner = Ring(count), Corner()
        others = [(ring.me + shift) % count for shift in range(1, count)]
        w_loads = [
            pltpu.make_async_copy(src, wqkv_ref.at[:, pl.ds(start, size)], w_sem.at[k])
            for k, (src, start, size) in enumerate(
                ((wq_far, 0, query_cols), (wk_far, query_cols, key_cols), (wv_far, query_cols + key_cols, key_cols))
            )
        ]
        for c in w_loads:
            c.start()
        length_here = len_ref[0]
        spread = jnp.concatenate([route_ref[...], jnp.zeros((rows, LANES - picks), jnp.int32)], axis=1)
        lab_ref[0:picks] = spread.T[0:picks]
        lab_ref[picks : 2 * picks] = jnp.full((picks, rows), length_here, jnp.int32)
        greet(others, [corner.core_peer, corner.chip_peer])

        g_ring = gather_steps(ring, ga_ref, *g_scr, own=cot_ref)
        next(g_ring)
        own_grad = pltpu.make_async_copy(cot_ref, ga_ref.at[ring.me], own_sem)
        own_grad.start()
        label_copy = lambda k, target: remote(
            lab_ref, lab_all.at[ring.me], l_send.at[k], l_recv.at[k], wide=target
        )
        for k, target in enumerate(others):
            label_copy(k, target).start()
        lab_all[ring.me] = lab_ref[...]

        source = h_ref[...].astype(F32)
        scale = lax.rsqrt(jnp.mean(source * source, axis=1, keepdims=True) + EPSILON)
        whole_ref[corner.here] = (source * scale * g1_ref[...]).astype(BF)
        sharing = Share(corner, whole_ref, *share)
        sharing.start()

        def project(block):
            span = pl.ds(pl.multiple_of(block * rows, rows), rows)
            lin = nn(whole_ref[block], wqkv_ref[...])
            cos, sin = cos_ref[span], sin_ref[span]
            for t in range(kv_here):
                lanes = slice(t * LANES, (t + 1) * LANES)
                q_ref[span, lanes] = turn_lanes(lin[:, lanes], cos, sin).astype(BF)
            keys = turn_lanes(lin[:, query_cols : query_cols + key_cols], cos, sin)
            values = lin[:, query_cols + key_cols :]
            k_ref[span] = keys.astype(BF)
            v_ref[span] = values.astype(BF)
            for t in range(kv_here):
                kd[t, span] = doubled(keys, t).astype(BF)
                vd[t, span] = doubled(values, t).astype(BF)

        for c in w_loads:
            c.wait()
        project(corner.here)
        sharing.wait_core()
        project(corner.core_peer)

        for k, target in enumerate(others):
            sender = (ring.me - (k + 1) + count) % count
            remote(lab_ref, lab_all.at[sender], l_send.at[k], l_recv.at[k], wide=target).wait_recv()
        places = corner.here * rows + lane_of((1, rows))
        first = ring.me * experts_here
        upper = jnp.where(
            lax.broadcasted_iota(jnp.int32, (rows, rows), 0) <= lane_of((rows, rows)), 1.0, 0.0
        ).astype(BF)

        def belongs(block, expert_rows):
            found = lab_all[block, 0:1] == expert_rows
            for k in range(1, picks):
                found = found | (lab_all[block, k : k + 1] == expert_rows)
            return found

        local_rows = lax.broadcasted_iota(jnp.int32, (8, rows), 0)
        own_rows = jnp.where(local_rows < experts_here, first + local_rows, -1)
        for b in range(count):
            mine = jnp.where(belongs(b, own_rows) & (places < lab_all[b, picks : picks + 1]), 1.0, 0.0)
            reached = nn(mine.astype(BF), upper)
            slots_ref[b] = jnp.where(mine > 0.0, reached, 0.0).astype(jnp.int32) - 1

        sharing.wait_chip()
        project(corner.chip_peer)
        next(g_ring)
        sharing.wait_far()
        project(corner.far_peer)

        folding = Fold(corner, *fold)
        before = None
        for block in (3, 2, 1, 0):
            span = pl.ds(block * rows, rows)
            for t in range(kv_here):
                lanes = slice(t * LANES, (t + 1) * LANES)
                queries = stacked(q_ref[span, lanes])
                highest = None
                for b in range(block + 1):
                    keys = pl.ds(b * rows, rows)
                    scores = masked_scores(kd[t, keys], queries, b * rows, block * rows, length_here, b == block)
                    s_scr[keys] = scores
                    top = jnp.max(scores, axis=0, keepdims=True)
                    highest = top if highest is None else jnp.maximum(highest, top)
                total = None
                for b in range(block + 1):
                    keys = pl.ds(b * rows, rows)
                    weights = jnp.exp(s_scr[keys] - highest)
                    p_scr[keys] = weights.astype(BF)
                    one = jnp.sum(weights, axis=0, keepdims=True)
                    total = one if total is None else total + one
                keys = pl.ds(0, (block + 1) * rows)
                context = tn(vd[t, keys], p_scr[keys]) / total
                ctx_ref[span, lanes] = unstacked(context).astype(BF)
                lse_ref[t * 4 + block : t * 4 + block + 1] = highest + jnp.log(total)
            folding.give(block, nn(ctx_ref[span], wout_ref[...]))
            if before is not None:
                folding.settle(before)
            before = block
            if block in (3, 1):
                next(g_ring)
        folding.settle(before)
        mixed = source + folding.total()
        mixed_ref[...] = mixed
        scale = lax.rsqrt(jnp.mean(mixed * mixed, axis=1, keepdims=True) + EPSILON)
        en_ref[...] = (mixed * scale * g2_ref[...]).astype(BF)
        for _ in g_ring:
            pass
        for k, target in enumerate(others):
            label_copy(k, target).wait_send()
        own_grad.wait()
        sharing.drain()
        folding.drain()

    vmem = pl.BlockSpec(memory_space=pltpu.VMEM)
    far = pl.BlockSpec(memory_space=pl.ANY)
    shape = jax.ShapeDtypeStruct
    out_shape = [
        shape((rows, width), BF),
        shape((count, rows, width), BF),
        shape((4, rows, width), BF),
        shape((seq, query_cols), BF),
        shape((seq, key_cols), BF),
        shape((seq, key_cols), BF),
        shape((seq, query_cols), BF),
        shape((8, 2 * rows), F32),
        shape((rows, width), F32),
        shape((count, 8, rows), jnp.int32),
        shape((count, 2 * picks, rows), jnp.int32),
    ]
    scratch = [
        pltpu.VMEM((kv_here, seq, LANES), BF),
        pltpu.VMEM((kv_here, seq, LANES), BF),
        pltpu.VMEM((seq, 2 * rows), F32),
        pltpu.VMEM((seq, 2 * rows), BF),
        pltpu.VMEM((width, query_cols + 2 * key_cols), BF),
        pltpu.VMEM((2 * picks, rows), jnp.int32),
        *Share.scratch(),
        *Fold.scratch(rows, width),
        *gather_scratch(count),
        pltpu.SemaphoreType.DMA((count - 1,)),
        pltpu.SemaphoreType.DMA((count - 1,)),
        pltpu.SemaphoreType.DMA,
        pltpu.SemaphoreType.DMA((3,)),
    ]
    return pl.pallas_call(
        kernel,
        out_shape=out_shape,
        in_specs=[vmem, far, vmem, pl.BlockSpec(memory_space=pltpu.SMEM)] + [vmem] + [far] * 3 + [vmem] * 4,
        out_specs=[vmem, far] + [vmem] * (len(out_shape) - 2),
        scratch_shapes=scratch,
        compiler_params=pltpu.CompilerParams(
            collective_id=cid, has_side_effects=True, vmem_limit_bytes=56 * 2**20
        ),
    )(hidden, cotangent, routes, length, attn_gain, w_query, w_key, w_value, w_out, moe_gain, cosine, sine)


def middle_kernel(entry, grad_all, labels_all, slots, router_turned, w_gate_up, w_down, capacity, picks, cid):
    rows, width = entry.shape
    count = grad_all.shape[0]
    experts_here, _, ffe2 = w_gate_up.shape
    ffe = ffe2 // 2
    experts = router_turned.shape[0]
    hops = count // 2
    shifts = [0] + [s for hop in range(1, hops) for s in (hop, -hop)] + [hops]
    room = count * capacity
    quarter_up, quarter_down = width // 4, ffe // 4
    quarter = quarter_up + quarter_down

    def kernel(*refs):
        refs = list(refs)
        take = lambda number: [refs.pop(0) for _ in range(number)]
        en_far, ga_far, lab_all, slots_ref, wr_ref, wgu_far, wd_far = take(7)
        ob_ref, op_ref, c_far, keep_far, got_far, shares_ref, wait_far = take(7)
        wgu, wd, e_buf, g_buf, pg, act_s, x_s, s_s, b_buf, c_slot, got_a, gates, pick_buf, last_c, last_b = take(15)
        held = take(3)
        e_scr = take(2)
        w_sem, g_sem, c_sem, p_send, p_recv, a_send, a_recv, x_send, x_recv, o_sem, f_sem, en_sem = take(12)
        ring, corner = Ring(count), Corner()
        others = [(ring.me + shift) % count for shift in range(1, count)]
        greet(others, [corner.core_peer, corner.chip_peer])

        def weights(e):
            return [
                pltpu.make_async_copy(wgu_far.at[e], wgu.at[e], w_sem.at[0, e]),
                pltpu.make_async_copy(wd_far.at[e], wd.at[e], w_sem.at[1, e]),
            ]

        def grads(p):
            block = ring.at(shifts[p])
            return pltpu.make_async_copy(ga_far.at[block], g_buf.at[block], g_sem.at[p])

        e_ring = gather_steps(ring, e_buf, *e_scr, own=en_far)
        next(e_ring)
        own_entry = pltpu.make_async_copy(en_far, e_buf.at[ring.me], en_sem)
        own_entry.start()
        for e in range(experts_here):
            for c in weights(e):
                c.start()
            if e == 0:
                for p in range(count):
                    grads(p).start()

        places = corner.here * rows + lane_of((1, rows))
        first = ring.me * experts_here
        every = lax.broadcasted_iota(jnp.int32, (experts, rows), 0)
        local_rows = lax.broadcasted_iota(jnp.int32, (8, rows), 0)
        slot_rows = lax.broadcasted_iota(jnp.int32, (capacity, rows), 0)

        def gate(block, home):
            logits = nt(wr_ref[...], e_buf[block])
            member = lab_all[block, 0:1] == every
            for k in range(1, picks):
                member = member | (lab_all[block, k : k + 1] == every)
            masked = jnp.where(member, logits, -jnp.inf)
            raised = jnp.exp(masked - jnp.max(masked, axis=0, keepdims=True))
            shares = raised / jnp.sum(raised, axis=0, keepdims=True)
            if home:
                shares_ref[...] = shares
            kept = jnp.where(places < lab_all[block, picks : picks + 1], shares, 0.0)
            own = jnp.zeros((8, rows), F32)
            for e in range(experts_here):
                row = jnp.sum(jnp.where(every == first + e, kept, 0.0), axis=0, keepdims=True)
                own = jnp.where(local_rows == e, row, own)
            gates[block] = own

        def pick_rows(block, e):
            return slot_rows == slots_ref[block, pl.ds(e, 1), :]

        def gather_rows(block, e):
            found = pick_rows(block, e)
            chosen = jnp.where(found, 1.0, 0.0).astype(BF)
            gate_col = jnp.sum(jnp.where(found, gates[block, pl.ds(e, 1), :], 0.0), axis=1, keepdims=True)
            return found, nn(chosen, e_buf[block]).astype(BF), nn(chosen, g_buf[block]), gate_col

        def chain(numbers, e, result_rows, back_rows, row, await_weights=False):
            blocks = [ring.at(shifts[p]) for p in numbers]
            size = len(numbers) * capacity
            here = pl.ds(pl.multiple_of(row, capacity), size)
            span = pl.ds(numbers[0] * capacity, size)
            if await_weights:
                for c in weights(e):
                    c.wait()
            parts = [gather_rows(block, e) for block in blocks]
            entries = jnp.concatenate([p[1] for p in parts], axis=0)
            grad_rows = jnp.concatenate([p[2] for p in parts], axis=0)
            gate_col = jnp.concatenate([p[3] for p in parts], axis=0)
            slot_grad = (gate_col * grad_rows).astype(BF)
            pre = nn(entries, wgu[e])
            act_grad = nt(slot_grad, wd[e])
            gate_part = pre[:, :ffe]
            up_part = pre[:, ffe:]
            sig = jax.nn.sigmoid(gate_part)
            swish = gate_part * sig
            act = (swish * up_part).astype(BF)
            act_s[e, span] = act
            gate_grad = act_grad * up_part * sig * (1.0 + gate_part * (1.0 - sig))
            pre_grad = jnp.concatenate([gate_grad, act_grad * swish], axis=1).astype(BF)
            pg[e, span] = pre_grad
            result = nn(act, wd[e]).astype(BF).astype(F32)
            back_rows[here] = nt(pre_grad, wgu[e]).astype(BF)
            result_rows[here] = (gate_col * result).astype(BF)
            pick_col = jnp.sum(result * grad_rows, axis=1, keepdims=True)
            for i, block in enumerate(blocks):
                pick = jnp.sum(
                    jnp.where(parts[i][0], pick_col[i * capacity : (i + 1) * capacity], 0.0),
                    axis=0, keepdims=True,
                )
                pick_buf[block] = jnp.where(local_rows == e, pick, pick_buf[block])

        def combine(number, result_rows, back_rows, row_of):
            block = ring.at(shifts[number])
            chosen = jnp.concatenate(
                [jnp.where(pick_rows(block, e), 1.0, 0.0).astype(BF) for e in range(experts_here)], axis=0
            )
            windows = [pl.ds(row_of(e), capacity) for e in range(experts_here)]
            if number >= 2:
                results(number - 2).wait()
            c_slot[number % 2] = tn(chosen, jnp.concatenate([result_rows[w] for w in windows], axis=0)).astype(BF)
            results(number).start()
            b_buf[block] = tn(chosen, jnp.concatenate([back_rows[w] for w in windows], axis=0)).astype(BF)

        def tile(numbers, await_weights):
            size = len(numbers) * capacity
            for p in numbers:
                grads(p).wait()

            def one(e, carry):
                chain(numbers, e, x_s, s_s, e * size, await_weights)
                return carry

            lax.fori_loop(0, experts_here, one, 0)
            for i, number in enumerate(numbers):
                combine(number, x_s, s_s, lambda e: e * size + i * capacity)

        def results(number):
            return pltpu.make_async_copy(
                c_slot.at[number % 2], c_far.at[ring.at(shifts[number])], c_sem.at[number]
            )

        def put(row, size, got):
            ob_ref[pl.ds(row, size)] = got

        b_ring = scatter_steps(ring, b_buf, *held, put)
        pick_buf[...] = jnp.zeros_like(pick_buf)
        own_entry.wait()
        gate(ring.me, True)
        tile([0], True)
        for hop in range(1, hops - 1):
            next(e_ring)
            gate(ring.at(hop), False)
            gate(ring.at(-hop), False)
            tile([2 * hop - 1, 2 * hop], False)
        def weight_grads(e):
            for p in range(count):
                _, entries, grad_rows, gate_col = gather_rows(ring.at(shifts[p]), e)
                span = pl.ds(p * capacity, capacity)
                x_s[span] = entries
                s_s[span] = (gate_col * grad_rows).astype(BF)

            def columns(j, carry):
                cols = pl.ds(pl.multiple_of(j * 256, 256), 256)
                wgu[e, :, cols] = tn(x_s[...], pg[e, :, cols]).astype(BF)
                wd[e, :, cols] = tn(act_s[e], s_s[:, cols]).astype(BF)
                return carry

            lax.fori_loop(0, width // 256, columns, 0)

        def pieces(e, owner):
            return (
                (wgu.at[e, pl.ds(owner * quarter_up, quarter_up)], 0, quarter_up),
                (wd.at[e, pl.ds(owner * quarter_down, quarter_down)], quarter_up, quarter_down),
            )

        landing = lambda e: got_a.at[e] if e < 2 else wait_far.at[e - 2]
        fetch = lambda e: pltpu.make_async_copy(wait_far.at[e - 2], got_a.at[e % 2], f_sem.at[e - 2])

        def to_core(e):
            return [
                remote(src, landing(e).at[x, pl.ds(start, size)], a_send.at[e, x, k], a_recv.at[e, x, k], narrow=corner.core_peer)
                for x in range(2)
                for k, (src, start, size) in enumerate(pieces(e, 2 * x + 1 - corner.core))
            ]

        def to_chip(e):
            return [
                remote(src, got_far.at[e, pl.ds(start, size)], x_send.at[e, k], x_recv.at[e, k], narrow=corner.chip_peer)
                for k, (src, start, size) in enumerate(pieces(e, 2 * (1 - corner.chip) + corner.core))
            ]

        def own_out(e):
            return [
                pltpu.make_async_copy(src, keep_far.at[e, pl.ds(start, size)], o_sem.at[e, k])
                for k, (src, start, size) in enumerate(pieces(e, corner.here))
            ]

        def send_core(e):
            for c in to_core(e):
                c.start()

        def first_sum(e):
            for c in to_core(e):
                c.wait_recv()
            if e >= 2:
                fetch(e).start()
                fetch(e).wait()
            for number in range(2):
                x = 1 - corner.chip if number == 0 else corner.chip
                for src, start, size in pieces(e, 2 * x + corner.core):
                    block_add(src, src, got_a.at[e % 2, x, pl.ds(start, size)], size)
                for c in to_chip(e) if number == 0 else own_out(e):
                    c.start()

        last = [count - 3, count - 2, count - 1]
        row_at = lambda e, i: (e * 3 + i) * capacity
        next(e_ring)
        gate(ring.at(hops - 1), False)
        gate(ring.at(1 - hops), False)
        for p in last:
            grads(p).wait()

        def several(start, stop, numbers):
            def one(e, carry):
                chain(numbers, e, last_c, last_b, row_at(e, numbers[0] - last[0]))
                return carry

            lax.fori_loop(start, stop, one, 0)

        several(0, 2, last[:2])
        for _ in e_ring:
            pass
        gate(ring.at(hops), False)
        next(b_ring)
        chain(last[2:], 0, last_c, last_b, row_at(0, 2))
        weight_grads(0)
        send_core(0)
        chain(last[2:], 1, last_c, last_b, row_at(1, 2))
        several(2, experts_here, last[:2])
        first_sum(0)
        next(b_ring)
        weight_grads(1)
        send_core(1)
        several(2, experts_here, last[2:])
        first_sum(1)
        for i, number in enumerate(last):
            combine(number, last_c, last_b, lambda e: row_at(e, i))
        next(b_ring)
        pick_copy = lambda k, target: remote(
            pick_buf.at[target], op_ref.at[ring.me], p_send.at[k], p_recv.at[k], wide=target
        )
        for k, target in enumerate(others):
            pick_copy(k, target).start()
        op_ref[ring.me] = pick_buf[ring.me]
        for e in range(2, experts_here):
            weight_grads(e)
            send_core(e)
            next(b_ring)
            first_sum(e)
            next(b_ring, None)
        for _ in b_ring:
            pass
        for e in range(experts_here):
            for c in to_core(e):
                c.wait_send()
            for c in to_chip(e):
                c.wait()
            for c in own_out(e):
                c.wait()
        for number in range(max(0, count - 2), count):
            results(number).wait()
        for k, target in enumerate(others):
            sender = (ring.me - (k + 1) + count) % count
            remote(
                pick_buf.at[sender], op_ref.at[sender], p_send.at[k], p_recv.at[k], wide=target
            ).wait_recv()
            pick_copy(k, target).wait_send()

    vmem = pl.BlockSpec(memory_space=pltpu.VMEM)
    far = pl.BlockSpec(memory_space=pl.ANY)
    shape = jax.ShapeDtypeStruct
    out_shape = [
        shape((rows, width), F32),
        shape((count, 8, rows), F32),
        shape((count, rows, width), BF),
        shape((experts_here, quarter, width), BF),
        shape((experts_here, quarter, width), BF),
        shape((experts, rows), F32),
        shape((experts_here - 2, 2, quarter, width), BF),
    ]
    dma = pltpu.SemaphoreType.DMA
    scratch = [
        pltpu.VMEM(w_gate_up.shape, BF),
        pltpu.VMEM(w_down.shape, BF),
        pltpu.VMEM((count, rows, width), BF),
        pltpu.VMEM((count, rows, width), BF),
        pltpu.VMEM((experts_here, room, 2 * ffe), BF),
        pltpu.VMEM((experts_here, room, ffe), BF),
        pltpu.VMEM((room, width), BF),
        pltpu.VMEM((room, width), BF),
        pltpu.VMEM((count, rows, width), BF),
        pltpu.VMEM((2, rows, width), BF),
        pltpu.VMEM((2, 2, quarter, width), BF),
        pltpu.VMEM((count, 8, rows), F32),
        pltpu.VMEM((count, 8, rows), F32),
        pltpu.VMEM((3 * experts_here * capacity, width), BF),
        pltpu.VMEM((3 * experts_here * capacity, width), BF),
        *scatter_scratch(count, rows, width),
        *gather_scratch(count),
        dma((2, experts_here)), dma((count,)), dma((count,)),
        dma((count - 1,)), dma((count - 1,)),
        dma((experts_here, 2, 2)), dma((experts_here, 2, 2)),
        dma((experts_here, 2)), dma((experts_here, 2)), dma((experts_here, 2)), dma((experts_here - 2,)), dma,
    ]
    return pl.pallas_call(
        kernel,
        out_shape=out_shape,
        in_specs=[far, far, vmem, vmem, vmem, far, far],
        out_specs=[vmem, vmem, far, far, far, vmem, far],
        scratch_shapes=scratch,
        compiler_params=pltpu.CompilerParams(
            collective_id=cid, has_side_effects=True, vmem_limit_bytes=63 * 2**20
        ),
    )(entry, grad_all, labels_all, slots, router_turned, w_gate_up, w_down)


def tail_kernel(entry_home, pick_home, shares, router_turned, mixed, cotangent, hidden, length, attn_gain, moe_gain, w_query, w_key, w_value, w_out, queries, keys, values, context, whole, lse, cosine, sine, expert_part, kept, arrived, shapes, cid):
    count, rows, width = expert_part.shape
    seq = 4 * rows
    query_cols, key_cols = w_out.shape[0], w_key.shape[1]
    cols = query_cols + 2 * key_cols
    kv_here = key_cols // HEAD_DIM
    experts_all = router_turned.shape[0]
    small_rows = (experts_all + 2 + 15) // 16 * 16
    block = -(-(cols + query_cols + small_rows) // (32 * count)) * 32
    experts, quarter, _ = kept.shape
    up_shape, down_shape = shapes
    quarter_up, quarter_down = up_shape[1] // 4, down_shape[1] // 4
    base = [0, rows, 3 * rows, 6 * rows]
    small_at = cols + query_cols

    def kernel(*refs):
        refs = list(refs)
        take = lambda number: [refs.pop(0) for _ in range(number)]
        eh_ref, pick_ref, shares_ref, wr_ref, mixed_ref, cot_ref, h_ref, len_ref, g1_ref, g2_ref = take(10)
        wq_far, wk_far, wv_far, wout_ref, q_ref, k_ref, v_ref, ctx_ref, whole_ref, lse_ref, cos_ref, sin_ref = take(12)
        c_far, keep_far, got_far = take(3)
        out_ref, gh_ref, turned_ref, go_ref, small_ref, up_ref, down_ref = take(7)
        gw, mg_s, kd, vd, p_all, dp_scr, ds_scr, dctx, dk, dv, qg, packed, small_got, expert_sum, c_ref, sum_ref, own, got, wqkv_ref, wt_ref, gain_got = take(21)
        share, fold = take(2), take(9)
        c_sem, w_sem, o_sem = take(3)
        c_scr, s_scr, g_scr = take(3), take(3), take(2)
        sm_send, sm_recv, ga_send, ga_recv = take(4)
        c_send, c_recv, x_send, x_recv, f_send, f_recv, l_sem = take(7)
        ring, corner = Ring(count), Corner()
        greet(list(ring.peers), [corner.core_peer, corner.chip_peer, corner.far_peer])
        length_here = len_ref[0]

        own_loads = lambda e: [
            pltpu.make_async_copy(keep_far.at[e], own.at[e], o_sem.at[0, e]),
            pltpu.make_async_copy(got_far.at[e], got.at[e], o_sem.at[1, e]),
        ]
        w_loads = [
            pltpu.make_async_copy(src, wqkv_ref.at[:, pl.ds(start, size)], w_sem.at[k])
            for k, (src, start, size) in enumerate(
                ((wq_far, 0, query_cols), (wk_far, query_cols, key_cols), (wv_far, query_cols + key_cols, key_cols))
            )
        ]
        for c in w_loads:
            c.start()
        for e in range(experts):
            for c in own_loads(e):
                c.start()

        def own_sum(e):
            for c in own_loads(e):
                c.wait()
            block_add(own.at[e], own.at[e], got.at[e], quarter)
            send_out(e)
            for c in send(e, core_sems, corner.core_peer) + own_copy(e):
                c.start()

        def put(row, size, value):
            expert_sum[pl.ds(row, size)] = value

        c_load = pltpu.make_async_copy(c_far, c_ref, c_sem)
        c_load.start()
        c_ring = scatter_steps(ring, c_ref, *c_scr, put)

        def places(e, owner):
            mine = own.at[e]
            return (
                (mine.at[pl.ds(0, quarter_up)], up_ref.at[e, pl.ds(owner * quarter_up, quarter_up)]),
                (mine.at[pl.ds(quarter_up, quarter_down)], down_ref.at[e, pl.ds(owner * quarter_down, quarter_down)]),
            )

        def send(e, sems, peer):
            return [
                remote(src, dst, sems[0].at[e, k], sems[1].at[e, k], narrow=peer)
                for k, (src, dst) in enumerate(places(e, corner.here))
            ]

        def forward(e, owner, sems):
            return [
                remote(dst, dst, sems[0].at[e, k], sems[1].at[e, k], narrow=corner.core_peer)
                for k, (src, dst) in enumerate(places(e, owner))
            ]

        core_sems, chip_sems, far_sems = (c_send, c_recv), (x_send, x_recv), (f_send, f_recv)

        def own_copy(e):
            return [
                pltpu.make_async_copy(src, dst, l_sem.at[e, k])
                for k, (src, dst) in enumerate(places(e, corner.here))
            ]

        def send_out(e):
            for c in send(e, chip_sems, corner.chip_peer):
                c.start()

        def pass_on(e):
            for c in forward(e, corner.chip_peer, chip_sems):
                c.wait_recv()
            for c in forward(e, corner.chip_peer, far_sems):
                c.start()

        picked, held_shares = pick_ref[...], shares_ref[...]
        logit_grad = held_shares * (picked - jnp.sum(held_shares * picked, axis=0, keepdims=True))
        high = logit_grad.astype(BF)
        low = (logit_grad - high.astype(F32)).astype(BF)
        entry_grad = eh_ref[...] + (tn(high, wr_ref[...]) + tn(low, wr_ref[...]))
        mixed_here = mixed_ref[...]
        scale = lax.rsqrt(jnp.mean(mixed_here * mixed_here, axis=1, keepdims=True) + EPSILON)
        unit = mixed_here * scale
        inner = entry_grad * g2_ref[...]
        from_norm = scale * (inner - unit * jnp.mean(inner * unit, axis=1, keepdims=True))
        at = corner.here * rows + lax.broadcasted_iota(jnp.int32, (rows, 1), 0)
        valid = jnp.where(at < length_here, 1.0, 0.0)
        mixed_grad = valid * cot_ref[...].astype(F32) + from_norm
        mg_s[...] = mixed_grad
        gw[corner.here] = mixed_grad.astype(BF)
        sharing = Share(corner, gw, *share)
        sharing.start()
        entry = (unit * g2_ref[...]).astype(BF)
        small_got[3] = jnp.concatenate(
            [
                nn(high, entry) + nn(low, entry),
                jnp.sum(entry_grad * unit, axis=0, keepdims=True),
                jnp.zeros((small_rows - experts_all - 1, width), F32),
            ],
            axis=0,
        ).astype(BF)
        peers = (corner.core_peer, corner.chip_peer, corner.far_peer)
        small_copy = lambda k, peer: remote(
            small_got.at[3], small_got.at[k], sm_send.at[k], sm_recv.at[k], narrow=peer
        )
        for k, peer in enumerate(peers):
            small_copy(k, peer).start()

        for t in range(kv_here):
            kd[t] = doubled(k_ref[...].astype(F32), t).astype(BF)
            vd[t] = doubled(v_ref[...].astype(F32), t).astype(BF)

        def chances(b):
            for t in range(kv_here):
                lanes = slice(t * LANES, (t + 1) * LANES)
                stack = stacked(q_ref[pl.ds(b * rows, rows), lanes])
                log_sum = lse_ref[t * 4 + b : t * 4 + b + 1]
                for kb in range(b + 1):
                    scores = masked_scores(
                        kd[t, pl.ds(kb * rows, rows)], stack, kb * rows, b * rows, length_here, kb == b
                    )
                    p_all[t, pl.ds(base[b] + kb * rows, rows)] = jnp.exp(scores - log_sum).astype(BF)

        def pull(owner):
            dctx[owner] = nt(gw[owner], wout_ref[...]).astype(BF)

        pull(corner.here)
        c_load.wait()
        next(c_ring)
        chances(3)
        next(c_ring)
        sharing.wait_core()
        pull(corner.core_peer)
        chances(2)
        next(c_ring)
        chances(1)
        chances(0)
        sharing.wait_chip()
        own_sum(0)
        pull(corner.chip_peer)
        sharing.wait_far()
        pull(corner.far_peer)
        dk[...] = jnp.zeros_like(dk)
        dv[...] = jnp.zeros_like(dv)

        folding = Fold(corner, *fold)
        before = None
        for b in (3, 2, 1, 0):
            span = pl.ds(b * rows, rows)
            cos, sin = cos_ref[span], sin_ref[span]
            for t in range(kv_here):
                lanes = slice(t * LANES, (t + 1) * LANES)
                stack = stacked(q_ref[span, lanes])
                grad_stack = stacked(dctx[b, :, lanes])
                inner = None
                for kb in range(b + 1):
                    chance = p_all[t, pl.ds(base[b] + kb * rows, rows)]
                    grad = nt(vd[t, pl.ds(kb * rows, rows)], grad_stack)
                    dp_scr[pl.ds(kb * rows, rows)] = grad
                    one = jnp.sum(chance.astype(F32) * grad, axis=0, keepdims=True)
                    inner = one if inner is None else inner + one
                for kb in range(b + 1):
                    key_span = pl.ds(kb * rows, rows)
                    chance = p_all[t, pl.ds(base[b] + kb * rows, rows)]
                    score_grad = (chance.astype(F32) * (dp_scr[key_span] - inner)).astype(BF)
                    ds_scr[key_span] = score_grad
                    dk[t, key_span] += nn(score_grad, stack)
                    dv[t, key_span] += nn(chance, grad_stack)
                every = pl.ds(0, (b + 1) * rows)
                query_grad = unstacked(tn(kd[t, every], ds_scr[every])) * HEAD_DIM ** (-0.5)
                qg[span, lanes] = turn_lanes(query_grad, cos, -sin).astype(BF)
            low_lanes = lane_of((rows, LANES)) < HEAD_DIM
            both = lambda ref, t: ref[t, span] + pltpu.roll(ref[t, span], HEAD_DIM, 1)
            key_grad = jnp.where(low_lanes, both(dk, 0), both(dk, 1)) * HEAD_DIM ** (-0.5)
            qg[span, query_cols : query_cols + key_cols] = turn_lanes(key_grad, cos, -sin).astype(BF)
            qg[span, query_cols + key_cols :] = jnp.where(low_lanes, both(dv, 0), both(dv, 1)).astype(BF)
            if b == 3:
                for c in w_loads:
                    c.wait()
            folding.give(b, nt(qg[span], wqkv_ref[...]))
            if before is not None:
                folding.settle(before)
            before = b
            next(c_ring)
            if b == 2:
                own_sum(1)
        folding.settle(before)

        def store(row, value):
            for start in range(0, value.shape[0], 16):
                size = min(16, value.shape[0] - start)
                at_row = row + start
                packed[at_row // block, pl.ds(at_row % block, size)] = value[start : start + size].astype(BF)

        weight_grad = tn(qg[...], whole_ref[...])
        wt_ref[...] = wqkv_ref[...].astype(F32).T
        gain_one = jnp.sum(weight_grad * wt_ref[...], axis=0, keepdims=True) / g1_ref[...]
        store(0, weight_grad)
        store(cols, tn(ctx_ref[...], gw[...].reshape(seq, width)))
        rest = small_at + small_rows
        store(rest, jnp.zeros((count * block - rest, width), F32))
        for k, peer in enumerate(peers):
            small_copy(k, peer).wait_recv()
        small_sum = sum(small_got[k].astype(F32) for k in range(4))
        row_at = lax.broadcasted_iota(jnp.int32, (small_rows, width), 0)
        store(small_at, jnp.where(row_at == experts_all + 1, gain_one, small_sum))

        def finish(row, size, got):
            sum_ref[ring.me, pl.ds(row, size)] = got.astype(BF)

        sums = scatter_steps(ring, packed, *s_scr, finish)
        next(sums)
        own_sum(2)
        next(sums)
        normed_grad = folding.total()
        source = h_ref[...].astype(F32)
        scale = lax.rsqrt(jnp.mean(source * source, axis=1, keepdims=True) + EPSILON)
        unit = source * scale
        inner = normed_grad * g1_ref[...]
        from_norm = scale * (inner - unit * jnp.mean(inner * unit, axis=1, keepdims=True))
        gh_ref[...] = (mg_s[...] + from_norm).astype(BF)
        next(sums)
        pass_on(0)
        own_sum(3)
        for _ in c_ring:
            next(sums, None)
        out_ref[...] = (valid * (mixed_here + expert_sum[...])).astype(BF)
        for _ in sums:
            pass
        gathers = gather_steps(ring, sum_ref, *g_scr)
        next(gathers)
        pass_on(1)
        for _ in gathers:
            pass
        whole_sum = lambda row, size: jnp.concatenate(
            [sum_ref[b] for b in range(row // block, (row + size) // block)], axis=0
        )
        gain_got[3] = sum_ref[small_at // block, small_rows - 16 : small_rows]
        gain_copy = lambda k, peer: remote(
            gain_got.at[3], gain_got.at[k], ga_send.at[k], ga_recv.at[k], narrow=peer
        )
        for k, peer in enumerate(peers):
            gain_copy(k, peer).start()
        for row in range(0, cols, block):
            turned_ref[:, row : row + block] = sum_ref[row // block].astype(F32).T.astype(BF)
        go_ref[...] = whole_sum(cols, query_cols)
        for k, peer in enumerate(peers):
            gain_copy(k, peer).wait_recv()
        gain_sum = sum(gain_got[k].astype(F32) for k in range(4))
        small_ref[0 : small_rows - 16] = sum_ref[small_at // block, 0 : small_rows - 16]
        last_rows = small_rows - 16 + lax.broadcasted_iota(jnp.int32, (16, width), 0)
        small_ref[small_rows - 16 : small_rows] = jnp.where(
            last_rows == experts_all + 1, gain_sum, gain_got[3].astype(F32)
        ).astype(BF)
        for e in range(2, experts):
            pass_on(e)
        for k, peer in enumerate(peers):
            gain_copy(k, peer).wait_send()
        for k, peer in enumerate(peers):
            small_copy(k, peer).wait_send()
        for e in range(experts):
            for c in own_copy(e):
                c.wait()
            for c in send(e, chip_sems, corner.chip_peer) + send(e, core_sems, corner.core_peer):
                c.wait_send()
            for c in forward(e, corner.core_peer, core_sems):
                c.wait_recv()
            for c in forward(e, corner.chip_peer, far_sems):
                c.wait_send()
            for c in forward(e, corner.far_peer, far_sems):
                c.wait_recv()
        sharing.drain()
        folding.drain()

    vmem = pl.BlockSpec(memory_space=pltpu.VMEM)
    far = pl.BlockSpec(memory_space=pl.ANY)
    shape = jax.ShapeDtypeStruct
    out_shape = [
        shape((rows, width), BF),
        shape((rows, width), BF),
        shape((width, cols), BF),
        shape((query_cols, width), BF),
        shape((small_rows, width), BF),
        shape(up_shape, BF),
        shape(down_shape, BF),
    ]
    scratch = [
        pltpu.VMEM((4, rows, width), BF),
        pltpu.VMEM((rows, width), F32),
        pltpu.VMEM((kv_here, seq, LANES), BF),
        pltpu.VMEM((kv_here, seq, LANES), BF),
        pltpu.VMEM((kv_here, 10 * rows, 2 * rows), BF),
        pltpu.VMEM((seq, 2 * rows), F32),
        pltpu.VMEM((seq, 2 * rows), BF),
        pltpu.VMEM((4, rows, query_cols), BF),
        pltpu.VMEM((kv_here, seq, LANES), F32),
        pltpu.VMEM((kv_here, seq, LANES), F32),
        pltpu.VMEM((seq, cols), BF),
        pltpu.VMEM((count, block, width), BF),
        pltpu.VMEM((4, small_rows, width), BF),
        pltpu.VMEM((rows, width), F32),
        pltpu.VMEM((count, rows, width), BF),
        pltpu.VMEM((count, block, width), BF),
        pltpu.VMEM((experts, quarter, width), BF),
        pltpu.VMEM((experts, quarter, width), BF),
        pltpu.VMEM((width, cols), BF),
        pltpu.VMEM((cols, width), F32),
        pltpu.VMEM((4, 16, width), BF),
        *Share.scratch(),
        *Fold.scratch(rows, width),
        pltpu.SemaphoreType.DMA,
        pltpu.SemaphoreType.DMA((3,)),
        pltpu.SemaphoreType.DMA((2, experts)),
        *scatter_scratch(count, rows, width),
        *scatter_scratch(count, block, width),
        *gather_scratch(count),
        *[pltpu.SemaphoreType.DMA((3,))] * 4,
    ] + [pltpu.SemaphoreType.DMA((experts, 2))] * 7
    return pl.pallas_call(
        kernel,
        out_shape=out_shape,
        in_specs=[vmem] * 7 + [pl.BlockSpec(memory_space=pltpu.SMEM)] + [vmem] * 2 + [far] * 3 + [vmem] * 9 + [far] * 3,
        out_specs=[vmem] * 5 + [far] * 2,
        scratch_shapes=scratch,
        compiler_params=pltpu.CompilerParams(
            collective_id=cid, has_side_effects=True, vmem_limit_bytes=62 * 2**20
        ),
    )(entry_home, pick_home, shares, router_turned, mixed, cotangent, hidden, length, attn_gain, moe_gain,
      w_query, w_key, w_value, w_out, queries, keys, values, context, whole, lse, cosine, sine, expert_part, kept, arrived)


def final_kernel(out, grad_hidden, turned, out_grad, small, up_grad, down_grad, query_cols, key_cols, experts):
    here, width, ffe2 = up_grad.shape
    ffe = down_grad.shape[1]
    step = 256
    parts = [(0, e, r) for e in range(here) for r in range(0, width, step)]
    parts += [(1, e, r) for e in range(here) for r in range(0, ffe, step)]
    parts.sort(key=lambda p: (p[1], p[0], p[2]))

    def kernel(o_in, gh_in, t_in, go_in, s_in, up_in, down_in, o_ref, gh_ref, gq, gk, gv, go, g1, g2, gr, up_ref, down_ref, low, full, in_sem, out_sem):
        near = lambda i: (up_in, down_in)[parts[i][0]].at[parts[i][1], pl.ds(parts[i][2], step)]
        away = lambda i: (up_ref, down_ref)[parts[i][0]].at[parts[i][1], pl.ds(parts[i][2], step)]
        inward = lambda i: pltpu.make_async_copy(near(i), low.at[i], in_sem.at[i])
        outward = lambda i: pltpu.make_async_copy(full.at[i], away(i), out_sem.at[i])
        for i in range(len(parts)):
            inward(i).start()
        o_ref[...] = o_in[...]
        gh_ref[...] = gh_in[...]
        gq[...] = t_in[:, :query_cols].astype(F32)
        gk[...] = t_in[:, query_cols : query_cols + key_cols].astype(F32)
        gv[...] = t_in[:, query_cols + key_cols :].astype(F32)
        go[...] = go_in[...].astype(F32)
        rows = s_in[...].astype(F32)
        g1[...] = rows[experts + 1 : experts + 2]
        g2[...] = rows[experts : experts + 1]
        gr[...] = rows[:experts]
        for i in range(len(parts)):
            inward(i).wait()
            full[i] = low[i].astype(F32)
            outward(i).start()
        for i in range(len(parts)):
            outward(i).wait()

    shape = jax.ShapeDtypeStruct
    vmem = pl.BlockSpec(memory_space=pltpu.VMEM)
    far = pl.BlockSpec(memory_space=pl.ANY)
    small_shapes = [
        shape(out.shape, BF), shape(grad_hidden.shape, BF), shape((width, query_cols), F32),
        shape((width, key_cols), F32), shape((width, key_cols), F32), shape(out_grad.shape, F32),
        shape((1, width), F32), shape((1, width), F32), shape((experts, width), F32),
    ]
    return pl.pallas_call(
        kernel,
        out_shape=small_shapes + [shape(up_grad.shape, F32), shape(down_grad.shape, F32)],
        in_specs=[vmem] * 5 + [far] * 2,
        out_specs=[vmem] * 9 + [far] * 2,
        scratch_shapes=[
            pltpu.VMEM((len(parts), step, width), BF),
            pltpu.VMEM((len(parts), step, width), F32),
            pltpu.SemaphoreType.DMA((len(parts),)),
            pltpu.SemaphoreType.DMA((len(parts),)),
        ],
        compiler_params=pltpu.CompilerParams(vmem_limit_bytes=62 * 2**20),
    )(out, grad_hidden, turned, out_grad, small, up_grad, down_grad)


def turn_tables(count, head_dim):
    inverse = THETA ** (-np.arange(head_dim // 2, dtype=np.float32) * np.float32(2.0 / head_dim))
    angles = np.arange(count, dtype=np.float32)[:, None] * inverse.astype(np.float32)[None, :]
    cosine, sine = np.cos(angles), np.sin(angles)
    return (
        jnp.asarray(np.concatenate([cosine] * 4, axis=1), F32),
        jnp.asarray(np.concatenate([-sine, sine] * 2, axis=1), F32),
    )


def local_general(
    hidden,
    lengths,
    routes,
    cotangent,
    attn_gain,
    w_query,
    w_key,
    w_value,
    w_out,
    moe_gain,
    w_router,
    w_gate_up,
    w_down,
):
    rows_here = hidden.shape[1]
    width = hidden.shape[2]
    seq_len = rows_here * lax.axis_size("narrow")
    head_dim = HEAD_DIM
    group_size = HEADS // KV_HEADS
    kv_here = w_key.shape[1] // head_dim
    query_cols = kv_here * group_size * head_dim
    key_cols = kv_here * head_dim
    scaling = head_dim ** (-0.5)
    block_rows = min(512, seq_len)
    block_count = seq_len // block_rows
    length_here = lengths[0]
    offset = lax.axis_index("narrow") * rows_here
    local_places = offset + jnp.arange(rows_here, dtype=jnp.int32)
    valid = (local_places < length_here).astype(jnp.float32)[:, None]
    source = hidden[0].astype(jnp.float32)
    normed, scale_one = norm_forward(source, attn_gain)
    normed_low = normed.astype(jnp.bfloat16)
    whole = lax.all_gather(normed_low, "narrow", axis=0, tiled=True)
    w_qkv = jnp.concatenate([w_query, w_key, w_value], axis=1)
    projected = jnp.dot(whole, w_qkv, preferred_element_type=jnp.float32)
    cosine, sine_part = rope_tables(seq_len, head_dim)
    query_rot = turn(
        projected[:, :query_cols].reshape(seq_len, kv_here, group_size, head_dim),
        cosine,
        sine_part,
        1.0,
    )
    key_rot = turn(
        projected[:, query_cols : query_cols + key_cols].reshape(seq_len, kv_here, head_dim),
        cosine,
        sine_part,
        1.0,
    )
    queries = (
        query_rot.astype(jnp.bfloat16)
        .reshape(block_count, block_rows, kv_here, group_size, head_dim)
        .transpose(0, 2, 3, 1, 4)
    )
    keys_low = key_rot.astype(jnp.bfloat16).transpose(1, 0, 2)
    values_low = (
        projected[:, query_cols + key_cols :]
        .astype(jnp.bfloat16)
        .reshape(seq_len, kv_here, head_dim)
        .transpose(1, 0, 2)
    )
    context, log_sums = attend_forward(queries, keys_low, values_low, length_here, scaling)
    context_rows = context.transpose(0, 3, 1, 2, 4).reshape(seq_len, query_cols)
    piece = context_rows
    attn_part = lax.psum_scatter(
        jnp.dot(piece, w_out, preferred_element_type=jnp.float32).astype(jnp.bfloat16),
        "narrow",
        scatter_dimension=0,
        tiled=True,
    ).astype(jnp.float32)
    mixed = source + attn_part
    normed_two, scale_two = norm_forward(mixed, moe_gain)
    entry = normed_two.astype(jnp.bfloat16)
    logits = jnp.dot(entry, w_router, preferred_element_type=jnp.float32)
    route_here = routes[0]
    tokens_here, picks = route_here.shape
    expert_total = w_router.shape[1]
    capacity = 2 * tokens_here * picks // expert_total
    member = (
        route_here[:, :, None] == jnp.arange(expert_total, dtype=jnp.int32)[None, None, :]
    ).astype(jnp.int32)
    flat_member = member.reshape(tokens_here * picks, expert_total)
    earlier = jnp.cumsum(flat_member, axis=0) - flat_member
    slot_index = jnp.sum(earlier * flat_member, axis=1)
    places = route_here.reshape(-1) * capacity + slot_index
    member_float = member.astype(jnp.float32)
    chosen = jnp.einsum("tke,te->tk", member_float, logits, precision=HIGHEST)
    highest = jnp.max(chosen, axis=-1, keepdims=True)
    raised = jnp.exp(chosen - highest)
    shares = raised / jnp.sum(raised, axis=-1, keepdims=True)
    gates = shares * valid
    outgoing = (
        jnp.zeros((expert_total * capacity, width), jnp.bfloat16)
        .at[places]
        .set(jnp.repeat(entry, picks, axis=0))
    )
    received = lax.all_to_all(
        outgoing.reshape(expert_total, capacity, width),
        "wide",
        split_axis=0,
        concat_axis=1,
        tiled=True,
    )
    expert_pre = jnp.einsum("erd,edf->erf", received, w_gate_up, preferred_element_type=jnp.float32)
    ffe_width = w_down.shape[1]
    gate_part = expert_pre[..., :ffe_width]
    up_part = expert_pre[..., ffe_width:]
    sigmoid_gate = jax.nn.sigmoid(gate_part)
    swish = gate_part * sigmoid_gate
    act_low = (swish * up_part).astype(jnp.bfloat16)
    expert_result = jnp.einsum(
        "erf,efd->erd", act_low, w_down, preferred_element_type=jnp.float32
    ).astype(jnp.bfloat16)
    returned = lax.all_to_all(expert_result, "wide", split_axis=1, concat_axis=0, tiled=True)
    picked = returned.reshape(expert_total * capacity, width)[places].reshape(
        tokens_here, picks, width
    )
    expert_sum = jnp.einsum("tk,tkd->td", gates, picked, precision=HIGHEST)
    output_rows = (valid * (mixed + expert_sum)).astype(jnp.bfloat16)
    grad_rows_here = cotangent[0].astype(jnp.float32) * valid
    slot_grad = (gates[:, :, None] * grad_rows_here[:, None, :]).astype(jnp.bfloat16)
    grad_outgoing = (
        jnp.zeros((expert_total * capacity, width), jnp.bfloat16)
        .at[places]
        .set(slot_grad.reshape(tokens_here * picks, width))
    )
    grad_received = lax.all_to_all(
        grad_outgoing.reshape(expert_total, capacity, width),
        "wide",
        split_axis=0,
        concat_axis=1,
        tiled=True,
    )
    act_grad = jnp.einsum("erd,efd->erf", grad_received, w_down, preferred_element_type=jnp.float32)
    down_grad = jnp.einsum(
        "erf,erd->efd", act_low, grad_received, preferred_element_type=jnp.float32
    )
    gate_grad = act_grad * up_part * sigmoid_gate * (1.0 + gate_part * (1.0 - sigmoid_gate))
    pre_grad = jnp.concatenate([gate_grad, act_grad * swish], axis=-1).astype(jnp.bfloat16)
    gate_up_grad = jnp.einsum(
        "erd,erf->edf", received, pre_grad, preferred_element_type=jnp.float32
    )
    entry_back = jnp.einsum(
        "erf,edf->erd", pre_grad, w_gate_up, preferred_element_type=jnp.float32
    ).astype(jnp.bfloat16)
    entry_home = lax.all_to_all(entry_back, "wide", split_axis=1, concat_axis=0, tiled=True)
    entry_rows = entry_home.reshape(expert_total * capacity, width)[places].reshape(
        tokens_here, picks, width
    )
    entry_grad = jnp.sum(entry_rows, axis=1, dtype=jnp.float32)
    pick_grad = jnp.einsum("td,tkd->tk", grad_rows_here, picked, precision=HIGHEST) * valid
    chosen_grad = shares * (pick_grad - jnp.sum(shares * pick_grad, axis=-1, keepdims=True))
    logit_grad = jnp.einsum("tk,tke->te", chosen_grad, member_float, precision=HIGHEST)
    router_grad = lax.dot_general(
        entry.astype(jnp.float32), logit_grad, (((0,), (0,)), ((), ())), precision=HIGHEST
    )
    entry_grad = entry_grad + lax.dot_general(
        logit_grad, w_router.astype(jnp.float32), (((1,), (1,)), ((), ())), precision=HIGHEST
    )
    mixed_from_norm, gain_two_grad = norm_backward(mixed, scale_two, moe_gain, entry_grad)
    mixed_grad = grad_rows_here + mixed_from_norm
    attn_grad_low = mixed_grad.astype(jnp.bfloat16)
    grad_whole = lax.all_gather(attn_grad_low, "narrow", axis=0, tiled=True)
    context_grad = lax.dot_general(
        grad_whole, w_out, (((1,), (1,)), ((), ())), preferred_element_type=jnp.float32
    ).astype(jnp.bfloat16)
    out_grad = lax.dot_general(
        context_rows, grad_whole, (((0,), (0,)), ((), ())), preferred_element_type=jnp.float32
    )
    context_blocks = context_grad.reshape(
        block_count, block_rows, kv_here, group_size, head_dim
    ).transpose(0, 2, 3, 1, 4)
    query_grad, key_grad, value_grad = attend_backward(
        queries, keys_low, values_low, context_blocks, log_sums, length_here, scaling
    )
    query_rows = turn(
        query_grad.transpose(0, 3, 1, 2, 4).reshape(seq_len, kv_here, group_size, head_dim),
        cosine,
        sine_part,
        -1.0,
    )
    key_rows = turn(key_grad.transpose(1, 0, 2), cosine, sine_part, -1.0)
    value_rows = value_grad.transpose(1, 0, 2)
    qkv_grad = jnp.concatenate(
        [
            query_rows.reshape(seq_len, query_cols),
            key_rows.reshape(seq_len, key_cols),
            value_rows.reshape(seq_len, key_cols),
        ],
        axis=1,
    ).astype(jnp.bfloat16)
    qkv_weight_grad = lax.dot_general(
        whole, qkv_grad, (((0,), (0,)), ((), ())), preferred_element_type=jnp.float32
    )
    piece = qkv_grad
    normed_grad = lax.psum_scatter(
        lax.dot_general(
            piece, w_qkv, (((1,), (1,)), ((), ())), preferred_element_type=jnp.float32
        ).astype(jnp.bfloat16),
        "narrow",
        scatter_dimension=0,
        tiled=True,
    ).astype(jnp.float32)
    source_from_norm, gain_one_grad = norm_backward(source, scale_one, attn_gain, normed_grad)
    grad_input = (mixed_grad + source_from_norm).astype(jnp.bfloat16)
    gate_up_grad, down_grad, router_grad, gain_one_grad, gain_two_grad = (
        lax.psum(gate_up_grad.astype(jnp.bfloat16), "narrow").astype(jnp.float32),
        lax.psum(down_grad.astype(jnp.bfloat16), "narrow").astype(jnp.float32),
        lax.psum(router_grad.astype(jnp.bfloat16), "narrow").astype(jnp.float32),
        lax.psum(gain_one_grad.astype(jnp.bfloat16), "narrow").astype(jnp.float32),
        lax.psum(gain_two_grad.astype(jnp.bfloat16), "narrow").astype(jnp.float32),
    )
    qkv_weight_grad, out_grad, router_grad, gain_one_grad, gain_two_grad = (
        lax.psum(qkv_weight_grad.astype(jnp.bfloat16), "wide").astype(jnp.float32),
        lax.psum(out_grad.astype(jnp.bfloat16), "wide").astype(jnp.float32),
        lax.psum(router_grad.astype(jnp.bfloat16), "wide").astype(jnp.float32),
        lax.psum(gain_one_grad.astype(jnp.bfloat16), "wide").astype(jnp.float32),
        lax.psum(gain_two_grad.astype(jnp.bfloat16), "wide").astype(jnp.float32),
    )
    query_weight_grad = qkv_weight_grad[:, :query_cols]
    key_weight_grad = qkv_weight_grad[:, query_cols : query_cols + key_cols]
    value_weight_grad = qkv_weight_grad[:, query_cols + key_cols :]
    return (
        output_rows[None],
        grad_input[None],
        gain_one_grad,
        query_weight_grad,
        key_weight_grad,
        value_weight_grad,
        out_grad,
        gain_two_grad,
        router_grad,
        gate_up_grad,
        down_grad,
    )


def local(
    hidden,
    lengths,
    routes,
    cotangent,
    attn_gain,
    w_query,
    w_key,
    w_value,
    w_out,
    moe_gain,
    w_router,
    w_gate_up,
    w_down,
):
    kv_here = w_key.shape[1] // HEAD_DIM
    rows, width = hidden.shape[1:]
    if lax.axis_size("narrow") != 4 or kv_here != 2 or rows != 256:
        return local_general(
            hidden, lengths, routes, cotangent, attn_gain, w_query, w_key, w_value, w_out,
            moe_gain, w_router, w_gate_up, w_down,
        )
    count = lax.axis_size("wide")
    picks = routes.shape[2]
    expert_total = w_router.shape[1]
    expert_here = w_gate_up.shape[0]
    capacity = 2 * rows * picks // expert_total
    query_cols, key_cols = w_query.shape[1], w_key.shape[1]
    cosine, sine = turn_tables(4 * rows, HEAD_DIM)
    router_turned = w_router.T
    gain_one, gain_two = attn_gain[None], moe_gain[None]
    entry, grad_all, whole, queries, keys, values, context, lse, mixed, slots, labels_all = front_kernel(
        hidden[0], cotangent[0], routes[0], lengths, gain_one, w_query, w_key, w_value, w_out, gain_two,
        cosine, sine, count, expert_here, 1,
    )
    entry_home, pick_home, expert_part, kept, arrived, shares, _ = middle_kernel(
        entry, grad_all, labels_all, slots, router_turned, w_gate_up, w_down, capacity, picks, 2
    )
    results = tail_kernel(
        entry_home, pick_home[:, :expert_here].reshape(expert_total, rows), shares, router_turned, mixed,
        cotangent[0], hidden[0], lengths, gain_one, gain_two, w_query, w_key, w_value, w_out, queries, keys,
        values, context, whole.reshape(4 * rows, width), lse, cosine, sine, expert_part, kept, arrived,
        (w_gate_up.shape, w_down.shape), 3,
    )
    out, grad_hidden, grad_q, grad_k, grad_v, grad_out, grad_one, grad_two, grad_router, grad_up, grad_down = final_kernel(
        *results, query_cols, key_cols, expert_total
    )
    return (
        out[None], grad_hidden[None], grad_one[0], grad_q, grad_k, grad_v, grad_out, grad_two[0], grad_router.T,
        grad_up, grad_down,
    )


def solution(mesh):
    in_specs = (
        P("wide", "narrow", None),
        P("wide"),
        P("wide", "narrow", None),
        P("wide", "narrow", None),
        P(),
        P(None, "narrow"),
        P(None, "narrow"),
        P(None, "narrow"),
        P("narrow", None),
        P(),
        P(),
        P("wide", None, None),
        P("wide", None, None),
    )
    out_specs = (
        P("wide", "narrow", None),
        P("wide", "narrow", None),
        P(),
        P(None, "narrow"),
        P(None, "narrow"),
        P(None, "narrow"),
        P("narrow", None),
        P(),
        P(),
        P("wide", None, None),
        P("wide", None, None),
    )
    return jax.shard_map(local, mesh=mesh, in_specs=in_specs, out_specs=out_specs, check_vma=False)
```

```python
import jax
import numpy as np
import jax.numpy as jnp
from jax import lax
from jax.experimental import pallas as pl
from jax.experimental.pallas import tpu as pltpu
from jax.sharding import PartitionSpec as P

HEADS = 16
KV_HEADS = 8
HEAD_DIM = 64
BF = jnp.bfloat16
F32 = jnp.float32
MESH = pl.DeviceIdType.MESH
EPSILON = 1e-06
THETA = 10000.0
HIGHEST = lax.Precision.HIGHEST


def rope_tables(count, head_dim):
    half_dim = head_dim // 2
    inverse = THETA ** (-jnp.arange(half_dim, dtype=jnp.float32) * 2.0 / head_dim)
    angles = jnp.arange(count, dtype=jnp.float32)[:, None] * inverse[None, :]
    return (jnp.cos(angles), jnp.sin(angles))


def turn(values, cosine, sine_part, direction):
    half_dim = values.shape[-1] // 2
    shape_here = (cosine.shape[0],) + (1,) * (values.ndim - 2) + (half_dim,)
    cosine = cosine.reshape(shape_here)
    sine_part = direction * sine_part.reshape(shape_here)
    first = values[..., :half_dim]
    second = values[..., half_dim:]
    return jnp.concatenate(
        [first * cosine - second * sine_part, second * cosine + first * sine_part], axis=-1
    )


def norm_forward(values, gain):
    scaling = lax.rsqrt(jnp.mean(values * values, axis=-1, keepdims=True) + EPSILON)
    return (values * scaling * gain, scaling)


def norm_backward(values, scaling, gain, incoming):
    unit_values = values * scaling
    gain_grad = jnp.sum(incoming * unit_values, axis=0)
    inner = incoming * gain
    input_grad = scaling * (
        inner - unit_values * jnp.mean(inner * unit_values, axis=-1, keepdims=True)
    )
    return (input_grad, gain_grad)


def visible(start, block_rows, key_places, length_here):
    query_places = start + jnp.arange(block_rows, dtype=jnp.int32)
    return (key_places[None, :] <= query_places[:, None]) & (key_places[None, :] < length_here)


def attend_forward(queries, keys_low, values_low, length_here, scaling):
    key_places = jnp.arange(keys_low.shape[1], dtype=jnp.int32)
    block_rows = queries.shape[3]

    def one_block(inputs):
        query_block, start = inputs
        scores = (
            jnp.einsum("kgqd,ksd->kgqs", query_block, keys_low, preferred_element_type=jnp.float32)
            * scaling
        )
        scores = jnp.where(visible(start, block_rows, key_places, length_here), scores, -1e30)
        highest = jnp.max(scores, axis=-1, keepdims=True)
        weights = jnp.exp(scores - highest)
        totals = jnp.sum(weights, axis=-1, keepdims=True)
        chances = (weights / totals).astype(jnp.bfloat16)
        context = jnp.einsum(
            "kgqs,ksd->kgqd", chances, values_low, preferred_element_type=jnp.float32
        )
        return (context.astype(jnp.bfloat16), (highest + jnp.log(totals))[..., 0])

    starts = jnp.arange(queries.shape[0], dtype=jnp.int32) * block_rows
    return lax.map(one_block, (queries, starts))


def attend_backward(queries, keys_low, values_low, context_grad, log_sums, length_here, scaling):
    key_places = jnp.arange(keys_low.shape[1], dtype=jnp.int32)
    block_rows = queries.shape[3]

    def one_block(carry, inputs):
        key_grad, value_grad = carry
        query_block, grad_block, sum_block, start = inputs
        scores = (
            jnp.einsum("kgqd,ksd->kgqs", query_block, keys_low, preferred_element_type=jnp.float32)
            * scaling
        )
        allowed = visible(start, block_rows, key_places, length_here)
        scores = jnp.where(allowed, scores, -1e30)
        chances = jnp.where(allowed, jnp.exp(scores - sum_block[..., None]), 0.0)
        chance_grad = jnp.einsum(
            "kgqd,ksd->kgqs", grad_block, values_low, preferred_element_type=jnp.float32
        )
        inner = jnp.sum(chances * chance_grad, axis=-1, keepdims=True)
        score_grad = (chances * (chance_grad - inner)).astype(jnp.bfloat16)
        query_grad = (
            jnp.einsum("kgqs,ksd->kgqd", score_grad, keys_low, preferred_element_type=jnp.float32)
            * scaling
        )
        key_grad = (
            key_grad
            + jnp.einsum(
                "kgqs,kgqd->ksd", score_grad, query_block, preferred_element_type=jnp.float32
            )
            * scaling
        )
        value_grad = value_grad + jnp.einsum(
            "kgqs,kgqd->ksd",
            chances.astype(jnp.bfloat16),
            grad_block,
            preferred_element_type=jnp.float32,
        )
        return ((key_grad, value_grad), query_grad)

    starts = jnp.arange(queries.shape[0], dtype=jnp.int32) * block_rows
    zeros = jnp.zeros(keys_low.shape, jnp.float32)
    (key_grad, value_grad), query_grad = lax.scan(
        one_block, (zeros, zeros), (queries, context_grad, log_sums, starts)
    )
    return (query_grad, key_grad, value_grad)


def ring_place(index, count):
    half = index // 2
    odd = index % 2
    return (1 - odd) * half + odd * (count - 1 - half)

def ring_index(place, count):
    odd = place // (count // 2)
    half = (1 - odd) * place + odd * (count - 1 - place)
    return 2 * half + odd


def add_low(one, two):
    return (one.astype(F32) + two.astype(F32)).astype(BF)

class Ring:
    def __init__(self, count):
        self.count = count
        self.me = lax.axis_index("wide")
        self.place = ring_place(self.me, count)
        self.peers = (self.at(1), self.at(-1))

    def at(self, shift):
        return ring_index((self.place + shift + 2 * self.count) % self.count, self.count)

def greet(wide_peers, narrow_peers):
    barrier = pltpu.get_barrier_semaphore()
    for peer in wide_peers:
        pl.semaphore_signal(barrier, inc=1, device_id={"wide": peer}, device_id_type=MESH)
    for peer in narrow_peers:
        pl.semaphore_signal(barrier, inc=1, device_id={"narrow": peer}, device_id_type=MESH)
    pl.semaphore_wait(barrier, len(wide_peers) + len(narrow_peers))

def remote(source, target, send, recv, **device):
    return pltpu.make_async_remote_copy(
        src_ref=source, dst_ref=target, send_sem=send, recv_sem=recv,
        device_id=device, device_id_type=MESH,
    )

def cuts(rows):
    first = (rows // 2 + 15) // 16 * 16
    return ((0, first), (first, rows - first))

def scatter_steps(ring, p_ref, held, send_sem, recv_sem, finish):
    count = ring.count
    lane = p_ref.shape[1] // 2

    def copy(way, step, k):
        sign = 1 if way == 0 else -1
        start, size = cuts(lane)[k]
        src = (
            p_ref.at[ring.at(-sign), pl.ds(way * lane + start, size)]
            if step == 0
            else held.at[way, step - 1, pl.ds(start, size)]
        )
        return remote(
            src, held.at[way, step, pl.ds(start, size)],
            send_sem.at[way, step, k], recv_sem.at[way, step, k], wide=ring.peers[way],
        )

    for step in range(count - 1):
        for k in range(2):
            for way in range(2):
                sign = 1 if way == 0 else -1
                start, size = cuts(lane)[k]
                if step > 0:
                    copy(way, step - 1, k).wait_recv()
                    span = pl.ds(start, size)
                    mine = p_ref[ring.at(-sign * (1 + step)), pl.ds(way * lane + start, size)]
                    held[way, step - 1, span] = add_low(held[way, step - 1, span], mine)
                copy(way, step, k).start()
        yield
    for k in range(2):
        for way in range(2):
            start, size = cuts(lane)[k]
            copy(way, count - 2, k).wait_recv()
            row = way * lane + start
            finish(
                row, size,
                held[way, count - 2, pl.ds(start, size)].astype(F32)
                + p_ref[ring.me, pl.ds(row, size)].astype(F32),
            )
    for step in range(count - 1):
        for k in range(2):
            for way in range(2):
                copy(way, step, k).wait_send()
    yield

def gather_steps(ring, o_ref, send_sem, recv_sem, own=None, left=0):
    count = ring.count
    hops = count // 2
    rows = o_ref.shape[1]
    live = lambda way, hop, k: hop < hops - 1 or k == way

    def copy(way, hop, k, shift):
        sign = 1 if way == 0 else -1
        start, size = cuts(rows)[k]
        block = o_ref.at[ring.at(-sign * (hop + shift)), pl.ds(start, size)]
        from_own = own is not None and hop == 0 and shift == 0
        return remote(
            own.at[pl.ds(start, size)] if from_own else block, block, send_sem.at[way, hop, k], recv_sem.at[way, hop, k], wide=ring.peers[way]
        )

    for hop in range(hops - left):
        for k in range(2):
            for way in range(2):
                if hop > 0:
                    copy(way, hop - 1, k, 1).wait_recv()
                if live(way, hop, k):
                    copy(way, hop, k, 0).start()
        yield
    for k in range(2):
        for way in range(2):
            if live(way, hops - left - 1, k):
                copy(way, hops - left - 1, k, 1).wait_recv()
    for hop in range(hops - left):
        for k in range(2):
            for way in range(2):
                if live(way, hop, k):
                    copy(way, hop, k, 0).wait_send()
    yield

def scatter_scratch(count, rows, cols):
    return [
        pltpu.VMEM((2, count - 1, rows // 2, cols), BF),
        pltpu.SemaphoreType.DMA((2, count - 1, 2)),
        pltpu.SemaphoreType.DMA((2, count - 1, 2)),
    ]

def gather_scratch(count):
    return [pltpu.SemaphoreType.DMA((2, count // 2, 2)), pltpu.SemaphoreType.DMA((2, count // 2, 2))]

def run(*makers):
    live = list(makers)
    while live:
        for one in list(live):
            if next(one, "end") == "end":
                live.remove(one)

def block_add(out, one, two, rows):
    def step(i, carry):
        span = pl.ds(pl.multiple_of(i * 128, 128), 128)
        out[span] = add_low(one[span], two[span])
        return carry
    lax.fori_loop(0, rows // 128, step, 0)


def nt(a, b):
    return lax.dot_general(a, b, (((1,), (1,)), ((), ())), preferred_element_type=F32)

def tn(a, b):
    return lax.dot_general(a, b, (((0,), (0,)), ((), ())), preferred_element_type=F32)

def nn(a, b):
    return jnp.dot(a, b, preferred_element_type=F32)

LANES = 128

def lane_of(shape):
    return lax.broadcasted_iota(jnp.int32, shape, len(shape) - 1)

def turn_lanes(values, cosine, signed_sine):
    low = lane_of(values.shape) % HEAD_DIM < HEAD_DIM // 2
    swapped = jnp.where(
        low,
        pltpu.roll(values, LANES - HEAD_DIM // 2, 1),
        pltpu.roll(values, HEAD_DIM // 2, 1),
    )
    return values * cosine + swapped * signed_sine

def doubled(tile, head):
    other = pltpu.roll(tile, HEAD_DIM, 1)
    low = lane_of(tile.shape) < HEAD_DIM
    return jnp.where(low, tile, other) if head == 0 else jnp.where(low, other, tile)

def stacked(tile):
    low = lane_of(tile.shape) < HEAD_DIM
    zero = jnp.zeros_like(tile)
    return jnp.concatenate([jnp.where(low, tile, zero), jnp.where(low, zero, tile)], axis=0)

def unstacked(turned):
    full = turned.T
    rows = full.shape[0] // 2
    return jnp.where(lane_of((rows, LANES)) < HEAD_DIM, full[:rows], full[rows:])

def masked_scores(keys, queries, key_start, query_start, length, causal):
    scores = nt(keys, queries) * HEAD_DIM ** (-0.5)
    half = queries.shape[0] // 2
    key_at = key_start + lax.broadcasted_iota(jnp.int32, scores.shape, 0)
    allowed = key_at < length
    if causal:
        query_at = query_start + lane_of(scores.shape) % half
        allowed = allowed & (key_at <= query_at)
    return jnp.where(allowed, scores, -1e30)

class Corner:
    def __init__(self):
        self.here = lax.axis_index("narrow")
        self.chip, self.core = self.here // 2, self.here % 2
        self.core_peer = 2 * self.chip + 1 - self.core
        self.chip_peer = 2 * (1 - self.chip) + self.core
        self.far_peer = 2 * (1 - self.chip) + 1 - self.core

class Share:
    def __init__(self, corner, ref, send, recv):
        self.corner, self.ref, self.sems = corner, ref, (send, recv)

    def copy(self, kind, k, owner, peer):
        start, size = cuts(self.ref.shape[1])[k]
        block = self.ref.at[owner, pl.ds(start, size)]
        return remote(block, block, self.sems[0].at[kind, k], self.sems[1].at[kind, k], narrow=peer)

    def start(self):
        c = self.corner
        for k in range(2):
            self.copy(1, k, c.here, c.chip_peer).start()
        for k in range(2):
            self.copy(0, k, c.here, c.core_peer).start()

    def wait_core(self):
        c = self.corner
        for k in range(2):
            self.copy(0, k, c.core_peer, c.core_peer).wait_recv()

    def wait_chip(self):
        c = self.corner
        for k in range(2):
            self.copy(1, k, c.chip_peer, c.chip_peer).wait_recv()
            self.copy(2, k, c.chip_peer, c.core_peer).start()

    def wait_far(self):
        c = self.corner
        for k in range(2):
            self.copy(2, k, c.far_peer, c.core_peer).wait_recv()

    def drain(self):
        c = self.corner
        for k in range(2):
            self.copy(0, k, c.here, c.core_peer).wait_send()
            self.copy(1, k, c.here, c.chip_peer).wait_send()
            self.copy(2, k, c.chip_peer, c.core_peer).wait_send()

    scratch = lambda: [pltpu.SemaphoreType.DMA((3, 2)), pltpu.SemaphoreType.DMA((3, 2))]

class Fold:
    def __init__(self, corner, out_c, got_c, out_x, got_x, held, c_send, c_recv, x_send, x_recv):
        self.corner, self.held = corner, held
        self.out_c, self.got_c, self.out_x, self.got_x = out_c, got_c, out_x, got_x
        self.sems = (c_send, c_recv, x_send, x_recv)

    def to_core(self, x):
        return remote(
            self.out_c.at[x], self.got_c.at[x], self.sems[0].at[x], self.sems[1].at[x],
            narrow=self.corner.core_peer,
        )

    def to_chip(self):
        return remote(self.out_x, self.got_x, self.sems[2], self.sems[3], narrow=self.corner.chip_peer)

    def give(self, block, part):
        x, c = block // 2, block % 2

        @pl.when(self.corner.core != c)
        def _():
            self.out_c[x] = part.astype(BF)
            self.to_core(x).start()

        @pl.when(self.corner.core == c)
        def _():
            self.held[x] = part

    def settle(self, block):
        x, c = block // 2, block % 2

        @pl.when(self.corner.core == c)
        def _():
            self.to_core(x).wait_recv()

            @pl.when(self.corner.chip != x)
            def _():
                self.out_x[...] = (self.held[x] + self.got_c[x].astype(F32)).astype(BF)
                self.to_chip().start()

    def total(self):
        chip = self.corner.chip
        near = self.held[chip] + self.got_c[chip].astype(F32)
        self.to_chip().wait_recv()
        return near + self.got_x[...].astype(F32)

    def drain(self):
        for x in range(2):
            self.to_core(x).wait_send()
        self.to_chip().wait_send()

    def scratch(rows, cols):
        return [
            pltpu.VMEM((2, rows, cols), BF),
            pltpu.VMEM((2, rows, cols), BF),
            pltpu.VMEM((rows, cols), BF),
            pltpu.VMEM((rows, cols), BF),
            pltpu.VMEM((2, rows, cols), F32),
            pltpu.SemaphoreType.DMA((2,)),
            pltpu.SemaphoreType.DMA((2,)),
            pltpu.SemaphoreType.DMA,
            pltpu.SemaphoreType.DMA,
        ]

def front_kernel(hidden, cotangent, routes, length, attn_gain, w_query, w_key, w_value, w_out, moe_gain, cosine, sine, count, experts_here, cid):
    rows, width = hidden.shape
    seq = 4 * rows
    query_cols, key_cols = w_query.shape[1], w_key.shape[1]
    picks = routes.shape[1]
    kv_here = key_cols // HEAD_DIM

    def kernel(*refs):
        refs = list(refs)
        take = lambda number: [refs.pop(0) for _ in range(number)]
        h_ref, cot_ref, route_ref, len_ref, g1_ref, wq_far, wk_far, wv_far, wout_ref, g2_ref, cos_ref, sin_ref = take(12)
        en_ref, ga_ref, whole_ref, q_ref, k_ref, v_ref, ctx_ref, lse_ref, mixed_ref, slots_ref, lab_all = take(11)
        kd, vd, s_scr, p_scr, wqkv_ref, lab_ref = take(6)
        share = take(2)
        fold = take(9)
        g_scr = take(2)
        l_send, l_recv, own_sem, w_sem = take(4)
        ring, corner = Ring(count), Corner()
        others = [(ring.me + shift) % count for shift in range(1, count)]
        w_loads = [
            pltpu.make_async_copy(src, wqkv_ref.at[:, pl.ds(start, size)], w_sem.at[k])
            for k, (src, start, size) in enumerate(
                ((wq_far, 0, query_cols), (wk_far, query_cols, key_cols), (wv_far, query_cols + key_cols, key_cols))
            )
        ]
        for c in w_loads:
            c.start()
        length_here = len_ref[0]
        spread = jnp.concatenate([route_ref[...], jnp.zeros((rows, LANES - picks), jnp.int32)], axis=1)
        lab_ref[0:picks] = spread.T[0:picks]
        lab_ref[picks : 2 * picks] = jnp.full((picks, rows), length_here, jnp.int32)
        greet(others, [corner.core_peer, corner.chip_peer])

        g_ring = gather_steps(ring, ga_ref, *g_scr, own=cot_ref, left=1)
        next(g_ring)
        own_grad = pltpu.make_async_copy(cot_ref, ga_ref.at[ring.me], own_sem)
        own_grad.start()
        label_copy = lambda k, target: remote(
            lab_ref, lab_all.at[ring.me], l_send.at[k], l_recv.at[k], wide=target
        )
        for k, target in enumerate(others):
            label_copy(k, target).start()
        lab_all[ring.me] = lab_ref[...]

        source = h_ref[...].astype(F32)
        scale = lax.rsqrt(jnp.mean(source * source, axis=1, keepdims=True) + EPSILON)
        whole_ref[corner.here] = (source * scale * g1_ref[...]).astype(BF)
        sharing = Share(corner, whole_ref, *share)
        sharing.start()

        def project(block):
            span = pl.ds(pl.multiple_of(block * rows, rows), rows)
            lin = nn(whole_ref[block], wqkv_ref[...])
            cos, sin = cos_ref[span], sin_ref[span]
            for t in range(kv_here):
                lanes = slice(t * LANES, (t + 1) * LANES)
                q_ref[span, lanes] = turn_lanes(lin[:, lanes], cos, sin).astype(BF)
            keys = turn_lanes(lin[:, query_cols : query_cols + key_cols], cos, sin)
            values = lin[:, query_cols + key_cols :]
            k_ref[span] = keys.astype(BF)
            v_ref[span] = values.astype(BF)
            for t in range(kv_here):
                kd[t, span] = doubled(keys, t).astype(BF)
                vd[t, span] = doubled(values, t).astype(BF)

        for c in w_loads:
            c.wait()
        project(corner.here)
        sharing.wait_core()
        project(corner.core_peer)

        for k, target in enumerate(others):
            sender = (ring.me - (k + 1) + count) % count
            remote(lab_ref, lab_all.at[sender], l_send.at[k], l_recv.at[k], wide=target).wait_recv()
        places = corner.here * rows + lane_of((1, rows))
        first = ring.me * experts_here
        upper = jnp.where(
            lax.broadcasted_iota(jnp.int32, (rows, rows), 0) <= lane_of((rows, rows)), 1.0, 0.0
        ).astype(BF)

        def belongs(block, expert_rows):
            found = lab_all[block, 0:1] == expert_rows
            for k in range(1, picks):
                found = found | (lab_all[block, k : k + 1] == expert_rows)
            return found

        local_rows = lax.broadcasted_iota(jnp.int32, (8, rows), 0)
        own_rows = jnp.where(local_rows < experts_here, first + local_rows, -1)
        for b in range(count):
            mine = jnp.where(belongs(b, own_rows) & (places < lab_all[b, picks : picks + 1]), 1.0, 0.0)
            reached = nn(mine.astype(BF), upper)
            slots_ref[b] = jnp.where(mine > 0.0, reached, 0.0).astype(jnp.int32) - 1

        sharing.wait_chip()
        project(corner.chip_peer)
        next(g_ring)
        sharing.wait_far()
        project(corner.far_peer)

        folding = Fold(corner, *fold)
        before = None
        for block in (3, 2, 1, 0):
            span = pl.ds(block * rows, rows)
            for t in range(kv_here):
                lanes = slice(t * LANES, (t + 1) * LANES)
                queries = stacked(q_ref[span, lanes])
                highest = None
                for b in range(block + 1):
                    keys = pl.ds(b * rows, rows)
                    scores = masked_scores(kd[t, keys], queries, b * rows, block * rows, length_here, b == block)
                    s_scr[keys] = scores
                    top = jnp.max(scores, axis=0, keepdims=True)
                    highest = top if highest is None else jnp.maximum(highest, top)
                total = None
                for b in range(block + 1):
                    keys = pl.ds(b * rows, rows)
                    weights = jnp.exp(s_scr[keys] - highest)
                    p_scr[keys] = weights.astype(BF)
                    one = jnp.sum(weights, axis=0, keepdims=True)
                    total = one if total is None else total + one
                keys = pl.ds(0, (block + 1) * rows)
                context = tn(vd[t, keys], p_scr[keys]) / total
                ctx_ref[span, lanes] = unstacked(context).astype(BF)
                lse_ref[t * 4 + block : t * 4 + block + 1] = highest + jnp.log(total)
            folding.give(block, nn(ctx_ref[span], wout_ref[...]))
            if before is not None:
                folding.settle(before)
            before = block
            if block == 1:
                next(g_ring)
        folding.settle(before)
        mixed = source + folding.total()
        mixed_ref[...] = mixed
        scale = lax.rsqrt(jnp.mean(mixed * mixed, axis=1, keepdims=True) + EPSILON)
        en_ref[...] = (mixed * scale * g2_ref[...]).astype(BF)
        for _ in g_ring:
            pass
        for k, target in enumerate(others):
            label_copy(k, target).wait_send()
        own_grad.wait()
        sharing.drain()
        folding.drain()

    vmem = pl.BlockSpec(memory_space=pltpu.VMEM)
    far = pl.BlockSpec(memory_space=pl.ANY)
    shape = jax.ShapeDtypeStruct
    out_shape = [
        shape((rows, width), BF),
        shape((count, rows, width), BF),
        shape((4, rows, width), BF),
        shape((seq, query_cols), BF),
        shape((seq, key_cols), BF),
        shape((seq, key_cols), BF),
        shape((seq, query_cols), BF),
        shape((8, 2 * rows), F32),
        shape((rows, width), F32),
        shape((count, 8, rows), jnp.int32),
        shape((count, 2 * picks, rows), jnp.int32),
    ]
    scratch = [
        pltpu.VMEM((kv_here, seq, LANES), BF),
        pltpu.VMEM((kv_here, seq, LANES), BF),
        pltpu.VMEM((seq, 2 * rows), F32),
        pltpu.VMEM((seq, 2 * rows), BF),
        pltpu.VMEM((width, query_cols + 2 * key_cols), BF),
        pltpu.VMEM((2 * picks, rows), jnp.int32),
        *Share.scratch(),
        *Fold.scratch(rows, width),
        *gather_scratch(count),
        pltpu.SemaphoreType.DMA((count - 1,)),
        pltpu.SemaphoreType.DMA((count - 1,)),
        pltpu.SemaphoreType.DMA,
        pltpu.SemaphoreType.DMA((3,)),
    ]
    return pl.pallas_call(
        kernel,
        out_shape=out_shape,
        in_specs=[vmem, far, vmem, pl.BlockSpec(memory_space=pltpu.SMEM)] + [vmem] + [far] * 3 + [vmem] * 4,
        out_specs=[vmem, far] + [vmem] * (len(out_shape) - 2),
        scratch_shapes=scratch,
        compiler_params=pltpu.CompilerParams(
            collective_id=cid, has_side_effects=True, vmem_limit_bytes=56 * 2**20
        ),
    )(hidden, cotangent, routes, length, attn_gain, w_query, w_key, w_value, w_out, moe_gain, cosine, sine)


def middle_kernel(entry, grad_all, labels_all, slots, router_turned, w_gate_up, w_down, capacity, picks, cid):
    rows, width = entry.shape
    count = grad_all.shape[0]
    experts_here, _, ffe2 = w_gate_up.shape
    ffe = ffe2 // 2
    experts = router_turned.shape[0]
    hops = count // 2
    shifts = [0] + [s for hop in range(1, hops) for s in (hop, -hop)] + [hops]
    room = count * capacity
    quarter_up, quarter_down = width // 4, ffe // 4
    quarter = quarter_up + quarter_down

    def kernel(*refs):
        refs = list(refs)
        take = lambda number: [refs.pop(0) for _ in range(number)]
        en_far, ga_far, lab_all, slots_ref, wr_ref, wgu_far, wd_far = take(7)
        ob_ref, op_ref, c_far, keep_far, got_far, shares_ref, wait_far = take(7)
        wgu, wd, e_buf, g_buf, pg, act_s, x_s, s_s, b_buf, c_slot, got_a, gates, pick_buf, last_c, last_b = take(15)
        held = take(3)
        e_scr = take(2)
        w_sem, g_sem, c_sem, p_send, p_recv, a_send, a_recv, x_send, x_recv, o_sem, f_sem, en_sem, far_send, far_recv = take(14)
        ring, corner = Ring(count), Corner()
        others = [(ring.me + shift) % count for shift in range(1, count)]
        greet(others, [corner.core_peer, corner.chip_peer])

        def weights(e):
            return [
                pltpu.make_async_copy(wgu_far.at[e], wgu.at[e], w_sem.at[0, e]),
                pltpu.make_async_copy(wd_far.at[e], wd.at[e], w_sem.at[1, e]),
            ]

        def grads(p):
            block = ring.at(shifts[p])
            return pltpu.make_async_copy(ga_far.at[block], g_buf.at[block], g_sem.at[p])

        def far_grads(way, shift):
            sign = 1 if way == 0 else -1
            block = ring.at(-sign * (hops - 1 + shift))
            start, size = cuts(rows)[way]
            source = ga_far if shift == 0 else g_buf
            return remote(
                source.at[block, pl.ds(start, size)], g_buf.at[block, pl.ds(start, size)],
                far_send.at[way], far_recv.at[way], wide=ring.peers[way],
            )

        e_ring = gather_steps(ring, e_buf, *e_scr, own=en_far)
        next(e_ring)
        own_entry = pltpu.make_async_copy(en_far, e_buf.at[ring.me], en_sem)
        own_entry.start()
        for e in range(experts_here):
            for c in weights(e):
                c.start()
            if e == 0:
                for p in range(count - 1):
                    grads(p).start()

        places = corner.here * rows + lane_of((1, rows))
        first = ring.me * experts_here
        every = lax.broadcasted_iota(jnp.int32, (experts, rows), 0)
        local_rows = lax.broadcasted_iota(jnp.int32, (8, rows), 0)
        slot_rows = lax.broadcasted_iota(jnp.int32, (capacity, rows), 0)

        def gate(block, home):
            logits = nt(wr_ref[...], e_buf[block])
            member = lab_all[block, 0:1] == every
            for k in range(1, picks):
                member = member | (lab_all[block, k : k + 1] == every)
            masked = jnp.where(member, logits, -jnp.inf)
            raised = jnp.exp(masked - jnp.max(masked, axis=0, keepdims=True))
            shares = raised / jnp.sum(raised, axis=0, keepdims=True)
            if home:
                shares_ref[...] = shares
            kept = jnp.where(places < lab_all[block, picks : picks + 1], shares, 0.0)
            own = jnp.zeros((8, rows), F32)
            for e in range(experts_here):
                row = jnp.sum(jnp.where(every == first + e, kept, 0.0), axis=0, keepdims=True)
                own = jnp.where(local_rows == e, row, own)
            gates[block] = own

        def pick_rows(block, e):
            return slot_rows == slots_ref[block, pl.ds(e, 1), :]

        def gather_rows(block, e):
            found = pick_rows(block, e)
            chosen = jnp.where(found, 1.0, 0.0).astype(BF)
            gate_col = jnp.sum(jnp.where(found, gates[block, pl.ds(e, 1), :], 0.0), axis=1, keepdims=True)
            return found, nn(chosen, e_buf[block]).astype(BF), nn(chosen, g_buf[block]), gate_col

        def chain(numbers, e, result_rows, back_rows, row, await_weights=False):
            blocks = [ring.at(shifts[p]) for p in numbers]
            size = len(numbers) * capacity
            here = pl.ds(pl.multiple_of(row, capacity), size)
            span = pl.ds(numbers[0] * capacity, size)
            if await_weights:
                for c in weights(e):
                    c.wait()
            parts = [gather_rows(block, e) for block in blocks]
            entries = jnp.concatenate([p[1] for p in parts], axis=0)
            grad_rows = jnp.concatenate([p[2] for p in parts], axis=0)
            gate_col = jnp.concatenate([p[3] for p in parts], axis=0)
            slot_grad = (gate_col * grad_rows).astype(BF)
            pre = nn(entries, wgu[e])
            act_grad = nt(slot_grad, wd[e])
            gate_part = pre[:, :ffe]
            up_part = pre[:, ffe:]
            sig = jax.nn.sigmoid(gate_part)
            swish = gate_part * sig
            act = (swish * up_part).astype(BF)
            act_s[e, span] = act
            gate_grad = act_grad * up_part * sig * (1.0 + gate_part * (1.0 - sig))
            pre_grad = jnp.concatenate([gate_grad, act_grad * swish], axis=1).astype(BF)
            pg[e, span] = pre_grad
            result = nn(act, wd[e]).astype(BF).astype(F32)
            back_rows[here] = nt(pre_grad, wgu[e]).astype(BF)
            result_rows[here] = (gate_col * result).astype(BF)
            pick_col = jnp.sum(result * grad_rows, axis=1, keepdims=True)
            for i, block in enumerate(blocks):
                pick = jnp.sum(
                    jnp.where(parts[i][0], pick_col[i * capacity : (i + 1) * capacity], 0.0),
                    axis=0, keepdims=True,
                )
                pick_buf[block] = jnp.where(local_rows == e, pick, pick_buf[block])

        def combine(number, result_rows, back_rows, row_of):
            block = ring.at(shifts[number])
            chosen = jnp.concatenate(
                [jnp.where(pick_rows(block, e), 1.0, 0.0).astype(BF) for e in range(experts_here)], axis=0
            )
            windows = [pl.ds(row_of(e), capacity) for e in range(experts_here)]
            if number >= 2:
                results(number - 2).wait()
            c_slot[number % 2] = tn(chosen, jnp.concatenate([result_rows[w] for w in windows], axis=0)).astype(BF)
            results(number).start()
            b_buf[block] = tn(chosen, jnp.concatenate([back_rows[w] for w in windows], axis=0)).astype(BF)

        def tile(numbers, await_weights):
            size = len(numbers) * capacity
            for p in numbers:
                grads(p).wait()

            def one(e, carry):
                chain(numbers, e, x_s, s_s, e * size, await_weights)
                return carry

            lax.fori_loop(0, experts_here, one, 0)
            for i, number in enumerate(numbers):
                combine(number, x_s, s_s, lambda e: e * size + i * capacity)

        def results(number):
            return pltpu.make_async_copy(
                c_slot.at[number % 2], c_far.at[ring.at(shifts[number])], c_sem.at[number]
            )

        def put(row, size, got):
            ob_ref[pl.ds(row, size)] = got

        b_ring = scatter_steps(ring, b_buf, *held, put)
        pick_buf[...] = jnp.zeros_like(pick_buf)
        own_entry.wait()
        gate(ring.me, True)
        tile([0], True)
        for hop in range(1, hops - 1):
            next(e_ring)
            gate(ring.at(hop), False)
            gate(ring.at(-hop), False)
            if hop == 1:
                for way in range(2):
                    far_grads(way, 0).start()
            tile([2 * hop - 1, 2 * hop], False)
        def weight_grads(e):
            for p in range(count):
                _, entries, grad_rows, gate_col = gather_rows(ring.at(shifts[p]), e)
                span = pl.ds(p * capacity, capacity)
                x_s[span] = entries
                s_s[span] = (gate_col * grad_rows).astype(BF)

            def columns(j, carry):
                cols = pl.ds(pl.multiple_of(j * 256, 256), 256)
                wgu[e, :, cols] = tn(x_s[...], pg[e, :, cols]).astype(BF)
                wd[e, :, cols] = tn(act_s[e], s_s[:, cols]).astype(BF)
                return carry

            lax.fori_loop(0, width // 256, columns, 0)

        def pieces(e, owner):
            return (
                (wgu.at[e, pl.ds(owner * quarter_up, quarter_up)], 0, quarter_up),
                (wd.at[e, pl.ds(owner * quarter_down, quarter_down)], quarter_up, quarter_down),
            )

        landing = lambda e: got_a.at[e] if e < 2 else wait_far.at[e - 2]
        fetch = lambda e: pltpu.make_async_copy(wait_far.at[e - 2], got_a.at[e % 2], f_sem.at[e - 2])

        def to_core(e):
            return [
                remote(src, landing(e).at[x, pl.ds(start, size)], a_send.at[e, x, k], a_recv.at[e, x, k], narrow=corner.core_peer)
                for x in range(2)
                for k, (src, start, size) in enumerate(pieces(e, 2 * x + 1 - corner.core))
            ]

        def to_chip(e):
            return [
                remote(src, got_far.at[e, pl.ds(start, size)], x_send.at[e, k], x_recv.at[e, k], narrow=corner.chip_peer)
                for k, (src, start, size) in enumerate(pieces(e, 2 * (1 - corner.chip) + corner.core))
            ]

        def own_out(e):
            return [
                pltpu.make_async_copy(src, keep_far.at[e, pl.ds(start, size)], o_sem.at[e, k])
                for k, (src, start, size) in enumerate(pieces(e, corner.here))
            ]

        def send_core(e):
            for c in to_core(e):
                c.start()

        def first_sum(e):
            for c in to_core(e):
                c.wait_recv()
            if e >= 2:
                fetch(e).start()
                fetch(e).wait()
            for number in range(2):
                x = 1 - corner.chip if number == 0 else corner.chip
                for src, start, size in pieces(e, 2 * x + corner.core):
                    block_add(src, src, got_a.at[e % 2, x, pl.ds(start, size)], size)
                for c in to_chip(e) if number == 0 else own_out(e):
                    c.start()

        last = [count - 3, count - 2, count - 1]
        row_at = lambda e, i: (e * 3 + i) * capacity
        next(e_ring)
        gate(ring.at(hops - 1), False)
        gate(ring.at(1 - hops), False)
        for p in last[:2]:
            grads(p).wait()

        def several(start, stop, numbers):
            def one(e, carry):
                chain(numbers, e, last_c, last_b, row_at(e, numbers[0] - last[0]))
                return carry

            lax.fori_loop(start, stop, one, 0)

        several(0, 2, last[:2])
        for _ in e_ring:
            pass
        gate(ring.at(hops), False)
        for way in range(2):
            far_grads(way, 1).wait_recv()
        next(b_ring)
        chain(last[2:], 0, last_c, last_b, row_at(0, 2))
        weight_grads(0)
        send_core(0)
        chain(last[2:], 1, last_c, last_b, row_at(1, 2))
        several(2, experts_here, last[:2])
        first_sum(0)
        next(b_ring)
        weight_grads(1)
        send_core(1)
        several(2, experts_here, last[2:])
        first_sum(1)
        for i, number in enumerate(last):
            combine(number, last_c, last_b, lambda e: row_at(e, i))
        next(b_ring)
        pick_copy = lambda k, target: remote(
            pick_buf.at[target], op_ref.at[ring.me], p_send.at[k], p_recv.at[k], wide=target
        )
        for k, target in enumerate(others):
            pick_copy(k, target).start()
        op_ref[ring.me] = pick_buf[ring.me]
        for e in range(2, experts_here):
            weight_grads(e)
            send_core(e)
            next(b_ring)
            first_sum(e)
            next(b_ring, None)
        for _ in b_ring:
            pass
        for e in range(experts_here):
            for c in to_core(e):
                c.wait_send()
            for c in to_chip(e):
                c.wait()
            for c in own_out(e):
                c.wait()
        for number in range(max(0, count - 2), count):
            results(number).wait()
        for way in range(2):
            far_grads(way, 0).wait_send()
        for k, target in enumerate(others):
            sender = (ring.me - (k + 1) + count) % count
            remote(
                pick_buf.at[sender], op_ref.at[sender], p_send.at[k], p_recv.at[k], wide=target
            ).wait_recv()
            pick_copy(k, target).wait_send()

    vmem = pl.BlockSpec(memory_space=pltpu.VMEM)
    far = pl.BlockSpec(memory_space=pl.ANY)
    shape = jax.ShapeDtypeStruct
    out_shape = [
        shape((rows, width), F32),
        shape((count, 8, rows), F32),
        shape((count, rows, width), BF),
        shape((experts_here, quarter, width), BF),
        shape((experts_here, quarter, width), BF),
        shape((experts, rows), F32),
        shape((experts_here - 2, 2, quarter, width), BF),
    ]
    dma = pltpu.SemaphoreType.DMA
    scratch = [
        pltpu.VMEM(w_gate_up.shape, BF),
        pltpu.VMEM(w_down.shape, BF),
        pltpu.VMEM((count, rows, width), BF),
        pltpu.VMEM((count, rows, width), BF),
        pltpu.VMEM((experts_here, room, 2 * ffe), BF),
        pltpu.VMEM((experts_here, room, ffe), BF),
        pltpu.VMEM((room, width), BF),
        pltpu.VMEM((room, width), BF),
        pltpu.VMEM((count, rows, width), BF),
        pltpu.VMEM((2, rows, width), BF),
        pltpu.VMEM((2, 2, quarter, width), BF),
        pltpu.VMEM((count, 8, rows), F32),
        pltpu.VMEM((count, 8, rows), F32),
        pltpu.VMEM((3 * experts_here * capacity, width), BF),
        pltpu.VMEM((3 * experts_here * capacity, width), BF),
        *scatter_scratch(count, rows, width),
        *gather_scratch(count),
        dma((2, experts_here)), dma((count,)), dma((count,)),
        dma((count - 1,)), dma((count - 1,)),
        dma((experts_here, 2, 2)), dma((experts_here, 2, 2)),
        dma((experts_here, 2)), dma((experts_here, 2)), dma((experts_here, 2)), dma((experts_here - 2,)), dma, dma((2,)), dma((2,)),
    ]
    return pl.pallas_call(
        kernel,
        out_shape=out_shape,
        in_specs=[far, far, vmem, vmem, vmem, far, far],
        out_specs=[vmem, vmem, far, far, far, vmem, far],
        scratch_shapes=scratch,
        compiler_params=pltpu.CompilerParams(
            collective_id=cid, has_side_effects=True, vmem_limit_bytes=63 * 2**20
        ),
    )(entry, grad_all, labels_all, slots, router_turned, w_gate_up, w_down)


def tail_kernel(entry_home, pick_home, shares, router_turned, mixed, cotangent, hidden, length, attn_gain, moe_gain, w_query, w_key, w_value, w_out, queries, keys, values, context, whole, lse, cosine, sine, expert_part, kept, arrived, shapes, cid):
    count, rows, width = expert_part.shape
    seq = 4 * rows
    query_cols, key_cols = w_out.shape[0], w_key.shape[1]
    cols = query_cols + 2 * key_cols
    kv_here = key_cols // HEAD_DIM
    experts_all = router_turned.shape[0]
    small_rows = (experts_all + 2 + 15) // 16 * 16
    block = -(-(cols + query_cols + small_rows) // (32 * count)) * 32
    experts, quarter, _ = kept.shape
    up_shape, down_shape = shapes
    quarter_up, quarter_down = up_shape[1] // 4, down_shape[1] // 4
    base = [0, rows, 3 * rows, 6 * rows]
    small_at = cols + query_cols

    def kernel(*refs):
        refs = list(refs)
        take = lambda number: [refs.pop(0) for _ in range(number)]
        eh_ref, pick_ref, shares_ref, wr_ref, mixed_ref, cot_ref, h_ref, len_ref, g1_ref, g2_ref = take(10)
        wq_far, wk_far, wv_far, wout_ref, q_ref, k_ref, v_ref, ctx_ref, whole_ref, lse_ref, cos_ref, sin_ref = take(12)
        c_far, keep_far, got_far = take(3)
        out_ref, gh_ref, turned_ref, go_ref, small_ref, up_ref, down_ref = take(7)
        gw, mg_s, kd, vd, p_all, dp_scr, ds_scr, dctx, dk, dv, qg, packed, small_got, expert_sum, c_ref, sum_ref, own, got, wqkv_ref, wt_ref, gain_got = take(21)
        share, fold = take(2), take(9)
        c_sem, w_sem, o_sem = take(3)
        c_scr, s_scr, g_scr = take(3), take(3), take(2)
        sm_send, sm_recv, ga_send, ga_recv = take(4)
        c_send, c_recv, x_send, x_recv, f_send, f_recv, l_sem = take(7)
        ring, corner = Ring(count), Corner()
        greet(list(ring.peers), [corner.core_peer, corner.chip_peer, corner.far_peer])
        length_here = len_ref[0]

        own_loads = lambda e: [
            pltpu.make_async_copy(keep_far.at[e], own.at[e], o_sem.at[0, e]),
            pltpu.make_async_copy(got_far.at[e], got.at[e], o_sem.at[1, e]),
        ]
        w_loads = [
            pltpu.make_async_copy(src, wqkv_ref.at[:, pl.ds(start, size)], w_sem.at[k])
            for k, (src, start, size) in enumerate(
                ((wq_far, 0, query_cols), (wk_far, query_cols, key_cols), (wv_far, query_cols + key_cols, key_cols))
            )
        ]
        for c in w_loads:
            c.start()
        for e in range(experts):
            for c in own_loads(e):
                c.start()

        def own_sum(e):
            for c in own_loads(e):
                c.wait()
            block_add(own.at[e], own.at[e], got.at[e], quarter)
            send_out(e)
            for c in send(e, core_sems, corner.core_peer) + own_copy(e):
                c.start()

        def put(row, size, value):
            expert_sum[pl.ds(row, size)] = value

        c_load = pltpu.make_async_copy(c_far, c_ref, c_sem)
        c_load.start()
        c_ring = scatter_steps(ring, c_ref, *c_scr, put)

        def places(e, owner):
            mine = own.at[e]
            return (
                (mine.at[pl.ds(0, quarter_up)], up_ref.at[e, pl.ds(owner * quarter_up, quarter_up)]),
                (mine.at[pl.ds(quarter_up, quarter_down)], down_ref.at[e, pl.ds(owner * quarter_down, quarter_down)]),
            )

        def send(e, sems, peer):
            return [
                remote(src, dst, sems[0].at[e, k], sems[1].at[e, k], narrow=peer)
                for k, (src, dst) in enumerate(places(e, corner.here))
            ]

        def forward(e, owner, sems):
            return [
                remote(dst, dst, sems[0].at[e, k], sems[1].at[e, k], narrow=corner.core_peer)
                for k, (src, dst) in enumerate(places(e, owner))
            ]

        core_sems, chip_sems, far_sems = (c_send, c_recv), (x_send, x_recv), (f_send, f_recv)

        def own_copy(e):
            return [
                pltpu.make_async_copy(src, dst, l_sem.at[e, k])
                for k, (src, dst) in enumerate(places(e, corner.here))
            ]

        def send_out(e):
            for c in send(e, chip_sems, corner.chip_peer):
                c.start()

        def pass_on(e):
            for c in forward(e, corner.chip_peer, chip_sems):
                c.wait_recv()
            for c in forward(e, corner.chip_peer, far_sems):
                c.start()

        picked, held_shares = pick_ref[...], shares_ref[...]
        logit_grad = held_shares * (picked - jnp.sum(held_shares * picked, axis=0, keepdims=True))
        high = logit_grad.astype(BF)
        low = (logit_grad - high.astype(F32)).astype(BF)
        entry_grad = eh_ref[...] + (tn(high, wr_ref[...]) + tn(low, wr_ref[...]))
        mixed_here = mixed_ref[...]
        scale = lax.rsqrt(jnp.mean(mixed_here * mixed_here, axis=1, keepdims=True) + EPSILON)
        unit = mixed_here * scale
        inner = entry_grad * g2_ref[...]
        from_norm = scale * (inner - unit * jnp.mean(inner * unit, axis=1, keepdims=True))
        at = corner.here * rows + lax.broadcasted_iota(jnp.int32, (rows, 1), 0)
        valid = jnp.where(at < length_here, 1.0, 0.0)
        mixed_grad = valid * cot_ref[...].astype(F32) + from_norm
        mg_s[...] = mixed_grad
        gw[corner.here] = mixed_grad.astype(BF)
        sharing = Share(corner, gw, *share)
        sharing.start()
        entry = (unit * g2_ref[...]).astype(BF)
        small_got[3] = jnp.concatenate(
            [
                nn(high, entry) + nn(low, entry),
                jnp.sum(entry_grad * unit, axis=0, keepdims=True),
                jnp.zeros((small_rows - experts_all - 1, width), F32),
            ],
            axis=0,
        ).astype(BF)
        peers = (corner.core_peer, corner.chip_peer, corner.far_peer)
        small_copy = lambda k, peer: remote(
            small_got.at[3], small_got.at[k], sm_send.at[k], sm_recv.at[k], narrow=peer
        )
        for k, peer in enumerate(peers):
            small_copy(k, peer).start()

        for t in range(kv_here):
            kd[t] = doubled(k_ref[...].astype(F32), t).astype(BF)
            vd[t] = doubled(v_ref[...].astype(F32), t).astype(BF)

        def chances(b):
            for t in range(kv_here):
                lanes = slice(t * LANES, (t + 1) * LANES)
                stack = stacked(q_ref[pl.ds(b * rows, rows), lanes])
                log_sum = lse_ref[t * 4 + b : t * 4 + b + 1]
                for kb in range(b + 1):
                    scores = masked_scores(
                        kd[t, pl.ds(kb * rows, rows)], stack, kb * rows, b * rows, length_here, kb == b
                    )
                    p_all[t, pl.ds(base[b] + kb * rows, rows)] = jnp.exp(scores - log_sum).astype(BF)

        def pull(owner):
            dctx[owner] = nt(gw[owner], wout_ref[...]).astype(BF)

        pull(corner.here)
        c_load.wait()
        next(c_ring)
        chances(3)
        next(c_ring)
        sharing.wait_core()
        pull(corner.core_peer)
        chances(2)
        next(c_ring)
        chances(1)
        chances(0)
        sharing.wait_chip()
        own_sum(0)
        pull(corner.chip_peer)
        sharing.wait_far()
        pull(corner.far_peer)
        dk[...] = jnp.zeros_like(dk)
        dv[...] = jnp.zeros_like(dv)

        folding = Fold(corner, *fold)
        before = None
        for b in (3, 2, 1, 0):
            span = pl.ds(b * rows, rows)
            cos, sin = cos_ref[span], sin_ref[span]
            for t in range(kv_here):
                lanes = slice(t * LANES, (t + 1) * LANES)
                stack = stacked(q_ref[span, lanes])
                grad_stack = stacked(dctx[b, :, lanes])
                inner = None
                for kb in range(b + 1):
                    chance = p_all[t, pl.ds(base[b] + kb * rows, rows)]
                    grad = nt(vd[t, pl.ds(kb * rows, rows)], grad_stack)
                    dp_scr[pl.ds(kb * rows, rows)] = grad
                    one = jnp.sum(chance.astype(F32) * grad, axis=0, keepdims=True)
                    inner = one if inner is None else inner + one
                for kb in range(b + 1):
                    key_span = pl.ds(kb * rows, rows)
                    chance = p_all[t, pl.ds(base[b] + kb * rows, rows)]
                    score_grad = (chance.astype(F32) * (dp_scr[key_span] - inner)).astype(BF)
                    ds_scr[key_span] = score_grad
                    dk[t, key_span] += nn(score_grad, stack)
                    dv[t, key_span] += nn(chance, grad_stack)
                every = pl.ds(0, (b + 1) * rows)
                query_grad = unstacked(tn(kd[t, every], ds_scr[every])) * HEAD_DIM ** (-0.5)
                qg[span, lanes] = turn_lanes(query_grad, cos, -sin).astype(BF)
            low_lanes = lane_of((rows, LANES)) < HEAD_DIM
            both = lambda ref, t: ref[t, span] + pltpu.roll(ref[t, span], HEAD_DIM, 1)
            key_grad = jnp.where(low_lanes, both(dk, 0), both(dk, 1)) * HEAD_DIM ** (-0.5)
            qg[span, query_cols : query_cols + key_cols] = turn_lanes(key_grad, cos, -sin).astype(BF)
            qg[span, query_cols + key_cols :] = jnp.where(low_lanes, both(dv, 0), both(dv, 1)).astype(BF)
            if b == 3:
                for c in w_loads:
                    c.wait()
            folding.give(b, nt(qg[span], wqkv_ref[...]))
            if before is not None:
                folding.settle(before)
            before = b
            next(c_ring)
            if b == 2:
                own_sum(1)
        folding.settle(before)

        def store(row, value):
            for start in range(0, value.shape[0], 16):
                size = min(16, value.shape[0] - start)
                at_row = row + start
                packed[at_row // block, pl.ds(at_row % block, size)] = value[start : start + size].astype(BF)

        weight_grad = tn(qg[...], whole_ref[...])
        wt_ref[...] = wqkv_ref[...].astype(F32).T
        gain_one = jnp.sum(weight_grad * wt_ref[...], axis=0, keepdims=True) / g1_ref[...]
        store(0, weight_grad)
        store(cols, tn(ctx_ref[...], gw[...].reshape(seq, width)))
        rest = small_at + small_rows
        store(rest, jnp.zeros((count * block - rest, width), F32))
        for k, peer in enumerate(peers):
            small_copy(k, peer).wait_recv()
        small_sum = sum(small_got[k].astype(F32) for k in range(4))
        row_at = lax.broadcasted_iota(jnp.int32, (small_rows, width), 0)
        store(small_at, jnp.where(row_at == experts_all + 1, gain_one, small_sum))

        def finish(row, size, got):
            sum_ref[ring.me, pl.ds(row, size)] = got.astype(BF)

        sums = scatter_steps(ring, packed, *s_scr, finish)
        next(sums)
        own_sum(2)
        own_sum(3)
        for _ in sums:
            pass
        for _ in gather_steps(ring, sum_ref, *g_scr):
            pass
        whole_sum = lambda row, size: jnp.concatenate(
            [sum_ref[b] for b in range(row // block, (row + size) // block)], axis=0
        )
        gain_got[3] = sum_ref[small_at // block, small_rows - 16 : small_rows]
        gain_copy = lambda k, peer: remote(
            gain_got.at[3], gain_got.at[k], ga_send.at[k], ga_recv.at[k], narrow=peer
        )
        for k, peer in enumerate(peers):
            gain_copy(k, peer).start()
        for row in range(0, cols, block):
            turned_ref[:, row : row + block] = sum_ref[row // block].astype(F32).T.astype(BF)
        go_ref[...] = whole_sum(cols, query_cols)
        normed_grad = folding.total()
        source = h_ref[...].astype(F32)
        scale = lax.rsqrt(jnp.mean(source * source, axis=1, keepdims=True) + EPSILON)
        unit = source * scale
        inner = normed_grad * g1_ref[...]
        from_norm = scale * (inner - unit * jnp.mean(inner * unit, axis=1, keepdims=True))
        gh_ref[...] = (mg_s[...] + from_norm).astype(BF)
        for e in range(2):
            pass_on(e)
        for _ in c_ring:
            pass
        out_ref[...] = (valid * (mixed_here + expert_sum[...])).astype(BF)
        for k, peer in enumerate(peers):
            gain_copy(k, peer).wait_recv()
        gain_sum = sum(gain_got[k].astype(F32) for k in range(4))
        small_ref[0 : small_rows - 16] = sum_ref[small_at // block, 0 : small_rows - 16]
        last_rows = small_rows - 16 + lax.broadcasted_iota(jnp.int32, (16, width), 0)
        small_ref[small_rows - 16 : small_rows] = jnp.where(
            last_rows == experts_all + 1, gain_sum, gain_got[3].astype(F32)
        ).astype(BF)
        for e in range(2, experts):
            pass_on(e)
        for k, peer in enumerate(peers):
            gain_copy(k, peer).wait_send()
        for k, peer in enumerate(peers):
            small_copy(k, peer).wait_send()
        for e in range(experts):
            for c in own_copy(e):
                c.wait()
            for c in send(e, chip_sems, corner.chip_peer) + send(e, core_sems, corner.core_peer):
                c.wait_send()
            for c in forward(e, corner.core_peer, core_sems):
                c.wait_recv()
            for c in forward(e, corner.chip_peer, far_sems):
                c.wait_send()
            for c in forward(e, corner.far_peer, far_sems):
                c.wait_recv()
        sharing.drain()
        folding.drain()

    vmem = pl.BlockSpec(memory_space=pltpu.VMEM)
    far = pl.BlockSpec(memory_space=pl.ANY)
    shape = jax.ShapeDtypeStruct
    out_shape = [
        shape((rows, width), BF),
        shape((rows, width), BF),
        shape((width, cols), BF),
        shape((query_cols, width), BF),
        shape((small_rows, width), BF),
        shape(up_shape, BF),
        shape(down_shape, BF),
    ]
    scratch = [
        pltpu.VMEM((4, rows, width), BF),
        pltpu.VMEM((rows, width), F32),
        pltpu.VMEM((kv_here, seq, LANES), BF),
        pltpu.VMEM((kv_here, seq, LANES), BF),
        pltpu.VMEM((kv_here, 10 * rows, 2 * rows), BF),
        pltpu.VMEM((seq, 2 * rows), F32),
        pltpu.VMEM((seq, 2 * rows), BF),
        pltpu.VMEM((4, rows, query_cols), BF),
        pltpu.VMEM((kv_here, seq, LANES), F32),
        pltpu.VMEM((kv_here, seq, LANES), F32),
        pltpu.VMEM((seq, cols), BF),
        pltpu.VMEM((count, block, width), BF),
        pltpu.VMEM((4, small_rows, width), BF),
        pltpu.VMEM((rows, width), F32),
        pltpu.VMEM((count, rows, width), BF),
        pltpu.VMEM((count, block, width), BF),
        pltpu.VMEM((experts, quarter, width), BF),
        pltpu.VMEM((experts, quarter, width), BF),
        pltpu.VMEM((width, cols), BF),
        pltpu.VMEM((cols, width), F32),
        pltpu.VMEM((4, 16, width), BF),
        *Share.scratch(),
        *Fold.scratch(rows, width),
        pltpu.SemaphoreType.DMA,
        pltpu.SemaphoreType.DMA((3,)),
        pltpu.SemaphoreType.DMA((2, experts)),
        *scatter_scratch(count, rows, width),
        *scatter_scratch(count, block, width),
        *gather_scratch(count),
        *[pltpu.SemaphoreType.DMA((3,))] * 4,
    ] + [pltpu.SemaphoreType.DMA((experts, 2))] * 7
    return pl.pallas_call(
        kernel,
        out_shape=out_shape,
        in_specs=[vmem] * 7 + [pl.BlockSpec(memory_space=pltpu.SMEM)] + [vmem] * 2 + [far] * 3 + [vmem] * 9 + [far] * 3,
        out_specs=[vmem] * 5 + [far] * 2,
        scratch_shapes=scratch,
        compiler_params=pltpu.CompilerParams(
            collective_id=cid, has_side_effects=True, vmem_limit_bytes=62 * 2**20
        ),
    )(entry_home, pick_home, shares, router_turned, mixed, cotangent, hidden, length, attn_gain, moe_gain,
      w_query, w_key, w_value, w_out, queries, keys, values, context, whole, lse, cosine, sine, expert_part, kept, arrived)


def final_kernel(out, grad_hidden, turned, out_grad, small, up_grad, down_grad, query_cols, key_cols, experts):
    here, width, ffe2 = up_grad.shape
    ffe = down_grad.shape[1]
    step = 256
    parts = [(0, e, r) for e in range(here) for r in range(0, width, step)]
    parts += [(1, e, r) for e in range(here) for r in range(0, ffe, step)]
    parts.sort(key=lambda p: (p[1], p[0], p[2]))

    def kernel(o_in, gh_in, t_in, go_in, s_in, up_in, down_in, o_ref, gh_ref, gq, gk, gv, go, g1, g2, gr, up_ref, down_ref, low, full, in_sem, out_sem):
        near = lambda i: (up_in, down_in)[parts[i][0]].at[parts[i][1], pl.ds(parts[i][2], step)]
        away = lambda i: (up_ref, down_ref)[parts[i][0]].at[parts[i][1], pl.ds(parts[i][2], step)]
        inward = lambda i: pltpu.make_async_copy(near(i), low.at[i], in_sem.at[i])
        outward = lambda i: pltpu.make_async_copy(full.at[i], away(i), out_sem.at[i])
        for i in range(len(parts)):
            inward(i).start()
        o_ref[...] = o_in[...]
        gh_ref[...] = gh_in[...]
        gq[...] = t_in[:, :query_cols].astype(F32)
        gk[...] = t_in[:, query_cols : query_cols + key_cols].astype(F32)
        gv[...] = t_in[:, query_cols + key_cols :].astype(F32)
        go[...] = go_in[...].astype(F32)
        rows = s_in[...].astype(F32)
        g1[...] = rows[experts + 1 : experts + 2]
        g2[...] = rows[experts : experts + 1]
        gr[...] = rows[:experts]
        for i in range(len(parts)):
            inward(i).wait()
            full[i] = low[i].astype(F32)
            outward(i).start()
        for i in range(len(parts)):
            outward(i).wait()

    shape = jax.ShapeDtypeStruct
    vmem = pl.BlockSpec(memory_space=pltpu.VMEM)
    far = pl.BlockSpec(memory_space=pl.ANY)
    small_shapes = [
        shape(out.shape, BF), shape(grad_hidden.shape, BF), shape((width, query_cols), F32),
        shape((width, key_cols), F32), shape((width, key_cols), F32), shape(out_grad.shape, F32),
        shape((1, width), F32), shape((1, width), F32), shape((experts, width), F32),
    ]
    return pl.pallas_call(
        kernel,
        out_shape=small_shapes + [shape(up_grad.shape, F32), shape(down_grad.shape, F32)],
        in_specs=[vmem] * 5 + [far] * 2,
        out_specs=[vmem] * 9 + [far] * 2,
        scratch_shapes=[
            pltpu.VMEM((len(parts), step, width), BF),
            pltpu.VMEM((len(parts), step, width), F32),
            pltpu.SemaphoreType.DMA((len(parts),)),
            pltpu.SemaphoreType.DMA((len(parts),)),
        ],
        compiler_params=pltpu.CompilerParams(vmem_limit_bytes=62 * 2**20),
    )(out, grad_hidden, turned, out_grad, small, up_grad, down_grad)


def turn_tables(count, head_dim):
    inverse = THETA ** (-np.arange(head_dim // 2, dtype=np.float32) * np.float32(2.0 / head_dim))
    angles = np.arange(count, dtype=np.float32)[:, None] * inverse.astype(np.float32)[None, :]
    cosine, sine = np.cos(angles), np.sin(angles)
    return (
        jnp.asarray(np.concatenate([cosine] * 4, axis=1), F32),
        jnp.asarray(np.concatenate([-sine, sine] * 2, axis=1), F32),
    )


def local_general(
    hidden,
    lengths,
    routes,
    cotangent,
    attn_gain,
    w_query,
    w_key,
    w_value,
    w_out,
    moe_gain,
    w_router,
    w_gate_up,
    w_down,
):
    rows_here = hidden.shape[1]
    width = hidden.shape[2]
    seq_len = rows_here * lax.axis_size("narrow")
    head_dim = HEAD_DIM
    group_size = HEADS // KV_HEADS
    kv_here = w_key.shape[1] // head_dim
    query_cols = kv_here * group_size * head_dim
    key_cols = kv_here * head_dim
    scaling = head_dim ** (-0.5)
    block_rows = min(512, seq_len)
    block_count = seq_len // block_rows
    length_here = lengths[0]
    offset = lax.axis_index("narrow") * rows_here
    local_places = offset + jnp.arange(rows_here, dtype=jnp.int32)
    valid = (local_places < length_here).astype(jnp.float32)[:, None]
    source = hidden[0].astype(jnp.float32)
    normed, scale_one = norm_forward(source, attn_gain)
    normed_low = normed.astype(jnp.bfloat16)
    whole = lax.all_gather(normed_low, "narrow", axis=0, tiled=True)
    w_qkv = jnp.concatenate([w_query, w_key, w_value], axis=1)
    projected = jnp.dot(whole, w_qkv, preferred_element_type=jnp.float32)
    cosine, sine_part = rope_tables(seq_len, head_dim)
    query_rot = turn(
        projected[:, :query_cols].reshape(seq_len, kv_here, group_size, head_dim),
        cosine,
        sine_part,
        1.0,
    )
    key_rot = turn(
        projected[:, query_cols : query_cols + key_cols].reshape(seq_len, kv_here, head_dim),
        cosine,
        sine_part,
        1.0,
    )
    queries = (
        query_rot.astype(jnp.bfloat16)
        .reshape(block_count, block_rows, kv_here, group_size, head_dim)
        .transpose(0, 2, 3, 1, 4)
    )
    keys_low = key_rot.astype(jnp.bfloat16).transpose(1, 0, 2)
    values_low = (
        projected[:, query_cols + key_cols :]
        .astype(jnp.bfloat16)
        .reshape(seq_len, kv_here, head_dim)
        .transpose(1, 0, 2)
    )
    context, log_sums = attend_forward(queries, keys_low, values_low, length_here, scaling)
    context_rows = context.transpose(0, 3, 1, 2, 4).reshape(seq_len, query_cols)
    piece = context_rows
    attn_part = lax.psum_scatter(
        jnp.dot(piece, w_out, preferred_element_type=jnp.float32).astype(jnp.bfloat16),
        "narrow",
        scatter_dimension=0,
        tiled=True,
    ).astype(jnp.float32)
    mixed = source + attn_part
    normed_two, scale_two = norm_forward(mixed, moe_gain)
    entry = normed_two.astype(jnp.bfloat16)
    logits = jnp.dot(entry, w_router, preferred_element_type=jnp.float32)
    route_here = routes[0]
    tokens_here, picks = route_here.shape
    expert_total = w_router.shape[1]
    capacity = 2 * tokens_here * picks // expert_total
    member = (
        route_here[:, :, None] == jnp.arange(expert_total, dtype=jnp.int32)[None, None, :]
    ).astype(jnp.int32)
    flat_member = member.reshape(tokens_here * picks, expert_total)
    earlier = jnp.cumsum(flat_member, axis=0) - flat_member
    slot_index = jnp.sum(earlier * flat_member, axis=1)
    places = route_here.reshape(-1) * capacity + slot_index
    member_float = member.astype(jnp.float32)
    chosen = jnp.einsum("tke,te->tk", member_float, logits, precision=HIGHEST)
    highest = jnp.max(chosen, axis=-1, keepdims=True)
    raised = jnp.exp(chosen - highest)
    shares = raised / jnp.sum(raised, axis=-1, keepdims=True)
    gates = shares * valid
    outgoing = (
        jnp.zeros((expert_total * capacity, width), jnp.bfloat16)
        .at[places]
        .set(jnp.repeat(entry, picks, axis=0))
    )
    received = lax.all_to_all(
        outgoing.reshape(expert_total, capacity, width),
        "wide",
        split_axis=0,
        concat_axis=1,
        tiled=True,
    )
    expert_pre = jnp.einsum("erd,edf->erf", received, w_gate_up, preferred_element_type=jnp.float32)
    ffe_width = w_down.shape[1]
    gate_part = expert_pre[..., :ffe_width]
    up_part = expert_pre[..., ffe_width:]
    sigmoid_gate = jax.nn.sigmoid(gate_part)
    swish = gate_part * sigmoid_gate
    act_low = (swish * up_part).astype(jnp.bfloat16)
    expert_result = jnp.einsum(
        "erf,efd->erd", act_low, w_down, preferred_element_type=jnp.float32
    ).astype(jnp.bfloat16)
    returned = lax.all_to_all(expert_result, "wide", split_axis=1, concat_axis=0, tiled=True)
    picked = returned.reshape(expert_total * capacity, width)[places].reshape(
        tokens_here, picks, width
    )
    expert_sum = jnp.einsum("tk,tkd->td", gates, picked, precision=HIGHEST)
    output_rows = (valid * (mixed + expert_sum)).astype(jnp.bfloat16)
    grad_rows_here = cotangent[0].astype(jnp.float32) * valid
    slot_grad = (gates[:, :, None] * grad_rows_here[:, None, :]).astype(jnp.bfloat16)
    grad_outgoing = (
        jnp.zeros((expert_total * capacity, width), jnp.bfloat16)
        .at[places]
        .set(slot_grad.reshape(tokens_here * picks, width))
    )
    grad_received = lax.all_to_all(
        grad_outgoing.reshape(expert_total, capacity, width),
        "wide",
        split_axis=0,
        concat_axis=1,
        tiled=True,
    )
    act_grad = jnp.einsum("erd,efd->erf", grad_received, w_down, preferred_element_type=jnp.float32)
    down_grad = jnp.einsum(
        "erf,erd->efd", act_low, grad_received, preferred_element_type=jnp.float32
    )
    gate_grad = act_grad * up_part * sigmoid_gate * (1.0 + gate_part * (1.0 - sigmoid_gate))
    pre_grad = jnp.concatenate([gate_grad, act_grad * swish], axis=-1).astype(jnp.bfloat16)
    gate_up_grad = jnp.einsum(
        "erd,erf->edf", received, pre_grad, preferred_element_type=jnp.float32
    )
    entry_back = jnp.einsum(
        "erf,edf->erd", pre_grad, w_gate_up, preferred_element_type=jnp.float32
    ).astype(jnp.bfloat16)
    entry_home = lax.all_to_all(entry_back, "wide", split_axis=1, concat_axis=0, tiled=True)
    entry_rows = entry_home.reshape(expert_total * capacity, width)[places].reshape(
        tokens_here, picks, width
    )
    entry_grad = jnp.sum(entry_rows, axis=1, dtype=jnp.float32)
    pick_grad = jnp.einsum("td,tkd->tk", grad_rows_here, picked, precision=HIGHEST) * valid
    chosen_grad = shares * (pick_grad - jnp.sum(shares * pick_grad, axis=-1, keepdims=True))
    logit_grad = jnp.einsum("tk,tke->te", chosen_grad, member_float, precision=HIGHEST)
    router_grad = lax.dot_general(
        entry.astype(jnp.float32), logit_grad, (((0,), (0,)), ((), ())), precision=HIGHEST
    )
    entry_grad = entry_grad + lax.dot_general(
        logit_grad, w_router.astype(jnp.float32), (((1,), (1,)), ((), ())), precision=HIGHEST
    )
    mixed_from_norm, gain_two_grad = norm_backward(mixed, scale_two, moe_gain, entry_grad)
    mixed_grad = grad_rows_here + mixed_from_norm
    attn_grad_low = mixed_grad.astype(jnp.bfloat16)
    grad_whole = lax.all_gather(attn_grad_low, "narrow", axis=0, tiled=True)
    context_grad = lax.dot_general(
        grad_whole, w_out, (((1,), (1,)), ((), ())), preferred_element_type=jnp.float32
    ).astype(jnp.bfloat16)
    out_grad = lax.dot_general(
        context_rows, grad_whole, (((0,), (0,)), ((), ())), preferred_element_type=jnp.float32
    )
    context_blocks = context_grad.reshape(
        block_count, block_rows, kv_here, group_size, head_dim
    ).transpose(0, 2, 3, 1, 4)
    query_grad, key_grad, value_grad = attend_backward(
        queries, keys_low, values_low, context_blocks, log_sums, length_here, scaling
    )
    query_rows = turn(
        query_grad.transpose(0, 3, 1, 2, 4).reshape(seq_len, kv_here, group_size, head_dim),
        cosine,
        sine_part,
        -1.0,
    )
    key_rows = turn(key_grad.transpose(1, 0, 2), cosine, sine_part, -1.0)
    value_rows = value_grad.transpose(1, 0, 2)
    qkv_grad = jnp.concatenate(
        [
            query_rows.reshape(seq_len, query_cols),
            key_rows.reshape(seq_len, key_cols),
            value_rows.reshape(seq_len, key_cols),
        ],
        axis=1,
    ).astype(jnp.bfloat16)
    qkv_weight_grad = lax.dot_general(
        whole, qkv_grad, (((0,), (0,)), ((), ())), preferred_element_type=jnp.float32
    )
    piece = qkv_grad
    normed_grad = lax.psum_scatter(
        lax.dot_general(
            piece, w_qkv, (((1,), (1,)), ((), ())), preferred_element_type=jnp.float32
        ).astype(jnp.bfloat16),
        "narrow",
        scatter_dimension=0,
        tiled=True,
    ).astype(jnp.float32)
    source_from_norm, gain_one_grad = norm_backward(source, scale_one, attn_gain, normed_grad)
    grad_input = (mixed_grad + source_from_norm).astype(jnp.bfloat16)
    gate_up_grad, down_grad, router_grad, gain_one_grad, gain_two_grad = (
        lax.psum(gate_up_grad.astype(jnp.bfloat16), "narrow").astype(jnp.float32),
        lax.psum(down_grad.astype(jnp.bfloat16), "narrow").astype(jnp.float32),
        lax.psum(router_grad.astype(jnp.bfloat16), "narrow").astype(jnp.float32),
        lax.psum(gain_one_grad.astype(jnp.bfloat16), "narrow").astype(jnp.float32),
        lax.psum(gain_two_grad.astype(jnp.bfloat16), "narrow").astype(jnp.float32),
    )
    qkv_weight_grad, out_grad, router_grad, gain_one_grad, gain_two_grad = (
        lax.psum(qkv_weight_grad.astype(jnp.bfloat16), "wide").astype(jnp.float32),
        lax.psum(out_grad.astype(jnp.bfloat16), "wide").astype(jnp.float32),
        lax.psum(router_grad.astype(jnp.bfloat16), "wide").astype(jnp.float32),
        lax.psum(gain_one_grad.astype(jnp.bfloat16), "wide").astype(jnp.float32),
        lax.psum(gain_two_grad.astype(jnp.bfloat16), "wide").astype(jnp.float32),
    )
    query_weight_grad = qkv_weight_grad[:, :query_cols]
    key_weight_grad = qkv_weight_grad[:, query_cols : query_cols + key_cols]
    value_weight_grad = qkv_weight_grad[:, query_cols + key_cols :]
    return (
        output_rows[None],
        grad_input[None],
        gain_one_grad,
        query_weight_grad,
        key_weight_grad,
        value_weight_grad,
        out_grad,
        gain_two_grad,
        router_grad,
        gate_up_grad,
        down_grad,
    )


def local(
    hidden,
    lengths,
    routes,
    cotangent,
    attn_gain,
    w_query,
    w_key,
    w_value,
    w_out,
    moe_gain,
    w_router,
    w_gate_up,
    w_down,
):
    kv_here = w_key.shape[1] // HEAD_DIM
    rows, width = hidden.shape[1:]
    if lax.axis_size("narrow") != 4 or kv_here != 2 or rows != 256:
        return local_general(
            hidden, lengths, routes, cotangent, attn_gain, w_query, w_key, w_value, w_out,
            moe_gain, w_router, w_gate_up, w_down,
        )
    count = lax.axis_size("wide")
    picks = routes.shape[2]
    expert_total = w_router.shape[1]
    expert_here = w_gate_up.shape[0]
    capacity = 2 * rows * picks // expert_total
    query_cols, key_cols = w_query.shape[1], w_key.shape[1]
    cosine, sine = turn_tables(4 * rows, HEAD_DIM)
    router_turned = w_router.T
    gain_one, gain_two = attn_gain[None], moe_gain[None]
    entry, grad_all, whole, queries, keys, values, context, lse, mixed, slots, labels_all = front_kernel(
        hidden[0], cotangent[0], routes[0], lengths, gain_one, w_query, w_key, w_value, w_out, gain_two,
        cosine, sine, count, expert_here, 1,
    )
    entry_home, pick_home, expert_part, kept, arrived, shares, _ = middle_kernel(
        entry, grad_all, labels_all, slots, router_turned, w_gate_up, w_down, capacity, picks, 2
    )
    results = tail_kernel(
        entry_home, pick_home[:, :expert_here].reshape(expert_total, rows), shares, router_turned, mixed,
        cotangent[0], hidden[0], lengths, gain_one, gain_two, w_query, w_key, w_value, w_out, queries, keys,
        values, context, whole.reshape(4 * rows, width), lse, cosine, sine, expert_part, kept, arrived,
        (w_gate_up.shape, w_down.shape), 3,
    )
    out, grad_hidden, grad_q, grad_k, grad_v, grad_out, grad_one, grad_two, grad_router, grad_up, grad_down = final_kernel(
        *results, query_cols, key_cols, expert_total
    )
    return (
        out[None], grad_hidden[None], grad_one[0], grad_q, grad_k, grad_v, grad_out, grad_two[0], grad_router.T,
        grad_up, grad_down,
    )


def solution(mesh):
    in_specs = (
        P("wide", "narrow", None),
        P("wide"),
        P("wide", "narrow", None),
        P("wide", "narrow", None),
        P(),
        P(None, "narrow"),
        P(None, "narrow"),
        P(None, "narrow"),
        P("narrow", None),
        P(),
        P(),
        P("wide", None, None),
        P("wide", None, None),
    )
    out_specs = (
        P("wide", "narrow", None),
        P("wide", "narrow", None),
        P(),
        P(None, "narrow"),
        P(None, "narrow"),
        P(None, "narrow"),
        P("narrow", None),
        P(),
        P(),
        P("wide", None, None),
        P("wide", None, None),
    )
    return jax.shard_map(local, mesh=mesh, in_specs=in_specs, out_specs=out_specs, check_vma=False)
```

```python
import jax
import numpy as np
import jax.numpy as jnp
from jax import lax
from jax.experimental import pallas as pl
from jax.experimental.pallas import tpu as pltpu
from jax.sharding import PartitionSpec as P

HEADS = 16
KV_HEADS = 8
HEAD_DIM = 64
BF = jnp.bfloat16
F32 = jnp.float32
MESH = pl.DeviceIdType.MESH
EPSILON = 1e-06
THETA = 10000.0
HIGHEST = lax.Precision.HIGHEST


def rope_tables(count, head_dim):
    half_dim = head_dim // 2
    inverse = THETA ** (-jnp.arange(half_dim, dtype=jnp.float32) * 2.0 / head_dim)
    angles = jnp.arange(count, dtype=jnp.float32)[:, None] * inverse[None, :]
    return (jnp.cos(angles), jnp.sin(angles))


def turn(values, cosine, sine_part, direction):
    half_dim = values.shape[-1] // 2
    shape_here = (cosine.shape[0],) + (1,) * (values.ndim - 2) + (half_dim,)
    cosine = cosine.reshape(shape_here)
    sine_part = direction * sine_part.reshape(shape_here)
    first = values[..., :half_dim]
    second = values[..., half_dim:]
    return jnp.concatenate(
        [first * cosine - second * sine_part, second * cosine + first * sine_part], axis=-1
    )


def norm_forward(values, gain):
    scaling = lax.rsqrt(jnp.mean(values * values, axis=-1, keepdims=True) + EPSILON)
    return (values * scaling * gain, scaling)


def norm_backward(values, scaling, gain, incoming):
    unit_values = values * scaling
    gain_grad = jnp.sum(incoming * unit_values, axis=0)
    inner = incoming * gain
    input_grad = scaling * (
        inner - unit_values * jnp.mean(inner * unit_values, axis=-1, keepdims=True)
    )
    return (input_grad, gain_grad)


def visible(start, block_rows, key_places, length_here):
    query_places = start + jnp.arange(block_rows, dtype=jnp.int32)
    return (key_places[None, :] <= query_places[:, None]) & (key_places[None, :] < length_here)


def attend_forward(queries, keys_low, values_low, length_here, scaling):
    key_places = jnp.arange(keys_low.shape[1], dtype=jnp.int32)
    block_rows = queries.shape[3]

    def one_block(inputs):
        query_block, start = inputs
        scores = (
            jnp.einsum("kgqd,ksd->kgqs", query_block, keys_low, preferred_element_type=jnp.float32)
            * scaling
        )
        scores = jnp.where(visible(start, block_rows, key_places, length_here), scores, -1e30)
        highest = jnp.max(scores, axis=-1, keepdims=True)
        weights = jnp.exp(scores - highest)
        totals = jnp.sum(weights, axis=-1, keepdims=True)
        chances = (weights / totals).astype(jnp.bfloat16)
        context = jnp.einsum(
            "kgqs,ksd->kgqd", chances, values_low, preferred_element_type=jnp.float32
        )
        return (context.astype(jnp.bfloat16), (highest + jnp.log(totals))[..., 0])

    starts = jnp.arange(queries.shape[0], dtype=jnp.int32) * block_rows
    return lax.map(one_block, (queries, starts))


def attend_backward(queries, keys_low, values_low, context_grad, log_sums, length_here, scaling):
    key_places = jnp.arange(keys_low.shape[1], dtype=jnp.int32)
    block_rows = queries.shape[3]

    def one_block(carry, inputs):
        key_grad, value_grad = carry
        query_block, grad_block, sum_block, start = inputs
        scores = (
            jnp.einsum("kgqd,ksd->kgqs", query_block, keys_low, preferred_element_type=jnp.float32)
            * scaling
        )
        allowed = visible(start, block_rows, key_places, length_here)
        scores = jnp.where(allowed, scores, -1e30)
        chances = jnp.where(allowed, jnp.exp(scores - sum_block[..., None]), 0.0)
        chance_grad = jnp.einsum(
            "kgqd,ksd->kgqs", grad_block, values_low, preferred_element_type=jnp.float32
        )
        inner = jnp.sum(chances * chance_grad, axis=-1, keepdims=True)
        score_grad = (chances * (chance_grad - inner)).astype(jnp.bfloat16)
        query_grad = (
            jnp.einsum("kgqs,ksd->kgqd", score_grad, keys_low, preferred_element_type=jnp.float32)
            * scaling
        )
        key_grad = (
            key_grad
            + jnp.einsum(
                "kgqs,kgqd->ksd", score_grad, query_block, preferred_element_type=jnp.float32
            )
            * scaling
        )
        value_grad = value_grad + jnp.einsum(
            "kgqs,kgqd->ksd",
            chances.astype(jnp.bfloat16),
            grad_block,
            preferred_element_type=jnp.float32,
        )
        return ((key_grad, value_grad), query_grad)

    starts = jnp.arange(queries.shape[0], dtype=jnp.int32) * block_rows
    zeros = jnp.zeros(keys_low.shape, jnp.float32)
    (key_grad, value_grad), query_grad = lax.scan(
        one_block, (zeros, zeros), (queries, context_grad, log_sums, starts)
    )
    return (query_grad, key_grad, value_grad)


def ring_place(index, count):
    half = index // 2
    odd = index % 2
    return (1 - odd) * half + odd * (count - 1 - half)

def ring_index(place, count):
    odd = place // (count // 2)
    half = (1 - odd) * place + odd * (count - 1 - place)
    return 2 * half + odd


def add_low(one, two):
    return (one.astype(F32) + two.astype(F32)).astype(BF)

class Ring:
    def __init__(self, count):
        self.count = count
        self.me = lax.axis_index("wide")
        self.place = ring_place(self.me, count)
        self.peers = (self.at(1), self.at(-1))

    def at(self, shift):
        return ring_index((self.place + shift + 2 * self.count) % self.count, self.count)

def greet(wide_peers, narrow_peers):
    barrier = pltpu.get_barrier_semaphore()
    for peer in wide_peers:
        pl.semaphore_signal(barrier, inc=1, device_id={"wide": peer}, device_id_type=MESH)
    for peer in narrow_peers:
        pl.semaphore_signal(barrier, inc=1, device_id={"narrow": peer}, device_id_type=MESH)
    pl.semaphore_wait(barrier, len(wide_peers) + len(narrow_peers))

def remote(source, target, send, recv, **device):
    return pltpu.make_async_remote_copy(
        src_ref=source, dst_ref=target, send_sem=send, recv_sem=recv,
        device_id=device, device_id_type=MESH,
    )

def cuts(rows):
    first = (rows // 2 + 15) // 16 * 16
    return ((0, first), (first, rows - first))

def scatter_steps(ring, p_ref, held, send_sem, recv_sem, finish):
    count = ring.count
    lane = p_ref.shape[1] // 2

    def copy(way, step, k):
        sign = 1 if way == 0 else -1
        start, size = cuts(lane)[k]
        src = (
            p_ref.at[ring.at(-sign), pl.ds(way * lane + start, size)]
            if step == 0
            else held.at[way, step - 1, pl.ds(start, size)]
        )
        return remote(
            src, held.at[way, step, pl.ds(start, size)],
            send_sem.at[way, step, k], recv_sem.at[way, step, k], wide=ring.peers[way],
        )

    for step in range(count - 1):
        for k in range(2):
            for way in range(2):
                sign = 1 if way == 0 else -1
                start, size = cuts(lane)[k]
                if step > 0:
                    copy(way, step - 1, k).wait_recv()
                    span = pl.ds(start, size)
                    mine = p_ref[ring.at(-sign * (1 + step)), pl.ds(way * lane + start, size)]
                    held[way, step - 1, span] = add_low(held[way, step - 1, span], mine)
                copy(way, step, k).start()
        yield
    for k in range(2):
        for way in range(2):
            start, size = cuts(lane)[k]
            copy(way, count - 2, k).wait_recv()
            row = way * lane + start
            finish(
                row, size,
                held[way, count - 2, pl.ds(start, size)].astype(F32)
                + p_ref[ring.me, pl.ds(row, size)].astype(F32),
            )
    for step in range(count - 1):
        for k in range(2):
            for way in range(2):
                copy(way, step, k).wait_send()
    yield

def gather_steps(ring, o_ref, send_sem, recv_sem, own=None, left=0):
    count = ring.count
    hops = count // 2
    rows = o_ref.shape[1]
    live = lambda way, hop, k: hop < hops - 1 or k == way

    def copy(way, hop, k, shift):
        sign = 1 if way == 0 else -1
        start, size = cuts(rows)[k]
        block = o_ref.at[ring.at(-sign * (hop + shift)), pl.ds(start, size)]
        from_own = own is not None and hop == 0 and shift == 0
        return remote(
            own.at[pl.ds(start, size)] if from_own else block, block, send_sem.at[way, hop, k], recv_sem.at[way, hop, k], wide=ring.peers[way]
        )

    for hop in range(hops - left):
        for k in range(2):
            for way in range(2):
                if hop > 0:
                    copy(way, hop - 1, k, 1).wait_recv()
                if live(way, hop, k):
                    copy(way, hop, k, 0).start()
        yield
    for k in range(2):
        for way in range(2):
            if live(way, hops - left - 1, k):
                copy(way, hops - left - 1, k, 1).wait_recv()
    for hop in range(hops - left):
        for k in range(2):
            for way in range(2):
                if live(way, hop, k):
                    copy(way, hop, k, 0).wait_send()
    yield

def scatter_scratch(count, rows, cols):
    return [
        pltpu.VMEM((2, count - 1, rows // 2, cols), BF),
        pltpu.SemaphoreType.DMA((2, count - 1, 2)),
        pltpu.SemaphoreType.DMA((2, count - 1, 2)),
    ]

def gather_scratch(count):
    return [pltpu.SemaphoreType.DMA((2, count // 2, 2)), pltpu.SemaphoreType.DMA((2, count // 2, 2))]

def run(*makers):
    live = list(makers)
    while live:
        for one in list(live):
            if next(one, "end") == "end":
                live.remove(one)

def block_add(out, one, two, rows):
    def step(i, carry):
        span = pl.ds(pl.multiple_of(i * 128, 128), 128)
        out[span] = add_low(one[span], two[span])
        return carry
    lax.fori_loop(0, rows // 128, step, 0)


def nt(a, b):
    return lax.dot_general(a, b, (((1,), (1,)), ((), ())), preferred_element_type=F32)

def tn(a, b):
    return lax.dot_general(a, b, (((0,), (0,)), ((), ())), preferred_element_type=F32)

def nn(a, b):
    return jnp.dot(a, b, preferred_element_type=F32)

LANES = 128

def lane_of(shape):
    return lax.broadcasted_iota(jnp.int32, shape, len(shape) - 1)

def turn_lanes(values, cosine, signed_sine):
    low = lane_of(values.shape) % HEAD_DIM < HEAD_DIM // 2
    swapped = jnp.where(
        low,
        pltpu.roll(values, LANES - HEAD_DIM // 2, 1),
        pltpu.roll(values, HEAD_DIM // 2, 1),
    )
    return values * cosine + swapped * signed_sine

def doubled(tile, head):
    other = pltpu.roll(tile, HEAD_DIM, 1)
    low = lane_of(tile.shape) < HEAD_DIM
    return jnp.where(low, tile, other) if head == 0 else jnp.where(low, other, tile)

def stacked(tile):
    low = lane_of(tile.shape) < HEAD_DIM
    zero = jnp.zeros_like(tile)
    return jnp.concatenate([jnp.where(low, tile, zero), jnp.where(low, zero, tile)], axis=0)

def unstacked(turned):
    full = turned.T
    rows = full.shape[0] // 2
    return jnp.where(lane_of((rows, LANES)) < HEAD_DIM, full[:rows], full[rows:])

def masked_scores(keys, queries, key_start, query_start, length, causal):
    scores = nt(keys, queries) * HEAD_DIM ** (-0.5)
    half = queries.shape[0] // 2
    key_at = key_start + lax.broadcasted_iota(jnp.int32, scores.shape, 0)
    allowed = key_at < length
    if causal:
        query_at = query_start + lane_of(scores.shape) % half
        allowed = allowed & (key_at <= query_at)
    return jnp.where(allowed, scores, -1e30)

class Corner:
    def __init__(self):
        self.here = lax.axis_index("narrow")
        self.chip, self.core = self.here // 2, self.here % 2
        self.core_peer = 2 * self.chip + 1 - self.core
        self.chip_peer = 2 * (1 - self.chip) + self.core
        self.far_peer = 2 * (1 - self.chip) + 1 - self.core

class Share:
    def __init__(self, corner, ref, send, recv):
        self.corner, self.ref, self.sems = corner, ref, (send, recv)

    def copy(self, kind, k, owner, peer):
        start, size = cuts(self.ref.shape[1])[k]
        block = self.ref.at[owner, pl.ds(start, size)]
        return remote(block, block, self.sems[0].at[kind, k], self.sems[1].at[kind, k], narrow=peer)

    def start(self):
        c = self.corner
        for k in range(2):
            self.copy(1, k, c.here, c.chip_peer).start()
        for k in range(2):
            self.copy(0, k, c.here, c.core_peer).start()

    def wait_core(self):
        c = self.corner
        for k in range(2):
            self.copy(0, k, c.core_peer, c.core_peer).wait_recv()

    def wait_chip(self):
        c = self.corner
        for k in range(2):
            self.copy(1, k, c.chip_peer, c.chip_peer).wait_recv()
            self.copy(2, k, c.chip_peer, c.core_peer).start()

    def wait_far(self):
        c = self.corner
        for k in range(2):
            self.copy(2, k, c.far_peer, c.core_peer).wait_recv()

    def drain(self):
        c = self.corner
        for k in range(2):
            self.copy(0, k, c.here, c.core_peer).wait_send()
            self.copy(1, k, c.here, c.chip_peer).wait_send()
            self.copy(2, k, c.chip_peer, c.core_peer).wait_send()

    scratch = lambda: [pltpu.SemaphoreType.DMA((3, 2)), pltpu.SemaphoreType.DMA((3, 2))]

class Fold:
    def __init__(self, corner, out_c, got_c, out_x, got_x, held, c_send, c_recv, x_send, x_recv):
        self.corner, self.held = corner, held
        self.out_c, self.got_c, self.out_x, self.got_x = out_c, got_c, out_x, got_x
        self.sems = (c_send, c_recv, x_send, x_recv)

    def to_core(self, x):
        return remote(
            self.out_c.at[x], self.got_c.at[x], self.sems[0].at[x], self.sems[1].at[x],
            narrow=self.corner.core_peer,
        )

    def to_chip(self):
        return remote(self.out_x, self.got_x, self.sems[2], self.sems[3], narrow=self.corner.chip_peer)

    def give(self, block, part):
        x, c = block // 2, block % 2

        @pl.when(self.corner.core != c)
        def _():
            self.out_c[x] = part.astype(BF)
            self.to_core(x).start()

        @pl.when(self.corner.core == c)
        def _():
            self.held[x] = part

    def settle(self, block):
        x, c = block // 2, block % 2

        @pl.when(self.corner.core == c)
        def _():
            self.to_core(x).wait_recv()

            @pl.when(self.corner.chip != x)
            def _():
                self.out_x[...] = (self.held[x] + self.got_c[x].astype(F32)).astype(BF)
                self.to_chip().start()

    def total(self):
        chip = self.corner.chip
        near = self.held[chip] + self.got_c[chip].astype(F32)
        self.to_chip().wait_recv()
        return near + self.got_x[...].astype(F32)

    def drain(self):
        for x in range(2):
            self.to_core(x).wait_send()
        self.to_chip().wait_send()

    def scratch(rows, cols):
        return [
            pltpu.VMEM((2, rows, cols), BF),
            pltpu.VMEM((2, rows, cols), BF),
            pltpu.VMEM((rows, cols), BF),
            pltpu.VMEM((rows, cols), BF),
            pltpu.VMEM((2, rows, cols), F32),
            pltpu.SemaphoreType.DMA((2,)),
            pltpu.SemaphoreType.DMA((2,)),
            pltpu.SemaphoreType.DMA,
            pltpu.SemaphoreType.DMA,
        ]

def front_kernel(hidden, cotangent, routes, length, attn_gain, w_query, w_key, w_value, w_out, moe_gain, cosine, sine, count, experts_here, cid):
    rows, width = hidden.shape
    seq = 4 * rows
    query_cols, key_cols = w_query.shape[1], w_key.shape[1]
    picks = routes.shape[0]
    kv_here = key_cols // HEAD_DIM

    def kernel(*refs):
        refs = list(refs)
        take = lambda number: [refs.pop(0) for _ in range(number)]
        h_ref, cot_ref, route_ref, len_ref, g1_ref, wq_far, wk_far, wv_far, wout_ref, g2_ref, cos_ref, sin_ref = take(12)
        en_ref, ga_ref, whole_ref, q_ref, k_ref, v_ref, ctx_ref, lse_ref, mixed_ref, slots_ref, lab_all = take(11)
        kd, vd, s_scr, p_scr, wqkv_ref, lab_ref = take(6)
        share = take(2)
        fold = take(9)
        g_scr = take(2)
        l_send, l_recv, own_sem, w_sem = take(4)
        ring, corner = Ring(count), Corner()
        others = [(ring.me + shift) % count for shift in range(1, count)]
        w_loads = [
            pltpu.make_async_copy(src, wqkv_ref.at[:, pl.ds(start, size)], w_sem.at[k])
            for k, (src, start, size) in enumerate(
                ((wq_far, 0, query_cols), (wk_far, query_cols, key_cols), (wv_far, query_cols + key_cols, key_cols))
            )
        ]
        for c in w_loads:
            c.start()
        length_here = len_ref[0]
        lab_ref[0:picks] = route_ref[...]
        lab_ref[picks : 2 * picks] = jnp.full((picks, rows), length_here, jnp.int32)
        greet(others, [corner.core_peer, corner.chip_peer])

        g_ring = gather_steps(ring, ga_ref, *g_scr, own=cot_ref, left=1)
        next(g_ring)
        own_grad = pltpu.make_async_copy(cot_ref, ga_ref.at[ring.me], own_sem)
        own_grad.start()
        label_copy = lambda k, target: remote(
            lab_ref, lab_all.at[ring.me], l_send.at[k], l_recv.at[k], wide=target
        )
        for k, target in enumerate(others):
            label_copy(k, target).start()
        lab_all[ring.me] = lab_ref[...]

        source = h_ref[...].astype(F32)
        scale = lax.rsqrt(jnp.mean(source * source, axis=1, keepdims=True) + EPSILON)
        whole_ref[corner.here] = (source * scale * g1_ref[...]).astype(BF)
        sharing = Share(corner, whole_ref, *share)
        sharing.start()

        def project(block):
            span = pl.ds(pl.multiple_of(block * rows, rows), rows)
            lin = nn(whole_ref[block], wqkv_ref[...])
            cos, sin = cos_ref[span], sin_ref[span]
            for t in range(kv_here):
                lanes = slice(t * LANES, (t + 1) * LANES)
                q_ref[span, lanes] = turn_lanes(lin[:, lanes], cos, sin).astype(BF)
            keys = turn_lanes(lin[:, query_cols : query_cols + key_cols], cos, sin)
            values = lin[:, query_cols + key_cols :]
            k_ref[span] = keys.astype(BF)
            v_ref[span] = values.astype(BF)
            for t in range(kv_here):
                kd[t, span] = doubled(keys, t).astype(BF)
                vd[t, span] = doubled(values, t).astype(BF)

        for c in w_loads:
            c.wait()
        project(corner.here)
        sharing.wait_core()
        project(corner.core_peer)

        for k, target in enumerate(others):
            sender = (ring.me - (k + 1) + count) % count
            remote(lab_ref, lab_all.at[sender], l_send.at[k], l_recv.at[k], wide=target).wait_recv()
        places = corner.here * rows + lane_of((1, rows))
        first = ring.me * experts_here
        upper = jnp.where(
            lax.broadcasted_iota(jnp.int32, (rows, rows), 0) <= lane_of((rows, rows)), 1.0, 0.0
        ).astype(BF)

        def belongs(block, expert_rows):
            found = lab_all[block, 0:1] == expert_rows
            for k in range(1, picks):
                found = found | (lab_all[block, k : k + 1] == expert_rows)
            return found

        local_rows = lax.broadcasted_iota(jnp.int32, (8, rows), 0)
        own_rows = jnp.where(local_rows < experts_here, first + local_rows, -1)
        for b in range(count):
            mine = jnp.where(belongs(b, own_rows) & (places < lab_all[b, picks : picks + 1]), 1.0, 0.0)
            reached = nn(mine.astype(BF), upper)
            slots_ref[b] = jnp.where(mine > 0.0, reached, 0.0).astype(jnp.int32) - 1

        next(g_ring)
        sharing.wait_chip()
        project(corner.chip_peer)
        sharing.wait_far()
        project(corner.far_peer)

        folding = Fold(corner, *fold)
        before = None
        for block in (3, 2, 1, 0):
            span = pl.ds(block * rows, rows)
            for t in range(kv_here):
                lanes = slice(t * LANES, (t + 1) * LANES)
                queries = stacked(q_ref[span, lanes])
                highest = None
                for b in range(block + 1):
                    keys = pl.ds(b * rows, rows)
                    scores = masked_scores(kd[t, keys], queries, b * rows, block * rows, length_here, b == block)
                    s_scr[keys] = scores
                    top = jnp.max(scores, axis=0, keepdims=True)
                    highest = top if highest is None else jnp.maximum(highest, top)
                total = None
                for b in range(block + 1):
                    keys = pl.ds(b * rows, rows)
                    weights = jnp.exp(s_scr[keys] - highest)
                    p_scr[keys] = weights.astype(BF)
                    one = jnp.sum(weights, axis=0, keepdims=True)
                    total = one if total is None else total + one
                keys = pl.ds(0, (block + 1) * rows)
                context = tn(vd[t, keys], p_scr[keys]) / total
                ctx_ref[span, lanes] = unstacked(context).astype(BF)
                lse_ref[t * 4 + block : t * 4 + block + 1] = highest + jnp.log(total)
            folding.give(block, nn(ctx_ref[span], wout_ref[...]))
            if before is not None:
                folding.settle(before)
            before = block
            if block == 2:
                next(g_ring)
        folding.settle(before)
        mixed = source + folding.total()
        mixed_ref[...] = mixed
        scale = lax.rsqrt(jnp.mean(mixed * mixed, axis=1, keepdims=True) + EPSILON)
        en_ref[...] = (mixed * scale * g2_ref[...]).astype(BF)
        for _ in g_ring:
            pass
        for k, target in enumerate(others):
            label_copy(k, target).wait_send()
        own_grad.wait()
        sharing.drain()
        folding.drain()

    vmem = pl.BlockSpec(memory_space=pltpu.VMEM)
    far = pl.BlockSpec(memory_space=pl.ANY)
    shape = jax.ShapeDtypeStruct
    out_shape = [
        shape((rows, width), BF),
        shape((count, rows, width), BF),
        shape((4, rows, width), BF),
        shape((seq, query_cols), BF),
        shape((seq, key_cols), BF),
        shape((seq, key_cols), BF),
        shape((seq, query_cols), BF),
        shape((8, 2 * rows), F32),
        shape((rows, width), F32),
        shape((count, 8, rows), jnp.int32),
        shape((count, 2 * picks, rows), jnp.int32),
    ]
    scratch = [
        pltpu.VMEM((kv_here, seq, LANES), BF),
        pltpu.VMEM((kv_here, seq, LANES), BF),
        pltpu.VMEM((seq, 2 * rows), F32),
        pltpu.VMEM((seq, 2 * rows), BF),
        pltpu.VMEM((width, query_cols + 2 * key_cols), BF),
        pltpu.VMEM((2 * picks, rows), jnp.int32),
        *Share.scratch(),
        *Fold.scratch(rows, width),
        *gather_scratch(count),
        pltpu.SemaphoreType.DMA((count - 1,)),
        pltpu.SemaphoreType.DMA((count - 1,)),
        pltpu.SemaphoreType.DMA,
        pltpu.SemaphoreType.DMA((3,)),
    ]
    return pl.pallas_call(
        kernel,
        out_shape=out_shape,
        in_specs=[vmem, far, vmem, pl.BlockSpec(memory_space=pltpu.SMEM)] + [vmem] + [far] * 3 + [vmem] * 4,
        out_specs=[vmem, far] + [vmem] * (len(out_shape) - 2),
        scratch_shapes=scratch,
        compiler_params=pltpu.CompilerParams(
            collective_id=cid, has_side_effects=True, vmem_limit_bytes=56 * 2**20
        ),
    )(hidden, cotangent, routes, length, attn_gain, w_query, w_key, w_value, w_out, moe_gain, cosine, sine)


def middle_kernel(entry, grad_all, labels_all, slots, router_turned, w_gate_up, w_down, capacity, picks, cid):
    rows, width = entry.shape
    count = grad_all.shape[0]
    experts_here, _, ffe2 = w_gate_up.shape
    ffe = ffe2 // 2
    experts = router_turned.shape[0]
    hops = count // 2
    shifts = [0] + [s for hop in range(1, hops) for s in (hop, -hop)] + [hops]
    room = count * capacity
    quarter_up, quarter_down = width // 4, ffe // 4
    quarter = quarter_up + quarter_down

    def kernel(*refs):
        refs = list(refs)
        take = lambda number: [refs.pop(0) for _ in range(number)]
        en_far, ga_far, lab_all, slots_ref, wr_ref, wgu_far, wd_far = take(7)
        ob_ref, op_ref, c_far, keep_far, got_far, shares_ref, wait_far = take(7)
        wgu, wd, e_buf, g_buf, pg, act_s, x_s, s_s, b_buf, c_slot, got_a, gates, pick_buf, last_c, last_b = take(15)
        held = take(3)
        e_scr = take(2)
        w_sem, g_sem, c_sem, p_send, p_recv, a_send, a_recv, x_send, x_recv, o_sem, f_sem, en_sem, far_send, far_recv = take(14)
        ring, corner = Ring(count), Corner()
        others = [(ring.me + shift) % count for shift in range(1, count)]
        greet(others, [corner.core_peer, corner.chip_peer])

        def weights(e):
            return [
                pltpu.make_async_copy(wgu_far.at[e], wgu.at[e], w_sem.at[0, e]),
                pltpu.make_async_copy(wd_far.at[e], wd.at[e], w_sem.at[1, e]),
            ]

        def grads(p):
            block = ring.at(shifts[p])
            return pltpu.make_async_copy(ga_far.at[block], g_buf.at[block], g_sem.at[p])

        def far_grads(way, shift):
            sign = 1 if way == 0 else -1
            block = ring.at(-sign * (hops - 1 + shift))
            start, size = cuts(rows)[way]
            source = ga_far if shift == 0 else g_buf
            return remote(
                source.at[block, pl.ds(start, size)], g_buf.at[block, pl.ds(start, size)],
                far_send.at[way], far_recv.at[way], wide=ring.peers[way],
            )

        e_ring = gather_steps(ring, e_buf, *e_scr, own=en_far)
        next(e_ring)
        own_entry = pltpu.make_async_copy(en_far, e_buf.at[ring.me], en_sem)
        own_entry.start()
        for e in range(experts_here):
            for c in weights(e):
                c.start()
            if e == 0:
                for p in range(count - 1):
                    grads(p).start()

        places = corner.here * rows + lane_of((1, rows))
        first = ring.me * experts_here
        every = lax.broadcasted_iota(jnp.int32, (experts, rows), 0)
        local_rows = lax.broadcasted_iota(jnp.int32, (8, rows), 0)
        slot_rows = lax.broadcasted_iota(jnp.int32, (capacity, rows), 0)

        def gate(block, home):
            logits = nt(wr_ref[...], e_buf[block])
            member = lab_all[block, 0:1] == every
            for k in range(1, picks):
                member = member | (lab_all[block, k : k + 1] == every)
            masked = jnp.where(member, logits, -jnp.inf)
            raised = jnp.exp(masked - jnp.max(masked, axis=0, keepdims=True))
            shares = raised / jnp.sum(raised, axis=0, keepdims=True)
            if home:
                shares_ref[...] = shares
            kept = jnp.where(places < lab_all[block, picks : picks + 1], shares, 0.0)
            own = jnp.zeros((8, rows), F32)
            for e in range(experts_here):
                row = jnp.sum(jnp.where(every == first + e, kept, 0.0), axis=0, keepdims=True)
                own = jnp.where(local_rows == e, row, own)
            gates[block] = own

        def pick_rows(block, e):
            return slot_rows == slots_ref[block, pl.ds(e, 1), :]

        def gather_rows(block, e):
            found = pick_rows(block, e)
            chosen = jnp.where(found, 1.0, 0.0).astype(BF)
            gate_col = jnp.sum(jnp.where(found, gates[block, pl.ds(e, 1), :], 0.0), axis=1, keepdims=True)
            return found, nn(chosen, e_buf[block]).astype(BF), nn(chosen, g_buf[block]), gate_col

        def chain(numbers, e, result_rows, back_rows, row, await_weights=False):
            blocks = [ring.at(shifts[p]) for p in numbers]
            size = len(numbers) * capacity
            here = pl.ds(pl.multiple_of(row, capacity), size)
            span = pl.ds(numbers[0] * capacity, size)
            if await_weights:
                for c in weights(e):
                    c.wait()
            parts = [gather_rows(block, e) for block in blocks]
            entries = jnp.concatenate([p[1] for p in parts], axis=0)
            grad_rows = jnp.concatenate([p[2] for p in parts], axis=0)
            gate_col = jnp.concatenate([p[3] for p in parts], axis=0)
            slot_grad = (gate_col * grad_rows).astype(BF)
            pre = nn(entries, wgu[e])
            act_grad = nt(slot_grad, wd[e])
            gate_part = pre[:, :ffe]
            up_part = pre[:, ffe:]
            sig = jax.nn.sigmoid(gate_part)
            swish = gate_part * sig
            act = (swish * up_part).astype(BF)
            act_s[e, span] = act
            gate_grad = act_grad * up_part * sig * (1.0 + gate_part * (1.0 - sig))
            pre_grad = jnp.concatenate([gate_grad, act_grad * swish], axis=1).astype(BF)
            pg[e, span] = pre_grad
            result = nn(act, wd[e]).astype(BF).astype(F32)
            back_rows[here] = nt(pre_grad, wgu[e]).astype(BF)
            result_rows[here] = (gate_col * result).astype(BF)
            pick_col = jnp.sum(result * grad_rows, axis=1, keepdims=True)
            for i, block in enumerate(blocks):
                pick = jnp.sum(
                    jnp.where(parts[i][0], pick_col[i * capacity : (i + 1) * capacity], 0.0),
                    axis=0, keepdims=True,
                )
                pick_buf[block] = jnp.where(local_rows == e, pick, pick_buf[block])

        def combine(number, result_rows, back_rows, row_of):
            block = ring.at(shifts[number])
            chosen = jnp.concatenate(
                [jnp.where(pick_rows(block, e), 1.0, 0.0).astype(BF) for e in range(experts_here)], axis=0
            )
            windows = [pl.ds(row_of(e), capacity) for e in range(experts_here)]
            if number >= 2:
                results(number - 2).wait()
            c_slot[number % 2] = tn(chosen, jnp.concatenate([result_rows[w] for w in windows], axis=0)).astype(BF)
            results(number).start()
            b_buf[block] = tn(chosen, jnp.concatenate([back_rows[w] for w in windows], axis=0)).astype(BF)

        def tile(numbers, await_weights):
            size = len(numbers) * capacity
            for p in numbers:
                grads(p).wait()

            def one(e, carry):
                chain(numbers, e, x_s, s_s, e * size, await_weights)
                return carry

            lax.fori_loop(0, experts_here, one, 0)
            for i, number in enumerate(numbers):
                combine(number, x_s, s_s, lambda e: e * size + i * capacity)

        def results(number):
            return pltpu.make_async_copy(
                c_slot.at[number % 2], c_far.at[ring.at(shifts[number])], c_sem.at[number]
            )

        def put(row, size, got):
            ob_ref[pl.ds(row, size)] = got

        b_ring = scatter_steps(ring, b_buf, *held, put)
        pick_buf[...] = jnp.zeros_like(pick_buf)
        own_entry.wait()
        gate(ring.me, True)
        tile([0], True)
        for hop in range(1, hops - 1):
            next(e_ring)
            gate(ring.at(hop), False)
            gate(ring.at(-hop), False)
            if hop == 1:
                for way in range(2):
                    far_grads(way, 0).start()
            tile([2 * hop - 1, 2 * hop], False)
        def weight_grads(e):
            for p in range(count):
                _, entries, grad_rows, gate_col = gather_rows(ring.at(shifts[p]), e)
                span = pl.ds(p * capacity, capacity)
                x_s[span] = entries
                s_s[span] = (gate_col * grad_rows).astype(BF)

            def columns(j, carry):
                cols = pl.ds(pl.multiple_of(j * 256, 256), 256)
                wgu[e, :, cols] = tn(x_s[...], pg[e, :, cols]).astype(BF)
                wd[e, :, cols] = tn(act_s[e], s_s[:, cols]).astype(BF)
                return carry

            lax.fori_loop(0, width // 256, columns, 0)

        def pieces(e, owner):
            return (
                (wgu.at[e, pl.ds(owner * quarter_up, quarter_up)], 0, quarter_up),
                (wd.at[e, pl.ds(owner * quarter_down, quarter_down)], quarter_up, quarter_down),
            )

        landing = lambda e: got_a.at[e] if e < 2 else wait_far.at[e - 2]
        fetch = lambda e: pltpu.make_async_copy(wait_far.at[e - 2], got_a.at[e % 2], f_sem.at[e - 2])

        def to_core(e):
            return [
                remote(src, landing(e).at[x, pl.ds(start, size)], a_send.at[e, x, k], a_recv.at[e, x, k], narrow=corner.core_peer)
                for x in range(2)
                for k, (src, start, size) in enumerate(pieces(e, 2 * x + 1 - corner.core))
            ]

        def to_chip(e):
            return [
                remote(src, got_far.at[e, pl.ds(start, size)], x_send.at[e, k], x_recv.at[e, k], narrow=corner.chip_peer)
                for k, (src, start, size) in enumerate(pieces(e, 2 * (1 - corner.chip) + corner.core))
            ]

        def own_out(e):
            return [
                pltpu.make_async_copy(src, keep_far.at[e, pl.ds(start, size)], o_sem.at[e, k])
                for k, (src, start, size) in enumerate(pieces(e, corner.here))
            ]

        def send_core(e):
            for c in to_core(e):
                c.start()

        def first_sum(e):
            for c in to_core(e):
                c.wait_recv()
            if e >= 2:
                fetch(e).start()
                fetch(e).wait()
            for number in range(2):
                x = 1 - corner.chip if number == 0 else corner.chip
                for src, start, size in pieces(e, 2 * x + corner.core):
                    block_add(src, src, got_a.at[e % 2, x, pl.ds(start, size)], size)
                for c in to_chip(e) if number == 0 else own_out(e):
                    c.start()

        last = [count - 3, count - 2, count - 1]
        row_at = lambda e, i: (e * 3 + i) * capacity
        next(e_ring)
        gate(ring.at(hops - 1), False)
        gate(ring.at(1 - hops), False)
        for p in last[:2]:
            grads(p).wait()

        def several(start, stop, numbers):
            def one(e, carry):
                chain(numbers, e, last_c, last_b, row_at(e, numbers[0] - last[0]))
                return carry

            lax.fori_loop(start, stop, one, 0)

        several(0, 2, last[:2])
        for _ in e_ring:
            pass
        gate(ring.at(hops), False)
        for way in range(2):
            far_grads(way, 1).wait_recv()
        next(b_ring)
        chain(last[2:], 0, last_c, last_b, row_at(0, 2))
        weight_grads(0)
        send_core(0)
        chain(last[2:], 1, last_c, last_b, row_at(1, 2))
        several(2, 3, last[:2])
        first_sum(0)
        next(b_ring)
        several(3, experts_here, last[:2])
        weight_grads(1)
        send_core(1)
        several(2, experts_here, last[2:])
        first_sum(1)
        for i, number in enumerate(last):
            combine(number, last_c, last_b, lambda e: row_at(e, i))
        next(b_ring)
        pick_copy = lambda k, target: remote(
            pick_buf.at[target], op_ref.at[ring.me], p_send.at[k], p_recv.at[k], wide=target
        )
        for k, target in enumerate(others):
            pick_copy(k, target).start()
        op_ref[ring.me] = pick_buf[ring.me]
        for e in range(2, experts_here):
            weight_grads(e)
            send_core(e)
            next(b_ring)
            first_sum(e)
            next(b_ring, None)
        for _ in b_ring:
            pass
        for e in range(experts_here):
            for c in to_core(e):
                c.wait_send()
            for c in to_chip(e):
                c.wait()
            for c in own_out(e):
                c.wait()
        for number in range(max(0, count - 2), count):
            results(number).wait()
        for way in range(2):
            far_grads(way, 0).wait_send()
        for k, target in enumerate(others):
            sender = (ring.me - (k + 1) + count) % count
            remote(
                pick_buf.at[sender], op_ref.at[sender], p_send.at[k], p_recv.at[k], wide=target
            ).wait_recv()
            pick_copy(k, target).wait_send()

    vmem = pl.BlockSpec(memory_space=pltpu.VMEM)
    far = pl.BlockSpec(memory_space=pl.ANY)
    shape = jax.ShapeDtypeStruct
    out_shape = [
        shape((rows, width), F32),
        shape((count, 8, rows), F32),
        shape((count, rows, width), BF),
        shape((experts_here, quarter, width), BF),
        shape((experts_here, quarter, width), BF),
        shape((experts, rows), F32),
        shape((experts_here - 2, 2, quarter, width), BF),
    ]
    dma = pltpu.SemaphoreType.DMA
    scratch = [
        pltpu.VMEM(w_gate_up.shape, BF),
        pltpu.VMEM(w_down.shape, BF),
        pltpu.VMEM((count, rows, width), BF),
        pltpu.VMEM((count, rows, width), BF),
        pltpu.VMEM((experts_here, room, 2 * ffe), BF),
        pltpu.VMEM((experts_here, room, ffe), BF),
        pltpu.VMEM((room, width), BF),
        pltpu.VMEM((room, width), BF),
        pltpu.VMEM((count, rows, width), BF),
        pltpu.VMEM((2, rows, width), BF),
        pltpu.VMEM((2, 2, quarter, width), BF),
        pltpu.VMEM((count, 8, rows), F32),
        pltpu.VMEM((count, 8, rows), F32),
        pltpu.VMEM((3 * experts_here * capacity, width), BF),
        pltpu.VMEM((3 * experts_here * capacity, width), BF),
        *scatter_scratch(count, rows, width),
        *gather_scratch(count),
        dma((2, experts_here)), dma((count,)), dma((count,)),
        dma((count - 1,)), dma((count - 1,)),
        dma((experts_here, 2, 2)), dma((experts_here, 2, 2)),
        dma((experts_here, 2)), dma((experts_here, 2)), dma((experts_here, 2)), dma((experts_here - 2,)), dma, dma((2,)), dma((2,)),
    ]
    return pl.pallas_call(
        kernel,
        out_shape=out_shape,
        in_specs=[far, far, vmem, vmem, vmem, far, far],
        out_specs=[vmem, vmem, far, far, far, vmem, far],
        scratch_shapes=scratch,
        compiler_params=pltpu.CompilerParams(
            collective_id=cid, has_side_effects=True, vmem_limit_bytes=63 * 2**20
        ),
    )(entry, grad_all, labels_all, slots, router_turned, w_gate_up, w_down)


def tail_kernel(entry_home, pick_home, shares, router_turned, mixed, cotangent, hidden, length, attn_gain, moe_gain, w_query, w_key, w_value, w_out, queries, keys, values, context, whole, lse, cosine, sine, expert_part, kept, arrived, shapes, cid):
    count, rows, width = expert_part.shape
    seq = 4 * rows
    query_cols, key_cols = w_out.shape[0], w_key.shape[1]
    cols = query_cols + 2 * key_cols
    kv_here = key_cols // HEAD_DIM
    experts_all = router_turned.shape[0]
    small_rows = (experts_all + 2 + 15) // 16 * 16
    block = -(-(cols + query_cols + small_rows) // (32 * count)) * 32
    experts, quarter, _ = kept.shape
    up_shape, down_shape = shapes
    quarter_up, quarter_down = up_shape[1] // 4, down_shape[1] // 4
    base = [0, rows, 3 * rows, 6 * rows]
    small_at = cols + query_cols

    def kernel(*refs):
        refs = list(refs)
        take = lambda number: [refs.pop(0) for _ in range(number)]
        eh_ref, pick_ref, shares_ref, wr_ref, mixed_ref, cot_ref, h_ref, len_ref, g1_ref, g2_ref = take(10)
        wq_far, wk_far, wv_far, wout_ref, q_ref, k_ref, v_ref, ctx_ref, whole_ref, lse_ref, cos_ref, sin_ref = take(12)
        c_far, keep_far, got_far = take(3)
        out_ref, gh_ref, turned_ref, go_ref, small_ref, up_ref, down_ref = take(7)
        gw, mg_s, kd, vd, p_all, dp_scr, ds_scr, dctx, dk, dv, qg, packed, small_got, expert_sum, c_ref, sum_ref, own, got, wqkv_ref, wt_ref, gain_got = take(21)
        share, fold = take(2), take(9)
        c_sem, w_sem, o_sem = take(3)
        c_scr, s_scr, g_scr = take(3), take(3), take(2)
        sm_send, sm_recv, ga_send, ga_recv = take(4)
        c_send, c_recv, x_send, x_recv, f_send, f_recv, l_sem = take(7)
        ring, corner = Ring(count), Corner()
        greet(list(ring.peers), [corner.core_peer, corner.chip_peer, corner.far_peer])
        length_here = len_ref[0]

        own_loads = lambda e: [
            pltpu.make_async_copy(keep_far.at[e], own.at[e], o_sem.at[0, e]),
            pltpu.make_async_copy(got_far.at[e], got.at[e], o_sem.at[1, e]),
        ]
        w_loads = [
            pltpu.make_async_copy(src, wqkv_ref.at[:, pl.ds(start, size)], w_sem.at[k])
            for k, (src, start, size) in enumerate(
                ((wq_far, 0, query_cols), (wk_far, query_cols, key_cols), (wv_far, query_cols + key_cols, key_cols))
            )
        ]
        for c in w_loads:
            c.start()
        for e in range(experts):
            for c in own_loads(e):
                c.start()

        def own_sum(e):
            for c in own_loads(e):
                c.wait()
            block_add(own.at[e], own.at[e], got.at[e], quarter)
            send_out(e)
            for c in send(e, core_sems, corner.core_peer) + own_copy(e):
                c.start()

        def put(row, size, value):
            expert_sum[pl.ds(row, size)] = value

        c_load = pltpu.make_async_copy(c_far, c_ref, c_sem)
        c_load.start()
        c_ring = scatter_steps(ring, c_ref, *c_scr, put)

        def places(e, owner):
            mine = own.at[e]
            return (
                (mine.at[pl.ds(0, quarter_up)], up_ref.at[e, pl.ds(owner * quarter_up, quarter_up)]),
                (mine.at[pl.ds(quarter_up, quarter_down)], down_ref.at[e, pl.ds(owner * quarter_down, quarter_down)]),
            )

        def send(e, sems, peer):
            return [
                remote(src, dst, sems[0].at[e, k], sems[1].at[e, k], narrow=peer)
                for k, (src, dst) in enumerate(places(e, corner.here))
            ]

        def forward(e, owner, sems):
            return [
                remote(dst, dst, sems[0].at[e, k], sems[1].at[e, k], narrow=corner.core_peer)
                for k, (src, dst) in enumerate(places(e, owner))
            ]

        core_sems, chip_sems, far_sems = (c_send, c_recv), (x_send, x_recv), (f_send, f_recv)

        def own_copy(e):
            return [
                pltpu.make_async_copy(src, dst, l_sem.at[e, k])
                for k, (src, dst) in enumerate(places(e, corner.here))
            ]

        def send_out(e):
            for c in send(e, chip_sems, corner.chip_peer):
                c.start()

        def pass_on(e):
            for c in forward(e, corner.chip_peer, chip_sems):
                c.wait_recv()
            for c in forward(e, corner.chip_peer, far_sems):
                c.start()

        each = experts_all // count
        picked = jnp.concatenate([pick_ref[b, 0:each] for b in range(count)], axis=0)
        held_shares = shares_ref[...]
        logit_grad = held_shares * (picked - jnp.sum(held_shares * picked, axis=0, keepdims=True))
        high = logit_grad.astype(BF)
        low = (logit_grad - high.astype(F32)).astype(BF)
        entry_grad = eh_ref[...] + (tn(high, wr_ref[...]) + tn(low, wr_ref[...]))
        mixed_here = mixed_ref[...]
        scale = lax.rsqrt(jnp.mean(mixed_here * mixed_here, axis=1, keepdims=True) + EPSILON)
        unit = mixed_here * scale
        inner = entry_grad * g2_ref[...]
        from_norm = scale * (inner - unit * jnp.mean(inner * unit, axis=1, keepdims=True))
        at = corner.here * rows + lax.broadcasted_iota(jnp.int32, (rows, 1), 0)
        valid = jnp.where(at < length_here, 1.0, 0.0)
        mixed_grad = valid * cot_ref[...].astype(F32) + from_norm
        mg_s[...] = mixed_grad
        gw[corner.here] = mixed_grad.astype(BF)
        sharing = Share(corner, gw, *share)
        sharing.start()
        entry = (unit * g2_ref[...]).astype(BF)
        small_got[3] = jnp.concatenate(
            [
                nn(high, entry) + nn(low, entry),
                jnp.sum(entry_grad * unit, axis=0, keepdims=True),
                jnp.zeros((small_rows - experts_all - 1, width), F32),
            ],
            axis=0,
        ).astype(BF)
        peers = (corner.core_peer, corner.chip_peer, corner.far_peer)
        small_copy = lambda k, peer: remote(
            small_got.at[3], small_got.at[k], sm_send.at[k], sm_recv.at[k], narrow=peer
        )
        for k, peer in enumerate(peers):
            small_copy(k, peer).start()

        for t in range(kv_here):
            kd[t] = doubled(k_ref[...].astype(F32), t).astype(BF)
            vd[t] = doubled(v_ref[...].astype(F32), t).astype(BF)

        def chances(b):
            for t in range(kv_here):
                lanes = slice(t * LANES, (t + 1) * LANES)
                stack = stacked(q_ref[pl.ds(b * rows, rows), lanes])
                log_sum = lse_ref[t * 4 + b : t * 4 + b + 1]
                for kb in range(b + 1):
                    scores = masked_scores(
                        kd[t, pl.ds(kb * rows, rows)], stack, kb * rows, b * rows, length_here, kb == b
                    )
                    p_all[t, pl.ds(base[b] + kb * rows, rows)] = jnp.exp(scores - log_sum).astype(BF)

        def pull(owner):
            dctx[owner] = nt(gw[owner], wout_ref[...]).astype(BF)

        pull(corner.here)
        c_load.wait()
        next(c_ring)
        chances(3)
        next(c_ring)
        sharing.wait_core()
        pull(corner.core_peer)
        chances(2)
        next(c_ring)
        chances(1)
        chances(0)
        sharing.wait_chip()
        own_sum(0)
        pull(corner.chip_peer)
        sharing.wait_far()
        pull(corner.far_peer)
        dk[...] = jnp.zeros_like(dk)
        dv[...] = jnp.zeros_like(dv)

        folding = Fold(corner, *fold)
        before = None
        for b in (3, 2, 1, 0):
            span = pl.ds(b * rows, rows)
            cos, sin = cos_ref[span], sin_ref[span]
            for t in range(kv_here):
                lanes = slice(t * LANES, (t + 1) * LANES)
                stack = stacked(q_ref[span, lanes])
                grad_stack = stacked(dctx[b, :, lanes])
                inner = None
                for kb in range(b + 1):
                    chance = p_all[t, pl.ds(base[b] + kb * rows, rows)]
                    grad = nt(vd[t, pl.ds(kb * rows, rows)], grad_stack)
                    dp_scr[pl.ds(kb * rows, rows)] = grad
                    one = jnp.sum(chance.astype(F32) * grad, axis=0, keepdims=True)
                    inner = one if inner is None else inner + one
                for kb in range(b + 1):
                    key_span = pl.ds(kb * rows, rows)
                    chance = p_all[t, pl.ds(base[b] + kb * rows, rows)]
                    score_grad = (chance.astype(F32) * (dp_scr[key_span] - inner)).astype(BF)
                    ds_scr[key_span] = score_grad
                    dk[t, key_span] += nn(score_grad, stack)
                    dv[t, key_span] += nn(chance, grad_stack)
                every = pl.ds(0, (b + 1) * rows)
                query_grad = unstacked(tn(kd[t, every], ds_scr[every])) * HEAD_DIM ** (-0.5)
                qg[span, lanes] = turn_lanes(query_grad, cos, -sin).astype(BF)
            low_lanes = lane_of((rows, LANES)) < HEAD_DIM
            both = lambda ref, t: ref[t, span] + pltpu.roll(ref[t, span], HEAD_DIM, 1)
            key_grad = jnp.where(low_lanes, both(dk, 0), both(dk, 1)) * HEAD_DIM ** (-0.5)
            qg[span, query_cols : query_cols + key_cols] = turn_lanes(key_grad, cos, -sin).astype(BF)
            qg[span, query_cols + key_cols :] = jnp.where(low_lanes, both(dv, 0), both(dv, 1)).astype(BF)
            if b == 3:
                for c in w_loads:
                    c.wait()
            folding.give(b, nt(qg[span], wqkv_ref[...]))
            if before is not None:
                folding.settle(before)
            before = b
            next(c_ring)
            if b == 2:
                own_sum(1)
        folding.settle(before)

        def store(row, value):
            for start in range(0, value.shape[0], 16):
                size = min(16, value.shape[0] - start)
                at_row = row + start
                packed[at_row // block, pl.ds(at_row % block, size)] = value[start : start + size].astype(BF)

        weight_grad = tn(qg[...], whole_ref[...])
        wt_ref[...] = wqkv_ref[...].astype(F32).T
        gain_one = jnp.sum(weight_grad * wt_ref[...], axis=0, keepdims=True) / g1_ref[...]
        store(0, weight_grad)
        store(cols, tn(ctx_ref[...], gw[...].reshape(seq, width)))
        rest = small_at + small_rows
        store(rest, jnp.zeros((count * block - rest, width), F32))
        for k, peer in enumerate(peers):
            small_copy(k, peer).wait_recv()
        small_sum = sum(small_got[k].astype(F32) for k in range(4))
        row_at = lax.broadcasted_iota(jnp.int32, (small_rows, width), 0)
        store(small_at, jnp.where(row_at == experts_all + 1, gain_one, small_sum))

        def finish(row, size, got):
            sum_ref[ring.me, pl.ds(row, size)] = got.astype(BF)

        sums = scatter_steps(ring, packed, *s_scr, finish)
        next(sums)
        own_sum(2)
        own_sum(3)
        for _ in sums:
            pass
        for _ in gather_steps(ring, sum_ref, *g_scr):
            pass
        whole_sum = lambda row, size: jnp.concatenate(
            [sum_ref[b] for b in range(row // block, (row + size) // block)], axis=0
        )
        gain_got[3] = sum_ref[small_at // block, small_rows - 16 : small_rows]
        gain_copy = lambda k, peer: remote(
            gain_got.at[3], gain_got.at[k], ga_send.at[k], ga_recv.at[k], narrow=peer
        )
        for k, peer in enumerate(peers):
            gain_copy(k, peer).start()
        for row in range(0, cols, block):
            turned_ref[:, row : row + block] = sum_ref[row // block].astype(F32).T.astype(BF)
        go_ref[...] = whole_sum(cols, query_cols)
        normed_grad = folding.total()
        source = h_ref[...].astype(F32)
        scale = lax.rsqrt(jnp.mean(source * source, axis=1, keepdims=True) + EPSILON)
        unit = source * scale
        inner = normed_grad * g1_ref[...]
        from_norm = scale * (inner - unit * jnp.mean(inner * unit, axis=1, keepdims=True))
        gh_ref[...] = (mg_s[...] + from_norm).astype(BF)
        for e in range(2):
            pass_on(e)
        for _ in c_ring:
            pass
        out_ref[...] = (valid * (mixed_here + expert_sum[...])).astype(BF)
        for k, peer in enumerate(peers):
            gain_copy(k, peer).wait_recv()
        gain_sum = sum(gain_got[k].astype(F32) for k in range(4))
        small_ref[0 : small_rows - 16] = sum_ref[small_at // block, 0 : small_rows - 16]
        last_rows = small_rows - 16 + lax.broadcasted_iota(jnp.int32, (16, width), 0)
        small_ref[small_rows - 16 : small_rows] = jnp.where(
            last_rows == experts_all + 1, gain_sum, gain_got[3].astype(F32)
        ).astype(BF)
        for e in range(2, experts):
            pass_on(e)
        for k, peer in enumerate(peers):
            gain_copy(k, peer).wait_send()
        for k, peer in enumerate(peers):
            small_copy(k, peer).wait_send()
        for e in range(experts):
            for c in own_copy(e):
                c.wait()
            for c in send(e, chip_sems, corner.chip_peer) + send(e, core_sems, corner.core_peer):
                c.wait_send()
            for c in forward(e, corner.core_peer, core_sems):
                c.wait_recv()
            for c in forward(e, corner.chip_peer, far_sems):
                c.wait_send()
            for c in forward(e, corner.far_peer, far_sems):
                c.wait_recv()
        sharing.drain()
        folding.drain()

    vmem = pl.BlockSpec(memory_space=pltpu.VMEM)
    far = pl.BlockSpec(memory_space=pl.ANY)
    shape = jax.ShapeDtypeStruct
    out_shape = [
        shape((rows, width), BF),
        shape((rows, width), BF),
        shape((width, cols), BF),
        shape((query_cols, width), BF),
        shape((small_rows, width), BF),
        shape(up_shape, BF),
        shape(down_shape, BF),
    ]
    scratch = [
        pltpu.VMEM((4, rows, width), BF),
        pltpu.VMEM((rows, width), F32),
        pltpu.VMEM((kv_here, seq, LANES), BF),
        pltpu.VMEM((kv_here, seq, LANES), BF),
        pltpu.VMEM((kv_here, 10 * rows, 2 * rows), BF),
        pltpu.VMEM((seq, 2 * rows), F32),
        pltpu.VMEM((seq, 2 * rows), BF),
        pltpu.VMEM((4, rows, query_cols), BF),
        pltpu.VMEM((kv_here, seq, LANES), F32),
        pltpu.VMEM((kv_here, seq, LANES), F32),
        pltpu.VMEM((seq, cols), BF),
        pltpu.VMEM((count, block, width), BF),
        pltpu.VMEM((4, small_rows, width), BF),
        pltpu.VMEM((rows, width), F32),
        pltpu.VMEM((count, rows, width), BF),
        pltpu.VMEM((count, block, width), BF),
        pltpu.VMEM((experts, quarter, width), BF),
        pltpu.VMEM((experts, quarter, width), BF),
        pltpu.VMEM((width, cols), BF),
        pltpu.VMEM((cols, width), F32),
        pltpu.VMEM((4, 16, width), BF),
        *Share.scratch(),
        *Fold.scratch(rows, width),
        pltpu.SemaphoreType.DMA,
        pltpu.SemaphoreType.DMA((3,)),
        pltpu.SemaphoreType.DMA((2, experts)),
        *scatter_scratch(count, rows, width),
        *scatter_scratch(count, block, width),
        *gather_scratch(count),
        *[pltpu.SemaphoreType.DMA((3,))] * 4,
    ] + [pltpu.SemaphoreType.DMA((experts, 2))] * 7
    return pl.pallas_call(
        kernel,
        out_shape=out_shape,
        in_specs=[vmem] * 7 + [pl.BlockSpec(memory_space=pltpu.SMEM)] + [vmem] * 2 + [far] * 3 + [vmem] * 9 + [far] * 3,
        out_specs=[vmem] * 5 + [far] * 2,
        scratch_shapes=scratch,
        compiler_params=pltpu.CompilerParams(
            collective_id=cid, has_side_effects=True, vmem_limit_bytes=62 * 2**20
        ),
    )(entry_home, pick_home, shares, router_turned, mixed, cotangent, hidden, length, attn_gain, moe_gain,
      w_query, w_key, w_value, w_out, queries, keys, values, context, whole, lse, cosine, sine, expert_part, kept, arrived)


def final_kernel(out, grad_hidden, turned, out_grad, small, up_grad, down_grad, query_cols, key_cols, experts):
    here, width, ffe2 = up_grad.shape
    ffe = down_grad.shape[1]
    step = 256
    parts = [(0, e, r) for e in range(here) for r in range(0, width, step)]
    parts += [(1, e, r) for e in range(here) for r in range(0, ffe, step)]
    parts.sort(key=lambda p: (p[1], p[0], p[2]))

    def kernel(o_in, gh_in, t_in, go_in, s_in, up_in, down_in, o_ref, gh_ref, gq, gk, gv, go, g1, g2, gr, up_ref, down_ref, low, full, in_sem, out_sem):
        near = lambda i: (up_in, down_in)[parts[i][0]].at[parts[i][1], pl.ds(parts[i][2], step)]
        away = lambda i: (up_ref, down_ref)[parts[i][0]].at[parts[i][1], pl.ds(parts[i][2], step)]
        inward = lambda i: pltpu.make_async_copy(near(i), low.at[i], in_sem.at[i])
        outward = lambda i: pltpu.make_async_copy(full.at[i], away(i), out_sem.at[i])
        for i in range(len(parts)):
            inward(i).start()
        o_ref[...] = o_in[...]
        gh_ref[...] = gh_in[...]
        gq[...] = t_in[:, :query_cols].astype(F32)
        gk[...] = t_in[:, query_cols : query_cols + key_cols].astype(F32)
        gv[...] = t_in[:, query_cols + key_cols :].astype(F32)
        go[...] = go_in[...].astype(F32)
        rows = s_in[...].astype(F32)
        g1[...] = rows[experts + 1 : experts + 2]
        g2[...] = rows[experts : experts + 1]
        gr[...] = rows[:experts]
        for i in range(len(parts)):
            inward(i).wait()
            def widen(j, carry, i=i):
                span = pl.ds(pl.multiple_of(j * 32, 32), 32)
                full[i, span] = low[i, span].astype(F32)
                return carry

            lax.fori_loop(0, step // 32, widen, 0)
            outward(i).start()
        for i in range(len(parts)):
            outward(i).wait()

    shape = jax.ShapeDtypeStruct
    vmem = pl.BlockSpec(memory_space=pltpu.VMEM)
    far = pl.BlockSpec(memory_space=pl.ANY)
    small_shapes = [
        shape(out.shape, BF), shape(grad_hidden.shape, BF), shape((width, query_cols), F32),
        shape((width, key_cols), F32), shape((width, key_cols), F32), shape(out_grad.shape, F32),
        shape((1, width), F32), shape((1, width), F32), shape((experts, width), F32),
    ]
    return pl.pallas_call(
        kernel,
        out_shape=small_shapes + [shape(up_grad.shape, F32), shape(down_grad.shape, F32)],
        in_specs=[vmem] * 5 + [far] * 2,
        out_specs=[vmem] * 9 + [far] * 2,
        scratch_shapes=[
            pltpu.VMEM((len(parts), step, width), BF),
            pltpu.VMEM((len(parts), step, width), F32),
            pltpu.SemaphoreType.DMA((len(parts),)),
            pltpu.SemaphoreType.DMA((len(parts),)),
        ],
        compiler_params=pltpu.CompilerParams(vmem_limit_bytes=62 * 2**20),
    )(out, grad_hidden, turned, out_grad, small, up_grad, down_grad)


def turn_tables(count, head_dim):
    inverse = THETA ** (-np.arange(head_dim // 2, dtype=np.float32) * np.float32(2.0 / head_dim))
    angles = np.arange(count, dtype=np.float32)[:, None] * inverse.astype(np.float32)[None, :]
    cosine, sine = np.cos(angles), np.sin(angles)
    return (
        jnp.asarray(np.concatenate([cosine] * 4, axis=1), F32),
        jnp.asarray(np.concatenate([-sine, sine] * 2, axis=1), F32),
    )


def local_general(
    hidden,
    lengths,
    routes,
    cotangent,
    attn_gain,
    w_query,
    w_key,
    w_value,
    w_out,
    moe_gain,
    w_router,
    w_gate_up,
    w_down,
):
    rows_here = hidden.shape[1]
    width = hidden.shape[2]
    seq_len = rows_here * lax.axis_size("narrow")
    head_dim = HEAD_DIM
    group_size = HEADS // KV_HEADS
    kv_here = w_key.shape[1] // head_dim
    query_cols = kv_here * group_size * head_dim
    key_cols = kv_here * head_dim
    scaling = head_dim ** (-0.5)
    block_rows = min(512, seq_len)
    block_count = seq_len // block_rows
    length_here = lengths[0]
    offset = lax.axis_index("narrow") * rows_here
    local_places = offset + jnp.arange(rows_here, dtype=jnp.int32)
    valid = (local_places < length_here).astype(jnp.float32)[:, None]
    source = hidden[0].astype(jnp.float32)
    normed, scale_one = norm_forward(source, attn_gain)
    normed_low = normed.astype(jnp.bfloat16)
    whole = lax.all_gather(normed_low, "narrow", axis=0, tiled=True)
    w_qkv = jnp.concatenate([w_query, w_key, w_value], axis=1)
    projected = jnp.dot(whole, w_qkv, preferred_element_type=jnp.float32)
    cosine, sine_part = rope_tables(seq_len, head_dim)
    query_rot = turn(
        projected[:, :query_cols].reshape(seq_len, kv_here, group_size, head_dim),
        cosine,
        sine_part,
        1.0,
    )
    key_rot = turn(
        projected[:, query_cols : query_cols + key_cols].reshape(seq_len, kv_here, head_dim),
        cosine,
        sine_part,
        1.0,
    )
    queries = (
        query_rot.astype(jnp.bfloat16)
        .reshape(block_count, block_rows, kv_here, group_size, head_dim)
        .transpose(0, 2, 3, 1, 4)
    )
    keys_low = key_rot.astype(jnp.bfloat16).transpose(1, 0, 2)
    values_low = (
        projected[:, query_cols + key_cols :]
        .astype(jnp.bfloat16)
        .reshape(seq_len, kv_here, head_dim)
        .transpose(1, 0, 2)
    )
    context, log_sums = attend_forward(queries, keys_low, values_low, length_here, scaling)
    context_rows = context.transpose(0, 3, 1, 2, 4).reshape(seq_len, query_cols)
    piece = context_rows
    attn_part = lax.psum_scatter(
        jnp.dot(piece, w_out, preferred_element_type=jnp.float32).astype(jnp.bfloat16),
        "narrow",
        scatter_dimension=0,
        tiled=True,
    ).astype(jnp.float32)
    mixed = source + attn_part
    normed_two, scale_two = norm_forward(mixed, moe_gain)
    entry = normed_two.astype(jnp.bfloat16)
    logits = jnp.dot(entry, w_router, preferred_element_type=jnp.float32)
    route_here = routes[0]
    tokens_here, picks = route_here.shape
    expert_total = w_router.shape[1]
    capacity = 2 * tokens_here * picks // expert_total
    member = (
        route_here[:, :, None] == jnp.arange(expert_total, dtype=jnp.int32)[None, None, :]
    ).astype(jnp.int32)
    flat_member = member.reshape(tokens_here * picks, expert_total)
    earlier = jnp.cumsum(flat_member, axis=0) - flat_member
    slot_index = jnp.sum(earlier * flat_member, axis=1)
    places = route_here.reshape(-1) * capacity + slot_index
    member_float = member.astype(jnp.float32)
    chosen = jnp.einsum("tke,te->tk", member_float, logits, precision=HIGHEST)
    highest = jnp.max(chosen, axis=-1, keepdims=True)
    raised = jnp.exp(chosen - highest)
    shares = raised / jnp.sum(raised, axis=-1, keepdims=True)
    gates = shares * valid
    outgoing = (
        jnp.zeros((expert_total * capacity, width), jnp.bfloat16)
        .at[places]
        .set(jnp.repeat(entry, picks, axis=0))
    )
    received = lax.all_to_all(
        outgoing.reshape(expert_total, capacity, width),
        "wide",
        split_axis=0,
        concat_axis=1,
        tiled=True,
    )
    expert_pre = jnp.einsum("erd,edf->erf", received, w_gate_up, preferred_element_type=jnp.float32)
    ffe_width = w_down.shape[1]
    gate_part = expert_pre[..., :ffe_width]
    up_part = expert_pre[..., ffe_width:]
    sigmoid_gate = jax.nn.sigmoid(gate_part)
    swish = gate_part * sigmoid_gate
    act_low = (swish * up_part).astype(jnp.bfloat16)
    expert_result = jnp.einsum(
        "erf,efd->erd", act_low, w_down, preferred_element_type=jnp.float32
    ).astype(jnp.bfloat16)
    returned = lax.all_to_all(expert_result, "wide", split_axis=1, concat_axis=0, tiled=True)
    picked = returned.reshape(expert_total * capacity, width)[places].reshape(
        tokens_here, picks, width
    )
    expert_sum = jnp.einsum("tk,tkd->td", gates, picked, precision=HIGHEST)
    output_rows = (valid * (mixed + expert_sum)).astype(jnp.bfloat16)
    grad_rows_here = cotangent[0].astype(jnp.float32) * valid
    slot_grad = (gates[:, :, None] * grad_rows_here[:, None, :]).astype(jnp.bfloat16)
    grad_outgoing = (
        jnp.zeros((expert_total * capacity, width), jnp.bfloat16)
        .at[places]
        .set(slot_grad.reshape(tokens_here * picks, width))
    )
    grad_received = lax.all_to_all(
        grad_outgoing.reshape(expert_total, capacity, width),
        "wide",
        split_axis=0,
        concat_axis=1,
        tiled=True,
    )
    act_grad = jnp.einsum("erd,efd->erf", grad_received, w_down, preferred_element_type=jnp.float32)
    down_grad = jnp.einsum(
        "erf,erd->efd", act_low, grad_received, preferred_element_type=jnp.float32
    )
    gate_grad = act_grad * up_part * sigmoid_gate * (1.0 + gate_part * (1.0 - sigmoid_gate))
    pre_grad = jnp.concatenate([gate_grad, act_grad * swish], axis=-1).astype(jnp.bfloat16)
    gate_up_grad = jnp.einsum(
        "erd,erf->edf", received, pre_grad, preferred_element_type=jnp.float32
    )
    entry_back = jnp.einsum(
        "erf,edf->erd", pre_grad, w_gate_up, preferred_element_type=jnp.float32
    ).astype(jnp.bfloat16)
    entry_home = lax.all_to_all(entry_back, "wide", split_axis=1, concat_axis=0, tiled=True)
    entry_rows = entry_home.reshape(expert_total * capacity, width)[places].reshape(
        tokens_here, picks, width
    )
    entry_grad = jnp.sum(entry_rows, axis=1, dtype=jnp.float32)
    pick_grad = jnp.einsum("td,tkd->tk", grad_rows_here, picked, precision=HIGHEST) * valid
    chosen_grad = shares * (pick_grad - jnp.sum(shares * pick_grad, axis=-1, keepdims=True))
    logit_grad = jnp.einsum("tk,tke->te", chosen_grad, member_float, precision=HIGHEST)
    router_grad = lax.dot_general(
        entry.astype(jnp.float32), logit_grad, (((0,), (0,)), ((), ())), precision=HIGHEST
    )
    entry_grad = entry_grad + lax.dot_general(
        logit_grad, w_router.astype(jnp.float32), (((1,), (1,)), ((), ())), precision=HIGHEST
    )
    mixed_from_norm, gain_two_grad = norm_backward(mixed, scale_two, moe_gain, entry_grad)
    mixed_grad = grad_rows_here + mixed_from_norm
    attn_grad_low = mixed_grad.astype(jnp.bfloat16)
    grad_whole = lax.all_gather(attn_grad_low, "narrow", axis=0, tiled=True)
    context_grad = lax.dot_general(
        grad_whole, w_out, (((1,), (1,)), ((), ())), preferred_element_type=jnp.float32
    ).astype(jnp.bfloat16)
    out_grad = lax.dot_general(
        context_rows, grad_whole, (((0,), (0,)), ((), ())), preferred_element_type=jnp.float32
    )
    context_blocks = context_grad.reshape(
        block_count, block_rows, kv_here, group_size, head_dim
    ).transpose(0, 2, 3, 1, 4)
    query_grad, key_grad, value_grad = attend_backward(
        queries, keys_low, values_low, context_blocks, log_sums, length_here, scaling
    )
    query_rows = turn(
        query_grad.transpose(0, 3, 1, 2, 4).reshape(seq_len, kv_here, group_size, head_dim),
        cosine,
        sine_part,
        -1.0,
    )
    key_rows = turn(key_grad.transpose(1, 0, 2), cosine, sine_part, -1.0)
    value_rows = value_grad.transpose(1, 0, 2)
    qkv_grad = jnp.concatenate(
        [
            query_rows.reshape(seq_len, query_cols),
            key_rows.reshape(seq_len, key_cols),
            value_rows.reshape(seq_len, key_cols),
        ],
        axis=1,
    ).astype(jnp.bfloat16)
    qkv_weight_grad = lax.dot_general(
        whole, qkv_grad, (((0,), (0,)), ((), ())), preferred_element_type=jnp.float32
    )
    piece = qkv_grad
    normed_grad = lax.psum_scatter(
        lax.dot_general(
            piece, w_qkv, (((1,), (1,)), ((), ())), preferred_element_type=jnp.float32
        ).astype(jnp.bfloat16),
        "narrow",
        scatter_dimension=0,
        tiled=True,
    ).astype(jnp.float32)
    source_from_norm, gain_one_grad = norm_backward(source, scale_one, attn_gain, normed_grad)
    grad_input = (mixed_grad + source_from_norm).astype(jnp.bfloat16)
    gate_up_grad, down_grad, router_grad, gain_one_grad, gain_two_grad = (
        lax.psum(gate_up_grad.astype(jnp.bfloat16), "narrow").astype(jnp.float32),
        lax.psum(down_grad.astype(jnp.bfloat16), "narrow").astype(jnp.float32),
        lax.psum(router_grad.astype(jnp.bfloat16), "narrow").astype(jnp.float32),
        lax.psum(gain_one_grad.astype(jnp.bfloat16), "narrow").astype(jnp.float32),
        lax.psum(gain_two_grad.astype(jnp.bfloat16), "narrow").astype(jnp.float32),
    )
    qkv_weight_grad, out_grad, router_grad, gain_one_grad, gain_two_grad = (
        lax.psum(qkv_weight_grad.astype(jnp.bfloat16), "wide").astype(jnp.float32),
        lax.psum(out_grad.astype(jnp.bfloat16), "wide").astype(jnp.float32),
        lax.psum(router_grad.astype(jnp.bfloat16), "wide").astype(jnp.float32),
        lax.psum(gain_one_grad.astype(jnp.bfloat16), "wide").astype(jnp.float32),
        lax.psum(gain_two_grad.astype(jnp.bfloat16), "wide").astype(jnp.float32),
    )
    query_weight_grad = qkv_weight_grad[:, :query_cols]
    key_weight_grad = qkv_weight_grad[:, query_cols : query_cols + key_cols]
    value_weight_grad = qkv_weight_grad[:, query_cols + key_cols :]
    return (
        output_rows[None],
        grad_input[None],
        gain_one_grad,
        query_weight_grad,
        key_weight_grad,
        value_weight_grad,
        out_grad,
        gain_two_grad,
        router_grad,
        gate_up_grad,
        down_grad,
    )


def local(
    hidden,
    lengths,
    routes,
    cotangent,
    attn_gain,
    w_query,
    w_key,
    w_value,
    w_out,
    moe_gain,
    w_router,
    w_gate_up,
    w_down,
):
    kv_here = w_key.shape[1] // HEAD_DIM
    rows, width = hidden.shape[1:]
    if lax.axis_size("narrow") != 4 or kv_here != 2 or rows != 256:
        return local_general(
            hidden, lengths, routes, cotangent, attn_gain, w_query, w_key, w_value, w_out,
            moe_gain, w_router, w_gate_up, w_down,
        )
    count = lax.axis_size("wide")
    picks = routes.shape[2]
    expert_total = w_router.shape[1]
    expert_here = w_gate_up.shape[0]
    capacity = 2 * rows * picks // expert_total
    query_cols, key_cols = w_query.shape[1], w_key.shape[1]
    cosine, sine = turn_tables(4 * rows, HEAD_DIM)
    router_turned = w_router.T
    gain_one, gain_two = attn_gain[None], moe_gain[None]
    entry, grad_all, whole, queries, keys, values, context, lse, mixed, slots, labels_all = front_kernel(
        hidden[0], cotangent[0], routes[0].T, lengths, gain_one, w_query, w_key, w_value, w_out, gain_two,
        cosine, sine, count, expert_here, 1,
    )
    entry_home, pick_home, expert_part, kept, arrived, shares, _ = middle_kernel(
        entry, grad_all, labels_all, slots, router_turned, w_gate_up, w_down, capacity, picks, 2
    )
    results = tail_kernel(
        entry_home, pick_home, shares, router_turned, mixed,
        cotangent[0], hidden[0], lengths, gain_one, gain_two, w_query, w_key, w_value, w_out, queries, keys,
        values, context, whole.reshape(4 * rows, width), lse, cosine, sine, expert_part, kept, arrived,
        (w_gate_up.shape, w_down.shape), 3,
    )
    out, grad_hidden, grad_q, grad_k, grad_v, grad_out, grad_one, grad_two, grad_router, grad_up, grad_down = final_kernel(
        *results, query_cols, key_cols, expert_total
    )
    return (
        out[None], grad_hidden[None], grad_one[0], grad_q, grad_k, grad_v, grad_out, grad_two[0], grad_router.T,
        grad_up, grad_down,
    )


def solution(mesh):
    in_specs = (
        P("wide", "narrow", None),
        P("wide"),
        P("wide", "narrow", None),
        P("wide", "narrow", None),
        P(),
        P(None, "narrow"),
        P(None, "narrow"),
        P(None, "narrow"),
        P("narrow", None),
        P(),
        P(),
        P("wide", None, None),
        P("wide", None, None),
    )
    out_specs = (
        P("wide", "narrow", None),
        P("wide", "narrow", None),
        P(),
        P(None, "narrow"),
        P(None, "narrow"),
        P(None, "narrow"),
        P("narrow", None),
        P(),
        P(),
        P("wide", None, None),
        P("wide", None, None),
    )
    return jax.shard_map(local, mesh=mesh, in_specs=in_specs, out_specs=out_specs, check_vma=False)
```

```python
import jax
import numpy as np
import jax.numpy as jnp
from jax import lax
from jax.experimental import pallas as pl
from jax.experimental.pallas import tpu as pltpu
from jax.sharding import PartitionSpec as P

HEADS = 16
KV_HEADS = 8
HEAD_DIM = 64
BF = jnp.bfloat16
F32 = jnp.float32
MESH = pl.DeviceIdType.MESH
EPSILON = 1e-06
THETA = 10000.0
HIGHEST = lax.Precision.HIGHEST


def rope_tables(count, head_dim):
    half_dim = head_dim // 2
    inverse = THETA ** (-jnp.arange(half_dim, dtype=jnp.float32) * 2.0 / head_dim)
    angles = jnp.arange(count, dtype=jnp.float32)[:, None] * inverse[None, :]
    return (jnp.cos(angles), jnp.sin(angles))


def turn(values, cosine, sine_part, direction):
    half_dim = values.shape[-1] // 2
    shape_here = (cosine.shape[0],) + (1,) * (values.ndim - 2) + (half_dim,)
    cosine = cosine.reshape(shape_here)
    sine_part = direction * sine_part.reshape(shape_here)
    first = values[..., :half_dim]
    second = values[..., half_dim:]
    return jnp.concatenate(
        [first * cosine - second * sine_part, second * cosine + first * sine_part], axis=-1
    )


def norm_forward(values, gain):
    scaling = lax.rsqrt(jnp.mean(values * values, axis=-1, keepdims=True) + EPSILON)
    return (values * scaling * gain, scaling)


def norm_backward(values, scaling, gain, incoming):
    unit_values = values * scaling
    gain_grad = jnp.sum(incoming * unit_values, axis=0)
    inner = incoming * gain
    input_grad = scaling * (
        inner - unit_values * jnp.mean(inner * unit_values, axis=-1, keepdims=True)
    )
    return (input_grad, gain_grad)


def visible(start, block_rows, key_places, length_here):
    query_places = start + jnp.arange(block_rows, dtype=jnp.int32)
    return (key_places[None, :] <= query_places[:, None]) & (key_places[None, :] < length_here)


def attend_forward(queries, keys_low, values_low, length_here, scaling):
    key_places = jnp.arange(keys_low.shape[1], dtype=jnp.int32)
    block_rows = queries.shape[3]

    def one_block(inputs):
        query_block, start = inputs
        scores = (
            jnp.einsum("kgqd,ksd->kgqs", query_block, keys_low, preferred_element_type=jnp.float32)
            * scaling
        )
        scores = jnp.where(visible(start, block_rows, key_places, length_here), scores, -1e30)
        highest = jnp.max(scores, axis=-1, keepdims=True)
        weights = jnp.exp(scores - highest)
        totals = jnp.sum(weights, axis=-1, keepdims=True)
        chances = (weights / totals).astype(jnp.bfloat16)
        context = jnp.einsum(
            "kgqs,ksd->kgqd", chances, values_low, preferred_element_type=jnp.float32
        )
        return (context.astype(jnp.bfloat16), (highest + jnp.log(totals))[..., 0])

    starts = jnp.arange(queries.shape[0], dtype=jnp.int32) * block_rows
    return lax.map(one_block, (queries, starts))


def attend_backward(queries, keys_low, values_low, context_grad, log_sums, length_here, scaling):
    key_places = jnp.arange(keys_low.shape[1], dtype=jnp.int32)
    block_rows = queries.shape[3]

    def one_block(carry, inputs):
        key_grad, value_grad = carry
        query_block, grad_block, sum_block, start = inputs
        scores = (
            jnp.einsum("kgqd,ksd->kgqs", query_block, keys_low, preferred_element_type=jnp.float32)
            * scaling
        )
        allowed = visible(start, block_rows, key_places, length_here)
        scores = jnp.where(allowed, scores, -1e30)
        chances = jnp.where(allowed, jnp.exp(scores - sum_block[..., None]), 0.0)
        chance_grad = jnp.einsum(
            "kgqd,ksd->kgqs", grad_block, values_low, preferred_element_type=jnp.float32
        )
        inner = jnp.sum(chances * chance_grad, axis=-1, keepdims=True)
        score_grad = (chances * (chance_grad - inner)).astype(jnp.bfloat16)
        query_grad = (
            jnp.einsum("kgqs,ksd->kgqd", score_grad, keys_low, preferred_element_type=jnp.float32)
            * scaling
        )
        key_grad = (
            key_grad
            + jnp.einsum(
                "kgqs,kgqd->ksd", score_grad, query_block, preferred_element_type=jnp.float32
            )
            * scaling
        )
        value_grad = value_grad + jnp.einsum(
            "kgqs,kgqd->ksd",
            chances.astype(jnp.bfloat16),
            grad_block,
            preferred_element_type=jnp.float32,
        )
        return ((key_grad, value_grad), query_grad)

    starts = jnp.arange(queries.shape[0], dtype=jnp.int32) * block_rows
    zeros = jnp.zeros(keys_low.shape, jnp.float32)
    (key_grad, value_grad), query_grad = lax.scan(
        one_block, (zeros, zeros), (queries, context_grad, log_sums, starts)
    )
    return (query_grad, key_grad, value_grad)


def ring_place(index, count):
    half = index // 2
    odd = index % 2
    return (1 - odd) * half + odd * (count - 1 - half)

def ring_index(place, count):
    odd = place // (count // 2)
    half = (1 - odd) * place + odd * (count - 1 - place)
    return 2 * half + odd


def add_low(one, two):
    return (one.astype(F32) + two.astype(F32)).astype(BF)

class Ring:
    def __init__(self, count):
        self.count = count
        self.me = lax.axis_index("wide")
        self.place = ring_place(self.me, count)
        self.peers = (self.at(1), self.at(-1))

    def at(self, shift):
        return ring_index((self.place + shift + 2 * self.count) % self.count, self.count)

def greet(wide_peers, narrow_peers):
    barrier = pltpu.get_barrier_semaphore()
    for peer in wide_peers:
        pl.semaphore_signal(barrier, inc=1, device_id={"wide": peer}, device_id_type=MESH)
    for peer in narrow_peers:
        pl.semaphore_signal(barrier, inc=1, device_id={"narrow": peer}, device_id_type=MESH)
    pl.semaphore_wait(barrier, len(wide_peers) + len(narrow_peers))

def remote(source, target, send, recv, **device):
    return pltpu.make_async_remote_copy(
        src_ref=source, dst_ref=target, send_sem=send, recv_sem=recv,
        device_id=device, device_id_type=MESH,
    )

def cuts(rows):
    first = (rows // 2 + 15) // 16 * 16
    return ((0, first), (first, rows - first))

def scatter_steps(ring, p_ref, held, send_sem, recv_sem, finish):
    count = ring.count
    lane = p_ref.shape[1] // 2

    def copy(way, step, k):
        sign = 1 if way == 0 else -1
        start, size = cuts(lane)[k]
        src = (
            p_ref.at[ring.at(-sign), pl.ds(way * lane + start, size)]
            if step == 0
            else held.at[way, step - 1, pl.ds(start, size)]
        )
        return remote(
            src, held.at[way, step, pl.ds(start, size)],
            send_sem.at[way, step, k], recv_sem.at[way, step, k], wide=ring.peers[way],
        )

    for step in range(count - 1):
        for k in range(2):
            for way in range(2):
                sign = 1 if way == 0 else -1
                start, size = cuts(lane)[k]
                if step > 0:
                    copy(way, step - 1, k).wait_recv()
                    span = pl.ds(start, size)
                    mine = p_ref[ring.at(-sign * (1 + step)), pl.ds(way * lane + start, size)]
                    held[way, step - 1, span] = add_low(held[way, step - 1, span], mine)
                copy(way, step, k).start()
        yield
    for k in range(2):
        for way in range(2):
            start, size = cuts(lane)[k]
            copy(way, count - 2, k).wait_recv()
            row = way * lane + start
            finish(
                row, size,
                held[way, count - 2, pl.ds(start, size)].astype(F32)
                + p_ref[ring.me, pl.ds(row, size)].astype(F32),
            )
    for step in range(count - 1):
        for k in range(2):
            for way in range(2):
                copy(way, step, k).wait_send()
    yield

def gather_steps(ring, o_ref, send_sem, recv_sem, own=None, left=0):
    count = ring.count
    hops = count // 2
    rows = o_ref.shape[1]
    live = lambda way, hop, k: hop < hops - 1 or k == way

    def copy(way, hop, k, shift):
        sign = 1 if way == 0 else -1
        start, size = cuts(rows)[k]
        block = o_ref.at[ring.at(-sign * (hop + shift)), pl.ds(start, size)]
        from_own = own is not None and hop == 0 and shift == 0
        return remote(
            own.at[pl.ds(start, size)] if from_own else block, block, send_sem.at[way, hop, k], recv_sem.at[way, hop, k], wide=ring.peers[way]
        )

    for hop in range(hops - left):
        for k in range(2):
            for way in range(2):
                if hop > 0:
                    copy(way, hop - 1, k, 1).wait_recv()
                if live(way, hop, k):
                    copy(way, hop, k, 0).start()
        yield
    for k in range(2):
        for way in range(2):
            if live(way, hops - left - 1, k):
                copy(way, hops - left - 1, k, 1).wait_recv()
    for hop in range(hops - left):
        for k in range(2):
            for way in range(2):
                if live(way, hop, k):
                    copy(way, hop, k, 0).wait_send()
    yield

def scatter_scratch(count, rows, cols):
    return [
        pltpu.VMEM((2, count - 1, rows // 2, cols), BF),
        pltpu.SemaphoreType.DMA((2, count - 1, 2)),
        pltpu.SemaphoreType.DMA((2, count - 1, 2)),
    ]

def gather_scratch(count):
    return [pltpu.SemaphoreType.DMA((2, count // 2, 2)), pltpu.SemaphoreType.DMA((2, count // 2, 2))]

def run(*makers):
    live = list(makers)
    while live:
        for one in list(live):
            if next(one, "end") == "end":
                live.remove(one)

def block_add(out, one, two, rows):
    def step(i, carry):
        span = pl.ds(pl.multiple_of(i * 128, 128), 128)
        out[span] = add_low(one[span], two[span])
        return carry
    lax.fori_loop(0, rows // 128, step, 0)


def nt(a, b):
    return lax.dot_general(a, b, (((1,), (1,)), ((), ())), preferred_element_type=F32)

def tn(a, b):
    return lax.dot_general(a, b, (((0,), (0,)), ((), ())), preferred_element_type=F32)

def nn(a, b):
    return jnp.dot(a, b, preferred_element_type=F32)

LANES = 128

def lane_of(shape):
    return lax.broadcasted_iota(jnp.int32, shape, len(shape) - 1)

def turn_lanes(values, cosine, signed_sine):
    low = lane_of(values.shape) % HEAD_DIM < HEAD_DIM // 2
    swapped = jnp.where(
        low,
        pltpu.roll(values, LANES - HEAD_DIM // 2, 1),
        pltpu.roll(values, HEAD_DIM // 2, 1),
    )
    return values * cosine + swapped * signed_sine

def doubled(tile, head):
    other = pltpu.roll(tile, HEAD_DIM, 1)
    low = lane_of(tile.shape) < HEAD_DIM
    return jnp.where(low, tile, other) if head == 0 else jnp.where(low, other, tile)

def stacked(tile):
    low = lane_of(tile.shape) < HEAD_DIM
    zero = jnp.zeros_like(tile)
    return jnp.concatenate([jnp.where(low, tile, zero), jnp.where(low, zero, tile)], axis=0)

def unstacked(turned):
    full = turned.T
    rows = full.shape[0] // 2
    return jnp.where(lane_of((rows, LANES)) < HEAD_DIM, full[:rows], full[rows:])

def masked_scores(keys, queries, key_start, query_start, length, causal):
    scores = nt(keys, queries) * HEAD_DIM ** (-0.5)
    half = queries.shape[0] // 2
    key_at = key_start + lax.broadcasted_iota(jnp.int32, scores.shape, 0)
    allowed = key_at < length
    if causal:
        query_at = query_start + lane_of(scores.shape) % half
        allowed = allowed & (key_at <= query_at)
    return jnp.where(allowed, scores, -1e30)

class Corner:
    def __init__(self):
        self.here = lax.axis_index("narrow")
        self.chip, self.core = self.here // 2, self.here % 2
        self.core_peer = 2 * self.chip + 1 - self.core
        self.chip_peer = 2 * (1 - self.chip) + self.core
        self.far_peer = 2 * (1 - self.chip) + 1 - self.core

class Share:
    def __init__(self, corner, ref, send, recv):
        self.corner, self.ref, self.sems = corner, ref, (send, recv)

    def copy(self, kind, k, owner, peer):
        start, size = cuts(self.ref.shape[1])[k]
        block = self.ref.at[owner, pl.ds(start, size)]
        return remote(block, block, self.sems[0].at[kind, k], self.sems[1].at[kind, k], narrow=peer)

    def start(self):
        c = self.corner
        for k in range(2):
            self.copy(1, k, c.here, c.chip_peer).start()
        for k in range(2):
            self.copy(0, k, c.here, c.core_peer).start()

    def wait_core(self):
        c = self.corner
        for k in range(2):
            self.copy(0, k, c.core_peer, c.core_peer).wait_recv()

    def wait_chip(self):
        c = self.corner
        for k in range(2):
            self.copy(1, k, c.chip_peer, c.chip_peer).wait_recv()
            self.copy(2, k, c.chip_peer, c.core_peer).start()

    def wait_far(self):
        c = self.corner
        for k in range(2):
            self.copy(2, k, c.far_peer, c.core_peer).wait_recv()

    def drain(self):
        c = self.corner
        for k in range(2):
            self.copy(0, k, c.here, c.core_peer).wait_send()
            self.copy(1, k, c.here, c.chip_peer).wait_send()
            self.copy(2, k, c.chip_peer, c.core_peer).wait_send()

    scratch = lambda: [pltpu.SemaphoreType.DMA((3, 2)), pltpu.SemaphoreType.DMA((3, 2))]

class Fold:
    def __init__(self, corner, out_c, got_c, out_x, got_x, held, c_send, c_recv, x_send, x_recv):
        self.corner, self.held = corner, held
        self.out_c, self.got_c, self.out_x, self.got_x = out_c, got_c, out_x, got_x
        self.sems = (c_send, c_recv, x_send, x_recv)

    def to_core(self, x):
        return remote(
            self.out_c.at[x], self.got_c.at[x], self.sems[0].at[x], self.sems[1].at[x],
            narrow=self.corner.core_peer,
        )

    def to_chip(self):
        return remote(self.out_x, self.got_x, self.sems[2], self.sems[3], narrow=self.corner.chip_peer)

    def give(self, block, part):
        x, c = block // 2, block % 2

        @pl.when(self.corner.core != c)
        def _():
            self.out_c[x] = part.astype(BF)
            self.to_core(x).start()

        @pl.when(self.corner.core == c)
        def _():
            self.held[x] = part

    def settle(self, block):
        x, c = block // 2, block % 2

        @pl.when(self.corner.core == c)
        def _():
            self.to_core(x).wait_recv()

            @pl.when(self.corner.chip != x)
            def _():
                self.out_x[...] = (self.held[x] + self.got_c[x].astype(F32)).astype(BF)
                self.to_chip().start()

    def total(self):
        chip = self.corner.chip
        near = self.held[chip] + self.got_c[chip].astype(F32)
        self.to_chip().wait_recv()
        return near + self.got_x[...].astype(F32)

    def drain(self):
        for x in range(2):
            self.to_core(x).wait_send()
        self.to_chip().wait_send()

    def scratch(rows, cols):
        return [
            pltpu.VMEM((2, rows, cols), BF),
            pltpu.VMEM((2, rows, cols), BF),
            pltpu.VMEM((rows, cols), BF),
            pltpu.VMEM((rows, cols), BF),
            pltpu.VMEM((2, rows, cols), F32),
            pltpu.SemaphoreType.DMA((2,)),
            pltpu.SemaphoreType.DMA((2,)),
            pltpu.SemaphoreType.DMA,
            pltpu.SemaphoreType.DMA,
        ]

def front_kernel(hidden, cotangent, routes, length, attn_gain, w_query, w_key, w_value, w_out, moe_gain, cosine, sine, count, experts_here, cid):
    rows, width = hidden.shape
    seq = 4 * rows
    query_cols, key_cols = w_query.shape[1], w_key.shape[1]
    picks = routes.shape[0]
    kv_here = key_cols // HEAD_DIM

    def kernel(*refs):
        refs = list(refs)
        take = lambda number: [refs.pop(0) for _ in range(number)]
        h_ref, cot_ref, route_ref, len_ref, g1_ref, wq_far, wk_far, wv_far, wout_ref, g2_ref, cos_ref, sin_ref = take(12)
        en_ref, ga_ref, whole_ref, q_ref, k_ref, v_ref, ctx_ref, lse_ref, mixed_ref, slots_ref, lab_all = take(11)
        kd, vd, s_scr, p_scr, wqkv_ref, lab_ref = take(6)
        share = take(2)
        fold = take(9)
        g_scr = take(2)
        l_send, l_recv, own_sem, w_sem = take(4)
        ring, corner = Ring(count), Corner()
        others = [(ring.me + shift) % count for shift in range(1, count)]
        w_loads = [
            pltpu.make_async_copy(src, wqkv_ref.at[:, pl.ds(start, size)], w_sem.at[k])
            for k, (src, start, size) in enumerate(
                ((wq_far, 0, query_cols), (wk_far, query_cols, key_cols), (wv_far, query_cols + key_cols, key_cols))
            )
        ]
        for c in w_loads:
            c.start()
        length_here = len_ref[0]
        lab_ref[0:picks] = route_ref[...]
        lab_ref[picks : 2 * picks] = jnp.full((picks, rows), length_here, jnp.int32)
        greet(others, [corner.core_peer, corner.chip_peer])

        g_ring = gather_steps(ring, ga_ref, *g_scr, own=cot_ref, left=1)
        next(g_ring)
        own_grad = pltpu.make_async_copy(cot_ref, ga_ref.at[ring.me], own_sem)
        own_grad.start()
        label_copy = lambda k, target: remote(
            lab_ref, lab_all.at[ring.me], l_send.at[k], l_recv.at[k], wide=target
        )
        for k, target in enumerate(others):
            label_copy(k, target).start()
        lab_all[ring.me] = lab_ref[...]

        source = h_ref[...].astype(F32)
        scale = lax.rsqrt(jnp.mean(source * source, axis=1, keepdims=True) + EPSILON)
        whole_ref[corner.here] = (source * scale * g1_ref[...]).astype(BF)
        sharing = Share(corner, whole_ref, *share)
        sharing.start()

        def project(block):
            span = pl.ds(pl.multiple_of(block * rows, rows), rows)
            lin = nn(whole_ref[block], wqkv_ref[...])
            cos, sin = cos_ref[span], sin_ref[span]
            for t in range(kv_here):
                lanes = slice(t * LANES, (t + 1) * LANES)
                q_ref[span, lanes] = turn_lanes(lin[:, lanes], cos, sin).astype(BF)
            keys = turn_lanes(lin[:, query_cols : query_cols + key_cols], cos, sin)
            values = lin[:, query_cols + key_cols :]
            k_ref[span] = keys.astype(BF)
            v_ref[span] = values.astype(BF)
            for t in range(kv_here):
                kd[t, span] = doubled(keys, t).astype(BF)
                vd[t, span] = doubled(values, t).astype(BF)

        for c in w_loads:
            c.wait()
        project(corner.here)
        sharing.wait_core()
        project(corner.core_peer)

        for k, target in enumerate(others):
            sender = (ring.me - (k + 1) + count) % count
            remote(lab_ref, lab_all.at[sender], l_send.at[k], l_recv.at[k], wide=target).wait_recv()
        places = corner.here * rows + lane_of((1, rows))
        first = ring.me * experts_here
        upper = jnp.where(
            lax.broadcasted_iota(jnp.int32, (rows, rows), 0) <= lane_of((rows, rows)), 1.0, 0.0
        ).astype(BF)

        def belongs(block, expert_rows):
            found = lab_all[block, 0:1] == expert_rows
            for k in range(1, picks):
                found = found | (lab_all[block, k : k + 1] == expert_rows)
            return found

        local_rows = lax.broadcasted_iota(jnp.int32, (8, rows), 0)
        own_rows = jnp.where(local_rows < experts_here, first + local_rows, -1)
        for b in range(count):
            mine = jnp.where(belongs(b, own_rows) & (places < lab_all[b, picks : picks + 1]), 1.0, 0.0)
            reached = nn(mine.astype(BF), upper)
            slots_ref[b] = jnp.where(mine > 0.0, reached, 0.0).astype(jnp.int32) - 1

        sharing.wait_chip()
        next(g_ring)
        project(corner.chip_peer)
        sharing.wait_far()
        project(corner.far_peer)

        folding = Fold(corner, *fold)
        before = None
        for block in (3, 2, 1, 0):
            span = pl.ds(block * rows, rows)
            for t in range(kv_here):
                lanes = slice(t * LANES, (t + 1) * LANES)
                queries = stacked(q_ref[span, lanes])
                highest = None
                for b in range(block + 1):
                    keys = pl.ds(b * rows, rows)
                    scores = masked_scores(kd[t, keys], queries, b * rows, block * rows, length_here, b == block)
                    s_scr[keys] = scores
                    top = jnp.max(scores, axis=0, keepdims=True)
                    highest = top if highest is None else jnp.maximum(highest, top)
                total = None
                for b in range(block + 1):
                    keys = pl.ds(b * rows, rows)
                    weights = jnp.exp(s_scr[keys] - highest)
                    p_scr[keys] = weights.astype(BF)
                    one = jnp.sum(weights, axis=0, keepdims=True)
                    total = one if total is None else total + one
                keys = pl.ds(0, (block + 1) * rows)
                context = tn(vd[t, keys], p_scr[keys]) / total
                ctx_ref[span, lanes] = unstacked(context).astype(BF)
                lse_ref[t * 4 + block : t * 4 + block + 1] = highest + jnp.log(total)
            folding.give(block, nn(ctx_ref[span], wout_ref[...]))
            if before is not None:
                folding.settle(before)
            before = block
            if block == 1:
                next(g_ring)
        folding.settle(before)
        mixed = source + folding.total()
        mixed_ref[...] = mixed
        scale = lax.rsqrt(jnp.mean(mixed * mixed, axis=1, keepdims=True) + EPSILON)
        en_ref[...] = (mixed * scale * g2_ref[...]).astype(BF)
        for _ in g_ring:
            pass
        for k, target in enumerate(others):
            label_copy(k, target).wait_send()
        own_grad.wait()
        sharing.drain()
        folding.drain()

    vmem = pl.BlockSpec(memory_space=pltpu.VMEM)
    far = pl.BlockSpec(memory_space=pl.ANY)
    shape = jax.ShapeDtypeStruct
    out_shape = [
        shape((rows, width), BF),
        shape((count, rows, width), BF),
        shape((4, rows, width), BF),
        shape((seq, query_cols), BF),
        shape((seq, key_cols), BF),
        shape((seq, key_cols), BF),
        shape((seq, query_cols), BF),
        shape((8, 2 * rows), F32),
        shape((rows, width), F32),
        shape((count, 8, rows), jnp.int32),
        shape((count, 2 * picks, rows), jnp.int32),
    ]
    scratch = [
        pltpu.VMEM((kv_here, seq, LANES), BF),
        pltpu.VMEM((kv_here, seq, LANES), BF),
        pltpu.VMEM((seq, 2 * rows), F32),
        pltpu.VMEM((seq, 2 * rows), BF),
        pltpu.VMEM((width, query_cols + 2 * key_cols), BF),
        pltpu.VMEM((2 * picks, rows), jnp.int32),
        *Share.scratch(),
        *Fold.scratch(rows, width),
        *gather_scratch(count),
        pltpu.SemaphoreType.DMA((count - 1,)),
        pltpu.SemaphoreType.DMA((count - 1,)),
        pltpu.SemaphoreType.DMA,
        pltpu.SemaphoreType.DMA((3,)),
    ]
    return pl.pallas_call(
        kernel,
        out_shape=out_shape,
        in_specs=[vmem, far, vmem, pl.BlockSpec(memory_space=pltpu.SMEM)] + [vmem] + [far] * 3 + [vmem] * 4,
        out_specs=[vmem, far] + [vmem] * (len(out_shape) - 2),
        scratch_shapes=scratch,
        compiler_params=pltpu.CompilerParams(
            collective_id=cid, has_side_effects=True, vmem_limit_bytes=56 * 2**20
        ),
    )(hidden, cotangent, routes, length, attn_gain, w_query, w_key, w_value, w_out, moe_gain, cosine, sine)


def middle_kernel(entry, grad_all, labels_all, slots, router_turned, w_gate_up, w_down, capacity, picks, cid):
    rows, width = entry.shape
    count = grad_all.shape[0]
    experts_here, _, ffe2 = w_gate_up.shape
    ffe = ffe2 // 2
    experts = router_turned.shape[0]
    hops = count // 2
    shifts = [0] + [s for hop in range(1, hops) for s in (hop, -hop)] + [hops]
    room = count * capacity
    quarter_up, quarter_down = width // 4, ffe // 4
    quarter = quarter_up + quarter_down

    def kernel(*refs):
        refs = list(refs)
        take = lambda number: [refs.pop(0) for _ in range(number)]
        en_far, ga_far, lab_all, slots_ref, wr_ref, wgu_far, wd_far = take(7)
        ob_ref, op_ref, c_far, keep_far, got_far, shares_ref, wait_far = take(7)
        wgu, wd, e_buf, g_buf, pg, act_s, x_s, s_s, b_buf, c_slot, got_a, gates, pick_buf, last_c, last_b = take(15)
        held = take(3)
        e_scr = take(2)
        w_sem, g_sem, c_sem, p_send, p_recv, a_send, a_recv, x_send, x_recv, o_sem, f_sem, en_sem, far_send, far_recv = take(14)
        ring, corner = Ring(count), Corner()
        others = [(ring.me + shift) % count for shift in range(1, count)]
        greet(others, [corner.core_peer, corner.chip_peer])

        def weights(e):
            return [
                pltpu.make_async_copy(wgu_far.at[e], wgu.at[e], w_sem.at[0, e]),
                pltpu.make_async_copy(wd_far.at[e], wd.at[e], w_sem.at[1, e]),
            ]

        def grads(p):
            block = ring.at(shifts[p])
            return pltpu.make_async_copy(ga_far.at[block], g_buf.at[block], g_sem.at[p])

        def far_grads(way, shift):
            sign = 1 if way == 0 else -1
            block = ring.at(-sign * (hops - 1 + shift))
            start, size = cuts(rows)[way]
            source = ga_far if shift == 0 else g_buf
            return remote(
                source.at[block, pl.ds(start, size)], g_buf.at[block, pl.ds(start, size)],
                far_send.at[way], far_recv.at[way], wide=ring.peers[way],
            )

        e_ring = gather_steps(ring, e_buf, *e_scr, own=en_far)
        next(e_ring)
        own_entry = pltpu.make_async_copy(en_far, e_buf.at[ring.me], en_sem)
        own_entry.start()
        for e in range(experts_here):
            for c in weights(e):
                c.start()
            if e == 0:
                for p in range(count - 1):
                    grads(p).start()

        places = corner.here * rows + lane_of((1, rows))
        first = ring.me * experts_here
        every = lax.broadcasted_iota(jnp.int32, (experts, rows), 0)
        local_rows = lax.broadcasted_iota(jnp.int32, (8, rows), 0)
        slot_rows = lax.broadcasted_iota(jnp.int32, (capacity, rows), 0)

        def gate(block, home):
            logits = nt(wr_ref[...], e_buf[block])
            member = lab_all[block, 0:1] == every
            for k in range(1, picks):
                member = member | (lab_all[block, k : k + 1] == every)
            masked = jnp.where(member, logits, -jnp.inf)
            raised = jnp.exp(masked - jnp.max(masked, axis=0, keepdims=True))
            shares = raised / jnp.sum(raised, axis=0, keepdims=True)
            if home:
                shares_ref[...] = shares
            kept = jnp.where(places < lab_all[block, picks : picks + 1], shares, 0.0)
            own = jnp.zeros((8, rows), F32)
            for e in range(experts_here):
                row = jnp.sum(jnp.where(every == first + e, kept, 0.0), axis=0, keepdims=True)
                own = jnp.where(local_rows == e, row, own)
            gates[block] = own

        def pick_rows(block, e):
            return slot_rows == slots_ref[block, pl.ds(e, 1), :]

        def gather_rows(block, e):
            found = pick_rows(block, e)
            chosen = jnp.where(found, 1.0, 0.0).astype(BF)
            gate_col = jnp.sum(jnp.where(found, gates[block, pl.ds(e, 1), :], 0.0), axis=1, keepdims=True)
            return found, nn(chosen, e_buf[block]).astype(BF), nn(chosen, g_buf[block]), gate_col

        def chain(numbers, e, result_rows, back_rows, row, await_weights=False):
            blocks = [ring.at(shifts[p]) for p in numbers]
            size = len(numbers) * capacity
            here = pl.ds(pl.multiple_of(row, capacity), size)
            span = pl.ds(numbers[0] * capacity, size)
            if await_weights:
                for c in weights(e):
                    c.wait()
            parts = [gather_rows(block, e) for block in blocks]
            entries = jnp.concatenate([p[1] for p in parts], axis=0)
            grad_rows = jnp.concatenate([p[2] for p in parts], axis=0)
            gate_col = jnp.concatenate([p[3] for p in parts], axis=0)
            slot_grad = (gate_col * grad_rows).astype(BF)
            pre = nn(entries, wgu[e])
            act_grad = nt(slot_grad, wd[e])
            gate_part = pre[:, :ffe]
            up_part = pre[:, ffe:]
            sig = jax.nn.sigmoid(gate_part)
            swish = gate_part * sig
            act = (swish * up_part).astype(BF)
            act_s[e, span] = act
            gate_grad = act_grad * up_part * sig * (1.0 + gate_part * (1.0 - sig))
            pre_grad = jnp.concatenate([gate_grad, act_grad * swish], axis=1).astype(BF)
            pg[e, span] = pre_grad
            result = nn(act, wd[e]).astype(BF).astype(F32)
            back_rows[here] = nt(pre_grad, wgu[e]).astype(BF)
            result_rows[here] = (gate_col * result).astype(BF)
            pick_col = jnp.sum(result * grad_rows, axis=1, keepdims=True)
            for i, block in enumerate(blocks):
                pick = jnp.sum(
                    jnp.where(parts[i][0], pick_col[i * capacity : (i + 1) * capacity], 0.0),
                    axis=0, keepdims=True,
                )
                pick_buf[block] = jnp.where(local_rows == e, pick, pick_buf[block])

        def combine(number, result_rows, back_rows, row_of):
            block = ring.at(shifts[number])
            chosen = jnp.concatenate(
                [jnp.where(pick_rows(block, e), 1.0, 0.0).astype(BF) for e in range(experts_here)], axis=0
            )
            windows = [pl.ds(row_of(e), capacity) for e in range(experts_here)]
            if number >= 2:
                results(number - 2).wait()
            c_slot[number % 2] = tn(chosen, jnp.concatenate([result_rows[w] for w in windows], axis=0)).astype(BF)
            results(number).start()
            b_buf[block] = tn(chosen, jnp.concatenate([back_rows[w] for w in windows], axis=0)).astype(BF)

        def tile(numbers, await_weights):
            size = len(numbers) * capacity
            for p in numbers:
                grads(p).wait()

            def one(e, carry):
                chain(numbers, e, x_s, s_s, e * size, await_weights)
                return carry

            lax.fori_loop(0, experts_here, one, 0)
            for i, number in enumerate(numbers):
                combine(number, x_s, s_s, lambda e: e * size + i * capacity)

        def results(number):
            return pltpu.make_async_copy(
                c_slot.at[number % 2], c_far.at[ring.at(shifts[number])], c_sem.at[number]
            )

        def put(row, size, got):
            ob_ref[pl.ds(row, size)] = got

        b_ring = scatter_steps(ring, b_buf, *held, put)
        pick_buf[...] = jnp.zeros_like(pick_buf)
        own_entry.wait()
        gate(ring.me, True)
        tile([0], True)
        for hop in range(1, hops - 1):
            next(e_ring)
            gate(ring.at(hop), False)
            gate(ring.at(-hop), False)
            if hop == 1:
                for way in range(2):
                    far_grads(way, 0).start()
            tile([2 * hop - 1, 2 * hop], False)
        def weight_grads(e):
            for p in range(count):
                _, entries, grad_rows, gate_col = gather_rows(ring.at(shifts[p]), e)
                span = pl.ds(p * capacity, capacity)
                x_s[span] = entries
                s_s[span] = (gate_col * grad_rows).astype(BF)

            def columns(j, carry):
                cols = pl.ds(pl.multiple_of(j * 256, 256), 256)
                wgu[e, :, cols] = tn(x_s[...], pg[e, :, cols]).astype(BF)
                wd[e, :, cols] = tn(act_s[e], s_s[:, cols]).astype(BF)
                return carry

            lax.fori_loop(0, width // 256, columns, 0)

        def pieces(e, owner):
            return (
                (wgu.at[e, pl.ds(owner * quarter_up, quarter_up)], 0, quarter_up),
                (wd.at[e, pl.ds(owner * quarter_down, quarter_down)], quarter_up, quarter_down),
            )

        landing = lambda e: got_a.at[e] if e < 2 else wait_far.at[e - 2]
        fetch = lambda e: pltpu.make_async_copy(wait_far.at[e - 2], got_a.at[e % 2], f_sem.at[e - 2])

        def to_core(e):
            return [
                remote(src, landing(e).at[x, pl.ds(start, size)], a_send.at[e, x, k], a_recv.at[e, x, k], narrow=corner.core_peer)
                for x in range(2)
                for k, (src, start, size) in enumerate(pieces(e, 2 * x + 1 - corner.core))
            ]

        def to_chip(e):
            return [
                remote(src, got_far.at[e, pl.ds(start, size)], x_send.at[e, k], x_recv.at[e, k], narrow=corner.chip_peer)
                for k, (src, start, size) in enumerate(pieces(e, 2 * (1 - corner.chip) + corner.core))
            ]

        def own_out(e):
            return [
                pltpu.make_async_copy(src, keep_far.at[e, pl.ds(start, size)], o_sem.at[e, k])
                for k, (src, start, size) in enumerate(pieces(e, corner.here))
            ]

        def send_core(e):
            for c in to_core(e):
                c.start()

        def first_sum(e):
            for c in to_core(e):
                c.wait_recv()
            if e >= 2:
                fetch(e).start()
                fetch(e).wait()
            for number in range(2):
                x = 1 - corner.chip if number == 0 else corner.chip
                for src, start, size in pieces(e, 2 * x + corner.core):
                    block_add(src, src, got_a.at[e % 2, x, pl.ds(start, size)], size)
                for c in to_chip(e) if number == 0 else own_out(e):
                    c.start()

        last = [count - 3, count - 2, count - 1]
        row_at = lambda e, i: (e * 3 + i) * capacity
        next(e_ring)
        gate(ring.at(hops - 1), False)
        gate(ring.at(1 - hops), False)
        for p in last[:2]:
            grads(p).wait()

        def several(start, stop, numbers):
            def one(e, carry):
                chain(numbers, e, last_c, last_b, row_at(e, numbers[0] - last[0]))
                return carry

            lax.fori_loop(start, stop, one, 0)

        several(0, 2, last[:2])
        for _ in e_ring:
            pass
        gate(ring.at(hops), False)
        for way in range(2):
            far_grads(way, 1).wait_recv()
        next(b_ring)
        chain(last[2:], 0, last_c, last_b, row_at(0, 2))
        weight_grads(0)
        send_core(0)
        chain(last[2:], 1, last_c, last_b, row_at(1, 2))
        several(2, 3, last[:2])
        first_sum(0)
        next(b_ring)
        several(3, experts_here, last[:2])
        weight_grads(1)
        send_core(1)
        several(2, experts_here, last[2:])
        first_sum(1)
        for i, number in enumerate(last):
            combine(number, last_c, last_b, lambda e: row_at(e, i))
        next(b_ring)
        pick_copy = lambda k, target: remote(
            pick_buf.at[target], op_ref.at[ring.me], p_send.at[k], p_recv.at[k], wide=target
        )
        for k, target in enumerate(others):
            pick_copy(k, target).start()
        op_ref[ring.me] = pick_buf[ring.me]
        for e in range(2, experts_here):
            weight_grads(e)
            send_core(e)
            next(b_ring)
            first_sum(e)
            next(b_ring, None)
        for _ in b_ring:
            pass
        for e in range(experts_here):
            for c in to_core(e):
                c.wait_send()
            for c in to_chip(e):
                c.wait()
            for c in own_out(e):
                c.wait()
        for number in range(max(0, count - 2), count):
            results(number).wait()
        for way in range(2):
            far_grads(way, 0).wait_send()
        for k, target in enumerate(others):
            sender = (ring.me - (k + 1) + count) % count
            remote(
                pick_buf.at[sender], op_ref.at[sender], p_send.at[k], p_recv.at[k], wide=target
            ).wait_recv()
            pick_copy(k, target).wait_send()

    vmem = pl.BlockSpec(memory_space=pltpu.VMEM)
    far = pl.BlockSpec(memory_space=pl.ANY)
    shape = jax.ShapeDtypeStruct
    out_shape = [
        shape((rows, width), F32),
        shape((count, 8, rows), F32),
        shape((count, rows, width), BF),
        shape((experts_here, quarter, width), BF),
        shape((experts_here, quarter, width), BF),
        shape((experts, rows), F32),
        shape((experts_here - 2, 2, quarter, width), BF),
    ]
    dma = pltpu.SemaphoreType.DMA
    scratch = [
        pltpu.VMEM(w_gate_up.shape, BF),
        pltpu.VMEM(w_down.shape, BF),
        pltpu.VMEM((count, rows, width), BF),
        pltpu.VMEM((count, rows, width), BF),
        pltpu.VMEM((experts_here, room, 2 * ffe), BF),
        pltpu.VMEM((experts_here, room, ffe), BF),
        pltpu.VMEM((room, width), BF),
        pltpu.VMEM((room, width), BF),
        pltpu.VMEM((count, rows, width), BF),
        pltpu.VMEM((2, rows, width), BF),
        pltpu.VMEM((2, 2, quarter, width), BF),
        pltpu.VMEM((count, 8, rows), F32),
        pltpu.VMEM((count, 8, rows), F32),
        pltpu.VMEM((3 * experts_here * capacity, width), BF),
        pltpu.VMEM((3 * experts_here * capacity, width), BF),
        *scatter_scratch(count, rows, width),
        *gather_scratch(count),
        dma((2, experts_here)), dma((count,)), dma((count,)),
        dma((count - 1,)), dma((count - 1,)),
        dma((experts_here, 2, 2)), dma((experts_here, 2, 2)),
        dma((experts_here, 2)), dma((experts_here, 2)), dma((experts_here, 2)), dma((experts_here - 2,)), dma, dma((2,)), dma((2,)),
    ]
    return pl.pallas_call(
        kernel,
        out_shape=out_shape,
        in_specs=[far, far, vmem, vmem, vmem, far, far],
        out_specs=[vmem, vmem, far, far, far, vmem, far],
        scratch_shapes=scratch,
        compiler_params=pltpu.CompilerParams(
            collective_id=cid, has_side_effects=True, vmem_limit_bytes=63 * 2**20
        ),
    )(entry, grad_all, labels_all, slots, router_turned, w_gate_up, w_down)


def tail_kernel(entry_home, pick_home, shares, router_turned, mixed, cotangent, hidden, length, attn_gain, moe_gain, w_query, w_key, w_value, w_out, queries, keys, values, context, whole, lse, cosine, sine, expert_part, kept, arrived, shapes, cid):
    count, rows, width = expert_part.shape
    seq = 4 * rows
    query_cols, key_cols = w_out.shape[0], w_key.shape[1]
    cols = query_cols + 2 * key_cols
    kv_here = key_cols // HEAD_DIM
    experts_all = router_turned.shape[0]
    small_rows = (experts_all + 2 + 15) // 16 * 16
    block = -(-(cols + query_cols + small_rows) // (32 * count)) * 32
    experts, quarter, _ = kept.shape
    up_shape, down_shape = shapes
    quarter_up, quarter_down = up_shape[1] // 4, down_shape[1] // 4
    base = [0, rows, 3 * rows, 6 * rows]
    small_at = cols + query_cols

    def kernel(*refs):
        refs = list(refs)
        take = lambda number: [refs.pop(0) for _ in range(number)]
        eh_ref, pick_ref, shares_ref, wr_ref, mixed_ref, cot_ref, h_ref, len_ref, g1_ref, g2_ref = take(10)
        wq_far, wk_far, wv_far, wout_ref, q_ref, k_ref, v_ref, ctx_ref, whole_ref, lse_ref, cos_ref, sin_ref = take(12)
        c_far, keep_far, got_far = take(3)
        out_ref, gh_ref, turned_ref, go_ref, small_ref, up_ref, down_ref = take(7)
        gw, mg_s, kd, vd, p_all, dp_scr, ds_scr, dctx, dk, dv, qg, packed, small_got, expert_sum, c_ref, sum_ref, own, got, wqkv_ref, wt_ref, gain_got = take(21)
        share, fold = take(2), take(9)
        c_sem, w_sem, o_sem = take(3)
        c_scr, s_scr, g_scr = take(3), take(3), take(2)
        sm_send, sm_recv, ga_send, ga_recv = take(4)
        c_send, c_recv, x_send, x_recv, f_send, f_recv, l_sem = take(7)
        ring, corner = Ring(count), Corner()
        greet(list(ring.peers), [corner.core_peer, corner.chip_peer, corner.far_peer])
        length_here = len_ref[0]

        own_loads = lambda e: [
            pltpu.make_async_copy(keep_far.at[e], own.at[e], o_sem.at[0, e]),
            pltpu.make_async_copy(got_far.at[e], got.at[e], o_sem.at[1, e]),
        ]
        w_loads = [
            pltpu.make_async_copy(src, wqkv_ref.at[:, pl.ds(start, size)], w_sem.at[k])
            for k, (src, start, size) in enumerate(
                ((wq_far, 0, query_cols), (wk_far, query_cols, key_cols), (wv_far, query_cols + key_cols, key_cols))
            )
        ]
        for c in w_loads:
            c.start()
        for e in range(experts):
            for c in own_loads(e):
                c.start()

        def own_sum(e):
            for c in own_loads(e):
                c.wait()
            block_add(own.at[e], own.at[e], got.at[e], quarter)
            send_out(e)
            for c in send(e, core_sems, corner.core_peer) + own_copy(e):
                c.start()

        def put(row, size, value):
            expert_sum[pl.ds(row, size)] = value

        c_load = pltpu.make_async_copy(c_far, c_ref, c_sem)
        c_load.start()
        c_ring = scatter_steps(ring, c_ref, *c_scr, put)

        def places(e, owner):
            mine = own.at[e]
            return (
                (mine.at[pl.ds(0, quarter_up)], up_ref.at[e, pl.ds(owner * quarter_up, quarter_up)]),
                (mine.at[pl.ds(quarter_up, quarter_down)], down_ref.at[e, pl.ds(owner * quarter_down, quarter_down)]),
            )

        def send(e, sems, peer):
            return [
                remote(src, dst, sems[0].at[e, k], sems[1].at[e, k], narrow=peer)
                for k, (src, dst) in enumerate(places(e, corner.here))
            ]

        def forward(e, owner, sems):
            return [
                remote(dst, dst, sems[0].at[e, k], sems[1].at[e, k], narrow=corner.core_peer)
                for k, (src, dst) in enumerate(places(e, owner))
            ]

        core_sems, chip_sems, far_sems = (c_send, c_recv), (x_send, x_recv), (f_send, f_recv)

        def own_copy(e):
            return [
                pltpu.make_async_copy(src, dst, l_sem.at[e, k])
                for k, (src, dst) in enumerate(places(e, corner.here))
            ]

        def send_out(e):
            for c in send(e, chip_sems, corner.chip_peer):
                c.start()

        def pass_on(e):
            for c in forward(e, corner.chip_peer, chip_sems):
                c.wait_recv()
            for c in forward(e, corner.chip_peer, far_sems):
                c.start()

        each = experts_all // count
        picked = jnp.concatenate([pick_ref[b, 0:each] for b in range(count)], axis=0)
        held_shares = shares_ref[...]
        logit_grad = held_shares * (picked - jnp.sum(held_shares * picked, axis=0, keepdims=True))
        high = logit_grad.astype(BF)
        low = (logit_grad - high.astype(F32)).astype(BF)
        entry_grad = eh_ref[...] + (tn(high, wr_ref[...]) + tn(low, wr_ref[...]))
        mixed_here = mixed_ref[...]
        scale = lax.rsqrt(jnp.mean(mixed_here * mixed_here, axis=1, keepdims=True) + EPSILON)
        unit = mixed_here * scale
        inner = entry_grad * g2_ref[...]
        from_norm = scale * (inner - unit * jnp.mean(inner * unit, axis=1, keepdims=True))
        at = corner.here * rows + lax.broadcasted_iota(jnp.int32, (rows, 1), 0)
        valid = jnp.where(at < length_here, 1.0, 0.0)
        mixed_grad = valid * cot_ref[...].astype(F32) + from_norm
        mg_s[...] = mixed_grad
        gw[corner.here] = mixed_grad.astype(BF)
        sharing = Share(corner, gw, *share)
        sharing.start()
        entry = (unit * g2_ref[...]).astype(BF)
        small_got[3] = jnp.concatenate(
            [
                nn(high, entry) + nn(low, entry),
                jnp.sum(entry_grad * unit, axis=0, keepdims=True),
                jnp.zeros((small_rows - experts_all - 1, width), F32),
            ],
            axis=0,
        ).astype(BF)
        peers = (corner.core_peer, corner.chip_peer, corner.far_peer)
        small_copy = lambda k, peer: remote(
            small_got.at[3], small_got.at[k], sm_send.at[k], sm_recv.at[k], narrow=peer
        )
        for k, peer in enumerate(peers):
            small_copy(k, peer).start()

        for t in range(kv_here):
            kd[t] = doubled(k_ref[...].astype(F32), t).astype(BF)
            vd[t] = doubled(v_ref[...].astype(F32), t).astype(BF)

        def chances(b):
            for t in range(kv_here):
                lanes = slice(t * LANES, (t + 1) * LANES)
                stack = stacked(q_ref[pl.ds(b * rows, rows), lanes])
                log_sum = lse_ref[t * 4 + b : t * 4 + b + 1]
                for kb in range(b + 1):
                    scores = masked_scores(
                        kd[t, pl.ds(kb * rows, rows)], stack, kb * rows, b * rows, length_here, kb == b
                    )
                    p_all[t, pl.ds(base[b] + kb * rows, rows)] = jnp.exp(scores - log_sum).astype(BF)

        def pull(owner):
            dctx[owner] = nt(gw[owner], wout_ref[...]).astype(BF)

        pull(corner.here)
        c_load.wait()
        next(c_ring)
        chances(3)
        next(c_ring)
        sharing.wait_core()
        pull(corner.core_peer)
        chances(2)
        next(c_ring)
        chances(1)
        chances(0)
        sharing.wait_chip()
        own_sum(0)
        pull(corner.chip_peer)
        sharing.wait_far()
        pull(corner.far_peer)
        dk[...] = jnp.zeros_like(dk)
        dv[...] = jnp.zeros_like(dv)

        folding = Fold(corner, *fold)
        before = None
        for b in (3, 2, 1, 0):
            span = pl.ds(b * rows, rows)
            cos, sin = cos_ref[span], sin_ref[span]
            for t in range(kv_here):
                lanes = slice(t * LANES, (t + 1) * LANES)
                stack = stacked(q_ref[span, lanes])
                grad_stack = stacked(dctx[b, :, lanes])
                inner = None
                for kb in range(b + 1):
                    chance = p_all[t, pl.ds(base[b] + kb * rows, rows)]
                    grad = nt(vd[t, pl.ds(kb * rows, rows)], grad_stack)
                    dp_scr[pl.ds(kb * rows, rows)] = grad
                    one = jnp.sum(chance.astype(F32) * grad, axis=0, keepdims=True)
                    inner = one if inner is None else inner + one
                for kb in range(b + 1):
                    key_span = pl.ds(kb * rows, rows)
                    chance = p_all[t, pl.ds(base[b] + kb * rows, rows)]
                    score_grad = (chance.astype(F32) * (dp_scr[key_span] - inner)).astype(BF)
                    ds_scr[key_span] = score_grad
                    dk[t, key_span] += nn(score_grad, stack)
                    dv[t, key_span] += nn(chance, grad_stack)
                every = pl.ds(0, (b + 1) * rows)
                query_grad = unstacked(tn(kd[t, every], ds_scr[every])) * HEAD_DIM ** (-0.5)
                qg[span, lanes] = turn_lanes(query_grad, cos, -sin).astype(BF)
            low_lanes = lane_of((rows, LANES)) < HEAD_DIM
            both = lambda ref, t: ref[t, span] + pltpu.roll(ref[t, span], HEAD_DIM, 1)
            key_grad = jnp.where(low_lanes, both(dk, 0), both(dk, 1)) * HEAD_DIM ** (-0.5)
            qg[span, query_cols : query_cols + key_cols] = turn_lanes(key_grad, cos, -sin).astype(BF)
            qg[span, query_cols + key_cols :] = jnp.where(low_lanes, both(dv, 0), both(dv, 1)).astype(BF)
            if b == 3:
                for c in w_loads:
                    c.wait()
            folding.give(b, nt(qg[span], wqkv_ref[...]))
            if before is not None:
                folding.settle(before)
            before = b
            next(c_ring)
            if b == 2:
                own_sum(1)
        folding.settle(before)

        def store(row, value):
            for start in range(0, value.shape[0], 16):
                size = min(16, value.shape[0] - start)
                at_row = row + start
                packed[at_row // block, pl.ds(at_row % block, size)] = value[start : start + size].astype(BF)

        weight_grad = tn(qg[...], whole_ref[...])
        wt_ref[...] = wqkv_ref[...].astype(F32).T
        gain_one = jnp.sum(weight_grad * wt_ref[...], axis=0, keepdims=True) / g1_ref[...]
        store(0, weight_grad)
        store(cols, tn(ctx_ref[...], gw[...].reshape(seq, width)))
        rest = small_at + small_rows
        store(rest, jnp.zeros((count * block - rest, width), F32))
        for k, peer in enumerate(peers):
            small_copy(k, peer).wait_recv()
        small_sum = sum(small_got[k].astype(F32) for k in range(4))
        row_at = lax.broadcasted_iota(jnp.int32, (small_rows, width), 0)
        store(small_at, jnp.where(row_at == experts_all + 1, gain_one, small_sum))

        def finish(row, size, got):
            sum_ref[ring.me, pl.ds(row, size)] = got.astype(BF)

        sums = scatter_steps(ring, packed, *s_scr, finish)
        next(sums)
        own_sum(2)
        own_sum(3)
        for _ in sums:
            pass
        for _ in gather_steps(ring, sum_ref, *g_scr):
            pass
        whole_sum = lambda row, size: jnp.concatenate(
            [sum_ref[b] for b in range(row // block, (row + size) // block)], axis=0
        )
        gain_got[3] = sum_ref[small_at // block, small_rows - 16 : small_rows]
        gain_copy = lambda k, peer: remote(
            gain_got.at[3], gain_got.at[k], ga_send.at[k], ga_recv.at[k], narrow=peer
        )
        for k, peer in enumerate(peers):
            gain_copy(k, peer).start()
        for row in range(0, cols, block):
            turned_ref[:, row : row + block] = sum_ref[row // block].astype(F32).T.astype(BF)
        go_ref[...] = whole_sum(cols, query_cols)
        normed_grad = folding.total()
        source = h_ref[...].astype(F32)
        scale = lax.rsqrt(jnp.mean(source * source, axis=1, keepdims=True) + EPSILON)
        unit = source * scale
        inner = normed_grad * g1_ref[...]
        from_norm = scale * (inner - unit * jnp.mean(inner * unit, axis=1, keepdims=True))
        gh_ref[...] = (mg_s[...] + from_norm).astype(BF)
        for e in range(2):
            pass_on(e)
        for _ in c_ring:
            pass
        out_ref[...] = (valid * (mixed_here + expert_sum[...])).astype(BF)
        for k, peer in enumerate(peers):
            gain_copy(k, peer).wait_recv()
        gain_sum = sum(gain_got[k].astype(F32) for k in range(4))
        small_ref[0 : small_rows - 16] = sum_ref[small_at // block, 0 : small_rows - 16]
        last_rows = small_rows - 16 + lax.broadcasted_iota(jnp.int32, (16, width), 0)
        small_ref[small_rows - 16 : small_rows] = jnp.where(
            last_rows == experts_all + 1, gain_sum, gain_got[3].astype(F32)
        ).astype(BF)
        for e in range(2, experts):
            pass_on(e)
        for k, peer in enumerate(peers):
            gain_copy(k, peer).wait_send()
        for k, peer in enumerate(peers):
            small_copy(k, peer).wait_send()
        for e in range(experts):
            for c in own_copy(e):
                c.wait()
            for c in send(e, chip_sems, corner.chip_peer) + send(e, core_sems, corner.core_peer):
                c.wait_send()
            for c in forward(e, corner.core_peer, core_sems):
                c.wait_recv()
            for c in forward(e, corner.chip_peer, far_sems):
                c.wait_send()
            for c in forward(e, corner.far_peer, far_sems):
                c.wait_recv()
        sharing.drain()
        folding.drain()

    vmem = pl.BlockSpec(memory_space=pltpu.VMEM)
    far = pl.BlockSpec(memory_space=pl.ANY)
    shape = jax.ShapeDtypeStruct
    out_shape = [
        shape((rows, width), BF),
        shape((rows, width), BF),
        shape((width, cols), BF),
        shape((query_cols, width), BF),
        shape((small_rows, width), BF),
        shape(up_shape, BF),
        shape(down_shape, BF),
    ]
    scratch = [
        pltpu.VMEM((4, rows, width), BF),
        pltpu.VMEM((rows, width), F32),
        pltpu.VMEM((kv_here, seq, LANES), BF),
        pltpu.VMEM((kv_here, seq, LANES), BF),
        pltpu.VMEM((kv_here, 10 * rows, 2 * rows), BF),
        pltpu.VMEM((seq, 2 * rows), F32),
        pltpu.VMEM((seq, 2 * rows), BF),
        pltpu.VMEM((4, rows, query_cols), BF),
        pltpu.VMEM((kv_here, seq, LANES), F32),
        pltpu.VMEM((kv_here, seq, LANES), F32),
        pltpu.VMEM((seq, cols), BF),
        pltpu.VMEM((count, block, width), BF),
        pltpu.VMEM((4, small_rows, width), BF),
        pltpu.VMEM((rows, width), F32),
        pltpu.VMEM((count, rows, width), BF),
        pltpu.VMEM((count, block, width), BF),
        pltpu.VMEM((experts, quarter, width), BF),
        pltpu.VMEM((experts, quarter, width), BF),
        pltpu.VMEM((width, cols), BF),
        pltpu.VMEM((cols, width), F32),
        pltpu.VMEM((4, 16, width), BF),
        *Share.scratch(),
        *Fold.scratch(rows, width),
        pltpu.SemaphoreType.DMA,
        pltpu.SemaphoreType.DMA((3,)),
        pltpu.SemaphoreType.DMA((2, experts)),
        *scatter_scratch(count, rows, width),
        *scatter_scratch(count, block, width),
        *gather_scratch(count),
        *[pltpu.SemaphoreType.DMA((3,))] * 4,
    ] + [pltpu.SemaphoreType.DMA((experts, 2))] * 7
    return pl.pallas_call(
        kernel,
        out_shape=out_shape,
        in_specs=[vmem] * 7 + [pl.BlockSpec(memory_space=pltpu.SMEM)] + [vmem] * 2 + [far] * 3 + [vmem] * 9 + [far] * 3,
        out_specs=[vmem] * 5 + [far] * 2,
        scratch_shapes=scratch,
        compiler_params=pltpu.CompilerParams(
            collective_id=cid, has_side_effects=True, vmem_limit_bytes=62 * 2**20
        ),
    )(entry_home, pick_home, shares, router_turned, mixed, cotangent, hidden, length, attn_gain, moe_gain,
      w_query, w_key, w_value, w_out, queries, keys, values, context, whole, lse, cosine, sine, expert_part, kept, arrived)


def final_kernel(out, grad_hidden, turned, out_grad, small, up_grad, down_grad, query_cols, key_cols, experts):
    here, width, ffe2 = up_grad.shape
    ffe = down_grad.shape[1]
    step = 256
    parts = [(0, e, r) for e in range(here) for r in range(0, width, step)]
    parts += [(1, e, r) for e in range(here) for r in range(0, ffe, step)]
    parts.sort(key=lambda p: (p[1], p[0], p[2]))

    def kernel(o_in, gh_in, t_in, go_in, s_in, up_in, down_in, o_ref, gh_ref, gq, gk, gv, go, g1, g2, gr, up_ref, down_ref, low, full, in_sem, out_sem):
        near = lambda i: (up_in, down_in)[parts[i][0]].at[parts[i][1], pl.ds(parts[i][2], step)]
        away = lambda i: (up_ref, down_ref)[parts[i][0]].at[parts[i][1], pl.ds(parts[i][2], step)]
        inward = lambda i: pltpu.make_async_copy(near(i), low.at[i], in_sem.at[i])
        outward = lambda i: pltpu.make_async_copy(full.at[i], away(i), out_sem.at[i])
        for i in range(len(parts)):
            inward(i).start()
        o_ref[...] = o_in[...]
        gh_ref[...] = gh_in[...]
        gq[...] = t_in[:, :query_cols].astype(F32)
        gk[...] = t_in[:, query_cols : query_cols + key_cols].astype(F32)
        gv[...] = t_in[:, query_cols + key_cols :].astype(F32)
        go[...] = go_in[...].astype(F32)
        rows = s_in[...].astype(F32)
        g1[...] = rows[experts + 1 : experts + 2]
        g2[...] = rows[experts : experts + 1]
        gr[...] = rows[:experts]
        for i in range(len(parts)):
            inward(i).wait()
            def widen(j, carry, i=i):
                span = pl.ds(pl.multiple_of(j * 32, 32), 32)
                full[i, span] = low[i, span].astype(F32)
                return carry

            lax.fori_loop(0, step // 32, widen, 0)
            outward(i).start()
        for i in range(len(parts)):
            outward(i).wait()

    shape = jax.ShapeDtypeStruct
    vmem = pl.BlockSpec(memory_space=pltpu.VMEM)
    far = pl.BlockSpec(memory_space=pl.ANY)
    small_shapes = [
        shape(out.shape, BF), shape(grad_hidden.shape, BF), shape((width, query_cols), F32),
        shape((width, key_cols), F32), shape((width, key_cols), F32), shape(out_grad.shape, F32),
        shape((1, width), F32), shape((1, width), F32), shape((experts, width), F32),
    ]
    return pl.pallas_call(
        kernel,
        out_shape=small_shapes + [shape(up_grad.shape, F32), shape(down_grad.shape, F32)],
        in_specs=[vmem] * 5 + [far] * 2,
        out_specs=[vmem] * 9 + [far] * 2,
        scratch_shapes=[
            pltpu.VMEM((len(parts), step, width), BF),
            pltpu.VMEM((len(parts), step, width), F32),
            pltpu.SemaphoreType.DMA((len(parts),)),
            pltpu.SemaphoreType.DMA((len(parts),)),
        ],
        compiler_params=pltpu.CompilerParams(vmem_limit_bytes=62 * 2**20),
    )(out, grad_hidden, turned, out_grad, small, up_grad, down_grad)


def turn_tables(count, head_dim):
    inverse = THETA ** (-np.arange(head_dim // 2, dtype=np.float32) * np.float32(2.0 / head_dim))
    angles = np.arange(count, dtype=np.float32)[:, None] * inverse.astype(np.float32)[None, :]
    cosine, sine = np.cos(angles), np.sin(angles)
    return (
        jnp.asarray(np.concatenate([cosine] * 4, axis=1), F32),
        jnp.asarray(np.concatenate([-sine, sine] * 2, axis=1), F32),
    )


def local_general(
    hidden,
    lengths,
    routes,
    cotangent,
    attn_gain,
    w_query,
    w_key,
    w_value,
    w_out,
    moe_gain,
    w_router,
    w_gate_up,
    w_down,
):
    rows_here = hidden.shape[1]
    width = hidden.shape[2]
    seq_len = rows_here * lax.axis_size("narrow")
    head_dim = HEAD_DIM
    group_size = HEADS // KV_HEADS
    kv_here = w_key.shape[1] // head_dim
    query_cols = kv_here * group_size * head_dim
    key_cols = kv_here * head_dim
    scaling = head_dim ** (-0.5)
    block_rows = min(512, seq_len)
    block_count = seq_len // block_rows
    length_here = lengths[0]
    offset = lax.axis_index("narrow") * rows_here
    local_places = offset + jnp.arange(rows_here, dtype=jnp.int32)
    valid = (local_places < length_here).astype(jnp.float32)[:, None]
    source = hidden[0].astype(jnp.float32)
    normed, scale_one = norm_forward(source, attn_gain)
    normed_low = normed.astype(jnp.bfloat16)
    whole = lax.all_gather(normed_low, "narrow", axis=0, tiled=True)
    w_qkv = jnp.concatenate([w_query, w_key, w_value], axis=1)
    projected = jnp.dot(whole, w_qkv, preferred_element_type=jnp.float32)
    cosine, sine_part = rope_tables(seq_len, head_dim)
    query_rot = turn(
        projected[:, :query_cols].reshape(seq_len, kv_here, group_size, head_dim),
        cosine,
        sine_part,
        1.0,
    )
    key_rot = turn(
        projected[:, query_cols : query_cols + key_cols].reshape(seq_len, kv_here, head_dim),
        cosine,
        sine_part,
        1.0,
    )
    queries = (
        query_rot.astype(jnp.bfloat16)
        .reshape(block_count, block_rows, kv_here, group_size, head_dim)
        .transpose(0, 2, 3, 1, 4)
    )
    keys_low = key_rot.astype(jnp.bfloat16).transpose(1, 0, 2)
    values_low = (
        projected[:, query_cols + key_cols :]
        .astype(jnp.bfloat16)
        .reshape(seq_len, kv_here, head_dim)
        .transpose(1, 0, 2)
    )
    context, log_sums = attend_forward(queries, keys_low, values_low, length_here, scaling)
    context_rows = context.transpose(0, 3, 1, 2, 4).reshape(seq_len, query_cols)
    piece = context_rows
    attn_part = lax.psum_scatter(
        jnp.dot(piece, w_out, preferred_element_type=jnp.float32).astype(jnp.bfloat16),
        "narrow",
        scatter_dimension=0,
        tiled=True,
    ).astype(jnp.float32)
    mixed = source + attn_part
    normed_two, scale_two = norm_forward(mixed, moe_gain)
    entry = normed_two.astype(jnp.bfloat16)
    logits = jnp.dot(entry, w_router, preferred_element_type=jnp.float32)
    route_here = routes[0]
    tokens_here, picks = route_here.shape
    expert_total = w_router.shape[1]
    capacity = 2 * tokens_here * picks // expert_total
    member = (
        route_here[:, :, None] == jnp.arange(expert_total, dtype=jnp.int32)[None, None, :]
    ).astype(jnp.int32)
    flat_member = member.reshape(tokens_here * picks, expert_total)
    earlier = jnp.cumsum(flat_member, axis=0) - flat_member
    slot_index = jnp.sum(earlier * flat_member, axis=1)
    places = route_here.reshape(-1) * capacity + slot_index
    member_float = member.astype(jnp.float32)
    chosen = jnp.einsum("tke,te->tk", member_float, logits, precision=HIGHEST)
    highest = jnp.max(chosen, axis=-1, keepdims=True)
    raised = jnp.exp(chosen - highest)
    shares = raised / jnp.sum(raised, axis=-1, keepdims=True)
    gates = shares * valid
    outgoing = (
        jnp.zeros((expert_total * capacity, width), jnp.bfloat16)
        .at[places]
        .set(jnp.repeat(entry, picks, axis=0))
    )
    received = lax.all_to_all(
        outgoing.reshape(expert_total, capacity, width),
        "wide",
        split_axis=0,
        concat_axis=1,
        tiled=True,
    )
    expert_pre = jnp.einsum("erd,edf->erf", received, w_gate_up, preferred_element_type=jnp.float32)
    ffe_width = w_down.shape[1]
    gate_part = expert_pre[..., :ffe_width]
    up_part = expert_pre[..., ffe_width:]
    sigmoid_gate = jax.nn.sigmoid(gate_part)
    swish = gate_part * sigmoid_gate
    act_low = (swish * up_part).astype(jnp.bfloat16)
    expert_result = jnp.einsum(
        "erf,efd->erd", act_low, w_down, preferred_element_type=jnp.float32
    ).astype(jnp.bfloat16)
    returned = lax.all_to_all(expert_result, "wide", split_axis=1, concat_axis=0, tiled=True)
    picked = returned.reshape(expert_total * capacity, width)[places].reshape(
        tokens_here, picks, width
    )
    expert_sum = jnp.einsum("tk,tkd->td", gates, picked, precision=HIGHEST)
    output_rows = (valid * (mixed + expert_sum)).astype(jnp.bfloat16)
    grad_rows_here = cotangent[0].astype(jnp.float32) * valid
    slot_grad = (gates[:, :, None] * grad_rows_here[:, None, :]).astype(jnp.bfloat16)
    grad_outgoing = (
        jnp.zeros((expert_total * capacity, width), jnp.bfloat16)
        .at[places]
        .set(slot_grad.reshape(tokens_here * picks, width))
    )
    grad_received = lax.all_to_all(
        grad_outgoing.reshape(expert_total, capacity, width),
        "wide",
        split_axis=0,
        concat_axis=1,
        tiled=True,
    )
    act_grad = jnp.einsum("erd,efd->erf", grad_received, w_down, preferred_element_type=jnp.float32)
    down_grad = jnp.einsum(
        "erf,erd->efd", act_low, grad_received, preferred_element_type=jnp.float32
    )
    gate_grad = act_grad * up_part * sigmoid_gate * (1.0 + gate_part * (1.0 - sigmoid_gate))
    pre_grad = jnp.concatenate([gate_grad, act_grad * swish], axis=-1).astype(jnp.bfloat16)
    gate_up_grad = jnp.einsum(
        "erd,erf->edf", received, pre_grad, preferred_element_type=jnp.float32
    )
    entry_back = jnp.einsum(
        "erf,edf->erd", pre_grad, w_gate_up, preferred_element_type=jnp.float32
    ).astype(jnp.bfloat16)
    entry_home = lax.all_to_all(entry_back, "wide", split_axis=1, concat_axis=0, tiled=True)
    entry_rows = entry_home.reshape(expert_total * capacity, width)[places].reshape(
        tokens_here, picks, width
    )
    entry_grad = jnp.sum(entry_rows, axis=1, dtype=jnp.float32)
    pick_grad = jnp.einsum("td,tkd->tk", grad_rows_here, picked, precision=HIGHEST) * valid
    chosen_grad = shares * (pick_grad - jnp.sum(shares * pick_grad, axis=-1, keepdims=True))
    logit_grad = jnp.einsum("tk,tke->te", chosen_grad, member_float, precision=HIGHEST)
    router_grad = lax.dot_general(
        entry.astype(jnp.float32), logit_grad, (((0,), (0,)), ((), ())), precision=HIGHEST
    )
    entry_grad = entry_grad + lax.dot_general(
        logit_grad, w_router.astype(jnp.float32), (((1,), (1,)), ((), ())), precision=HIGHEST
    )
    mixed_from_norm, gain_two_grad = norm_backward(mixed, scale_two, moe_gain, entry_grad)
    mixed_grad = grad_rows_here + mixed_from_norm
    attn_grad_low = mixed_grad.astype(jnp.bfloat16)
    grad_whole = lax.all_gather(attn_grad_low, "narrow", axis=0, tiled=True)
    context_grad = lax.dot_general(
        grad_whole, w_out, (((1,), (1,)), ((), ())), preferred_element_type=jnp.float32
    ).astype(jnp.bfloat16)
    out_grad = lax.dot_general(
        context_rows, grad_whole, (((0,), (0,)), ((), ())), preferred_element_type=jnp.float32
    )
    context_blocks = context_grad.reshape(
        block_count, block_rows, kv_here, group_size, head_dim
    ).transpose(0, 2, 3, 1, 4)
    query_grad, key_grad, value_grad = attend_backward(
        queries, keys_low, values_low, context_blocks, log_sums, length_here, scaling
    )
    query_rows = turn(
        query_grad.transpose(0, 3, 1, 2, 4).reshape(seq_len, kv_here, group_size, head_dim),
        cosine,
        sine_part,
        -1.0,
    )
    key_rows = turn(key_grad.transpose(1, 0, 2), cosine, sine_part, -1.0)
    value_rows = value_grad.transpose(1, 0, 2)
    qkv_grad = jnp.concatenate(
        [
            query_rows.reshape(seq_len, query_cols),
            key_rows.reshape(seq_len, key_cols),
            value_rows.reshape(seq_len, key_cols),
        ],
        axis=1,
    ).astype(jnp.bfloat16)
    qkv_weight_grad = lax.dot_general(
        whole, qkv_grad, (((0,), (0,)), ((), ())), preferred_element_type=jnp.float32
    )
    piece = qkv_grad
    normed_grad = lax.psum_scatter(
        lax.dot_general(
            piece, w_qkv, (((1,), (1,)), ((), ())), preferred_element_type=jnp.float32
        ).astype(jnp.bfloat16),
        "narrow",
        scatter_dimension=0,
        tiled=True,
    ).astype(jnp.float32)
    source_from_norm, gain_one_grad = norm_backward(source, scale_one, attn_gain, normed_grad)
    grad_input = (mixed_grad + source_from_norm).astype(jnp.bfloat16)
    gate_up_grad, down_grad, router_grad, gain_one_grad, gain_two_grad = (
        lax.psum(gate_up_grad.astype(jnp.bfloat16), "narrow").astype(jnp.float32),
        lax.psum(down_grad.astype(jnp.bfloat16), "narrow").astype(jnp.float32),
        lax.psum(router_grad.astype(jnp.bfloat16), "narrow").astype(jnp.float32),
        lax.psum(gain_one_grad.astype(jnp.bfloat16), "narrow").astype(jnp.float32),
        lax.psum(gain_two_grad.astype(jnp.bfloat16), "narrow").astype(jnp.float32),
    )
    qkv_weight_grad, out_grad, router_grad, gain_one_grad, gain_two_grad = (
        lax.psum(qkv_weight_grad.astype(jnp.bfloat16), "wide").astype(jnp.float32),
        lax.psum(out_grad.astype(jnp.bfloat16), "wide").astype(jnp.float32),
        lax.psum(router_grad.astype(jnp.bfloat16), "wide").astype(jnp.float32),
        lax.psum(gain_one_grad.astype(jnp.bfloat16), "wide").astype(jnp.float32),
        lax.psum(gain_two_grad.astype(jnp.bfloat16), "wide").astype(jnp.float32),
    )
    query_weight_grad = qkv_weight_grad[:, :query_cols]
    key_weight_grad = qkv_weight_grad[:, query_cols : query_cols + key_cols]
    value_weight_grad = qkv_weight_grad[:, query_cols + key_cols :]
    return (
        output_rows[None],
        grad_input[None],
        gain_one_grad,
        query_weight_grad,
        key_weight_grad,
        value_weight_grad,
        out_grad,
        gain_two_grad,
        router_grad,
        gate_up_grad,
        down_grad,
    )


def local(
    hidden,
    lengths,
    routes,
    cotangent,
    attn_gain,
    w_query,
    w_key,
    w_value,
    w_out,
    moe_gain,
    w_router,
    w_gate_up,
    w_down,
):
    kv_here = w_key.shape[1] // HEAD_DIM
    rows, width = hidden.shape[1:]
    if lax.axis_size("narrow") != 4 or kv_here != 2 or rows != 256:
        return local_general(
            hidden, lengths, routes, cotangent, attn_gain, w_query, w_key, w_value, w_out,
            moe_gain, w_router, w_gate_up, w_down,
        )
    count = lax.axis_size("wide")
    picks = routes.shape[2]
    expert_total = w_router.shape[1]
    expert_here = w_gate_up.shape[0]
    capacity = 2 * rows * picks // expert_total
    query_cols, key_cols = w_query.shape[1], w_key.shape[1]
    cosine, sine = turn_tables(4 * rows, HEAD_DIM)
    router_turned = w_router.T
    gain_one, gain_two = attn_gain[None], moe_gain[None]
    entry, grad_all, whole, queries, keys, values, context, lse, mixed, slots, labels_all = front_kernel(
        hidden[0], cotangent[0], routes[0].T, lengths, gain_one, w_query, w_key, w_value, w_out, gain_two,
        cosine, sine, count, expert_here, 1,
    )
    entry_home, pick_home, expert_part, kept, arrived, shares, _ = middle_kernel(
        entry, grad_all, labels_all, slots, router_turned, w_gate_up, w_down, capacity, picks, 2
    )
    results = tail_kernel(
        entry_home, pick_home, shares, router_turned, mixed,
        cotangent[0], hidden[0], lengths, gain_one, gain_two, w_query, w_key, w_value, w_out, queries, keys,
        values, context, whole.reshape(4 * rows, width), lse, cosine, sine, expert_part, kept, arrived,
        (w_gate_up.shape, w_down.shape), 3,
    )
    out, grad_hidden, grad_q, grad_k, grad_v, grad_out, grad_one, grad_two, grad_router, grad_up, grad_down = final_kernel(
        *results, query_cols, key_cols, expert_total
    )
    return (
        out[None], grad_hidden[None], grad_one[0], grad_q, grad_k, grad_v, grad_out, grad_two[0], grad_router.T,
        grad_up, grad_down,
    )


def solution(mesh):
    in_specs = (
        P("wide", "narrow", None),
        P("wide"),
        P("wide", "narrow", None),
        P("wide", "narrow", None),
        P(),
        P(None, "narrow"),
        P(None, "narrow"),
        P(None, "narrow"),
        P("narrow", None),
        P(),
        P(),
        P("wide", None, None),
        P("wide", None, None),
    )
    out_specs = (
        P("wide", "narrow", None),
        P("wide", "narrow", None),
        P(),
        P(None, "narrow"),
        P(None, "narrow"),
        P(None, "narrow"),
        P("narrow", None),
        P(),
        P(),
        P("wide", None, None),
        P("wide", None, None),
    )
    return jax.shard_map(local, mesh=mesh, in_specs=in_specs, out_specs=out_specs, check_vma=False)
```

```python
import jax
import numpy as np
import jax.numpy as jnp
from jax import lax
from jax.experimental import pallas as pl
from jax.experimental.pallas import tpu as pltpu
from jax.sharding import PartitionSpec as P

HEADS = 16
KV_HEADS = 8
HEAD_DIM = 64
BF = jnp.bfloat16
F32 = jnp.float32
MESH = pl.DeviceIdType.MESH
EPSILON = 1e-06
THETA = 10000.0
HIGHEST = lax.Precision.HIGHEST


def rope_tables(count, head_dim):
    half_dim = head_dim // 2
    inverse = THETA ** (-jnp.arange(half_dim, dtype=jnp.float32) * 2.0 / head_dim)
    angles = jnp.arange(count, dtype=jnp.float32)[:, None] * inverse[None, :]
    return (jnp.cos(angles), jnp.sin(angles))


def turn(values, cosine, sine_part, direction):
    half_dim = values.shape[-1] // 2
    shape_here = (cosine.shape[0],) + (1,) * (values.ndim - 2) + (half_dim,)
    cosine = cosine.reshape(shape_here)
    sine_part = direction * sine_part.reshape(shape_here)
    first = values[..., :half_dim]
    second = values[..., half_dim:]
    return jnp.concatenate(
        [first * cosine - second * sine_part, second * cosine + first * sine_part], axis=-1
    )


def norm_forward(values, gain):
    scaling = lax.rsqrt(jnp.mean(values * values, axis=-1, keepdims=True) + EPSILON)
    return (values * scaling * gain, scaling)


def norm_backward(values, scaling, gain, incoming):
    unit_values = values * scaling
    gain_grad = jnp.sum(incoming * unit_values, axis=0)
    inner = incoming * gain
    input_grad = scaling * (
        inner - unit_values * jnp.mean(inner * unit_values, axis=-1, keepdims=True)
    )
    return (input_grad, gain_grad)


def visible(start, block_rows, key_places, length_here):
    query_places = start + jnp.arange(block_rows, dtype=jnp.int32)
    return (key_places[None, :] <= query_places[:, None]) & (key_places[None, :] < length_here)


def attend_forward(queries, keys_low, values_low, length_here, scaling):
    key_places = jnp.arange(keys_low.shape[1], dtype=jnp.int32)
    block_rows = queries.shape[3]

    def one_block(inputs):
        query_block, start = inputs
        scores = (
            jnp.einsum("kgqd,ksd->kgqs", query_block, keys_low, preferred_element_type=jnp.float32)
            * scaling
        )
        scores = jnp.where(visible(start, block_rows, key_places, length_here), scores, -1e30)
        highest = jnp.max(scores, axis=-1, keepdims=True)
        weights = jnp.exp(scores - highest)
        totals = jnp.sum(weights, axis=-1, keepdims=True)
        chances = (weights / totals).astype(jnp.bfloat16)
        context = jnp.einsum(
            "kgqs,ksd->kgqd", chances, values_low, preferred_element_type=jnp.float32
        )
        return (context.astype(jnp.bfloat16), (highest + jnp.log(totals))[..., 0])

    starts = jnp.arange(queries.shape[0], dtype=jnp.int32) * block_rows
    return lax.map(one_block, (queries, starts))


def attend_backward(queries, keys_low, values_low, context_grad, log_sums, length_here, scaling):
    key_places = jnp.arange(keys_low.shape[1], dtype=jnp.int32)
    block_rows = queries.shape[3]

    def one_block(carry, inputs):
        key_grad, value_grad = carry
        query_block, grad_block, sum_block, start = inputs
        scores = (
            jnp.einsum("kgqd,ksd->kgqs", query_block, keys_low, preferred_element_type=jnp.float32)
            * scaling
        )
        allowed = visible(start, block_rows, key_places, length_here)
        scores = jnp.where(allowed, scores, -1e30)
        chances = jnp.where(allowed, jnp.exp(scores - sum_block[..., None]), 0.0)
        chance_grad = jnp.einsum(
            "kgqd,ksd->kgqs", grad_block, values_low, preferred_element_type=jnp.float32
        )
        inner = jnp.sum(chances * chance_grad, axis=-1, keepdims=True)
        score_grad = (chances * (chance_grad - inner)).astype(jnp.bfloat16)
        query_grad = (
            jnp.einsum("kgqs,ksd->kgqd", score_grad, keys_low, preferred_element_type=jnp.float32)
            * scaling
        )
        key_grad = (
            key_grad
            + jnp.einsum(
                "kgqs,kgqd->ksd", score_grad, query_block, preferred_element_type=jnp.float32
            )
            * scaling
        )
        value_grad = value_grad + jnp.einsum(
            "kgqs,kgqd->ksd",
            chances.astype(jnp.bfloat16),
            grad_block,
            preferred_element_type=jnp.float32,
        )
        return ((key_grad, value_grad), query_grad)

    starts = jnp.arange(queries.shape[0], dtype=jnp.int32) * block_rows
    zeros = jnp.zeros(keys_low.shape, jnp.float32)
    (key_grad, value_grad), query_grad = lax.scan(
        one_block, (zeros, zeros), (queries, context_grad, log_sums, starts)
    )
    return (query_grad, key_grad, value_grad)


def ring_place(index, count):
    half = index // 2
    odd = index % 2
    return (1 - odd) * half + odd * (count - 1 - half)

def ring_index(place, count):
    odd = place // (count // 2)
    half = (1 - odd) * place + odd * (count - 1 - place)
    return 2 * half + odd


def add_low(one, two):
    return (one.astype(F32) + two.astype(F32)).astype(BF)

class Ring:
    def __init__(self, count):
        self.count = count
        self.me = lax.axis_index("wide")
        self.place = ring_place(self.me, count)
        self.peers = (self.at(1), self.at(-1))

    def at(self, shift):
        return ring_index((self.place + shift + 2 * self.count) % self.count, self.count)

def greet(wide_peers, narrow_peers):
    barrier = pltpu.get_barrier_semaphore()
    for peer in wide_peers:
        pl.semaphore_signal(barrier, inc=1, device_id={"wide": peer}, device_id_type=MESH)
    for peer in narrow_peers:
        pl.semaphore_signal(barrier, inc=1, device_id={"narrow": peer}, device_id_type=MESH)
    pl.semaphore_wait(barrier, len(wide_peers) + len(narrow_peers))

def remote(source, target, send, recv, **device):
    return pltpu.make_async_remote_copy(
        src_ref=source, dst_ref=target, send_sem=send, recv_sem=recv,
        device_id=device, device_id_type=MESH,
    )

def cuts(rows):
    first = (rows // 2 + 15) // 16 * 16
    return ((0, first), (first, rows - first))

def scatter_steps(ring, p_ref, held, send_sem, recv_sem, finish):
    count = ring.count
    lane = p_ref.shape[1] // 2

    def copy(way, step, k):
        sign = 1 if way == 0 else -1
        start, size = cuts(lane)[k]
        src = (
            p_ref.at[ring.at(-sign), pl.ds(way * lane + start, size)]
            if step == 0
            else held.at[way, step - 1, pl.ds(start, size)]
        )
        return remote(
            src, held.at[way, step, pl.ds(start, size)],
            send_sem.at[way, step, k], recv_sem.at[way, step, k], wide=ring.peers[way],
        )

    for step in range(count - 1):
        for k in range(2):
            for way in range(2):
                sign = 1 if way == 0 else -1
                start, size = cuts(lane)[k]
                if step > 0:
                    copy(way, step - 1, k).wait_recv()
                    span = pl.ds(start, size)
                    mine = p_ref[ring.at(-sign * (1 + step)), pl.ds(way * lane + start, size)]
                    held[way, step - 1, span] = add_low(held[way, step - 1, span], mine)
                copy(way, step, k).start()
        yield
    for k in range(2):
        for way in range(2):
            start, size = cuts(lane)[k]
            copy(way, count - 2, k).wait_recv()
            row = way * lane + start
            finish(
                row, size,
                held[way, count - 2, pl.ds(start, size)].astype(F32)
                + p_ref[ring.me, pl.ds(row, size)].astype(F32),
            )
    for step in range(count - 1):
        for k in range(2):
            for way in range(2):
                copy(way, step, k).wait_send()
    yield

def gather_steps(ring, o_ref, send_sem, recv_sem, own=None, left=0):
    count = ring.count
    hops = count // 2
    rows = o_ref.shape[1]
    live = lambda way, hop, k: hop < hops - 1 or k == way

    def copy(way, hop, k, shift):
        sign = 1 if way == 0 else -1
        start, size = cuts(rows)[k]
        block = o_ref.at[ring.at(-sign * (hop + shift)), pl.ds(start, size)]
        from_own = own is not None and hop == 0 and shift == 0
        return remote(
            own.at[pl.ds(start, size)] if from_own else block, block, send_sem.at[way, hop, k], recv_sem.at[way, hop, k], wide=ring.peers[way]
        )

    for hop in range(hops - left):
        for k in range(2):
            for way in range(2):
                if hop > 0:
                    copy(way, hop - 1, k, 1).wait_recv()
                if live(way, hop, k):
                    copy(way, hop, k, 0).start()
        yield
    for k in range(2):
        for way in range(2):
            if live(way, hops - left - 1, k):
                copy(way, hops - left - 1, k, 1).wait_recv()
    for hop in range(hops - left):
        for k in range(2):
            for way in range(2):
                if live(way, hop, k):
                    copy(way, hop, k, 0).wait_send()
    yield

def scatter_scratch(count, rows, cols):
    return [
        pltpu.VMEM((2, count - 1, rows // 2, cols), BF),
        pltpu.SemaphoreType.DMA((2, count - 1, 2)),
        pltpu.SemaphoreType.DMA((2, count - 1, 2)),
    ]

def gather_scratch(count):
    return [pltpu.SemaphoreType.DMA((2, count // 2, 2)), pltpu.SemaphoreType.DMA((2, count // 2, 2))]

def run(*makers):
    live = list(makers)
    while live:
        for one in list(live):
            if next(one, "end") == "end":
                live.remove(one)

def block_add(out, one, two, rows):
    def step(i, carry):
        span = pl.ds(pl.multiple_of(i * 128, 128), 128)
        out[span] = add_low(one[span], two[span])
        return carry
    lax.fori_loop(0, rows // 128, step, 0)


def nt(a, b):
    return lax.dot_general(a, b, (((1,), (1,)), ((), ())), preferred_element_type=F32)

def tn(a, b):
    return lax.dot_general(a, b, (((0,), (0,)), ((), ())), preferred_element_type=F32)

def nn(a, b):
    return jnp.dot(a, b, preferred_element_type=F32)

LANES = 128

def lane_of(shape):
    return lax.broadcasted_iota(jnp.int32, shape, len(shape) - 1)

def turn_lanes(values, cosine, signed_sine):
    low = lane_of(values.shape) % HEAD_DIM < HEAD_DIM // 2
    swapped = jnp.where(
        low,
        pltpu.roll(values, LANES - HEAD_DIM // 2, 1),
        pltpu.roll(values, HEAD_DIM // 2, 1),
    )
    return values * cosine + swapped * signed_sine

def doubled(tile, head):
    other = pltpu.roll(tile, HEAD_DIM, 1)
    low = lane_of(tile.shape) < HEAD_DIM
    return jnp.where(low, tile, other) if head == 0 else jnp.where(low, other, tile)

def stacked(tile):
    low = lane_of(tile.shape) < HEAD_DIM
    zero = jnp.zeros_like(tile)
    return jnp.concatenate([jnp.where(low, tile, zero), jnp.where(low, zero, tile)], axis=0)

def unstacked(turned):
    full = turned.T
    rows = full.shape[0] // 2
    return jnp.where(lane_of((rows, LANES)) < HEAD_DIM, full[:rows], full[rows:])

def masked_scores(keys, queries, key_start, query_start, length, causal):
    scores = nt(keys, queries) * HEAD_DIM ** (-0.5)
    half = queries.shape[0] // 2
    key_at = key_start + lax.broadcasted_iota(jnp.int32, scores.shape, 0)
    allowed = key_at < length
    if causal:
        query_at = query_start + lane_of(scores.shape) % half
        allowed = allowed & (key_at <= query_at)
    return jnp.where(allowed, scores, -1e30)

class Corner:
    def __init__(self):
        self.here = lax.axis_index("narrow")
        self.chip, self.core = self.here // 2, self.here % 2
        self.core_peer = 2 * self.chip + 1 - self.core
        self.chip_peer = 2 * (1 - self.chip) + self.core
        self.far_peer = 2 * (1 - self.chip) + 1 - self.core

class Share:
    def __init__(self, corner, ref, send, recv):
        self.corner, self.ref, self.sems = corner, ref, (send, recv)

    def copy(self, kind, k, owner, peer):
        start, size = cuts(self.ref.shape[1])[k]
        block = self.ref.at[owner, pl.ds(start, size)]
        return remote(block, block, self.sems[0].at[kind, k], self.sems[1].at[kind, k], narrow=peer)

    def start(self):
        c = self.corner
        for k in range(2):
            self.copy(1, k, c.here, c.chip_peer).start()
        for k in range(2):
            self.copy(0, k, c.here, c.core_peer).start()

    def wait_core(self):
        c = self.corner
        for k in range(2):
            self.copy(0, k, c.core_peer, c.core_peer).wait_recv()

    def wait_chip(self):
        c = self.corner
        for k in range(2):
            self.copy(1, k, c.chip_peer, c.chip_peer).wait_recv()
            self.copy(2, k, c.chip_peer, c.core_peer).start()

    def wait_far(self):
        c = self.corner
        for k in range(2):
            self.copy(2, k, c.far_peer, c.core_peer).wait_recv()

    def drain(self):
        c = self.corner
        for k in range(2):
            self.copy(0, k, c.here, c.core_peer).wait_send()
            self.copy(1, k, c.here, c.chip_peer).wait_send()
            self.copy(2, k, c.chip_peer, c.core_peer).wait_send()

    scratch = lambda: [pltpu.SemaphoreType.DMA((3, 2)), pltpu.SemaphoreType.DMA((3, 2))]

class Fold:
    def __init__(self, corner, out_c, got_c, out_x, got_x, held, c_send, c_recv, x_send, x_recv):
        self.corner, self.held = corner, held
        self.out_c, self.got_c, self.out_x, self.got_x = out_c, got_c, out_x, got_x
        self.sems = (c_send, c_recv, x_send, x_recv)

    def to_core(self, x):
        return remote(
            self.out_c.at[x], self.got_c.at[x], self.sems[0].at[x], self.sems[1].at[x],
            narrow=self.corner.core_peer,
        )

    def to_chip(self):
        return remote(self.out_x, self.got_x, self.sems[2], self.sems[3], narrow=self.corner.chip_peer)

    def give(self, block, part):
        x, c = block // 2, block % 2

        @pl.when(self.corner.core != c)
        def _():
            self.out_c[x] = part.astype(BF)
            self.to_core(x).start()

        @pl.when(self.corner.core == c)
        def _():
            self.held[x] = part

    def settle(self, block):
        x, c = block // 2, block % 2

        @pl.when(self.corner.core == c)
        def _():
            self.to_core(x).wait_recv()

            @pl.when(self.corner.chip != x)
            def _():
                self.out_x[...] = (self.held[x] + self.got_c[x].astype(F32)).astype(BF)
                self.to_chip().start()

    def total(self):
        chip = self.corner.chip
        near = self.held[chip] + self.got_c[chip].astype(F32)
        self.to_chip().wait_recv()
        return near + self.got_x[...].astype(F32)

    def drain(self):
        for x in range(2):
            self.to_core(x).wait_send()
        self.to_chip().wait_send()

    def scratch(rows, cols):
        return [
            pltpu.VMEM((2, rows, cols), BF),
            pltpu.VMEM((2, rows, cols), BF),
            pltpu.VMEM((rows, cols), BF),
            pltpu.VMEM((rows, cols), BF),
            pltpu.VMEM((2, rows, cols), F32),
            pltpu.SemaphoreType.DMA((2,)),
            pltpu.SemaphoreType.DMA((2,)),
            pltpu.SemaphoreType.DMA,
            pltpu.SemaphoreType.DMA,
        ]

def front_kernel(hidden, cotangent, routes, length, attn_gain, w_query, w_key, w_value, w_out, moe_gain, cosine, sine, count, experts_here, cid):
    rows, width = hidden.shape
    seq = 4 * rows
    query_cols, key_cols = w_query.shape[1], w_key.shape[1]
    picks = routes.shape[0]
    kv_here = key_cols // HEAD_DIM

    def kernel(*refs):
        refs = list(refs)
        take = lambda number: [refs.pop(0) for _ in range(number)]
        h_ref, cot_ref, route_ref, len_ref, g1_ref, wq_far, wk_far, wv_far, wout_ref, g2_ref, cos_ref, sin_ref = take(12)
        en_ref, ga_ref, whole_ref, q_ref, k_ref, v_ref, ctx_ref, lse_ref, mixed_ref, slots_ref, lab_all = take(11)
        kd, vd, s_scr, p_scr, wqkv_ref, lab_ref = take(6)
        share = take(2)
        fold = take(9)
        g_scr = take(2)
        l_send, l_recv, own_sem, w_sem = take(4)
        ring, corner = Ring(count), Corner()
        others = [(ring.me + shift) % count for shift in range(1, count)]
        w_loads = [
            pltpu.make_async_copy(src, wqkv_ref.at[:, pl.ds(start, size)], w_sem.at[k])
            for k, (src, start, size) in enumerate(
                ((wq_far, 0, query_cols), (wk_far, query_cols, key_cols), (wv_far, query_cols + key_cols, key_cols))
            )
        ]
        for c in w_loads:
            c.start()
        length_here = len_ref[0]
        lab_ref[0:picks] = route_ref[...]
        lab_ref[picks : 2 * picks] = jnp.full((picks, rows), length_here, jnp.int32)
        greet(others, [corner.core_peer, corner.chip_peer])

        g_ring = gather_steps(ring, ga_ref, *g_scr, own=cot_ref, left=1)
        next(g_ring)
        own_grad = pltpu.make_async_copy(cot_ref, ga_ref.at[ring.me], own_sem)
        own_grad.start()
        label_copy = lambda k, target: remote(
            lab_ref, lab_all.at[ring.me], l_send.at[k], l_recv.at[k], wide=target
        )
        for k, target in enumerate(others):
            label_copy(k, target).start()
        lab_all[ring.me] = lab_ref[...]

        source = h_ref[...].astype(F32)
        scale = lax.rsqrt(jnp.mean(source * source, axis=1, keepdims=True) + EPSILON)
        whole_ref[corner.here] = (source * scale * g1_ref[...]).astype(BF)
        sharing = Share(corner, whole_ref, *share)
        sharing.start()

        def project(block):
            span = pl.ds(pl.multiple_of(block * rows, rows), rows)
            lin = nn(whole_ref[block], wqkv_ref[...])
            cos, sin = cos_ref[span], sin_ref[span]
            for t in range(kv_here):
                lanes = slice(t * LANES, (t + 1) * LANES)
                q_ref[span, lanes] = turn_lanes(lin[:, lanes], cos, sin).astype(BF)
            keys = turn_lanes(lin[:, query_cols : query_cols + key_cols], cos, sin)
            values = lin[:, query_cols + key_cols :]
            k_ref[span] = keys.astype(BF)
            v_ref[span] = values.astype(BF)
            for t in range(kv_here):
                kd[t, span] = doubled(keys, t).astype(BF)
                vd[t, span] = doubled(values, t).astype(BF)

        for c in w_loads:
            c.wait()
        project(corner.here)
        sharing.wait_core()
        project(corner.core_peer)

        for k, target in enumerate(others):
            sender = (ring.me - (k + 1) + count) % count
            remote(lab_ref, lab_all.at[sender], l_send.at[k], l_recv.at[k], wide=target).wait_recv()
        places = corner.here * rows + lane_of((1, rows))
        first = ring.me * experts_here
        upper = jnp.where(
            lax.broadcasted_iota(jnp.int32, (rows, rows), 0) <= lane_of((rows, rows)), 1.0, 0.0
        ).astype(BF)

        def belongs(block, expert_rows):
            found = lab_all[block, 0:1] == expert_rows
            for k in range(1, picks):
                found = found | (lab_all[block, k : k + 1] == expert_rows)
            return found

        local_rows = lax.broadcasted_iota(jnp.int32, (8, rows), 0)
        own_rows = jnp.where(local_rows < experts_here, first + local_rows, -1)
        for b in range(count):
            mine = jnp.where(belongs(b, own_rows) & (places < lab_all[b, picks : picks + 1]), 1.0, 0.0)
            reached = nn(mine.astype(BF), upper)
            slots_ref[b] = jnp.where(mine > 0.0, reached, 0.0).astype(jnp.int32) - 1

        sharing.wait_chip()
        next(g_ring)
        project(corner.chip_peer)
        sharing.wait_far()
        project(corner.far_peer)

        folding = Fold(corner, *fold)
        before = None
        for block in (3, 2, 1, 0):
            span = pl.ds(block * rows, rows)
            for t in range(kv_here):
                lanes = slice(t * LANES, (t + 1) * LANES)
                queries = stacked(q_ref[span, lanes])
                highest = None
                for b in range(block + 1):
                    keys = pl.ds(b * rows, rows)
                    scores = masked_scores(kd[t, keys], queries, b * rows, block * rows, length_here, b == block)
                    s_scr[keys] = scores
                    top = jnp.max(scores, axis=0, keepdims=True)
                    highest = top if highest is None else jnp.maximum(highest, top)
                total = None
                for b in range(block + 1):
                    keys = pl.ds(b * rows, rows)
                    weights = jnp.exp(s_scr[keys] - highest)
                    p_scr[keys] = weights.astype(BF)
                    one = jnp.sum(weights, axis=0, keepdims=True)
                    total = one if total is None else total + one
                keys = pl.ds(0, (block + 1) * rows)
                context = tn(vd[t, keys], p_scr[keys]) / total
                ctx_ref[span, lanes] = unstacked(context).astype(BF)
                lse_ref[t * 4 + block : t * 4 + block + 1] = highest + jnp.log(total)
            folding.give(block, nn(ctx_ref[span], wout_ref[...]))
            if before is not None:
                folding.settle(before)
            before = block
            if block == 1:
                next(g_ring)
        folding.settle(before)
        mixed = source + folding.total()
        mixed_ref[...] = mixed
        scale = lax.rsqrt(jnp.mean(mixed * mixed, axis=1, keepdims=True) + EPSILON)
        en_ref[...] = (mixed * scale * g2_ref[...]).astype(BF)
        for _ in g_ring:
            pass
        for k, target in enumerate(others):
            label_copy(k, target).wait_send()
        own_grad.wait()
        sharing.drain()
        folding.drain()

    vmem = pl.BlockSpec(memory_space=pltpu.VMEM)
    far = pl.BlockSpec(memory_space=pl.ANY)
    shape = jax.ShapeDtypeStruct
    out_shape = [
        shape((rows, width), BF),
        shape((count, rows, width), BF),
        shape((4, rows, width), BF),
        shape((seq, query_cols), BF),
        shape((seq, key_cols), BF),
        shape((seq, key_cols), BF),
        shape((seq, query_cols), BF),
        shape((8, 2 * rows), F32),
        shape((rows, width), F32),
        shape((count, 8, rows), jnp.int32),
        shape((count, 2 * picks, rows), jnp.int32),
    ]
    scratch = [
        pltpu.VMEM((kv_here, seq, LANES), BF),
        pltpu.VMEM((kv_here, seq, LANES), BF),
        pltpu.VMEM((seq, 2 * rows), F32),
        pltpu.VMEM((seq, 2 * rows), BF),
        pltpu.VMEM((width, query_cols + 2 * key_cols), BF),
        pltpu.VMEM((2 * picks, rows), jnp.int32),
        *Share.scratch(),
        *Fold.scratch(rows, width),
        *gather_scratch(count),
        pltpu.SemaphoreType.DMA((count - 1,)),
        pltpu.SemaphoreType.DMA((count - 1,)),
        pltpu.SemaphoreType.DMA,
        pltpu.SemaphoreType.DMA((3,)),
    ]
    return pl.pallas_call(
        kernel,
        out_shape=out_shape,
        in_specs=[vmem, far, vmem, pl.BlockSpec(memory_space=pltpu.SMEM)] + [vmem] + [far] * 3 + [vmem] * 4,
        out_specs=[vmem, far] + [vmem] * (len(out_shape) - 2),
        scratch_shapes=scratch,
        compiler_params=pltpu.CompilerParams(
            collective_id=cid, has_side_effects=True, vmem_limit_bytes=56 * 2**20
        ),
    )(hidden, cotangent, routes, length, attn_gain, w_query, w_key, w_value, w_out, moe_gain, cosine, sine)


def middle_kernel(entry, grad_all, labels_all, slots, router_turned, w_gate_up, w_down, capacity, picks, cid):
    rows, width = entry.shape
    count = grad_all.shape[0]
    experts_here, _, ffe2 = w_gate_up.shape
    ffe = ffe2 // 2
    experts = router_turned.shape[0]
    hops = count // 2
    shifts = [0] + [s for hop in range(1, hops) for s in (hop, -hop)] + [hops]
    room = count * capacity
    quarter_up, quarter_down = width // 4, ffe // 4
    quarter = quarter_up + quarter_down

    def kernel(*refs):
        refs = list(refs)
        take = lambda number: [refs.pop(0) for _ in range(number)]
        en_far, ga_far, lab_all, slots_ref, wr_ref, wgu_far, wd_far = take(7)
        ob_ref, op_ref, c_far, keep_far, got_far, shares_ref, wait_far = take(7)
        wgu, wd, e_buf, g_buf, pg, act_s, x_s, s_s, b_buf, c_slot, got_a, gates, pick_buf, last_c, last_b = take(15)
        held = take(3)
        e_scr = take(2)
        w_sem, g_sem, c_sem, p_send, p_recv, a_send, a_recv, x_send, x_recv, o_sem, f_sem, en_sem, far_send, far_recv = take(14)
        ring, corner = Ring(count), Corner()
        others = [(ring.me + shift) % count for shift in range(1, count)]
        greet(others, [corner.core_peer, corner.chip_peer])

        def weights(e):
            return [
                pltpu.make_async_copy(wgu_far.at[e], wgu.at[e], w_sem.at[0, e]),
                pltpu.make_async_copy(wd_far.at[e], wd.at[e], w_sem.at[1, e]),
            ]

        def grads(p):
            block = ring.at(shifts[p])
            return pltpu.make_async_copy(ga_far.at[block], g_buf.at[block], g_sem.at[p])

        def far_grads(way, shift):
            sign = 1 if way == 0 else -1
            block = ring.at(-sign * (hops - 1 + shift))
            start, size = cuts(rows)[way]
            source = ga_far if shift == 0 else g_buf
            return remote(
                source.at[block, pl.ds(start, size)], g_buf.at[block, pl.ds(start, size)],
                far_send.at[way], far_recv.at[way], wide=ring.peers[way],
            )

        e_ring = gather_steps(ring, e_buf, *e_scr, own=en_far)
        next(e_ring)
        own_entry = pltpu.make_async_copy(en_far, e_buf.at[ring.me], en_sem)
        own_entry.start()
        for e in range(experts_here):
            for c in weights(e):
                c.start()
            if e == 0:
                for p in range(count - 1):
                    grads(p).start()

        places = corner.here * rows + lane_of((1, rows))
        first = ring.me * experts_here
        every = lax.broadcasted_iota(jnp.int32, (experts, rows), 0)
        local_rows = lax.broadcasted_iota(jnp.int32, (8, rows), 0)
        slot_rows = lax.broadcasted_iota(jnp.int32, (capacity, rows), 0)

        def gate(block, home):
            logits = nt(wr_ref[...], e_buf[block])
            member = lab_all[block, 0:1] == every
            for k in range(1, picks):
                member = member | (lab_all[block, k : k + 1] == every)
            masked = jnp.where(member, logits, -jnp.inf)
            raised = jnp.exp(masked - jnp.max(masked, axis=0, keepdims=True))
            shares = raised / jnp.sum(raised, axis=0, keepdims=True)
            if home:
                shares_ref[...] = shares
            kept = jnp.where(places < lab_all[block, picks : picks + 1], shares, 0.0)
            own = jnp.zeros((8, rows), F32)
            for e in range(experts_here):
                row = jnp.sum(jnp.where(every == first + e, kept, 0.0), axis=0, keepdims=True)
                own = jnp.where(local_rows == e, row, own)
            gates[block] = own

        def pick_rows(block, e):
            return slot_rows == slots_ref[block, pl.ds(e, 1), :]

        def gather_rows(block, e):
            found = pick_rows(block, e)
            chosen = jnp.where(found, 1.0, 0.0).astype(BF)
            gate_col = jnp.sum(jnp.where(found, gates[block, pl.ds(e, 1), :], 0.0), axis=1, keepdims=True)
            return found, nn(chosen, e_buf[block]).astype(BF), nn(chosen, g_buf[block]), gate_col

        def chain(numbers, e, result_rows, back_rows, row, await_weights=False):
            blocks = [ring.at(shifts[p]) for p in numbers]
            size = len(numbers) * capacity
            here = pl.ds(pl.multiple_of(row, capacity), size)
            span = pl.ds(numbers[0] * capacity, size)
            if await_weights:
                for c in weights(e):
                    c.wait()
            parts = [gather_rows(block, e) for block in blocks]
            entries = jnp.concatenate([p[1] for p in parts], axis=0)
            grad_rows = jnp.concatenate([p[2] for p in parts], axis=0)
            gate_col = jnp.concatenate([p[3] for p in parts], axis=0)
            slot_grad = (gate_col * grad_rows).astype(BF)
            pre = nn(entries, wgu[e])
            act_grad = nt(slot_grad, wd[e])
            gate_part = pre[:, :ffe]
            up_part = pre[:, ffe:]
            sig = jax.nn.sigmoid(gate_part)
            swish = gate_part * sig
            act = (swish * up_part).astype(BF)
            act_s[e, span] = act
            gate_grad = act_grad * up_part * sig * (1.0 + gate_part * (1.0 - sig))
            pre_grad = jnp.concatenate([gate_grad, act_grad * swish], axis=1).astype(BF)
            pg[e, span] = pre_grad
            result = nn(act, wd[e]).astype(BF).astype(F32)
            back_rows[here] = nt(pre_grad, wgu[e]).astype(BF)
            result_rows[here] = (gate_col * result).astype(BF)
            pick_col = jnp.sum(result * grad_rows, axis=1, keepdims=True)
            for i, block in enumerate(blocks):
                pick = jnp.sum(
                    jnp.where(parts[i][0], pick_col[i * capacity : (i + 1) * capacity], 0.0),
                    axis=0, keepdims=True,
                )
                pick_buf[block] = jnp.where(local_rows == e, pick, pick_buf[block])

        def combine(number, result_rows, back_rows, row_of):
            block = ring.at(shifts[number])
            chosen = jnp.concatenate(
                [jnp.where(pick_rows(block, e), 1.0, 0.0).astype(BF) for e in range(experts_here)], axis=0
            )
            windows = [pl.ds(row_of(e), capacity) for e in range(experts_here)]
            if number >= 2:
                results(number - 2).wait()
            c_slot[number % 2] = tn(chosen, jnp.concatenate([result_rows[w] for w in windows], axis=0)).astype(BF)
            results(number).start()
            b_buf[block] = tn(chosen, jnp.concatenate([back_rows[w] for w in windows], axis=0)).astype(BF)

        def tile(numbers, await_weights):
            size = len(numbers) * capacity
            for p in numbers:
                grads(p).wait()

            def one(e, carry):
                chain(numbers, e, x_s, s_s, e * size, await_weights)
                return carry

            lax.fori_loop(0, experts_here, one, 0)
            for i, number in enumerate(numbers):
                combine(number, x_s, s_s, lambda e: e * size + i * capacity)

        def results(number):
            return pltpu.make_async_copy(
                c_slot.at[number % 2], c_far.at[ring.at(shifts[number])], c_sem.at[number]
            )

        def put(row, size, got):
            ob_ref[pl.ds(row, size)] = got

        b_ring = scatter_steps(ring, b_buf, *held, put)
        pick_buf[...] = jnp.zeros_like(pick_buf)
        own_entry.wait()
        gate(ring.me, True)
        tile([0], True)
        for hop in range(1, hops - 1):
            next(e_ring)
            gate(ring.at(hop), False)
            gate(ring.at(-hop), False)
            if hop == 1:
                for way in range(2):
                    far_grads(way, 0).start()
            tile([2 * hop - 1, 2 * hop], False)
        def weight_grads(e):
            for p in range(count):
                _, entries, grad_rows, gate_col = gather_rows(ring.at(shifts[p]), e)
                span = pl.ds(p * capacity, capacity)
                x_s[span] = entries
                s_s[span] = (gate_col * grad_rows).astype(BF)

            def columns(j, carry):
                cols = pl.ds(pl.multiple_of(j * 256, 256), 256)
                wgu[e, :, cols] = tn(x_s[...], pg[e, :, cols]).astype(BF)
                wd[e, :, cols] = tn(act_s[e], s_s[:, cols]).astype(BF)
                return carry

            lax.fori_loop(0, width // 256, columns, 0)

        def pieces(e, owner):
            return (
                (wgu.at[e, pl.ds(owner * quarter_up, quarter_up)], 0, quarter_up),
                (wd.at[e, pl.ds(owner * quarter_down, quarter_down)], quarter_up, quarter_down),
            )

        landing = lambda e: got_a.at[e] if e < 2 else wait_far.at[e - 2]
        fetch = lambda e: pltpu.make_async_copy(wait_far.at[e - 2], got_a.at[e % 2], f_sem.at[e - 2])

        def to_core(e):
            return [
                remote(src, landing(e).at[x, pl.ds(start, size)], a_send.at[e, x, k], a_recv.at[e, x, k], narrow=corner.core_peer)
                for x in range(2)
                for k, (src, start, size) in enumerate(pieces(e, 2 * x + 1 - corner.core))
            ]

        def to_chip(e):
            return [
                remote(src, got_far.at[e, pl.ds(start, size)], x_send.at[e, k], x_recv.at[e, k], narrow=corner.chip_peer)
                for k, (src, start, size) in enumerate(pieces(e, 2 * (1 - corner.chip) + corner.core))
            ]

        def own_out(e):
            return [
                pltpu.make_async_copy(src, keep_far.at[e, pl.ds(start, size)], o_sem.at[e, k])
                for k, (src, start, size) in enumerate(pieces(e, corner.here))
            ]

        def send_core(e):
            for c in to_core(e):
                c.start()

        def first_sum(e):
            for c in to_core(e):
                c.wait_recv()
            if e >= 2:
                fetch(e).start()
                fetch(e).wait()
            for number in range(2):
                x = 1 - corner.chip if number == 0 else corner.chip
                for src, start, size in pieces(e, 2 * x + corner.core):
                    block_add(src, src, got_a.at[e % 2, x, pl.ds(start, size)], size)
                for c in to_chip(e) if number == 0 else own_out(e):
                    c.start()

        last = [count - 3, count - 2, count - 1]
        row_at = lambda e, i: (e * 3 + i) * capacity
        next(e_ring)
        gate(ring.at(hops - 1), False)
        gate(ring.at(1 - hops), False)
        for p in last[:2]:
            grads(p).wait()

        def several(start, stop, numbers):
            def one(e, carry):
                chain(numbers, e, last_c, last_b, row_at(e, numbers[0] - last[0]))
                return carry

            lax.fori_loop(start, stop, one, 0)

        several(0, 2, last[:2])
        for _ in e_ring:
            pass
        gate(ring.at(hops), False)
        for way in range(2):
            far_grads(way, 1).wait_recv()
        next(b_ring)
        chain(last[2:], 0, last_c, last_b, row_at(0, 2))
        weight_grads(0)
        send_core(0)
        chain(last[2:], 1, last_c, last_b, row_at(1, 2))
        first_sum(0)
        next(b_ring)
        several(2, experts_here, last[:2])
        weight_grads(1)
        send_core(1)
        several(2, experts_here, last[2:])
        first_sum(1)
        for i, number in enumerate(last):
            combine(number, last_c, last_b, lambda e: row_at(e, i))
        next(b_ring)
        pick_copy = lambda k, target: remote(
            pick_buf.at[target], op_ref.at[ring.me], p_send.at[k], p_recv.at[k], wide=target
        )
        for k, target in enumerate(others):
            pick_copy(k, target).start()
        op_ref[ring.me] = pick_buf[ring.me]
        for e in range(2, experts_here):
            weight_grads(e)
            send_core(e)
            next(b_ring)
            first_sum(e)
            next(b_ring, None)
        for _ in b_ring:
            pass
        for e in range(experts_here):
            for c in to_core(e):
                c.wait_send()
            for c in to_chip(e):
                c.wait()
            for c in own_out(e):
                c.wait()
        for number in range(max(0, count - 2), count):
            results(number).wait()
        for way in range(2):
            far_grads(way, 0).wait_send()
        for k, target in enumerate(others):
            sender = (ring.me - (k + 1) + count) % count
            remote(
                pick_buf.at[sender], op_ref.at[sender], p_send.at[k], p_recv.at[k], wide=target
            ).wait_recv()
            pick_copy(k, target).wait_send()

    vmem = pl.BlockSpec(memory_space=pltpu.VMEM)
    far = pl.BlockSpec(memory_space=pl.ANY)
    shape = jax.ShapeDtypeStruct
    out_shape = [
        shape((rows, width), F32),
        shape((count, 8, rows), F32),
        shape((count, rows, width), BF),
        shape((experts_here, quarter, width), BF),
        shape((experts_here, quarter, width), BF),
        shape((experts, rows), F32),
        shape((experts_here - 2, 2, quarter, width), BF),
    ]
    dma = pltpu.SemaphoreType.DMA
    scratch = [
        pltpu.VMEM(w_gate_up.shape, BF),
        pltpu.VMEM(w_down.shape, BF),
        pltpu.VMEM((count, rows, width), BF),
        pltpu.VMEM((count, rows, width), BF),
        pltpu.VMEM((experts_here, room, 2 * ffe), BF),
        pltpu.VMEM((experts_here, room, ffe), BF),
        pltpu.VMEM((room, width), BF),
        pltpu.VMEM((room, width), BF),
        pltpu.VMEM((count, rows, width), BF),
        pltpu.VMEM((2, rows, width), BF),
        pltpu.VMEM((2, 2, quarter, width), BF),
        pltpu.VMEM((count, 8, rows), F32),
        pltpu.VMEM((count, 8, rows), F32),
        pltpu.VMEM((3 * experts_here * capacity, width), BF),
        pltpu.VMEM((3 * experts_here * capacity, width), BF),
        *scatter_scratch(count, rows, width),
        *gather_scratch(count),
        dma((2, experts_here)), dma((count,)), dma((count,)),
        dma((count - 1,)), dma((count - 1,)),
        dma((experts_here, 2, 2)), dma((experts_here, 2, 2)),
        dma((experts_here, 2)), dma((experts_here, 2)), dma((experts_here, 2)), dma((experts_here - 2,)), dma, dma((2,)), dma((2,)),
    ]
    return pl.pallas_call(
        kernel,
        out_shape=out_shape,
        in_specs=[far, far, vmem, vmem, vmem, far, far],
        out_specs=[vmem, vmem, far, far, far, vmem, far],
        scratch_shapes=scratch,
        compiler_params=pltpu.CompilerParams(
            collective_id=cid, has_side_effects=True, vmem_limit_bytes=63 * 2**20
        ),
    )(entry, grad_all, labels_all, slots, router_turned, w_gate_up, w_down)


def tail_kernel(entry_home, pick_home, shares, router_turned, mixed, cotangent, hidden, length, attn_gain, moe_gain, w_query, w_key, w_value, w_out, queries, keys, values, context, whole, lse, cosine, sine, expert_part, kept, arrived, shapes, cid):
    count, rows, width = expert_part.shape
    seq = 4 * rows
    query_cols, key_cols = w_out.shape[0], w_key.shape[1]
    cols = query_cols + 2 * key_cols
    kv_here = key_cols // HEAD_DIM
    experts_all = router_turned.shape[0]
    small_rows = (experts_all + 2 + 15) // 16 * 16
    block = -(-(cols + query_cols + small_rows) // (32 * count)) * 32
    experts, quarter, _ = kept.shape
    up_shape, down_shape = shapes
    quarter_up, quarter_down = up_shape[1] // 4, down_shape[1] // 4
    base = [0, rows, 3 * rows, 6 * rows]
    small_at = cols + query_cols

    def kernel(*refs):
        refs = list(refs)
        take = lambda number: [refs.pop(0) for _ in range(number)]
        eh_ref, pick_ref, shares_ref, wr_ref, mixed_ref, cot_ref, h_ref, len_ref, g1_ref, g2_ref = take(10)
        wq_far, wk_far, wv_far, wout_ref, q_ref, k_ref, v_ref, ctx_ref, whole_ref, lse_ref, cos_ref, sin_ref = take(12)
        c_far, keep_far, got_far = take(3)
        out_ref, gh_ref, turned_ref, go_ref, small_ref, up_ref, down_ref = take(7)
        gw, mg_s, kd, vd, p_all, dp_scr, ds_scr, dctx, dk, dv, qg, packed, small_got, expert_sum, c_ref, sum_ref, own, got, wqkv_ref, wt_ref, gain_got = take(21)
        share, fold = take(2), take(9)
        c_sem, w_sem, o_sem = take(3)
        c_scr, s_scr, g_scr = take(3), take(3), take(2)
        sm_send, sm_recv, ga_send, ga_recv = take(4)
        c_send, c_recv, x_send, x_recv, f_send, f_recv, l_sem = take(7)
        ring, corner = Ring(count), Corner()
        greet(list(ring.peers), [corner.core_peer, corner.chip_peer, corner.far_peer])
        length_here = len_ref[0]

        own_loads = lambda e: [
            pltpu.make_async_copy(keep_far.at[e], own.at[e], o_sem.at[0, e]),
            pltpu.make_async_copy(got_far.at[e], got.at[e], o_sem.at[1, e]),
        ]
        w_loads = [
            pltpu.make_async_copy(src, wqkv_ref.at[:, pl.ds(start, size)], w_sem.at[k])
            for k, (src, start, size) in enumerate(
                ((wq_far, 0, query_cols), (wk_far, query_cols, key_cols), (wv_far, query_cols + key_cols, key_cols))
            )
        ]
        for c in w_loads:
            c.start()
        for e in range(experts):
            for c in own_loads(e):
                c.start()

        def own_sum(e):
            for c in own_loads(e):
                c.wait()
            block_add(own.at[e], own.at[e], got.at[e], quarter)
            send_out(e)
            for c in send(e, core_sems, corner.core_peer) + own_copy(e):
                c.start()

        def put(row, size, value):
            expert_sum[pl.ds(row, size)] = value

        c_load = pltpu.make_async_copy(c_far, c_ref, c_sem)
        c_load.start()
        c_ring = scatter_steps(ring, c_ref, *c_scr, put)

        def places(e, owner):
            mine = own.at[e]
            return (
                (mine.at[pl.ds(0, quarter_up)], up_ref.at[e, pl.ds(owner * quarter_up, quarter_up)]),
                (mine.at[pl.ds(quarter_up, quarter_down)], down_ref.at[e, pl.ds(owner * quarter_down, quarter_down)]),
            )

        def send(e, sems, peer):
            return [
                remote(src, dst, sems[0].at[e, k], sems[1].at[e, k], narrow=peer)
                for k, (src, dst) in enumerate(places(e, corner.here))
            ]

        def forward(e, owner, sems):
            return [
                remote(dst, dst, sems[0].at[e, k], sems[1].at[e, k], narrow=corner.core_peer)
                for k, (src, dst) in enumerate(places(e, owner))
            ]

        core_sems, chip_sems, far_sems = (c_send, c_recv), (x_send, x_recv), (f_send, f_recv)

        def own_copy(e):
            return [
                pltpu.make_async_copy(src, dst, l_sem.at[e, k])
                for k, (src, dst) in enumerate(places(e, corner.here))
            ]

        def send_out(e):
            for c in send(e, chip_sems, corner.chip_peer):
                c.start()

        def pass_on(e):
            for c in forward(e, corner.chip_peer, chip_sems):
                c.wait_recv()
            for c in forward(e, corner.chip_peer, far_sems):
                c.start()

        each = experts_all // count
        picked = jnp.concatenate([pick_ref[b, 0:each] for b in range(count)], axis=0)
        held_shares = shares_ref[...]
        logit_grad = held_shares * (picked - jnp.sum(held_shares * picked, axis=0, keepdims=True))
        high = logit_grad.astype(BF)
        low = (logit_grad - high.astype(F32)).astype(BF)
        entry_grad = eh_ref[...] + (tn(high, wr_ref[...]) + tn(low, wr_ref[...]))
        mixed_here = mixed_ref[...]
        scale = lax.rsqrt(jnp.mean(mixed_here * mixed_here, axis=1, keepdims=True) + EPSILON)
        unit = mixed_here * scale
        inner = entry_grad * g2_ref[...]
        from_norm = scale * (inner - unit * jnp.mean(inner * unit, axis=1, keepdims=True))
        at = corner.here * rows + lax.broadcasted_iota(jnp.int32, (rows, 1), 0)
        valid = jnp.where(at < length_here, 1.0, 0.0)
        mixed_grad = valid * cot_ref[...].astype(F32) + from_norm
        mg_s[...] = mixed_grad
        gw[corner.here] = mixed_grad.astype(BF)
        sharing = Share(corner, gw, *share)
        sharing.start()
        entry = (unit * g2_ref[...]).astype(BF)
        small_got[3] = jnp.concatenate(
            [
                nn(high, entry) + nn(low, entry),
                jnp.sum(entry_grad * unit, axis=0, keepdims=True),
                jnp.zeros((small_rows - experts_all - 1, width), F32),
            ],
            axis=0,
        ).astype(BF)
        peers = (corner.core_peer, corner.chip_peer, corner.far_peer)
        small_copy = lambda k, peer: remote(
            small_got.at[3], small_got.at[k], sm_send.at[k], sm_recv.at[k], narrow=peer
        )
        for k, peer in enumerate(peers):
            small_copy(k, peer).start()

        for t in range(kv_here):
            kd[t] = doubled(k_ref[...].astype(F32), t).astype(BF)
            vd[t] = doubled(v_ref[...].astype(F32), t).astype(BF)

        def chances(b):
            for t in range(kv_here):
                lanes = slice(t * LANES, (t + 1) * LANES)
                stack = stacked(q_ref[pl.ds(b * rows, rows), lanes])
                log_sum = lse_ref[t * 4 + b : t * 4 + b + 1]
                for kb in range(b + 1):
                    scores = masked_scores(
                        kd[t, pl.ds(kb * rows, rows)], stack, kb * rows, b * rows, length_here, kb == b
                    )
                    p_all[t, pl.ds(base[b] + kb * rows, rows)] = jnp.exp(scores - log_sum).astype(BF)

        def pull(owner):
            dctx[owner] = nt(gw[owner], wout_ref[...]).astype(BF)

        pull(corner.here)
        c_load.wait()
        next(c_ring)
        chances(3)
        next(c_ring)
        sharing.wait_core()
        pull(corner.core_peer)
        chances(2)
        next(c_ring)
        chances(1)
        chances(0)
        sharing.wait_chip()
        own_sum(0)
        pull(corner.chip_peer)
        sharing.wait_far()
        pull(corner.far_peer)
        dk[...] = jnp.zeros_like(dk)
        dv[...] = jnp.zeros_like(dv)

        folding = Fold(corner, *fold)
        before = None
        for b in (3, 2, 1, 0):
            span = pl.ds(b * rows, rows)
            cos, sin = cos_ref[span], sin_ref[span]
            for t in range(kv_here):
                lanes = slice(t * LANES, (t + 1) * LANES)
                stack = stacked(q_ref[span, lanes])
                grad_stack = stacked(dctx[b, :, lanes])
                inner = None
                for kb in range(b + 1):
                    chance = p_all[t, pl.ds(base[b] + kb * rows, rows)]
                    grad = nt(vd[t, pl.ds(kb * rows, rows)], grad_stack)
                    dp_scr[pl.ds(kb * rows, rows)] = grad
                    one = jnp.sum(chance.astype(F32) * grad, axis=0, keepdims=True)
                    inner = one if inner is None else inner + one
                for kb in range(b + 1):
                    key_span = pl.ds(kb * rows, rows)
                    chance = p_all[t, pl.ds(base[b] + kb * rows, rows)]
                    score_grad = (chance.astype(F32) * (dp_scr[key_span] - inner)).astype(BF)
                    ds_scr[key_span] = score_grad
                    dk[t, key_span] += nn(score_grad, stack)
                    dv[t, key_span] += nn(chance, grad_stack)
                every = pl.ds(0, (b + 1) * rows)
                query_grad = unstacked(tn(kd[t, every], ds_scr[every])) * HEAD_DIM ** (-0.5)
                qg[span, lanes] = turn_lanes(query_grad, cos, -sin).astype(BF)
            low_lanes = lane_of((rows, LANES)) < HEAD_DIM
            both = lambda ref, t: ref[t, span] + pltpu.roll(ref[t, span], HEAD_DIM, 1)
            key_grad = jnp.where(low_lanes, both(dk, 0), both(dk, 1)) * HEAD_DIM ** (-0.5)
            qg[span, query_cols : query_cols + key_cols] = turn_lanes(key_grad, cos, -sin).astype(BF)
            qg[span, query_cols + key_cols :] = jnp.where(low_lanes, both(dv, 0), both(dv, 1)).astype(BF)
            if b == 3:
                for c in w_loads:
                    c.wait()
            folding.give(b, nt(qg[span], wqkv_ref[...]))
            if before is not None:
                folding.settle(before)
            before = b
            next(c_ring)
            if b == 2:
                own_sum(1)
        folding.settle(before)

        def store(row, value):
            for start in range(0, value.shape[0], 16):
                size = min(16, value.shape[0] - start)
                at_row = row + start
                packed[at_row // block, pl.ds(at_row % block, size)] = value[start : start + size].astype(BF)

        weight_grad = tn(qg[...], whole_ref[...])
        wt_ref[...] = wqkv_ref[...].astype(F32).T
        gain_one = jnp.sum(weight_grad * wt_ref[...], axis=0, keepdims=True) / g1_ref[...]
        store(0, weight_grad)
        store(cols, tn(ctx_ref[...], gw[...].reshape(seq, width)))
        rest = small_at + small_rows
        store(rest, jnp.zeros((count * block - rest, width), F32))
        for k, peer in enumerate(peers):
            small_copy(k, peer).wait_recv()
        small_sum = sum(small_got[k].astype(F32) for k in range(4))
        row_at = lax.broadcasted_iota(jnp.int32, (small_rows, width), 0)
        store(small_at, jnp.where(row_at == experts_all + 1, gain_one, small_sum))

        def finish(row, size, got):
            sum_ref[ring.me, pl.ds(row, size)] = got.astype(BF)

        sums = scatter_steps(ring, packed, *s_scr, finish)
        next(sums)
        own_sum(2)
        own_sum(3)
        for _ in sums:
            pass
        for _ in gather_steps(ring, sum_ref, *g_scr):
            pass
        whole_sum = lambda row, size: jnp.concatenate(
            [sum_ref[b] for b in range(row // block, (row + size) // block)], axis=0
        )
        gain_got[3] = sum_ref[small_at // block, small_rows - 16 : small_rows]
        gain_copy = lambda k, peer: remote(
            gain_got.at[3], gain_got.at[k], ga_send.at[k], ga_recv.at[k], narrow=peer
        )
        for k, peer in enumerate(peers):
            gain_copy(k, peer).start()
        for row in range(0, cols, block):
            turned_ref[:, row : row + block] = sum_ref[row // block].astype(F32).T.astype(BF)
        go_ref[...] = whole_sum(cols, query_cols)
        normed_grad = folding.total()
        source = h_ref[...].astype(F32)
        scale = lax.rsqrt(jnp.mean(source * source, axis=1, keepdims=True) + EPSILON)
        unit = source * scale
        inner = normed_grad * g1_ref[...]
        from_norm = scale * (inner - unit * jnp.mean(inner * unit, axis=1, keepdims=True))
        gh_ref[...] = (mg_s[...] + from_norm).astype(BF)
        for e in range(2):
            pass_on(e)
        for _ in c_ring:
            pass
        out_ref[...] = (valid * (mixed_here + expert_sum[...])).astype(BF)
        for k, peer in enumerate(peers):
            gain_copy(k, peer).wait_recv()
        gain_sum = sum(gain_got[k].astype(F32) for k in range(4))
        small_ref[0 : small_rows - 16] = sum_ref[small_at // block, 0 : small_rows - 16]
        last_rows = small_rows - 16 + lax.broadcasted_iota(jnp.int32, (16, width), 0)
        small_ref[small_rows - 16 : small_rows] = jnp.where(
            last_rows == experts_all + 1, gain_sum, gain_got[3].astype(F32)
        ).astype(BF)
        for e in range(2, experts):
            pass_on(e)
        for k, peer in enumerate(peers):
            gain_copy(k, peer).wait_send()
        for k, peer in enumerate(peers):
            small_copy(k, peer).wait_send()
        for e in range(experts):
            for c in own_copy(e):
                c.wait()
            for c in send(e, chip_sems, corner.chip_peer) + send(e, core_sems, corner.core_peer):
                c.wait_send()
            for c in forward(e, corner.core_peer, core_sems):
                c.wait_recv()
            for c in forward(e, corner.chip_peer, far_sems):
                c.wait_send()
            for c in forward(e, corner.far_peer, far_sems):
                c.wait_recv()
        sharing.drain()
        folding.drain()

    vmem = pl.BlockSpec(memory_space=pltpu.VMEM)
    far = pl.BlockSpec(memory_space=pl.ANY)
    shape = jax.ShapeDtypeStruct
    out_shape = [
        shape((rows, width), BF),
        shape((rows, width), BF),
        shape((width, cols), BF),
        shape((query_cols, width), BF),
        shape((small_rows, width), BF),
        shape(up_shape, BF),
        shape(down_shape, BF),
    ]
    scratch = [
        pltpu.VMEM((4, rows, width), BF),
        pltpu.VMEM((rows, width), F32),
        pltpu.VMEM((kv_here, seq, LANES), BF),
        pltpu.VMEM((kv_here, seq, LANES), BF),
        pltpu.VMEM((kv_here, 10 * rows, 2 * rows), BF),
        pltpu.VMEM((seq, 2 * rows), F32),
        pltpu.VMEM((seq, 2 * rows), BF),
        pltpu.VMEM((4, rows, query_cols), BF),
        pltpu.VMEM((kv_here, seq, LANES), F32),
        pltpu.VMEM((kv_here, seq, LANES), F32),
        pltpu.VMEM((seq, cols), BF),
        pltpu.VMEM((count, block, width), BF),
        pltpu.VMEM((4, small_rows, width), BF),
        pltpu.VMEM((rows, width), F32),
        pltpu.VMEM((count, rows, width), BF),
        pltpu.VMEM((count, block, width), BF),
        pltpu.VMEM((experts, quarter, width), BF),
        pltpu.VMEM((experts, quarter, width), BF),
        pltpu.VMEM((width, cols), BF),
        pltpu.VMEM((cols, width), F32),
        pltpu.VMEM((4, 16, width), BF),
        *Share.scratch(),
        *Fold.scratch(rows, width),
        pltpu.SemaphoreType.DMA,
        pltpu.SemaphoreType.DMA((3,)),
        pltpu.SemaphoreType.DMA((2, experts)),
        *scatter_scratch(count, rows, width),
        *scatter_scratch(count, block, width),
        *gather_scratch(count),
        *[pltpu.SemaphoreType.DMA((3,))] * 4,
    ] + [pltpu.SemaphoreType.DMA((experts, 2))] * 7
    return pl.pallas_call(
        kernel,
        out_shape=out_shape,
        in_specs=[vmem] * 7 + [pl.BlockSpec(memory_space=pltpu.SMEM)] + [vmem] * 2 + [far] * 3 + [vmem] * 9 + [far] * 3,
        out_specs=[vmem] * 5 + [far] * 2,
        scratch_shapes=scratch,
        compiler_params=pltpu.CompilerParams(
            collective_id=cid, has_side_effects=True, vmem_limit_bytes=62 * 2**20
        ),
    )(entry_home, pick_home, shares, router_turned, mixed, cotangent, hidden, length, attn_gain, moe_gain,
      w_query, w_key, w_value, w_out, queries, keys, values, context, whole, lse, cosine, sine, expert_part, kept, arrived)


def final_kernel(out, grad_hidden, turned, out_grad, small, up_grad, down_grad, query_cols, key_cols, experts):
    here, width, ffe2 = up_grad.shape
    ffe = down_grad.shape[1]
    step = 256
    parts = [(0, e, r) for e in range(here) for r in range(0, width, step)]
    parts += [(1, e, r) for e in range(here) for r in range(0, ffe, step)]
    parts.sort(key=lambda p: (p[1], p[0], p[2]))

    def kernel(o_in, gh_in, t_in, go_in, s_in, up_in, down_in, o_ref, gh_ref, gq, gk, gv, go, g1, g2, gr, up_ref, down_ref, low, full, in_sem, out_sem):
        near = lambda i: (up_in, down_in)[parts[i][0]].at[parts[i][1], pl.ds(parts[i][2], step)]
        away = lambda i: (up_ref, down_ref)[parts[i][0]].at[parts[i][1], pl.ds(parts[i][2], step)]
        inward = lambda i: pltpu.make_async_copy(near(i), low.at[i], in_sem.at[i])
        outward = lambda i: pltpu.make_async_copy(full.at[i], away(i), out_sem.at[i])
        for i in range(len(parts)):
            inward(i).start()
        o_ref[...] = o_in[...]
        gh_ref[...] = gh_in[...]
        gq[...] = t_in[:, :query_cols].astype(F32)
        gk[...] = t_in[:, query_cols : query_cols + key_cols].astype(F32)
        gv[...] = t_in[:, query_cols + key_cols :].astype(F32)
        go[...] = go_in[...].astype(F32)
        rows = s_in[...].astype(F32)
        g1[...] = rows[experts + 1 : experts + 2]
        g2[...] = rows[experts : experts + 1]
        gr[...] = rows[:experts]
        for i in range(len(parts)):
            inward(i).wait()
            def widen(j, carry, i=i):
                span = pl.ds(pl.multiple_of(j * 32, 32), 32)
                full[i, span] = low[i, span].astype(F32)
                return carry

            lax.fori_loop(0, step // 32, widen, 0)
            outward(i).start()
        for i in range(len(parts)):
            outward(i).wait()

    shape = jax.ShapeDtypeStruct
    vmem = pl.BlockSpec(memory_space=pltpu.VMEM)
    far = pl.BlockSpec(memory_space=pl.ANY)
    small_shapes = [
        shape(out.shape, BF), shape(grad_hidden.shape, BF), shape((width, query_cols), F32),
        shape((width, key_cols), F32), shape((width, key_cols), F32), shape(out_grad.shape, F32),
        shape((1, width), F32), shape((1, width), F32), shape((experts, width), F32),
    ]
    return pl.pallas_call(
        kernel,
        out_shape=small_shapes + [shape(up_grad.shape, F32), shape(down_grad.shape, F32)],
        in_specs=[vmem] * 5 + [far] * 2,
        out_specs=[vmem] * 9 + [far] * 2,
        scratch_shapes=[
            pltpu.VMEM((len(parts), step, width), BF),
            pltpu.VMEM((len(parts), step, width), F32),
            pltpu.SemaphoreType.DMA((len(parts),)),
            pltpu.SemaphoreType.DMA((len(parts),)),
        ],
        compiler_params=pltpu.CompilerParams(vmem_limit_bytes=62 * 2**20),
    )(out, grad_hidden, turned, out_grad, small, up_grad, down_grad)


def turn_tables(count, head_dim):
    inverse = THETA ** (-np.arange(head_dim // 2, dtype=np.float32) * np.float32(2.0 / head_dim))
    angles = np.arange(count, dtype=np.float32)[:, None] * inverse.astype(np.float32)[None, :]
    cosine, sine = np.cos(angles), np.sin(angles)
    return (
        jnp.asarray(np.concatenate([cosine] * 4, axis=1), F32),
        jnp.asarray(np.concatenate([-sine, sine] * 2, axis=1), F32),
    )


def local_general(
    hidden,
    lengths,
    routes,
    cotangent,
    attn_gain,
    w_query,
    w_key,
    w_value,
    w_out,
    moe_gain,
    w_router,
    w_gate_up,
    w_down,
):
    rows_here = hidden.shape[1]
    width = hidden.shape[2]
    seq_len = rows_here * lax.axis_size("narrow")
    head_dim = HEAD_DIM
    group_size = HEADS // KV_HEADS
    kv_here = w_key.shape[1] // head_dim
    query_cols = kv_here * group_size * head_dim
    key_cols = kv_here * head_dim
    scaling = head_dim ** (-0.5)
    block_rows = min(512, seq_len)
    block_count = seq_len // block_rows
    length_here = lengths[0]
    offset = lax.axis_index("narrow") * rows_here
    local_places = offset + jnp.arange(rows_here, dtype=jnp.int32)
    valid = (local_places < length_here).astype(jnp.float32)[:, None]
    source = hidden[0].astype(jnp.float32)
    normed, scale_one = norm_forward(source, attn_gain)
    normed_low = normed.astype(jnp.bfloat16)
    whole = lax.all_gather(normed_low, "narrow", axis=0, tiled=True)
    w_qkv = jnp.concatenate([w_query, w_key, w_value], axis=1)
    projected = jnp.dot(whole, w_qkv, preferred_element_type=jnp.float32)
    cosine, sine_part = rope_tables(seq_len, head_dim)
    query_rot = turn(
        projected[:, :query_cols].reshape(seq_len, kv_here, group_size, head_dim),
        cosine,
        sine_part,
        1.0,
    )
    key_rot = turn(
        projected[:, query_cols : query_cols + key_cols].reshape(seq_len, kv_here, head_dim),
        cosine,
        sine_part,
        1.0,
    )
    queries = (
        query_rot.astype(jnp.bfloat16)
        .reshape(block_count, block_rows, kv_here, group_size, head_dim)
        .transpose(0, 2, 3, 1, 4)
    )
    keys_low = key_rot.astype(jnp.bfloat16).transpose(1, 0, 2)
    values_low = (
        projected[:, query_cols + key_cols :]
        .astype(jnp.bfloat16)
        .reshape(seq_len, kv_here, head_dim)
        .transpose(1, 0, 2)
    )
    context, log_sums = attend_forward(queries, keys_low, values_low, length_here, scaling)
    context_rows = context.transpose(0, 3, 1, 2, 4).reshape(seq_len, query_cols)
    piece = context_rows
    attn_part = lax.psum_scatter(
        jnp.dot(piece, w_out, preferred_element_type=jnp.float32).astype(jnp.bfloat16),
        "narrow",
        scatter_dimension=0,
        tiled=True,
    ).astype(jnp.float32)
    mixed = source + attn_part
    normed_two, scale_two = norm_forward(mixed, moe_gain)
    entry = normed_two.astype(jnp.bfloat16)
    logits = jnp.dot(entry, w_router, preferred_element_type=jnp.float32)
    route_here = routes[0]
    tokens_here, picks = route_here.shape
    expert_total = w_router.shape[1]
    capacity = 2 * tokens_here * picks // expert_total
    member = (
        route_here[:, :, None] == jnp.arange(expert_total, dtype=jnp.int32)[None, None, :]
    ).astype(jnp.int32)
    flat_member = member.reshape(tokens_here * picks, expert_total)
    earlier = jnp.cumsum(flat_member, axis=0) - flat_member
    slot_index = jnp.sum(earlier * flat_member, axis=1)
    places = route_here.reshape(-1) * capacity + slot_index
    member_float = member.astype(jnp.float32)
    chosen = jnp.einsum("tke,te->tk", member_float, logits, precision=HIGHEST)
    highest = jnp.max(chosen, axis=-1, keepdims=True)
    raised = jnp.exp(chosen - highest)
    shares = raised / jnp.sum(raised, axis=-1, keepdims=True)
    gates = shares * valid
    outgoing = (
        jnp.zeros((expert_total * capacity, width), jnp.bfloat16)
        .at[places]
        .set(jnp.repeat(entry, picks, axis=0))
    )
    received = lax.all_to_all(
        outgoing.reshape(expert_total, capacity, width),
        "wide",
        split_axis=0,
        concat_axis=1,
        tiled=True,
    )
    expert_pre = jnp.einsum("erd,edf->erf", received, w_gate_up, preferred_element_type=jnp.float32)
    ffe_width = w_down.shape[1]
    gate_part = expert_pre[..., :ffe_width]
    up_part = expert_pre[..., ffe_width:]
    sigmoid_gate = jax.nn.sigmoid(gate_part)
    swish = gate_part * sigmoid_gate
    act_low = (swish * up_part).astype(jnp.bfloat16)
    expert_result = jnp.einsum(
        "erf,efd->erd", act_low, w_down, preferred_element_type=jnp.float32
    ).astype(jnp.bfloat16)
    returned = lax.all_to_all(expert_result, "wide", split_axis=1, concat_axis=0, tiled=True)
    picked = returned.reshape(expert_total * capacity, width)[places].reshape(
        tokens_here, picks, width
    )
    expert_sum = jnp.einsum("tk,tkd->td", gates, picked, precision=HIGHEST)
    output_rows = (valid * (mixed + expert_sum)).astype(jnp.bfloat16)
    grad_rows_here = cotangent[0].astype(jnp.float32) * valid
    slot_grad = (gates[:, :, None] * grad_rows_here[:, None, :]).astype(jnp.bfloat16)
    grad_outgoing = (
        jnp.zeros((expert_total * capacity, width), jnp.bfloat16)
        .at[places]
        .set(slot_grad.reshape(tokens_here * picks, width))
    )
    grad_received = lax.all_to_all(
        grad_outgoing.reshape(expert_total, capacity, width),
        "wide",
        split_axis=0,
        concat_axis=1,
        tiled=True,
    )
    act_grad = jnp.einsum("erd,efd->erf", grad_received, w_down, preferred_element_type=jnp.float32)
    down_grad = jnp.einsum(
        "erf,erd->efd", act_low, grad_received, preferred_element_type=jnp.float32
    )
    gate_grad = act_grad * up_part * sigmoid_gate * (1.0 + gate_part * (1.0 - sigmoid_gate))
    pre_grad = jnp.concatenate([gate_grad, act_grad * swish], axis=-1).astype(jnp.bfloat16)
    gate_up_grad = jnp.einsum(
        "erd,erf->edf", received, pre_grad, preferred_element_type=jnp.float32
    )
    entry_back = jnp.einsum(
        "erf,edf->erd", pre_grad, w_gate_up, preferred_element_type=jnp.float32
    ).astype(jnp.bfloat16)
    entry_home = lax.all_to_all(entry_back, "wide", split_axis=1, concat_axis=0, tiled=True)
    entry_rows = entry_home.reshape(expert_total * capacity, width)[places].reshape(
        tokens_here, picks, width
    )
    entry_grad = jnp.sum(entry_rows, axis=1, dtype=jnp.float32)
    pick_grad = jnp.einsum("td,tkd->tk", grad_rows_here, picked, precision=HIGHEST) * valid
    chosen_grad = shares * (pick_grad - jnp.sum(shares * pick_grad, axis=-1, keepdims=True))
    logit_grad = jnp.einsum("tk,tke->te", chosen_grad, member_float, precision=HIGHEST)
    router_grad = lax.dot_general(
        entry.astype(jnp.float32), logit_grad, (((0,), (0,)), ((), ())), precision=HIGHEST
    )
    entry_grad = entry_grad + lax.dot_general(
        logit_grad, w_router.astype(jnp.float32), (((1,), (1,)), ((), ())), precision=HIGHEST
    )
    mixed_from_norm, gain_two_grad = norm_backward(mixed, scale_two, moe_gain, entry_grad)
    mixed_grad = grad_rows_here + mixed_from_norm
    attn_grad_low = mixed_grad.astype(jnp.bfloat16)
    grad_whole = lax.all_gather(attn_grad_low, "narrow", axis=0, tiled=True)
    context_grad = lax.dot_general(
        grad_whole, w_out, (((1,), (1,)), ((), ())), preferred_element_type=jnp.float32
    ).astype(jnp.bfloat16)
    out_grad = lax.dot_general(
        context_rows, grad_whole, (((0,), (0,)), ((), ())), preferred_element_type=jnp.float32
    )
    context_blocks = context_grad.reshape(
        block_count, block_rows, kv_here, group_size, head_dim
    ).transpose(0, 2, 3, 1, 4)
    query_grad, key_grad, value_grad = attend_backward(
        queries, keys_low, values_low, context_blocks, log_sums, length_here, scaling
    )
    query_rows = turn(
        query_grad.transpose(0, 3, 1, 2, 4).reshape(seq_len, kv_here, group_size, head_dim),
        cosine,
        sine_part,
        -1.0,
    )
    key_rows = turn(key_grad.transpose(1, 0, 2), cosine, sine_part, -1.0)
    value_rows = value_grad.transpose(1, 0, 2)
    qkv_grad = jnp.concatenate(
        [
            query_rows.reshape(seq_len, query_cols),
            key_rows.reshape(seq_len, key_cols),
            value_rows.reshape(seq_len, key_cols),
        ],
        axis=1,
    ).astype(jnp.bfloat16)
    qkv_weight_grad = lax.dot_general(
        whole, qkv_grad, (((0,), (0,)), ((), ())), preferred_element_type=jnp.float32
    )
    piece = qkv_grad
    normed_grad = lax.psum_scatter(
        lax.dot_general(
            piece, w_qkv, (((1,), (1,)), ((), ())), preferred_element_type=jnp.float32
        ).astype(jnp.bfloat16),
        "narrow",
        scatter_dimension=0,
        tiled=True,
    ).astype(jnp.float32)
    source_from_norm, gain_one_grad = norm_backward(source, scale_one, attn_gain, normed_grad)
    grad_input = (mixed_grad + source_from_norm).astype(jnp.bfloat16)
    gate_up_grad, down_grad, router_grad, gain_one_grad, gain_two_grad = (
        lax.psum(gate_up_grad.astype(jnp.bfloat16), "narrow").astype(jnp.float32),
        lax.psum(down_grad.astype(jnp.bfloat16), "narrow").astype(jnp.float32),
        lax.psum(router_grad.astype(jnp.bfloat16), "narrow").astype(jnp.float32),
        lax.psum(gain_one_grad.astype(jnp.bfloat16), "narrow").astype(jnp.float32),
        lax.psum(gain_two_grad.astype(jnp.bfloat16), "narrow").astype(jnp.float32),
    )
    qkv_weight_grad, out_grad, router_grad, gain_one_grad, gain_two_grad = (
        lax.psum(qkv_weight_grad.astype(jnp.bfloat16), "wide").astype(jnp.float32),
        lax.psum(out_grad.astype(jnp.bfloat16), "wide").astype(jnp.float32),
        lax.psum(router_grad.astype(jnp.bfloat16), "wide").astype(jnp.float32),
        lax.psum(gain_one_grad.astype(jnp.bfloat16), "wide").astype(jnp.float32),
        lax.psum(gain_two_grad.astype(jnp.bfloat16), "wide").astype(jnp.float32),
    )
    query_weight_grad = qkv_weight_grad[:, :query_cols]
    key_weight_grad = qkv_weight_grad[:, query_cols : query_cols + key_cols]
    value_weight_grad = qkv_weight_grad[:, query_cols + key_cols :]
    return (
        output_rows[None],
        grad_input[None],
        gain_one_grad,
        query_weight_grad,
        key_weight_grad,
        value_weight_grad,
        out_grad,
        gain_two_grad,
        router_grad,
        gate_up_grad,
        down_grad,
    )


def local(
    hidden,
    lengths,
    routes,
    cotangent,
    attn_gain,
    w_query,
    w_key,
    w_value,
    w_out,
    moe_gain,
    w_router,
    w_gate_up,
    w_down,
):
    kv_here = w_key.shape[1] // HEAD_DIM
    rows, width = hidden.shape[1:]
    if lax.axis_size("narrow") != 4 or kv_here != 2 or rows != 256:
        return local_general(
            hidden, lengths, routes, cotangent, attn_gain, w_query, w_key, w_value, w_out,
            moe_gain, w_router, w_gate_up, w_down,
        )
    count = lax.axis_size("wide")
    picks = routes.shape[2]
    expert_total = w_router.shape[1]
    expert_here = w_gate_up.shape[0]
    capacity = 2 * rows * picks // expert_total
    query_cols, key_cols = w_query.shape[1], w_key.shape[1]
    cosine, sine = turn_tables(4 * rows, HEAD_DIM)
    router_turned = w_router.T
    gain_one, gain_two = attn_gain[None], moe_gain[None]
    entry, grad_all, whole, queries, keys, values, context, lse, mixed, slots, labels_all = front_kernel(
        hidden[0], cotangent[0], routes[0].T, lengths, gain_one, w_query, w_key, w_value, w_out, gain_two,
        cosine, sine, count, expert_here, 1,
    )
    entry_home, pick_home, expert_part, kept, arrived, shares, _ = middle_kernel(
        entry, grad_all, labels_all, slots, router_turned, w_gate_up, w_down, capacity, picks, 2
    )
    results = tail_kernel(
        entry_home, pick_home, shares, router_turned, mixed,
        cotangent[0], hidden[0], lengths, gain_one, gain_two, w_query, w_key, w_value, w_out, queries, keys,
        values, context, whole.reshape(4 * rows, width), lse, cosine, sine, expert_part, kept, arrived,
        (w_gate_up.shape, w_down.shape), 3,
    )
    out, grad_hidden, grad_q, grad_k, grad_v, grad_out, grad_one, grad_two, grad_router, grad_up, grad_down = final_kernel(
        *results, query_cols, key_cols, expert_total
    )
    return (
        out[None], grad_hidden[None], grad_one[0], grad_q, grad_k, grad_v, grad_out, grad_two[0], grad_router.T,
        grad_up, grad_down,
    )


def solution(mesh):
    in_specs = (
        P("wide", "narrow", None),
        P("wide"),
        P("wide", "narrow", None),
        P("wide", "narrow", None),
        P(),
        P(None, "narrow"),
        P(None, "narrow"),
        P(None, "narrow"),
        P("narrow", None),
        P(),
        P(),
        P("wide", None, None),
        P("wide", None, None),
    )
    out_specs = (
        P("wide", "narrow", None),
        P("wide", "narrow", None),
        P(),
        P(None, "narrow"),
        P(None, "narrow"),
        P(None, "narrow"),
        P("narrow", None),
        P(),
        P(),
        P("wide", None, None),
        P("wide", None, None),
    )
    return jax.shard_map(local, mesh=mesh, in_specs=in_specs, out_specs=out_specs, check_vma=False)
```
